32 devices in a mesh: region: 16 (over z, y, x), split: 2 (over core).
Axes of the slice: x: 2, y: 2, z: 4, core: 2. Of those that a mesh axis runs over, the one named last changes fastest.
Arguments:
- vectors: float32 [18432, 256], P(('region', 'split'))
- hessian: bfloat16 [96, 12, 192, 192], P(('region', 'split')), may hold values from -0.125 to 0.125
- block_cols: int32 [96, 12], P(('region', 'split')), may hold values from 0 to 17, as said below
- live_blocks: int32 [96], P(('region', 'split')), may hold values from 6 to 12, as said below
- halo_lists: int32 [16, 2, 6], P('region'), may hold values from 0 to 5, as said below
- bounds: float32 [2], replicated, as said below
Outputs:
- basis: float32 [18432, 256], P(('region', 'split'))
- projected: float32 [256, 256], replicated
The draws below stay inside these ranges and needn't reach their ends.
Inputs may be any that keep to these rules, and one draw needn't show every extreme that they name: `block_cols`: in each row the entries are distinct and entry 0 is the row's own block within its region; values below 6 name blocks of the row's region, 6 + j the j-th block received from the lower region, 12 + j the j-th from the upper region. `live_blocks`: the first block row of every region has all 12 blocks intact. `halo_lists`: each list holds distinct block indices within the region. bounds[0] < 0 < bounds[1].
All inputs are finite; a program needn't handle non-finite values.
Results may differ from the reference program's by a relative error of at most 0.0005.
The reference program's roundings to bfloat16 on the way count: a program that leaves them out, or rounds other values in their place, can miss the bound.
Values may be sent and summed in bfloat16 or wider, within the bound.
No kernel may reach another device: no remote copies, remote signals or barrier semaphores. Data moves between devices by JAX's collectives and lax.ppermute only.
A program may use at most 64 MiB of HBM per device.

```python
import math
import jax
import jax.numpy as jnp
from jax import lax

BS = 192
M = 256
NNZ = 12
HB = 6
REGION_BLOCKS = 6
BLOCK_ROWS = 96
DOFS = 18432
CANDS = 18
N_REGION = 16


def draw_vectors(key, part):
    first_key, second_key = jax.random.split(key, 2)
    base = jax.random.normal(first_key, (DOFS, M), jnp.float32)
    rising = 1.0 + 2.0 * jnp.arange(DOFS, dtype=jnp.float32) / DOFS
    column_scale = jnp.exp(jax.random.uniform(second_key, (1, M), jnp.float32, 0.0, math.log(10.0)))
    return base * rising[:, None] * column_scale


def draw_block_cols(key, part):
    scores = jax.random.randint(jax.random.fold_in(key, 11), (BLOCK_ROWS, CANDS), 0, 65536)
    scores = scores * CANDS + jnp.arange(CANDS, dtype=jnp.int32)[None, :]
    cand_index = jnp.arange(CANDS, dtype=jnp.int32)[None, :]
    own_block = jnp.arange(BLOCK_ROWS, dtype=jnp.int32) % REGION_BLOCKS
    first_row = (own_block == 0)[:, None]
    scores = jnp.where(first_row & (cand_index == CANDS - 1), 2 ** 30 - 1, scores)
    scores = jnp.where(cand_index == own_block[:, None], 2 ** 30, scores)
    return lax.top_k(scores, NNZ)[1].astype(jnp.int32)


def draw_live_blocks(key, part):
    counts = jax.random.randint(jax.random.fold_in(key, 12), (BLOCK_ROWS,), NNZ // 2, NNZ + 1)
    return counts.at[::REGION_BLOCKS].set(NNZ).astype(jnp.int32)


def draw_halo_lists(key, part):
    scores = jax.random.randint(jax.random.fold_in(key, 13), (N_REGION, 2, REGION_BLOCKS), 0, 65536)
    scores = scores * REGION_BLOCKS + jnp.arange(REGION_BLOCKS, dtype=jnp.int32)
    scores = scores.at[0, 0, REGION_BLOCKS - 1].set(-1)
    scores = scores.at[0, 1, 0].set(-1)
    order = jnp.argsort(scores, axis=-1, stable=True)
    return order[:, :, :HB].astype(jnp.int32)


def draw_bounds(key, part):
    first_key, second_key = jax.random.split(jax.random.fold_in(key, 14))
    lower_end = jax.random.uniform(first_key, (1,), jnp.float32, -0.4, -0.05)
    upper_end = jax.random.uniform(second_key, (1,), jnp.float32, 0.9, 1.4)
    return jnp.concatenate([lower_end, upper_end], 0)


def level_of(stream_key, dims, pieces, smallest, largest):
    factor_of = 1.0
    for axis_at, parts in pieces:
        draws = jax.random.uniform(jax.random.fold_in(jax.random.fold_in(stream_key, 6), axis_at), (parts,), jnp.float32, smallest / len(pieces), largest / len(pieces))
        factor_of = factor_of * jnp.repeat(jnp.exp(draws), dims[axis_at] // parts).reshape((-1,) + (1,) * (len(dims) - 1 - axis_at))
    return factor_of


def centred(stream_key, dims, scale, limit, pieces=(), kind=jnp.bfloat16):
    result = jax.random.normal(stream_key, dims, jnp.float32) * scale
    if len(pieces) > 0:
        result = level_of(stream_key, dims, pieces, -0.22, 0.18) * result
    return jnp.clip(result, min=-limit, max=limit).astype(kind)


def setup_inputs(seed: int = 0) -> dict:
    key_of = jax.random.split(jax.random.key(seed), 7)
    return {
        "vectors": draw_vectors(jax.random.fold_in(key_of[6], 71), 0),
        "hessian": centred(key_of[1], (BLOCK_ROWS, NNZ, BS, BS), (NNZ * BS) ** -0.5, 0.125, ((0, 32),)),
        "block_cols": draw_block_cols(jax.random.fold_in(key_of[6], 71), 0),
        "live_blocks": draw_live_blocks(jax.random.fold_in(key_of[6], 71), 0),
        "halo_lists": draw_halo_lists(jax.random.fold_in(key_of[6], 71), 0),
        "bounds": draw_bounds(jax.random.fold_in(key_of[6], 71), 0),
    }


def apply_blocks(operand, hessian, block_cols, live_blocks, halo_lists):
    regions = operand.reshape(N_REGION, REGION_BLOCKS, BS, M)
    hess_regions = hessian.reshape(N_REGION, REGION_BLOCKS, NNZ, BS, BS)
    cols_regions = block_cols.reshape(N_REGION, REGION_BLOCKS, NNZ)
    live_regions = live_blocks.reshape(N_REGION, REGION_BLOCKS)

    def per_region(region_index):
        own_blocks = regions[region_index]
        lower_index = (region_index - 1) % N_REGION
        upper_index = (region_index + 1) % N_REGION
        from_lower = regions[lower_index][halo_lists[lower_index, 1]]
        from_upper = regions[upper_index][halo_lists[upper_index, 0]]
        candidates = jnp.concatenate([own_blocks, from_lower, from_upper], 0)
        picked = candidates[cols_regions[region_index]].astype(jnp.float32)
        used_mask = jnp.arange(NNZ)[None, :] < live_regions[region_index][:, None]
        picked = jnp.where(used_mask[:, :, None, None], picked, jnp.zeros((), jnp.float32))
        return jnp.einsum('rkij,rkjm->rim', hess_regions[region_index].astype(jnp.float32), picked)
    product = lax.map(per_region, jnp.arange(N_REGION, dtype=jnp.int32))
    return product.reshape(DOFS, M)

def reference(vectors, hessian, block_cols, live_blocks, halo_lists, bounds):
    centre = 0.5 * (bounds[0] + bounds[1])
    half_width = 0.5 * (bounds[1] - bounds[0])
    first = apply_blocks(vectors.astype(jnp.bfloat16), hessian, block_cols, live_blocks, halo_lists)
    filtered_one = (first - centre * vectors) / half_width
    second = apply_blocks(filtered_one.astype(jnp.bfloat16), hessian, block_cols, live_blocks, halo_lists)
    filtered_two = 2.0 * (second - centre * filtered_one) / half_width - vectors
    image = apply_blocks(filtered_two.astype(jnp.bfloat16), hessian, block_cols, live_blocks, halo_lists)
    gram = jnp.dot(filtered_two.T, filtered_two, precision=lax.Precision.HIGHEST) / DOFS
    cross = jnp.dot(filtered_two.T, image, precision=lax.Precision.HIGHEST) / DOFS
    lower = jnp.linalg.cholesky(gram)
    basis = jax.scipy.linalg.solve_triangular(lower, filtered_two.T, lower=True).T
    partial_left = jax.scipy.linalg.solve_triangular(lower, cross, lower=True)
    projected = jax.scipy.linalg.solve_triangular(lower, partial_left.T, lower=True).T
    return (basis, projected)
```

```python
import functools
import jax
import jax.numpy as jnp
from jax import lax
from jax.experimental import pallas as pl
from jax.experimental.pallas import tpu as pltpu
from jax.sharding import PartitionSpec as P

AXES = ("region", "split")
VMEM = pl.BlockSpec(memory_space=pltpu.VMEM)
SMEM = pl.BlockSpec(memory_space=pltpu.SMEM)
EXACT = lax.Precision.HIGHEST
NN = (((1,), (0,)), ((), ()))
NT = (((1,), (1,)), ((), ()))
TN = (((0,), (0,)), ((), ()))
VMEM_LIMIT = 48 * 1024 * 1024
GROUP = 8
TILE = 128


def shifted(value, axis, steps):
    count = lax.axis_size(axis)
    pairs = [(source, (source + steps) % count) for source in range(count)]
    return lax.ppermute(value, axis, pairs)


def exact_dot(left, right, dims=NN):
    return lax.dot_general(left, right, dims, precision=EXACT, preferred_element_type=jnp.float32)


def kernel_call(body, out_shape, in_specs, flops, bytes_accessed):
    return pl.pallas_call(
        body,
        out_shape=out_shape,
        in_specs=in_specs,
        out_specs=jax.tree.map(lambda _: VMEM, out_shape),
        compiler_params=pltpu.CompilerParams(vmem_limit_bytes=VMEM_LIMIT),
        cost_estimate=pl.CostEstimate(flops=flops, bytes_accessed=bytes_accessed, transcendentals=0),
    )


def candidate_dot(slots_ref, hessian_ref, first_slot, index, block):
    rows, _, size, _ = hessian_ref.shape
    parts = []
    for row in range(rows):
        slot = slots_ref[row, first_slot + index]
        live = jnp.where(slot >= 0, 1.0, 0.0).astype(jnp.float32)
        stored = hessian_ref[row, jnp.maximum(slot, 0)]
        parts.append(stored * jnp.broadcast_to(live, (size, size)).astype(jnp.bfloat16))
    return jnp.dot(jnp.concatenate(parts, 0), block, preferred_element_type=jnp.float32)


def accumulate(slots_ref, hessian_ref, first_slot, operand_ref, total):
    size = hessian_ref.shape[2]
    for index in range(operand_ref.shape[0] // size):
        block = operand_ref[index * size : (index + 1) * size, :]
        term = candidate_dot(slots_ref, hessian_ref, first_slot, index, block)
        total = term if total is None else total + term
    return total


def local_body(slots_ref, hessian_ref, region_ref, out_ref):
    out_ref[...] = accumulate(slots_ref, hessian_ref, 0, region_ref, None)


def halo_total(slots_ref, hessian_ref, lower_ref, upper_ref, local_ref):
    size = hessian_ref.shape[2]
    halo = lower_ref.shape[0] // size
    own = slots_ref.shape[1] - 2 * halo
    total = accumulate(slots_ref, hessian_ref, own, lower_ref, local_ref[...])
    return accumulate(slots_ref, hessian_ref, own + halo, upper_ref, total)


def first_body(slots_ref, bounds_ref, hessian_ref, lower_ref, upper_ref, local_ref, vectors_ref, one_ref, cast_ref):
    centre = 0.5 * (bounds_ref[0] + bounds_ref[1])
    half = 0.5 * (bounds_ref[1] - bounds_ref[0])
    total = halo_total(slots_ref, hessian_ref, lower_ref, upper_ref, local_ref)
    one = (total - centre * vectors_ref[...]) / half
    one_ref[...] = one
    cast_ref[...] = one.astype(jnp.bfloat16)


def second_body(slots_ref, bounds_ref, hessian_ref, lower_ref, upper_ref, local_ref, one_ref, vectors_ref, two_ref, cast_ref):
    centre = 0.5 * (bounds_ref[0] + bounds_ref[1])
    half = 0.5 * (bounds_ref[1] - bounds_ref[0])
    total = halo_total(slots_ref, hessian_ref, lower_ref, upper_ref, local_ref)
    two = 2.0 * (total - centre * one_ref[...]) / half - vectors_ref[...]
    two_ref[...] = two
    cast_ref[...] = two.astype(jnp.bfloat16)


def third_body(slots_ref, hessian_ref, lower_ref, upper_ref, local_ref, two_ref, sums_ref):
    modes = two_ref.shape[1]
    image = halo_total(slots_ref, hessian_ref, lower_ref, upper_ref, local_ref)
    two = two_ref[...]
    sums_ref[:modes, :] = exact_dot(two, two, TN)
    sums_ref[modes:, :] = exact_dot(two, image, TN)


def over_lanes(value, lane):
    return jnp.broadcast_to(value[:, lane : lane + 1], value.shape)


def over_rows(value, row):
    return jnp.broadcast_to(value[row : row + 1, :], value.shape)


def tile_inverse(tile):
    count = tile.shape[0] // GROUP
    rows = [tile[index * GROUP : (index + 1) * GROUP, :] for index in range(count)]
    sub = lax.broadcasted_iota(jnp.int32, rows[0].shape, 0)
    lane = lax.broadcasted_iota(jnp.int32, rows[0].shape, 1)
    done = []
    for step in range(count):
        start = step * GROUP
        pivot_cols = [over_lanes(rows[step], start + col) for col in range(GROUP)]
        factors = {
            below: [over_lanes(rows[below], start + col) for col in range(GROUP)]
            for below in range(step + 1, count)
        }
        inside = (lane >= start) & (lane < start + GROUP)
        forward = jnp.where(inside, jnp.where(lane - start == sub, 1.0, 0.0), rows[step])
        solved = forward
        for pivot in range(GROUP):
            here = sub == pivot
            value = over_rows(pivot_cols[pivot], pivot)
            inverse = 1.0 / value
            ratio = pivot_cols[pivot] * inverse
            row = over_rows(forward, pivot)
            forward = jnp.where(
                here, row * lax.rsqrt(value), jnp.where(sub > pivot, forward - ratio * row, forward)
            )
            solved = jnp.where(here, row * inverse, solved - ratio * row)
            for col in range(pivot + 1, GROUP):
                top = over_rows(pivot_cols[col], pivot)
                pivot_cols[col] = jnp.where(here, top * inverse, pivot_cols[col] - ratio * top)
        done.append(jnp.where(lane < start + GROUP, forward, 0.0))
        solved_rows = [over_rows(solved, pivot) for pivot in range(GROUP)]
        for below in range(step + 1, count):
            terms = [factors[below][col] * solved_rows[col] for col in range(GROUP)]
            while len(terms) > 1:
                terms = [terms[at] + terms[at + 1] for at in range(0, len(terms), 2)]
            rows[below] = jnp.where(inside, 0.0, rows[below]) - terms[0]
    return jnp.concatenate(done, 0)


def factor_inverse(gram):
    count = gram.shape[0] // TILE

    def part(row, col):
        return gram[row * TILE : (row + 1) * TILE, col * TILE : (col + 1) * TILE]

    rest = {(row, col): part(row, col) for row in range(count) for col in range(row + 1)}
    lower = {}
    inverse = {}
    for at in range(count):
        inverse[at, at] = tile_inverse(rest[at, at])
        for row in range(at + 1, count):
            lower[row, at] = exact_dot(rest[row, at], inverse[at, at], NT)
        for row in range(at + 1, count):
            for col in range(at + 1, row + 1):
                rest[row, col] = rest[row, col] - exact_dot(lower[row, at], lower[col, at], NT)
        for col in range(at):
            mixed = exact_dot(lower[at, col], inverse[col, col])
            for mid in range(col + 1, at):
                mixed = mixed + exact_dot(lower[at, mid], inverse[mid, col])
            inverse[at, col] = -exact_dot(inverse[at, at], mixed)
    zero = jnp.zeros((TILE, TILE), jnp.float32)
    return jnp.concatenate(
        [
            jnp.concatenate([inverse[row, col] if col <= row else zero for col in range(count)], 1)
            for row in range(count)
        ],
        0,
    )


def finish_body(total_rows, sums_ref, two_ref, basis_ref, projected_ref):
    modes = two_ref.shape[1]
    inverse = factor_inverse(sums_ref[:modes, :] / total_rows)
    basis_ref[...] = exact_dot(two_ref[...], inverse, NT)
    left = exact_dot(inverse, sums_ref[modes:, :] / total_rows)
    projected_ref[...] = exact_dot(left, inverse, NT)


def summed(part):
    count = lax.axis_size(AXES)
    pieces = part.reshape(count, part.shape[0] // count, part.shape[1])
    mine = jnp.sum(lax.all_to_all(pieces, AXES, 0, 0), axis=0)
    every = jnp.broadcast_to(mine[None], pieces.shape)
    return lax.all_to_all(every, AXES, 0, 0).reshape(part.shape)


def local(vectors, hessian, block_cols, live_blocks, halo_lists, bounds):
    row_blocks, stored, size, _ = hessian.shape
    rows, modes = vectors.shape
    splits = lax.axis_size("split")
    region_blocks = row_blocks * splits
    halo_blocks = halo_lists.shape[2]
    whole = halo_blocks == region_blocks
    total_rows = rows * lax.axis_size(AXES)

    def halos(operand, region):
        if whole:
            return shifted(operand, "region", 1), shifted(operand, "region", -1), 0
        width = modes // splits
        start = lax.axis_index("split") * width
        blocks = region.reshape(region_blocks, size, modes)
        share = lambda listed: lax.dynamic_slice_in_dim(blocks[listed], start, width, 2).reshape(-1, width)
        lower = shifted(share(halo_lists[0, 1]), "region", 1)
        upper = shifted(share(halo_lists[0, 0]), "region", -1)
        return lower, upper, 1

    def exchange(operand):
        region = lax.all_gather(operand, "split", axis=0, tiled=True)
        lower, upper, axis = halos(operand, region)
        gather = lambda value: lax.all_gather(value, "split", axis=axis, tiled=True)
        return region, lower, upper, gather

    if whole:
        lower_order = shifted(halo_lists[0, 1], "region", 1)
        upper_order = shifted(halo_lists[0, 0], "region", -1)
    else:
        lower_order = upper_order = jnp.arange(halo_blocks, dtype=jnp.int32)
    places = jnp.concatenate(
        [
            jnp.arange(region_blocks, dtype=jnp.int32),
            region_blocks + lower_order,
            region_blocks + halo_blocks + upper_order,
        ]
    )
    place = places[block_cols]
    candidates = region_blocks + 2 * halo_blocks
    order = jnp.arange(stored, dtype=jnp.int32)[None, None, :]
    meets = place[:, None, :] == jnp.arange(candidates, dtype=jnp.int32)[None, :, None]
    meets = meets & (order < live_blocks[:, None, None])
    slots = jnp.max(jnp.where(meets, order, -1), axis=2)

    wide = jax.ShapeDtypeStruct((rows, modes), jnp.float32)
    narrow = jax.ShapeDtypeStruct((rows, modes), jnp.bfloat16)
    work = 2 * rows * size * modes
    traffic = hessian.size * 2 + 3 * rows * modes * 4

    def local_part(region):
        call = kernel_call(local_body, wide, [SMEM, VMEM, VMEM], work * region_blocks, traffic)
        return call(slots, hessian, region)

    def step(body, outs, operand, scalars, extra):
        region, lower, upper, gather = exchange(operand)
        partial = local_part(region)
        specs = [SMEM] * (1 + len(scalars)) + [VMEM] * (4 + len(extra))
        call = kernel_call(body, outs, specs, work * 2 * halo_blocks, traffic)
        return call(slots, *scalars, hessian, gather(lower), gather(upper), partial, *extra)

    one, one_cast = step(first_body, (wide, narrow), vectors.astype(jnp.bfloat16), (bounds,), (vectors,))
    two, two_cast = step(second_body, (wide, narrow), one_cast, (bounds,), (one, vectors))
    pair = jax.ShapeDtypeStruct((2 * modes, modes), jnp.float32)
    sums = summed(step(third_body, pair, two_cast, (), (two,)))
    square = jax.ShapeDtypeStruct((modes, modes), jnp.float32)
    call = kernel_call(
        functools.partial(finish_body, float(total_rows)), (wide, square), [VMEM, VMEM], 8 * rows * modes * modes, traffic
    )
    return call(sums, two)


def solution(mesh):
    placed = (
        P(("region", "split"), None),
        P(("region", "split"), None, None, None),
        P(("region", "split"), None),
        P(("region", "split")),
        P("region", None, None),
        P(),
    )
    return jax.shard_map(
        local,
        mesh=mesh,
        in_specs=placed,
        out_specs=(P(("region", "split"), None), P()),
        check_vma=False,
    )
```

```python
import functools
import jax
import jax.numpy as jnp
from jax import lax
from jax.experimental import pallas as pl
from jax.experimental.pallas import tpu as pltpu
from jax.sharding import PartitionSpec as P

AXES = ("region", "split")
VMEM = pl.BlockSpec(memory_space=pltpu.VMEM)
SMEM = pl.BlockSpec(memory_space=pltpu.SMEM)
EXACT = lax.Precision.HIGHEST
NN = (((1,), (0,)), ((), ()))
NT = (((1,), (1,)), ((), ()))
TN = (((0,), (0,)), ((), ()))
VMEM_LIMIT = 48 * 1024 * 1024
GROUP = 8
TILE = 128
LIST_ROWS = 16


def shifted(value, axis, steps):
    count = lax.axis_size(axis)
    pairs = [(source, (source + steps) % count) for source in range(count)]
    return lax.ppermute(value, axis, pairs)


def exact_dot(left, right, dims=NN):
    return lax.dot_general(left, right, dims, precision=EXACT, preferred_element_type=jnp.float32)


def kernel_call(body, out_shape, in_specs, flops, bytes_accessed):
    return pl.pallas_call(
        body,
        out_shape=out_shape,
        in_specs=in_specs,
        out_specs=jax.tree.map(lambda _: VMEM, out_shape),
        compiler_params=pltpu.CompilerParams(vmem_limit_bytes=VMEM_LIMIT),
        cost_estimate=pl.CostEstimate(flops=flops, bytes_accessed=bytes_accessed, transcendentals=0),
    )


def candidate_dot(slots_ref, hessian_ref, first_slot, index, block):
    rows, _, size, _ = hessian_ref.shape
    parts = []
    for row in range(rows):
        slot = slots_ref[row, first_slot + index]
        live = jnp.where(slot >= 0, 1.0, 0.0).astype(jnp.float32)
        stored = hessian_ref[row, jnp.maximum(slot, 0)]
        parts.append(stored * jnp.broadcast_to(live, (size, size)).astype(jnp.bfloat16))
    return jnp.dot(jnp.concatenate(parts, 0), block, preferred_element_type=jnp.float32)


def accumulate(slots_ref, hessian_ref, first_slot, operand_ref, total):
    size = hessian_ref.shape[2]
    shards, shard_rows, _ = operand_ref.shape
    each = shard_rows // size
    for index in range(shards * each):
        start = index % each * size
        block = operand_ref[index // each, start : start + size, :]
        term = candidate_dot(slots_ref, hessian_ref, first_slot, index, block)
        total = term if total is None else total + term
    return total


def local_body(slots_ref, hessian_ref, region_ref, out_ref):
    out_ref[...] = accumulate(slots_ref, hessian_ref, 0, region_ref, None)


def halo_total(slots_ref, hessian_ref, lower_ref, upper_ref, local_ref):
    size = hessian_ref.shape[2]
    halo = lower_ref.shape[0] * (lower_ref.shape[1] // size)
    total = accumulate(slots_ref, hessian_ref, 0, lower_ref, local_ref[...])
    return accumulate(slots_ref, hessian_ref, halo, upper_ref, total)


def first_body(slots_ref, bounds_ref, hessian_ref, lower_ref, upper_ref, local_ref, vectors_ref, one_ref, cast_ref):
    centre = 0.5 * (bounds_ref[0] + bounds_ref[1])
    half = 0.5 * (bounds_ref[1] - bounds_ref[0])
    total = halo_total(slots_ref, hessian_ref, lower_ref, upper_ref, local_ref)
    one = (total - centre * vectors_ref[...]) / half
    one_ref[...] = one
    cast_ref[...] = one.astype(jnp.bfloat16)


def second_body(slots_ref, bounds_ref, hessian_ref, lower_ref, upper_ref, local_ref, one_ref, vectors_ref, two_ref, cast_ref):
    centre = 0.5 * (bounds_ref[0] + bounds_ref[1])
    half = 0.5 * (bounds_ref[1] - bounds_ref[0])
    total = halo_total(slots_ref, hessian_ref, lower_ref, upper_ref, local_ref)
    two = 2.0 * (total - centre * one_ref[...]) / half - vectors_ref[...]
    two_ref[...] = two
    cast_ref[...] = two.astype(jnp.bfloat16)


def third_body(slots_ref, hessian_ref, lower_ref, upper_ref, local_ref, two_ref, sums_ref):
    modes = two_ref.shape[1]
    image = halo_total(slots_ref, hessian_ref, lower_ref, upper_ref, local_ref)
    two = two_ref[...]
    sums_ref[:modes, :] = exact_dot(two, two, TN)
    sums_ref[modes:, :] = exact_dot(two, image, TN)


def over_lanes(value, lane):
    return jnp.broadcast_to(value[:, lane : lane + 1], value.shape)


def over_rows(value, row):
    return jnp.broadcast_to(value[row : row + 1, :], value.shape)


def tile_inverse(tile):
    count = tile.shape[0] // GROUP
    rows = [tile[index * GROUP : (index + 1) * GROUP, :] for index in range(count)]
    sub = lax.broadcasted_iota(jnp.int32, rows[0].shape, 0)
    lane = lax.broadcasted_iota(jnp.int32, rows[0].shape, 1)
    done = []
    for step in range(count):
        start = step * GROUP
        pivot_cols = [over_lanes(rows[step], start + col) for col in range(GROUP)]
        factors = {
            below: [over_lanes(rows[below], start + col) for col in range(GROUP)]
            for below in range(step + 1, count)
        }
        inside = (lane >= start) & (lane < start + GROUP)
        forward = jnp.where(inside, jnp.where(lane - start == sub, 1.0, 0.0), rows[step])
        solved = forward
        for pivot in range(GROUP):
            here = sub == pivot
            value = over_rows(pivot_cols[pivot], pivot)
            inverse = 1.0 / value
            ratio = pivot_cols[pivot] * inverse
            row = over_rows(forward, pivot)
            forward = jnp.where(
                here, row * lax.rsqrt(value), jnp.where(sub > pivot, forward - ratio * row, forward)
            )
            solved = jnp.where(here, row * inverse, solved - ratio * row)
            for col in range(pivot + 1, GROUP):
                top = over_rows(pivot_cols[col], pivot)
                pivot_cols[col] = jnp.where(here, top * inverse, pivot_cols[col] - ratio * top)
        done.append(jnp.where(lane < start + GROUP, forward, 0.0))
        solved_rows = [over_rows(solved, pivot) for pivot in range(GROUP)]
        for below in range(step + 1, count):
            terms = [factors[below][col] * solved_rows[col] for col in range(GROUP)]
            while len(terms) > 1:
                terms = [terms[at] + terms[at + 1] for at in range(0, len(terms), 2)]
            rows[below] = jnp.where(inside, 0.0, rows[below]) - terms[0]
    return jnp.concatenate(done, 0)


def factor_inverse(gram):
    count = gram.shape[0] // TILE

    def part(row, col):
        return gram[row * TILE : (row + 1) * TILE, col * TILE : (col + 1) * TILE]

    rest = {(row, col): part(row, col) for row in range(count) for col in range(row + 1)}
    lower = {}
    inverse = {}
    for at in range(count):
        inverse[at, at] = tile_inverse(rest[at, at])
        for row in range(at + 1, count):
            lower[row, at] = exact_dot(rest[row, at], inverse[at, at], NT)
        for row in range(at + 1, count):
            for col in range(at + 1, row + 1):
                rest[row, col] = rest[row, col] - exact_dot(lower[row, at], lower[col, at], NT)
        for col in range(at):
            mixed = exact_dot(lower[at, col], inverse[col, col])
            for mid in range(col + 1, at):
                mixed = mixed + exact_dot(lower[at, mid], inverse[mid, col])
            inverse[at, col] = -exact_dot(inverse[at, at], mixed)
    zero = jnp.zeros((TILE, TILE), jnp.float32)
    return jnp.concatenate(
        [
            jnp.concatenate([inverse[row, col] if col <= row else zero for col in range(count)], 1)
            for row in range(count)
        ],
        0,
    )


def finish_body(total_rows, sums_ref, two_ref, basis_ref, projected_ref):
    modes = two_ref.shape[1]
    inverse = factor_inverse(sums_ref[:modes, :] / total_rows)
    basis_ref[...] = exact_dot(two_ref[...], inverse, NT)
    left = exact_dot(inverse, sums_ref[modes:, :] / total_rows)
    projected_ref[...] = exact_dot(left, inverse, NT)


def region_groups():
    count = lax.axis_size("region")
    near = 1
    while near * near < count:
        near *= 2
    if count % near:
        near = count
    minor = [[first + at for at in range(near)] for first in range(0, count, near)]
    major = [[at + first for first in range(0, count, near)] for at in range(near)]
    return [groups for groups in (minor, major) if len(groups[0]) > 1]


def summed(part):
    width = part.shape[1]
    stages = [("split", None, lax.axis_size("split"))]
    stages += [("region", groups, len(groups[0])) for groups in region_groups()]
    value = part
    for axis, groups, count in stages:
        pieces = value.reshape(count, value.shape[0] // count, width)
        value = jnp.sum(lax.all_to_all(pieces, axis, 0, 0, axis_index_groups=groups), axis=0)
    for axis, groups, count in reversed(stages):
        if groups is None:
            value = lax.all_gather(value, axis, axis=0, tiled=True)
        else:
            every = jnp.broadcast_to(value[None], (count,) + value.shape)
            value = lax.all_to_all(every, axis, 0, 0, axis_index_groups=groups).reshape(-1, width)
    return value


def local(vectors, hessian, block_cols, live_blocks, halo_lists, bounds):
    row_blocks, stored, size, _ = hessian.shape
    rows, modes = vectors.shape
    splits = lax.axis_size("split")
    region_blocks = row_blocks * splits
    halo_blocks = halo_lists.shape[2]
    whole = halo_blocks == region_blocks and region_blocks <= 256
    total_rows = rows * lax.axis_size(AXES)

    def halos(operand, region):
        if whole:
            return shifted(operand, "region", 1), shifted(operand, "region", -1)
        width = modes // splits
        start = lax.axis_index("split") * width
        blocks = region[:, :rows].reshape(region_blocks, size, modes)
        share = lambda listed: lax.dynamic_slice_in_dim(blocks[listed], start, width, 2).reshape(-1, width)
        lower = shifted(share(halo_lists[0, 1]), "region", 1)
        upper = shifted(share(halo_lists[0, 0]), "region", -1)
        return lower, upper

    def gather(value):
        if whole:
            return lax.all_gather(value, "split", axis=0)
        return lax.all_gather(value, "split", axis=1, tiled=True)[None]

    listed = jnp.pad(halo_lists[0], ((0, LIST_ROWS - 2), (0, modes - halo_blocks)))
    first = vectors.astype(jnp.bfloat16)
    if whole:
        first = jnp.concatenate([first, listed.astype(jnp.bfloat16)], 0)
    first_region = lax.all_gather(first, "split", axis=0)
    first_lower, first_upper = halos(first, first_region)
    if whole:
        lower_order = first_lower[rows + 1, :halo_blocks].astype(jnp.int32)
        upper_order = first_upper[rows, :halo_blocks].astype(jnp.int32)
    else:
        lower_order = upper_order = jnp.arange(halo_blocks, dtype=jnp.int32)
    near_places = jnp.arange(region_blocks, dtype=jnp.int32)
    lower_places = region_blocks + lower_order
    upper_places = region_blocks + halo_blocks + upper_order

    order = jnp.arange(stored, dtype=jnp.int32)[None, None, :]
    live = order < live_blocks[:, None, None]

    def slots_of(place, first_place, count):
        meets = place[:, None, :] == first_place + jnp.arange(count, dtype=jnp.int32)[None, :, None]
        return jnp.max(jnp.where(meets & live, order, -1), axis=2)

    near_slots = slots_of(block_cols, 0, region_blocks)
    places = jnp.concatenate([near_places, lower_places, upper_places])
    far_slots = slots_of(places[block_cols], region_blocks, 2 * halo_blocks)

    wide = jax.ShapeDtypeStruct((rows, modes), jnp.float32)
    narrow = jax.ShapeDtypeStruct((rows, modes), jnp.bfloat16)
    work = 2 * rows * size * modes
    traffic = hessian.size * 2 + 3 * rows * modes * 4

    def local_part(region):
        call = kernel_call(local_body, wide, [SMEM, VMEM, VMEM], work * region_blocks, traffic)
        return call(near_slots, hessian, region)

    def step(body, outs, region, lower, upper, scalars, extra):
        partial = local_part(region)
        specs = [SMEM] * (1 + len(scalars)) + [VMEM] * (4 + len(extra))
        call = kernel_call(body, outs, specs, work * 2 * halo_blocks, traffic)
        return call(far_slots, *scalars, hessian, gather(lower), gather(upper), partial, *extra)

    def later(body, outs, operand, scalars, extra):
        region = lax.all_gather(operand, "split", axis=0)
        return step(body, outs, region, *halos(operand, region), scalars, extra)

    one, one_cast = step(first_body, (wide, narrow), first_region, first_lower, first_upper, (bounds,), (vectors,))
    two, two_cast = later(second_body, (wide, narrow), one_cast, (bounds,), (one, vectors))
    pair = jax.ShapeDtypeStruct((2 * modes, modes), jnp.float32)
    sums = summed(later(third_body, pair, two_cast, (), (two,)))
    square = jax.ShapeDtypeStruct((modes, modes), jnp.float32)
    call = kernel_call(
        functools.partial(finish_body, float(total_rows)), (wide, square), [VMEM, VMEM], 8 * rows * modes * modes, traffic
    )
    return call(sums, two)


def solution(mesh):
    placed = (
        P(("region", "split"), None),
        P(("region", "split"), None, None, None),
        P(("region", "split"), None),
        P(("region", "split")),
        P("region", None, None),
        P(),
    )
    return jax.shard_map(
        local,
        mesh=mesh,
        in_specs=placed,
        out_specs=(P(("region", "split"), None), P()),
        check_vma=False,
    )
```

```python
import functools
import jax
import jax.numpy as jnp
from jax import lax
from jax.experimental import pallas as pl
from jax.experimental.pallas import tpu as pltpu
from jax.sharding import PartitionSpec as P

AXES = ("region", "split")
VMEM = pl.BlockSpec(memory_space=pltpu.VMEM)
SMEM = pl.BlockSpec(memory_space=pltpu.SMEM)
EXACT = lax.Precision.HIGHEST
NN = (((1,), (0,)), ((), ()))
NT = (((1,), (1,)), ((), ()))
TN = (((0,), (0,)), ((), ()))
GROUP = 8
TILE = 128
LIST_ROWS = 16


def shifted(value, axis, steps):
    count = lax.axis_size(axis)
    pairs = [(source, (source + steps) % count) for source in range(count)]
    return lax.ppermute(value, axis, pairs)


def exact_dot(left, right, dims=NN):
    return lax.dot_general(left, right, dims, precision=EXACT, preferred_element_type=jnp.float32)


def kernel_call(body, out_shape, in_specs, flops, bytes_accessed, vmem=20):
    return pl.pallas_call(
        body,
        out_shape=out_shape,
        in_specs=in_specs,
        out_specs=jax.tree.map(lambda _: VMEM, out_shape),
        compiler_params=pltpu.CompilerParams(vmem_limit_bytes=vmem * 1024 * 1024),
        cost_estimate=pl.CostEstimate(flops=flops, bytes_accessed=bytes_accessed, transcendentals=0),
    )


def candidate_dot(slots_ref, hessian_ref, first_slot, index, block):
    rows, _, size, _ = hessian_ref.shape
    parts = []
    for row in range(rows):
        slot = slots_ref[row, first_slot + index]
        live = jnp.where(slot >= 0, 1.0, 0.0).astype(jnp.float32)
        stored = hessian_ref[row, jnp.maximum(slot, 0)]
        parts.append(stored * jnp.broadcast_to(live, (size, size)).astype(jnp.bfloat16))
    return jnp.dot(jnp.concatenate(parts, 0), block, preferred_element_type=jnp.float32)


def accumulate(slots_ref, hessian_ref, first_slot, operand_ref, total):
    size = hessian_ref.shape[2]
    shards, shard_rows, _ = operand_ref.shape
    each = shard_rows // size
    for index in range(shards * each):
        start = index % each * size
        block = operand_ref[index // each, start : start + size, :]
        term = candidate_dot(slots_ref, hessian_ref, first_slot, index, block)
        total = term if total is None else total + term
    return total


def local_body(slots_ref, hessian_ref, region_ref, out_ref):
    out_ref[...] = accumulate(slots_ref, hessian_ref, 0, region_ref, None)


def lower_body(slots_ref, hessian_ref, lower_ref, local_ref, out_ref):
    out_ref[...] = accumulate(slots_ref, hessian_ref, 0, lower_ref, local_ref[...])


def first_body(slots_ref, bounds_ref, hessian_ref, upper_ref, partial_ref, vectors_ref, one_ref, cast_ref):
    centre = 0.5 * (bounds_ref[0] + bounds_ref[1])
    half = 0.5 * (bounds_ref[1] - bounds_ref[0])
    total = accumulate(slots_ref, hessian_ref, 0, upper_ref, partial_ref[...])
    one = (total - centre * vectors_ref[...]) / half
    one_ref[...] = one
    cast_ref[...] = one.astype(jnp.bfloat16)


def second_body(slots_ref, bounds_ref, hessian_ref, upper_ref, partial_ref, one_ref, vectors_ref, two_ref, cast_ref):
    centre = 0.5 * (bounds_ref[0] + bounds_ref[1])
    half = 0.5 * (bounds_ref[1] - bounds_ref[0])
    total = accumulate(slots_ref, hessian_ref, 0, upper_ref, partial_ref[...])
    two = 2.0 * (total - centre * one_ref[...]) / half - vectors_ref[...]
    two_ref[...] = two
    cast_ref[...] = two.astype(jnp.bfloat16)


def third_body(slots_ref, hessian_ref, upper_ref, partial_ref, two_ref, sums_ref):
    modes = two_ref.shape[1]
    image = accumulate(slots_ref, hessian_ref, 0, upper_ref, partial_ref[...])
    two = two_ref[...]
    sums_ref[:modes, :] = exact_dot(two, two, TN)
    sums_ref[modes:, :] = exact_dot(two, image, TN)


def over_lanes(value, lane):
    return jnp.broadcast_to(value[:, lane : lane + 1], value.shape)


def over_rows(value, row):
    return jnp.broadcast_to(value[row : row + 1, :], value.shape)


def tile_inverse(tile):
    count = tile.shape[0] // GROUP
    rows = [tile[index * GROUP : (index + 1) * GROUP, :] for index in range(count)]
    sub = lax.broadcasted_iota(jnp.int32, rows[0].shape, 0)
    lane = lax.broadcasted_iota(jnp.int32, rows[0].shape, 1)
    done = []
    for step in range(count):
        start = step * GROUP
        pivot_cols = [over_lanes(rows[step], start + col) for col in range(GROUP)]
        factors = {
            below: [over_lanes(rows[below], start + col) for col in range(GROUP)]
            for below in range(step + 1, count)
        }
        inside = (lane >= start) & (lane < start + GROUP)
        forward = jnp.where(inside, jnp.where(lane - start == sub, 1.0, 0.0), rows[step])
        solved = forward
        for pivot in range(GROUP):
            here = sub == pivot
            value = over_rows(pivot_cols[pivot], pivot)
            inverse = 1.0 / value
            ratio = pivot_cols[pivot] * inverse
            row = over_rows(forward, pivot)
            forward = jnp.where(
                here, row * lax.rsqrt(value), jnp.where(sub > pivot, forward - ratio * row, forward)
            )
            solved = jnp.where(here, row * inverse, solved - ratio * row)
            for col in range(pivot + 1, GROUP):
                top = over_rows(pivot_cols[col], pivot)
                pivot_cols[col] = jnp.where(here, top * inverse, pivot_cols[col] - ratio * top)
        done.append(jnp.where(lane < start + GROUP, forward, 0.0))
        solved_rows = [over_rows(solved, pivot) for pivot in range(GROUP)]
        for below in range(step + 1, count):
            terms = [factors[below][col] * solved_rows[col] for col in range(GROUP)]
            while len(terms) > 1:
                terms = [terms[at] + terms[at + 1] for at in range(0, len(terms), 2)]
            rows[below] = jnp.where(inside, 0.0, rows[below]) - terms[0]
    return jnp.concatenate(done, 0)


def factor_inverse(gram):
    count = gram.shape[0] // TILE

    def part(row, col):
        return gram[row * TILE : (row + 1) * TILE, col * TILE : (col + 1) * TILE]

    rest = {(row, col): part(row, col) for row in range(count) for col in range(row + 1)}
    lower = {}
    inverse = {}
    for at in range(count):
        inverse[at, at] = tile_inverse(rest[at, at])
        for row in range(at + 1, count):
            lower[row, at] = exact_dot(rest[row, at], inverse[at, at], NT)
        for row in range(at + 1, count):
            for col in range(at + 1, row + 1):
                rest[row, col] = rest[row, col] - exact_dot(lower[row, at], lower[col, at], NT)
        for col in range(at):
            mixed = exact_dot(lower[at, col], inverse[col, col])
            for mid in range(col + 1, at):
                mixed = mixed + exact_dot(lower[at, mid], inverse[mid, col])
            inverse[at, col] = -exact_dot(inverse[at, at], mixed)
    zero = jnp.zeros((TILE, TILE), jnp.float32)
    return jnp.concatenate(
        [
            jnp.concatenate([inverse[row, col] if col <= row else zero for col in range(count)], 1)
            for row in range(count)
        ],
        0,
    )


def finish_body(total_rows, sums_ref, two_ref, basis_ref, projected_ref):
    modes = two_ref.shape[1]
    inverse = factor_inverse(sums_ref[:modes, :] / total_rows)
    basis_ref[...] = exact_dot(two_ref[...], inverse, NT)
    left = exact_dot(inverse, sums_ref[modes:, :] / total_rows)
    projected_ref[...] = exact_dot(left, inverse, NT)


def region_groups():
    count = lax.axis_size("region")
    near = 1
    while near * near < count:
        near *= 2
    if count % near:
        near = count
    minor = [[first + at for at in range(near)] for first in range(0, count, near)]
    major = [[at + first for first in range(0, count, near)] for at in range(near)]
    return [groups for groups in (minor, major) if len(groups[0]) > 1]


def summed(part):
    width = part.shape[1]
    stages = [("split", None, lax.axis_size("split"))]
    stages += [("region", groups, len(groups[0])) for groups in region_groups()]
    value = part
    for axis, groups, count in stages:
        pieces = value.reshape(count, value.shape[0] // count, width)
        value = jnp.sum(lax.all_to_all(pieces, axis, 0, 0, axis_index_groups=groups), axis=0)
    for axis, groups, count in reversed(stages):
        value = lax.all_gather(value, axis, axis=0, tiled=True, axis_index_groups=groups)
    return value


def local(vectors, hessian, block_cols, live_blocks, halo_lists, bounds):
    row_blocks, stored, size, _ = hessian.shape
    rows, modes = vectors.shape
    splits = lax.axis_size("split")
    region_blocks = row_blocks * splits
    halo_blocks = halo_lists.shape[2]
    whole = halo_blocks == region_blocks and region_blocks <= 256
    total_rows = rows * lax.axis_size(AXES)

    def halos(operand, region):
        if whole:
            return shifted(operand, "region", 1), shifted(operand, "region", -1)
        width = modes // splits
        start = lax.axis_index("split") * width
        blocks = region[:, :rows].reshape(region_blocks, size, modes)
        share = lambda listed: lax.dynamic_slice_in_dim(blocks[listed], start, width, 2).reshape(-1, width)
        lower = shifted(share(halo_lists[0, 1]), "region", 1)
        upper = shifted(share(halo_lists[0, 0]), "region", -1)
        return lower, upper

    def gather(value):
        if whole:
            return lax.all_gather(value, "split", axis=0)
        return lax.all_gather(value, "split", axis=1, tiled=True)[None]

    listed = jnp.pad(halo_lists[0], ((0, LIST_ROWS - 2), (0, modes - halo_blocks)))
    first = vectors.astype(jnp.bfloat16)
    if whole:
        first = jnp.concatenate([first, listed.astype(jnp.bfloat16)], 0)
    first_region = lax.all_gather(first, "split", axis=0)
    first_lower, first_upper = halos(first, first_region)
    if whole:
        lower_order = first_lower[rows + 1, :halo_blocks].astype(jnp.int32)
        upper_order = first_upper[rows, :halo_blocks].astype(jnp.int32)
    else:
        lower_order = upper_order = jnp.arange(halo_blocks, dtype=jnp.int32)
    order = jnp.arange(stored, dtype=jnp.int32)[None, None, :]
    live = order < live_blocks[:, None, None]

    def slots_of(place, first_place, count):
        meets = place[:, None, :] == first_place + jnp.arange(count, dtype=jnp.int32)[None, :, None]
        return jnp.max(jnp.where(meets & live, order, -1), axis=2)

    def halo_slots(first_place, listed_order):
        inside = (block_cols >= first_place) & (block_cols < first_place + halo_blocks)
        place = listed_order[jnp.clip(block_cols - first_place, 0, halo_blocks - 1)]
        return slots_of(jnp.where(inside, place, -1), 0, halo_blocks)

    near_slots = slots_of(block_cols, 0, region_blocks)
    lower_slots = halo_slots(region_blocks, lower_order)
    upper_slots = halo_slots(region_blocks + halo_blocks, upper_order)

    wide = jax.ShapeDtypeStruct((rows, modes), jnp.float32)
    narrow = jax.ShapeDtypeStruct((rows, modes), jnp.bfloat16)
    work = 2 * rows * size * modes
    traffic = hessian.size * 2 + 3 * rows * modes * 4

    def local_part(region):
        call = kernel_call(local_body, wide, [SMEM, VMEM, VMEM], work * region_blocks, traffic)
        return call(near_slots, hessian, region)

    def step(body, outs, region, lower, upper, scalars, extra):
        partial = local_part(region)
        call = kernel_call(lower_body, wide, [SMEM] + [VMEM] * 3, work * halo_blocks, traffic)
        partial = call(lower_slots, hessian, gather(lower), partial)
        specs = [SMEM] * (1 + len(scalars)) + [VMEM] * (3 + len(extra))
        call = kernel_call(body, outs, specs, work * halo_blocks, traffic)
        return call(upper_slots, *scalars, hessian, gather(upper), partial, *extra)

    def later(body, outs, operand, scalars, extra):
        region = lax.all_gather(operand, "split", axis=0)
        return step(body, outs, region, *halos(operand, region), scalars, extra)

    one, one_cast = step(first_body, (wide, narrow), first_region, first_lower, first_upper, (bounds,), (vectors,))
    two, two_cast = later(second_body, (wide, narrow), one_cast, (bounds,), (one, vectors))
    pair = jax.ShapeDtypeStruct((2 * modes, modes), jnp.float32)
    sums = summed(later(third_body, pair, two_cast, (), (two,)))
    square = jax.ShapeDtypeStruct((modes, modes), jnp.float32)
    call = kernel_call(
        functools.partial(finish_body, float(total_rows)), (wide, square), [VMEM, VMEM], 8 * rows * modes * modes, traffic
    )
    return call(sums, two)


def solution(mesh):
    placed = (
        P(("region", "split"), None),
        P(("region", "split"), None, None, None),
        P(("region", "split"), None),
        P(("region", "split")),
        P("region", None, None),
        P(),
    )
    return jax.shard_map(
        local,
        mesh=mesh,
        in_specs=placed,
        out_specs=(P(("region", "split"), None), P()),
        check_vma=False,
    )
```

```python
import functools
import jax
import jax.numpy as jnp
from jax import lax
from jax.experimental import pallas as pl
from jax.experimental.pallas import tpu as pltpu
from jax.sharding import PartitionSpec as P

AXES = ("region", "split")
VMEM = pl.BlockSpec(memory_space=pltpu.VMEM)
SMEM = pl.BlockSpec(memory_space=pltpu.SMEM)
EXACT = lax.Precision.HIGHEST
NN = (((1,), (0,)), ((), ()))
NT = (((1,), (1,)), ((), ()))
TN = (((0,), (0,)), ((), ()))
GROUP = 8
TILE = 128
VMEM_LIMIT = 20 * 1024 * 1024
LIST_ROWS = 16
PIECES = 4


def shifted(value, axis, steps):
    count = lax.axis_size(axis)
    pairs = [(source, (source + steps) % count) for source in range(count)]
    return lax.ppermute(value, axis, pairs)


def exact_dot(left, right, dims=NN):
    return lax.dot_general(left, right, dims, precision=EXACT, preferred_element_type=jnp.float32)


def kernel_call(body, out_shape, in_specs, flops, bytes_accessed, slots=None):
    return pl.pallas_call(
        body,
        out_shape=out_shape,
        in_specs=in_specs,
        out_specs=jax.tree.map(lambda _: VMEM, out_shape),
        scratch_shapes=[] if slots is None else [pltpu.SMEM(slots, jnp.int32)],
        compiler_params=pltpu.CompilerParams(vmem_limit_bytes=VMEM_LIMIT),
        cost_estimate=pl.CostEstimate(flops=flops, bytes_accessed=bytes_accessed, transcendentals=0),
    )


def fill_slots(slots_ref, cols_ref, live_ref, first, place_of):
    rows, stored = cols_ref.shape
    count = slots_ref.shape[1]
    for row in range(rows):
        for index in range(count):
            slots_ref[row, index] = -1
        for at in range(stored):
            name = cols_ref[row, at] - first

            @pl.when((name >= 0) & (name < count) & (at < live_ref[row]))
            def _():
                slots_ref[row, place_of(name)] = at


def accumulate(slots_ref, hessian_ref, operand_ref, total):
    rows, _, size, _ = hessian_ref.shape
    shards, shard_rows, _ = operand_ref.shape
    each = shard_rows // size
    for index in range(shards * each):
        start = index % each * size
        block = operand_ref[index // each, start : start + size, :]
        parts = []
        for row in range(rows):
            slot = slots_ref[row, index]
            live = jnp.where(slot >= 0, 1.0, 0.0).astype(jnp.float32)
            stored = hessian_ref[row, jnp.maximum(slot, 0)]
            parts.append(stored * jnp.broadcast_to(live, (size, size)).astype(jnp.bfloat16))
        term = jnp.dot(jnp.concatenate(parts, 0), block, preferred_element_type=jnp.float32)
        total = term if total is None else total + term
    return total


def local_body(cols_ref, live_ref, hessian_ref, region_ref, out_ref, slots_ref):
    fill_slots(slots_ref, cols_ref, live_ref, 0, lambda name: name)
    out_ref[...] = accumulate(slots_ref, hessian_ref, region_ref, None)


def lower_body(first, cols_ref, live_ref, list_ref, hessian_ref, lower_ref, local_ref, out_ref, slots_ref):
    fill_slots(slots_ref, cols_ref, live_ref, first, lambda name: list_ref[name])
    out_ref[...] = accumulate(slots_ref, hessian_ref, lower_ref, local_ref[...])


def upper_total(first, cols_ref, live_ref, list_ref, hessian_ref, upper_ref, partial_ref, slots_ref):
    fill_slots(slots_ref, cols_ref, live_ref, first, lambda name: list_ref[name])
    return accumulate(slots_ref, hessian_ref, upper_ref, partial_ref[...])


def interval(bounds_ref):
    return 0.5 * (bounds_ref[0] + bounds_ref[1]), 0.5 * (bounds_ref[1] - bounds_ref[0])


def first_body(first, cols_ref, live_ref, list_ref, bounds_ref, hessian_ref, upper_ref, partial_ref, vectors_ref, one_ref, cast_ref, slots_ref):
    centre, half = interval(bounds_ref)
    total = upper_total(first, cols_ref, live_ref, list_ref, hessian_ref, upper_ref, partial_ref, slots_ref)
    one = (total - centre * vectors_ref[...]) / half
    one_ref[...] = one
    cast_ref[...] = one.astype(jnp.bfloat16)


def second_body(first, cols_ref, live_ref, list_ref, bounds_ref, hessian_ref, upper_ref, partial_ref, one_ref, vectors_ref, two_ref, cast_ref, slots_ref):
    centre, half = interval(bounds_ref)
    total = upper_total(first, cols_ref, live_ref, list_ref, hessian_ref, upper_ref, partial_ref, slots_ref)
    two = 2.0 * (total - centre * one_ref[...]) / half - vectors_ref[...]
    two_ref[...] = two
    cast_ref[...] = two.astype(jnp.bfloat16)


def place_rows(number_ref, piece, rows):
    return pl.ds(pl.multiple_of((piece ^ number_ref[0]) * rows, GROUP), rows)


def scatter_pieces(number_ref, out_ref, value):
    rows = out_ref.shape[0] // PIECES
    for piece in range(PIECES):
        out_ref[place_rows(number_ref, piece, rows), :] = value[piece * rows : (piece + 1) * rows, :]


def ordered_pieces(number_ref, in_ref):
    rows = in_ref.shape[0] // PIECES
    return jnp.concatenate([in_ref[place_rows(number_ref, piece, rows), :] for piece in range(PIECES)], 0)


def lower_tiles(count):
    return [(row, col) for row in range(count) for col in range(row + 1)]


def gram_body(number_ref, two_ref, out_ref):
    two = two_ref[...]
    cols = [two[:, at * TILE : (at + 1) * TILE] for at in range(two.shape[1] // TILE)]
    tiles = [exact_dot(cols[row], cols[col], TN) for row, col in lower_tiles(len(cols))]
    scatter_pieces(number_ref, out_ref, jnp.concatenate(tiles, 0))


def third_body(first, cols_ref, live_ref, list_ref, number_ref, hessian_ref, upper_ref, partial_ref, two_ref, out_ref, slots_ref):
    image = upper_total(first, cols_ref, live_ref, list_ref, hessian_ref, upper_ref, partial_ref, slots_ref)
    scatter_pieces(number_ref, out_ref, exact_dot(two_ref[...], image, TN))


def over_lanes(value, lane):
    return jnp.broadcast_to(value[:, lane : lane + 1], value.shape)


def over_rows(value, row):
    return jnp.broadcast_to(value[row : row + 1, :], value.shape)


def tile_inverse(tile):
    count = tile.shape[0] // GROUP
    rows = [tile[index * GROUP : (index + 1) * GROUP, :] for index in range(count)]
    sub = lax.broadcasted_iota(jnp.int32, rows[0].shape, 0)
    lane = lax.broadcasted_iota(jnp.int32, rows[0].shape, 1)
    done = []
    for step in range(count):
        start = step * GROUP
        pivot_cols = [over_lanes(rows[step], start + col) for col in range(GROUP)]
        factors = {
            below: [over_lanes(rows[below], start + col) for col in range(GROUP)]
            for below in range(step + 1, count)
        }
        inside = (lane >= start) & (lane < start + GROUP)
        forward = jnp.where(inside, jnp.where(lane - start == sub, 1.0, 0.0), rows[step])
        solved = forward
        for pivot in range(GROUP):
            here = sub == pivot
            value = over_rows(pivot_cols[pivot], pivot)
            inverse = 1.0 / value
            ratio = pivot_cols[pivot] * inverse
            row = over_rows(forward, pivot)
            forward = jnp.where(
                here, row * lax.rsqrt(value), jnp.where(sub > pivot, forward - ratio * row, forward)
            )
            solved = jnp.where(here, row * inverse, solved - ratio * row)
            for col in range(pivot + 1, GROUP):
                top = over_rows(pivot_cols[col], pivot)
                pivot_cols[col] = jnp.where(here, top * inverse, pivot_cols[col] - ratio * top)
        done.append(jnp.where(lane < start + GROUP, forward, 0.0))
        solved_rows = [over_rows(solved, pivot) for pivot in range(GROUP)]
        for below in range(step + 1, count):
            terms = [factors[below][col] * solved_rows[col] for col in range(GROUP)]
            while len(terms) > 1:
                terms = [terms[at] + terms[at + 1] for at in range(0, len(terms), 2)]
            rows[below] = jnp.where(inside, 0.0, rows[below]) - terms[0]
    return jnp.concatenate(done, 0)


def factor_inverse(tiles, count):
    rest = {at: tiles[index * TILE : (index + 1) * TILE] for index, at in enumerate(lower_tiles(count))}
    lower = {}
    inverse = {}
    for at in range(count):
        inverse[at, at] = tile_inverse(rest[at, at])
        for row in range(at + 1, count):
            lower[row, at] = exact_dot(rest[row, at], inverse[at, at], NT)
        for row in range(at + 1, count):
            for col in range(at + 1, row + 1):
                rest[row, col] = rest[row, col] - exact_dot(lower[row, at], lower[col, at], NT)
        for col in range(at):
            mixed = exact_dot(lower[at, col], inverse[col, col])
            for mid in range(col + 1, at):
                mixed = mixed + exact_dot(lower[at, mid], inverse[mid, col])
            inverse[at, col] = -exact_dot(inverse[at, at], mixed)
    zero = jnp.zeros((TILE, TILE), jnp.float32)
    return jnp.concatenate(
        [
            jnp.concatenate([inverse[row, col] if col <= row else zero for col in range(count)], 1)
            for row in range(count)
        ],
        0,
    )


def basis_body(total_rows, number_ref, gram_ref, two_ref, basis_ref, inverse_ref):
    tiles = ordered_pieces(number_ref, gram_ref) / total_rows
    inverse = factor_inverse(tiles, two_ref.shape[1] // TILE)
    inverse_ref[...] = inverse
    basis_ref[...] = exact_dot(two_ref[...], inverse, NT)


def projected_body(total_rows, number_ref, cross_ref, inverse_ref, projected_ref):
    cross = ordered_pieces(number_ref, cross_ref) / total_rows
    projected_ref[...] = exact_dot(exact_dot(inverse_ref[...], cross), inverse_ref[...], NT)


def partner_value(value, axis, bit):
    return lax.ppermute(value, axis, [(at, at ^ bit) for at in range(lax.axis_size(axis))])


def halving_bits():
    bits = []
    for axis in ("split", "region"):
        size = lax.axis_size(axis)
        bits.append([(axis, 1 << at) for at in range(size.bit_length() - 1)])
    halved = [bits[0][0], bits[1][0]]
    return halved, bits[1][1:] + bits[0][1:]


def device_number():
    halved, _ = halving_bits()
    number = 0
    for axis, bit in halved:
        number = number * 2 + (lax.axis_index(axis) // bit) % 2
    return number.astype(jnp.int32).reshape(1)


def summed(value):
    halved, doubled = halving_bits()
    for axis, bit in halved:
        half = value.shape[0] // 2
        value = value[:half] + partner_value(value[half:], axis, bit)
    for axis, bit in doubled:
        value = value + partner_value(value, axis, bit)
    for axis, bit in reversed(halved):
        value = jnp.concatenate([value, partner_value(value, axis, bit)], 0)
    return value


def local(vectors, hessian, block_cols, live_blocks, halo_lists, bounds):
    row_blocks, stored, size, _ = hessian.shape
    rows, modes = vectors.shape
    splits = lax.axis_size("split")
    region_blocks = row_blocks * splits
    halo_blocks = halo_lists.shape[2]
    whole = halo_blocks == region_blocks and region_blocks <= 256
    total_rows = rows * lax.axis_size(AXES)

    def halos(operand, region):
        if whole:
            return shifted(operand, "region", 1), shifted(operand, "region", -1)
        width = modes // splits
        start = lax.axis_index("split") * width
        blocks = region[:, :rows].reshape(region_blocks, size, modes)
        share = lambda listed: lax.dynamic_slice_in_dim(blocks[listed], start, width, 2).reshape(-1, width)
        lower = shifted(share(halo_lists[0, 1]), "region", 1)
        upper = shifted(share(halo_lists[0, 0]), "region", -1)
        return lower, upper

    def gather(value):
        if whole:
            return lax.all_gather(value, "split", axis=0)
        return lax.all_gather(value, "split", axis=1, tiled=True)[None]

    listed = jnp.pad(halo_lists[0], ((0, LIST_ROWS - 2), (0, modes - halo_blocks)))
    first = vectors.astype(jnp.bfloat16)
    if whole:
        first = jnp.concatenate([first, listed.astype(jnp.bfloat16)], 0)
    first_region = lax.all_gather(first, "split", axis=0)
    first_lower, first_upper = halos(first, first_region)
    if whole:
        lower_order = first_lower[rows + 1, :halo_blocks].astype(jnp.int32)
        upper_order = first_upper[rows, :halo_blocks].astype(jnp.int32)
    else:
        lower_order = upper_order = jnp.arange(halo_blocks, dtype=jnp.int32)
    wide = jax.ShapeDtypeStruct((rows, modes), jnp.float32)
    narrow = jax.ShapeDtypeStruct((rows, modes), jnp.bfloat16)
    square = jax.ShapeDtypeStruct((modes, modes), jnp.float32)
    tile_rows = len(lower_tiles(modes // TILE)) * TILE
    work = 2 * rows * size * modes
    square_work = 2 * rows * modes * modes
    traffic = hessian.size * 2 + 3 * rows * modes * 4
    number = device_number()
    halo_slots = (row_blocks, halo_blocks)
    upper_first = region_blocks + halo_blocks

    def step(body, outs, region, lower, upper, scalars, extra):
        slots = (row_blocks, region_blocks)
        call = kernel_call(local_body, wide, [SMEM] * 2 + [VMEM] * 2, work * region_blocks, traffic, slots)
        partial = call(block_cols, live_blocks, hessian, region)
        body_of = functools.partial(lower_body, region_blocks)
        call = kernel_call(body_of, wide, [SMEM] * 3 + [VMEM] * 3, work * halo_blocks, traffic, halo_slots)
        partial = call(block_cols, live_blocks, lower_order, hessian, gather(lower), partial)
        specs = [SMEM] * (3 + len(scalars)) + [VMEM] * (3 + len(extra))
        call = kernel_call(functools.partial(body, upper_first), outs, specs, work * halo_blocks, traffic, halo_slots)
        return call(block_cols, live_blocks, upper_order, *scalars, hessian, gather(upper), partial, *extra)

    def later(body, outs, operand, scalars, extra):
        region = lax.all_gather(operand, "split", axis=0)
        return step(body, outs, region, *halos(operand, region), scalars, extra)

    one, one_cast = step(first_body, (wide, narrow), first_region, first_lower, first_upper, (bounds,), (vectors,))
    two, two_cast = later(second_body, (wide, narrow), one_cast, (bounds,), (one, vectors))
    packed = jax.ShapeDtypeStruct((tile_rows, TILE), jnp.float32)
    gram = summed(kernel_call(gram_body, packed, [SMEM, VMEM], square_work, traffic)(number, two))
    cross = summed(later(third_body, square, two_cast, (number,), (two,)))
    body_of = functools.partial(basis_body, float(total_rows))
    call = kernel_call(body_of, (wide, square), [SMEM] + [VMEM] * 2, 160 * square_work, traffic)
    basis, inverse = call(number, gram, two)
    body_of = functools.partial(projected_body, float(total_rows))
    call = kernel_call(body_of, square, [SMEM] + [VMEM] * 2, 2 * square_work, traffic)
    return basis, call(number, cross, inverse)


def solution(mesh):
    placed = (
        P(("region", "split"), None),
        P(("region", "split"), None, None, None),
        P(("region", "split"), None),
        P(("region", "split")),
        P("region", None, None),
        P(),
    )
    return jax.shard_map(
        local,
        mesh=mesh,
        in_specs=placed,
        out_specs=(P(("region", "split"), None), P()),
        check_vma=False,
    )
```

```python
import functools
import jax
import jax.numpy as jnp
from jax import lax
from jax.experimental import pallas as pl
from jax.experimental.pallas import tpu as pltpu
from jax.sharding import PartitionSpec as P

AXES = ("region", "split")
VMEM = pl.BlockSpec(memory_space=pltpu.VMEM)
SMEM = pl.BlockSpec(memory_space=pltpu.SMEM)
EXACT = lax.Precision.HIGHEST
NN = (((1,), (0,)), ((), ()))
NT = (((1,), (1,)), ((), ()))
TN = (((0,), (0,)), ((), ()))
GROUP = 8
TILE = 128
VMEM_LIMIT = 20 * 1024 * 1024
LIST_ROWS = 16
PIECES = 4
EARLY = 2


def shifted(value, axis, steps):
    count = lax.axis_size(axis)
    pairs = [(source, (source + steps) % count) for source in range(count)]
    return lax.ppermute(value, axis, pairs)


def exact_dot(left, right, dims=NN):
    return lax.dot_general(left, right, dims, precision=EXACT, preferred_element_type=jnp.float32)


def kernel_call(body, out_shape, in_specs, flops, bytes_accessed, slots=None):
    return pl.pallas_call(
        body,
        out_shape=out_shape,
        in_specs=in_specs,
        out_specs=jax.tree.map(lambda _: VMEM, out_shape),
        scratch_shapes=[] if slots is None else [pltpu.SMEM(slots, jnp.int32)],
        compiler_params=pltpu.CompilerParams(vmem_limit_bytes=VMEM_LIMIT),
        cost_estimate=pl.CostEstimate(flops=flops, bytes_accessed=bytes_accessed, transcendentals=0),
    )


def fill_slots(slots_ref, cols_ref, live_ref, first, place_of):
    rows, stored = cols_ref.shape
    count = slots_ref.shape[1]
    for row in range(rows):
        for index in range(count):
            slots_ref[row, index] = -1
        for at in range(stored):
            name = cols_ref[row, at] - first

            @pl.when((name >= 0) & (name < count) & (at < live_ref[row]))
            def _():
                slots_ref[row, place_of(name)] = at


def accumulate(slots_ref, hessian_ref, operand_ref, base, total):
    rows, _, size, _ = hessian_ref.shape
    shards, shard_rows, _ = operand_ref.shape
    each = shard_rows // size
    for index in range(shards * each):
        start = index % each * size
        block = operand_ref[index // each, start : start + size, :]
        parts = []
        for row in range(rows):
            slot = slots_ref[row, base + index]
            live = jnp.where(slot >= 0, 1.0, 0.0).astype(jnp.float32)
            stored = hessian_ref[row, jnp.maximum(slot, 0)]
            parts.append(stored * jnp.broadcast_to(live, (size, size)).astype(jnp.bfloat16))
        term = jnp.dot(jnp.concatenate(parts, 0), block, preferred_element_type=jnp.float32)
        total = term if total is None else total + term
    return total


def near_body(count, *refs):
    cols_ref, live_ref, bases_ref, hessian_ref = refs[:4]
    operands, (out_ref, slots_ref) = refs[4:-2], refs[-2:]
    fill_slots(slots_ref, cols_ref, live_ref, 0, lambda name: name)
    total = None
    for at, operand_ref in enumerate(operands):
        total = accumulate(slots_ref, hessian_ref, operand_ref, bases_ref[at], total)
    out_ref[...] = total


def halo_total(first, which, cols_ref, live_ref, lists_ref, bases_ref, hessian_ref, lower_ref, upper_ref, total_ref, slots_ref):
    halo = lists_ref.shape[1]
    fill_slots(slots_ref, cols_ref, live_ref, first, lambda name: list_place(lists_ref, name))
    total = accumulate(slots_ref, hessian_ref, lower_ref, bases_ref[which], total_ref[...])
    return accumulate(slots_ref, hessian_ref, upper_ref, halo + bases_ref[which], total)


def list_place(lists_ref, name):
    halo = lists_ref.shape[1]
    side = jnp.where(name >= halo, 1, 0).astype(jnp.int32)
    return side * halo + lists_ref[side, name - side * halo]


def middle_body(first, which, *refs):
    out_ref, slots_ref = refs[-2:]
    out_ref[...] = halo_total(first, which, *refs[:-2], slots_ref)


def interval(bounds_ref):
    return 0.5 * (bounds_ref[0] + bounds_ref[1]), 0.5 * (bounds_ref[1] - bounds_ref[0])


def first_body(first, which, *refs):
    *operands, bounds_ref, vectors_ref, one_ref, cast_ref, slots_ref = refs
    centre, half = interval(bounds_ref)
    total = halo_total(first, which, *operands, slots_ref)
    one = (total - centre * vectors_ref[...]) / half
    one_ref[...] = one
    cast_ref[...] = one.astype(jnp.bfloat16)


def second_body(first, which, *refs):
    *operands, bounds_ref, one_ref, vectors_ref, two_ref, cast_ref, slots_ref = refs
    centre, half = interval(bounds_ref)
    total = halo_total(first, which, *operands, slots_ref)
    two = 2.0 * (total - centre * one_ref[...]) / half - vectors_ref[...]
    two_ref[...] = two
    cast_ref[...] = two.astype(jnp.bfloat16)


def place_rows(number_ref, piece, rows):
    return pl.ds(pl.multiple_of((piece ^ number_ref[0]) * rows, GROUP), rows)


def scatter_pieces(number_ref, out_ref, value):
    rows = out_ref.shape[0] // PIECES
    for piece in range(PIECES):
        out_ref[place_rows(number_ref, piece, rows), :] = value[piece * rows : (piece + 1) * rows, :]


def ordered_pieces(number_ref, in_ref):
    rows = in_ref.shape[0] // PIECES
    return jnp.concatenate([in_ref[place_rows(number_ref, piece, rows), :] for piece in range(PIECES)], 0)


def lower_tiles(count):
    return [(row, col) for row in range(count) for col in range(row + 1)]


def gram_body(number_ref, two_ref, out_ref):
    two = two_ref[...]
    cols = [two[:, at * TILE : (at + 1) * TILE] for at in range(two.shape[1] // TILE)]
    tiles = [exact_dot(cols[row], cols[col], TN) for row, col in lower_tiles(len(cols))]
    scatter_pieces(number_ref, out_ref, jnp.concatenate(tiles, 0))


def third_body(first, which, *refs):
    *operands, number_ref, two_ref, out_ref, slots_ref = refs
    image = halo_total(first, which, *operands, slots_ref)
    scatter_pieces(number_ref, out_ref, exact_dot(two_ref[...], image, TN))


def over_lanes(value, lane):
    return jnp.broadcast_to(value[:, lane : lane + 1], value.shape)


def over_rows(value, row):
    return jnp.broadcast_to(value[row : row + 1, :], value.shape)


def eliminate(tile, first, last):
    count = tile.shape[0] // GROUP
    rows = [tile[index * GROUP : (index + 1) * GROUP, :] for index in range(count)]
    sub = lax.broadcasted_iota(jnp.int32, rows[0].shape, 0)
    lane = lax.broadcasted_iota(jnp.int32, rows[0].shape, 1)
    for step in range(first, last):
        start = step * GROUP
        pivot_cols = [over_lanes(rows[step], start + col) for col in range(GROUP)]
        factors = {
            below: [over_lanes(rows[below], start + col) for col in range(GROUP)]
            for below in range(step + 1, count)
        }
        inside = (lane >= start) & (lane < start + GROUP)
        forward = jnp.where(inside, jnp.where(lane - start == sub, 1.0, 0.0), rows[step])
        solved = forward
        for pivot in range(GROUP):
            here = sub == pivot
            value = over_rows(pivot_cols[pivot], pivot)
            inverse = 1.0 / value
            ratio = pivot_cols[pivot] * inverse
            row = over_rows(forward, pivot)
            forward = jnp.where(
                here, row * lax.rsqrt(value), jnp.where(sub > pivot, forward - ratio * row, forward)
            )
            solved = jnp.where(here, row * inverse, solved - ratio * row)
            for col in range(pivot + 1, GROUP):
                top = over_rows(pivot_cols[col], pivot)
                pivot_cols[col] = jnp.where(here, top * inverse, pivot_cols[col] - ratio * top)
        rows[step] = jnp.where(lane < start + GROUP, forward, 0.0)
        solved_rows = [over_rows(solved, pivot) for pivot in range(GROUP)]
        for below in range(step + 1, count):
            terms = [factors[below][col] * solved_rows[col] for col in range(GROUP)]
            while len(terms) > 1:
                terms = [terms[at] + terms[at + 1] for at in range(0, len(terms), 2)]
            rows[below] = jnp.where(inside, 0.0, rows[below]) - terms[0]
    return jnp.concatenate(rows, 0)


def unpack_body(total_rows, number_ref, gram_ref, *tile_refs):
    tiles = ordered_pieces(number_ref, gram_ref) / total_rows
    for at, tile_ref in enumerate(tile_refs):
        tile_ref[...] = tiles[at * TILE : (at + 1) * TILE, :]


def eliminate_body(first, last, tile_ref, out_ref):
    out_ref[...] = eliminate(tile_ref[...], first, last)


def update_body(at, count, *refs):
    inputs = refs[: len(refs) // 2]
    outputs = refs[len(refs) // 2 :]
    names = [name for name in lower_tiles(count) if name[1] >= at]
    tiles = {name: ref[...] for name, ref in zip(names, inputs)}
    column = {row: exact_dot(tiles[row, at], tiles[at, at], NT) for row in range(at + 1, count)}
    for (row, col), out_ref in zip(names, outputs):
        if row == at:
            out_ref[...] = tiles[row, col]
        elif col == at:
            out_ref[...] = column[row]
        else:
            out_ref[...] = tiles[row, col] - exact_dot(column[row], column[col], NT)


def basis_body(count, *refs):
    *tile_refs, two_ref, basis_ref, inverse_ref = refs
    tiles = {name: ref[...] for name, ref in zip(lower_tiles(count), tile_refs)}
    inverse = {}
    for row in range(count):
        inverse[row, row] = tiles[row, row]
        for col in range(row):
            mixed = exact_dot(tiles[row, col], inverse[col, col])
            for mid in range(col + 1, row):
                mixed = mixed + exact_dot(tiles[row, mid], inverse[mid, col])
            inverse[row, col] = -exact_dot(tiles[row, row], mixed)
    zero = jnp.zeros((TILE, TILE), jnp.float32)
    whole = jnp.concatenate(
        [
            jnp.concatenate([inverse[row, col] if col <= row else zero for col in range(count)], 1)
            for row in range(count)
        ],
        0,
    )
    inverse_ref[...] = whole
    basis_ref[...] = exact_dot(two_ref[...], whole, NT)


def projected_body(total_rows, number_ref, cross_ref, inverse_ref, projected_ref):
    cross = ordered_pieces(number_ref, cross_ref) / total_rows
    projected_ref[...] = exact_dot(exact_dot(inverse_ref[...], cross), inverse_ref[...], NT)


def factor_stages(total_rows, count, number, two):
    rows, modes = two.shape
    tile = jax.ShapeDtypeStruct((TILE, TILE), jnp.float32)
    names = lower_tiles(count)
    work = 4 * 10 ** 9

    def unpack(gram):
        body = functools.partial(unpack_body, total_rows)
        return kernel_call(body, (tile,) * len(names), [SMEM, VMEM], work // 8, gram.size)(number, gram)

    def elimination(at, first, last):
        def stage(tiles):
            place = names.index((at, at))
            call = kernel_call(functools.partial(eliminate_body, first, last), tile, [VMEM], work // 2, TILE * TILE)
            return tiles[:place] + (call(tiles[place]),) + tiles[place + 1 :]

        return stage

    def update(at):
        def stage(tiles):
            picked = [index for index, name in enumerate(names) if name[1] >= at]
            body = functools.partial(update_body, at, count)
            call = kernel_call(body, (tile,) * len(picked), [VMEM] * len(picked), work // 4, TILE * TILE)
            new = call(*[tiles[index] for index in picked])
            return tuple(new[picked.index(index)] if index in picked else old for index, old in enumerate(tiles))

        return stage

    def finish(tiles):
        outs = (jax.ShapeDtypeStruct((rows, modes), jnp.float32), jax.ShapeDtypeStruct((modes, modes), jnp.float32))
        body = functools.partial(basis_body, count)
        return kernel_call(body, outs, [VMEM] * (len(names) + 1), work // 2, rows * modes)(*tiles, two)

    groups = TILE // GROUP
    cuts = [0, groups // 4, groups // 2 + 1, groups]
    stages = [unpack]
    for at in range(count):
        stages += [elimination(at, first, last) for first, last in zip(cuts, cuts[1:])]
        if at + 1 < count:
            stages.append(update(at))
    return stages + [finish]


def tied(left, right):
    return lax.optimization_barrier((left, right))


def partner_value(value, axis, bit):
    return lax.ppermute(value, axis, [(at, at ^ bit) for at in range(lax.axis_size(axis))])


def halving_bits():
    bits = []
    for axis in ("split", "region"):
        size = lax.axis_size(axis)
        bits.append([(axis, 1 << at) for at in range(size.bit_length() - 1)])
    cores, regions = bits
    return [cores[0], regions[1]], cores[1:] + regions[2:] + regions[:1]


def device_number():
    halved, _ = halving_bits()
    number = 0
    for axis, bit in halved:
        number = number * 2 + (lax.axis_index(axis) // bit) % 2
    return number.astype(jnp.int32).reshape(1)


def sum_steps():
    halved, doubled = halving_bits()

    def halving(axis, bit):
        send = lambda value: partner_value(value[value.shape[0] // 2 :], axis, bit)
        return send, lambda value, got: value[: value.shape[0] // 2] + got

    def doubling(axis, bit):
        return lambda value: partner_value(value, axis, bit), lambda value, got: value + got

    def joining(axis, bit):
        send = lambda value: partner_value(value, axis, bit)
        return send, lambda value, got: jnp.concatenate([value, got], 0)

    steps = [halving(axis, bit) for axis, bit in halved]
    steps += [doubling(axis, bit) for axis, bit in doubled]
    return steps + [joining(axis, bit) for axis, bit in reversed(halved)]


def run_steps(value, steps):
    for send, join in steps:
        value = join(value, send(value))
    return value


def run_beside(value, steps, state, stages):
    stages = list(stages)
    for index, (send, join) in enumerate(steps):
        value, state = tied(value, state)
        got = send(value)
        due = -(-len(stages) // (len(steps) - index))
        for _ in range(due):
            state = stages.pop(0)(state)
        if due:
            got, state = tied(got, state)
        value = join(value, got)
    return value, state


def local(vectors, hessian, block_cols, live_blocks, halo_lists, bounds):
    row_blocks, stored, size, _ = hessian.shape
    rows, modes = vectors.shape
    splits = lax.axis_size("split")
    region_blocks = row_blocks * splits
    halo_blocks = halo_lists.shape[2]
    whole = halo_blocks == region_blocks and region_blocks <= 256
    total_rows = rows * lax.axis_size(AXES)

    paired = whole and splits == 2
    core = lax.axis_index("split").astype(jnp.int32)
    swapped = lambda value: lax.ppermute(value, "split", [(0, 1), (1, 0)])
    near_first = [core * row_blocks, (1 - core) * row_blocks] if paired else [0]
    bases = jnp.stack(near_first).astype(jnp.int32) if paired else jnp.zeros((1,), jnp.int32)

    def sent(operand, region):
        if whole:
            return operand, operand
        width = modes // splits
        start = core * width
        blocks = region[:, :rows].reshape(region_blocks, size, modes)
        share = lambda listed: lax.dynamic_slice_in_dim(blocks[listed], start, width, 2).reshape(-1, width)
        return share(halo_lists[0, 1]), share(halo_lists[0, 0])

    def gathered(value):
        if paired:
            return [value[None], swapped(value)[None]]
        if whole:
            return [lax.all_gather(value, "split", axis=0)]
        return [lax.all_gather(value, "split", axis=1, tiled=True)[None]]

    listed = jnp.pad(halo_lists[0], ((0, LIST_ROWS - 2), (0, modes - halo_blocks)))
    first = vectors.astype(jnp.bfloat16)
    if whole:
        first = jnp.concatenate([first, listed.astype(jnp.bfloat16)], 0)

    def near_parts(operand):
        if paired:
            return [operand[None], swapped(operand)[None]]
        return [lax.all_gather(operand, "split", axis=0)]

    def exchange(operand, hold=lambda value: value):
        near = near_parts(operand)
        up, down = sent(operand, near[0])
        lower = shifted(up, "region", 1)
        return near, lower, shifted(hold(down), "region", -1)

    first_near, first_lower, first_upper = exchange(first)
    if whole:
        orders = [first_lower[rows + 1, :halo_blocks], first_upper[rows, :halo_blocks]]
        lists = jnp.stack(orders).astype(jnp.int32)
    else:
        lists = jnp.broadcast_to(jnp.arange(halo_blocks, dtype=jnp.int32), (2, halo_blocks))

    wide = jax.ShapeDtypeStruct((rows, modes), jnp.float32)
    narrow = jax.ShapeDtypeStruct((rows, modes), jnp.bfloat16)
    square = jax.ShapeDtypeStruct((modes, modes), jnp.float32)
    tile_rows = len(lower_tiles(modes // TILE)) * TILE
    work = 2 * rows * size * modes
    square_work = 2 * rows * modes * modes
    traffic = hessian.size * 2 + 3 * rows * modes * 4
    number = device_number()
    halo_slots = (row_blocks, 2 * halo_blocks)

    def step(body, outs, near, lower, upper, scalars, extra):
        call = kernel_call(
            functools.partial(near_body, region_blocks),
            wide,
            [SMEM] * 3 + [VMEM] * (1 + len(near)),
            work * region_blocks,
            traffic,
            (row_blocks, region_blocks),
        )
        total = call(block_cols, live_blocks, bases, hessian, *near)
        pairs = list(zip(gathered(lower), gathered(upper)))
        for which, pair in enumerate(pairs):
            last = which == len(pairs) - 1
            given = (block_cols, live_blocks, lists, bases, hessian, *pair, total) + ((*scalars, *extra) if last else ())
            specs = [SMEM] * 4 + [VMEM] * 4 + ([SMEM] * len(scalars) + [VMEM] * len(extra) if last else [])
            body_of = functools.partial(body if last else middle_body, region_blocks, which)
            cost = 2 * work * halo_blocks // len(pairs)
            total = kernel_call(body_of, outs if last else wide, specs, cost, traffic, halo_slots)(*given)
        return total

    one, one_cast = step(first_body, (wide, narrow), first_near, first_lower, first_upper, (bounds,), (vectors,))
    two, two_cast = step(second_body, (wide, narrow), *exchange(one_cast), (bounds,), (one, vectors))

    steps = sum_steps()
    packed = jax.ShapeDtypeStruct((tile_rows, TILE), jnp.float32)
    gram = kernel_call(gram_body, packed, [SMEM, VMEM], square_work, traffic)(number, two)
    gram = run_steps(gram, steps[:EARLY])

    def hold(value):
        nonlocal gram
        value, gram = tied(value, gram)
        return value

    third = exchange(two_cast, hold)
    gram = run_steps(gram, steps[EARLY:])
    cross = step(third_body, square, *third, (number,), (two,))
    stages = factor_stages(float(total_rows), modes // TILE, number, two)
    cross, (basis, inverse) = run_beside(cross, steps, gram, stages)
    body_of = functools.partial(projected_body, float(total_rows))
    call = kernel_call(body_of, square, [SMEM] + [VMEM] * 2, 2 * square_work, traffic)
    return basis, call(number, cross, inverse)


def solution(mesh):
    placed = (
        P(("region", "split"), None),
        P(("region", "split"), None, None, None),
        P(("region", "split"), None),
        P(("region", "split")),
        P("region", None, None),
        P(),
    )
    return jax.shard_map(
        local,
        mesh=mesh,
        in_specs=placed,
        out_specs=(P(("region", "split"), None), P()),
        check_vma=False,
    )
```

```python
import functools
import jax
import jax.numpy as jnp
from jax import lax
from jax.experimental import pallas as pl
from jax.experimental.pallas import tpu as pltpu
from jax.sharding import PartitionSpec as P

AXES = ("region", "split")
VMEM = pl.BlockSpec(memory_space=pltpu.VMEM)
SMEM = pl.BlockSpec(memory_space=pltpu.SMEM)
EXACT = lax.Precision.HIGHEST
NN = (((1,), (0,)), ((), ()))
NT = (((1,), (1,)), ((), ()))
TN = (((0,), (0,)), ((), ()))
GROUP = 8
TILE = 128
VMEM_LIMIT = 20 * 1024 * 1024
LIST_ROWS = 16
PIECES = 4


def shifted(value, axis, steps):
    count = lax.axis_size(axis)
    pairs = [(source, (source + steps) % count) for source in range(count)]
    return lax.ppermute(value, axis, pairs)


def exact_dot(left, right, dims=NN):
    return lax.dot_general(left, right, dims, precision=EXACT, preferred_element_type=jnp.float32)


def kernel_call(body, out_shape, in_specs, flops, bytes_accessed, slots=None):
    return pl.pallas_call(
        body,
        out_shape=out_shape,
        in_specs=in_specs,
        out_specs=jax.tree.map(lambda _: VMEM, out_shape),
        scratch_shapes=[] if slots is None else [pltpu.SMEM(slots, jnp.int32)],
        compiler_params=pltpu.CompilerParams(vmem_limit_bytes=VMEM_LIMIT),
        cost_estimate=pl.CostEstimate(flops=flops, bytes_accessed=bytes_accessed, transcendentals=0),
    )


def fill_slots(slots_ref, cols_ref, live_ref, first, place_of):
    rows, stored = cols_ref.shape
    count = slots_ref.shape[1] - 1
    for row in range(rows):
        for index in range(count):
            slots_ref[row, index] = -1
        for at in range(stored):
            name = cols_ref[row, at] - first
            inside = (name >= 0) & (name < count) & (at < live_ref[row])
            slots_ref[row, jnp.where(inside, place_of(jnp.clip(name, 0, count - 1)), count)] = at


def accumulate(slots_ref, hessian_ref, operand_ref, base, total):
    rows, _, size, _ = hessian_ref.shape
    shards, shard_rows, _ = operand_ref.shape
    each = shard_rows // size
    for index in range(shards * each):
        start = index % each * size
        block = operand_ref[index // each, start : start + size, :]
        parts = []
        for row in range(rows):
            slot = slots_ref[row, base + index]
            live = jnp.where(slot >= 0, 1.0, 0.0).astype(jnp.float32)
            stored = hessian_ref[row, jnp.maximum(slot, 0)]
            parts.append(stored * jnp.broadcast_to(live, (size, size)).astype(jnp.bfloat16))
        term = jnp.dot(jnp.concatenate(parts, 0), block, preferred_element_type=jnp.float32)
        total = term if total is None else total + term
    return total


def near_body(count, *refs):
    cols_ref, live_ref, bases_ref, hessian_ref = refs[:4]
    operands, (out_ref, slots_ref) = refs[4:-2], refs[-2:]
    fill_slots(slots_ref, cols_ref, live_ref, 0, lambda name: name)
    total = None
    for at, operand_ref in enumerate(operands):
        total = accumulate(slots_ref, hessian_ref, operand_ref, bases_ref[at], total)
    out_ref[...] = total


def halo_total(first, which, cols_ref, live_ref, lists_ref, bases_ref, hessian_ref, lower_ref, upper_ref, total_ref, slots_ref):
    halo = lists_ref.shape[1]
    fill_slots(slots_ref, cols_ref, live_ref, first, lambda name: list_place(lists_ref, name))
    total = accumulate(slots_ref, hessian_ref, lower_ref, bases_ref[which], total_ref[...])
    return accumulate(slots_ref, hessian_ref, upper_ref, halo + bases_ref[which], total)


def list_place(lists_ref, name):
    halo = lists_ref.shape[1]
    side = jnp.where(name >= halo, 1, 0).astype(jnp.int32)
    return side * halo + lists_ref[side, name - side * halo]


def middle_body(first, which, *refs):
    out_ref, slots_ref = refs[-2:]
    out_ref[...] = halo_total(first, which, *refs[:-2], slots_ref)


def interval(bounds_ref):
    return 0.5 * (bounds_ref[0] + bounds_ref[1]), 0.5 * (bounds_ref[1] - bounds_ref[0])


def first_body(first, which, *refs):
    *operands, bounds_ref, vectors_ref, one_ref, cast_ref, slots_ref = refs
    centre, half = interval(bounds_ref)
    total = halo_total(first, which, *operands, slots_ref)
    one = (total - centre * vectors_ref[...]) / half
    one_ref[...] = one
    cast_ref[...] = one.astype(jnp.bfloat16)


def second_body(first, which, *refs):
    *operands, bounds_ref, one_ref, vectors_ref, two_ref, cast_ref, slots_ref = refs
    centre, half = interval(bounds_ref)
    total = halo_total(first, which, *operands, slots_ref)
    two = 2.0 * (total - centre * one_ref[...]) / half - vectors_ref[...]
    two_ref[...] = two
    cast_ref[...] = two.astype(jnp.bfloat16)


def place_rows(number_ref, piece, rows):
    return pl.ds(pl.multiple_of((piece ^ number_ref[0]) * rows, GROUP), rows)


def scatter_pieces(number_ref, out_ref, value):
    rows = out_ref.shape[0] // PIECES
    for piece in range(PIECES):
        out_ref[place_rows(number_ref, piece, rows), :] = value[piece * rows : (piece + 1) * rows, :]


def ordered_pieces(number_ref, in_ref):
    rows = in_ref.shape[0] // PIECES
    return jnp.concatenate([in_ref[place_rows(number_ref, piece, rows), :] for piece in range(PIECES)], 0)


def lower_tiles(count):
    return [(row, col) for row in range(count) for col in range(row + 1)]


def gram_body(number_ref, two_ref, out_ref):
    two = two_ref[...]
    cols = [two[:, at * TILE : (at + 1) * TILE] for at in range(two.shape[1] // TILE)]
    tiles = [exact_dot(cols[row], cols[col], TN) for row, col in lower_tiles(len(cols))]
    scatter_pieces(number_ref, out_ref, jnp.concatenate(tiles, 0))


def third_body(first, which, *refs):
    *operands, number_ref, two_ref, out_ref, slots_ref = refs
    image = halo_total(first, which, *operands, slots_ref)
    scatter_pieces(number_ref, out_ref, exact_dot(two_ref[...], image, TN))


def over_lanes(value, lane):
    return jnp.broadcast_to(value[:, lane : lane + 1], value.shape)


def over_rows(value, row):
    return jnp.broadcast_to(value[row : row + 1, :], value.shape)


def eliminate(tile, first, last):
    count = tile.shape[0] // GROUP
    rows = [tile[index * GROUP : (index + 1) * GROUP, :] for index in range(count)]
    sub = lax.broadcasted_iota(jnp.int32, rows[0].shape, 0)
    lane = lax.broadcasted_iota(jnp.int32, rows[0].shape, 1)
    for step in range(first, last):
        start = step * GROUP
        pivot_cols = [over_lanes(rows[step], start + col) for col in range(GROUP)]
        factors = {
            below: [over_lanes(rows[below], start + col) for col in range(GROUP)]
            for below in range(step + 1, count)
        }
        inside = (lane >= start) & (lane < start + GROUP)
        forward = jnp.where(inside, jnp.where(lane - start == sub, 1.0, 0.0), rows[step])
        solved = forward
        for pivot in range(GROUP):
            here = sub == pivot
            value = over_rows(pivot_cols[pivot], pivot)
            inverse = 1.0 / value
            ratio = pivot_cols[pivot] * inverse
            row = over_rows(forward, pivot)
            forward = jnp.where(
                here, row * lax.rsqrt(value), jnp.where(sub > pivot, forward - ratio * row, forward)
            )
            solved = jnp.where(here, row * inverse, solved - ratio * row)
            for col in range(pivot + 1, GROUP):
                top = over_rows(pivot_cols[col], pivot)
                pivot_cols[col] = jnp.where(here, top * inverse, pivot_cols[col] - ratio * top)
        rows[step] = jnp.where(lane < start + GROUP, forward, 0.0)
        solved_rows = [over_rows(solved, pivot) for pivot in range(GROUP)]
        for below in range(step + 1, count):
            terms = [factors[below][col] * solved_rows[col] for col in range(GROUP)]
            while len(terms) > 1:
                terms = [terms[at] + terms[at + 1] for at in range(0, len(terms), 2)]
            rows[below] = jnp.where(inside, 0.0, rows[below]) - terms[0]
    return jnp.concatenate(rows, 0)


def unpack_body(total_rows, number_ref, gram_ref, *tile_refs):
    tiles = ordered_pieces(number_ref, gram_ref) / total_rows
    for at, tile_ref in enumerate(tile_refs):
        tile_ref[...] = tiles[at * TILE : (at + 1) * TILE, :]


def eliminate_body(first, last, tile_ref, out_ref):
    out_ref[...] = eliminate(tile_ref[...], first, last)


def update_body(at, count, *refs):
    inputs = refs[: len(refs) // 2]
    outputs = refs[len(refs) // 2 :]
    names = [name for name in lower_tiles(count) if name[1] >= at]
    tiles = {name: ref[...] for name, ref in zip(names, inputs)}
    column = {row: exact_dot(tiles[row, at], tiles[at, at], NT) for row in range(at + 1, count)}
    for (row, col), out_ref in zip(names, outputs):
        if row == at:
            out_ref[...] = tiles[row, col]
        elif col == at:
            out_ref[...] = column[row]
        else:
            out_ref[...] = tiles[row, col] - exact_dot(column[row], column[col], NT)


def basis_body(count, *refs):
    *tile_refs, two_ref, basis_ref, inverse_ref = refs
    tiles = {name: ref[...] for name, ref in zip(lower_tiles(count), tile_refs)}
    inverse = {}
    for row in range(count):
        inverse[row, row] = tiles[row, row]
        for col in range(row):
            mixed = exact_dot(tiles[row, col], inverse[col, col])
            for mid in range(col + 1, row):
                mixed = mixed + exact_dot(tiles[row, mid], inverse[mid, col])
            inverse[row, col] = -exact_dot(tiles[row, row], mixed)
    zero = jnp.zeros((TILE, TILE), jnp.float32)
    whole = jnp.concatenate(
        [
            jnp.concatenate([inverse[row, col] if col <= row else zero for col in range(count)], 1)
            for row in range(count)
        ],
        0,
    )
    inverse_ref[...] = whole
    basis_ref[...] = exact_dot(two_ref[...], whole, NT)


def projected_body(total_rows, number_ref, cross_ref, inverse_ref, projected_ref):
    cross = ordered_pieces(number_ref, cross_ref) / total_rows
    projected_ref[...] = exact_dot(exact_dot(inverse_ref[...], cross), inverse_ref[...], NT)


def factor_stages(total_rows, count, number, two):
    rows, modes = two.shape
    tile = jax.ShapeDtypeStruct((TILE, TILE), jnp.float32)
    names = lower_tiles(count)
    work = 4 * 10 ** 9

    def unpack(gram):
        body = functools.partial(unpack_body, total_rows)
        return kernel_call(body, (tile,) * len(names), [SMEM, VMEM], work // 8, gram.size)(number, gram)

    def elimination(at, first, last):
        def stage(tiles):
            place = names.index((at, at))
            call = kernel_call(functools.partial(eliminate_body, first, last), tile, [VMEM], work // 2, TILE * TILE)
            return tiles[:place] + (call(tiles[place]),) + tiles[place + 1 :]

        return stage

    def update(at):
        def stage(tiles):
            picked = [index for index, name in enumerate(names) if name[1] >= at]
            body = functools.partial(update_body, at, count)
            call = kernel_call(body, (tile,) * len(picked), [VMEM] * len(picked), work // 4, TILE * TILE)
            new = call(*[tiles[index] for index in picked])
            return tuple(new[picked.index(index)] if index in picked else old for index, old in enumerate(tiles))

        return stage

    def finish(tiles):
        outs = (jax.ShapeDtypeStruct((rows, modes), jnp.float32), jax.ShapeDtypeStruct((modes, modes), jnp.float32))
        body = functools.partial(basis_body, count)
        return kernel_call(body, outs, [VMEM] * (len(names) + 1), work // 2, rows * modes)(*tiles, two)

    groups = TILE // GROUP
    cuts = [0, groups // 4, groups // 2 + 1, groups]
    stages = [unpack]
    for at in range(count):
        stages += [elimination(at, first, last) for first, last in zip(cuts, cuts[1:])]
        if at + 1 < count:
            stages.append(update(at))
    return stages + [finish]


def tied(left, right):
    return lax.optimization_barrier((left, right))


def partner_value(value, axis, bit):
    return lax.ppermute(value, axis, [(at, at ^ bit) for at in range(lax.axis_size(axis))])


def halving_bits():
    bits = []
    for axis in ("split", "region"):
        size = lax.axis_size(axis)
        bits.append([(axis, 1 << at) for at in range(size.bit_length() - 1)])
    cores, regions = bits
    return [cores[0], regions[1]], cores[1:] + regions[2:] + regions[:1]


def device_number():
    halved, _ = halving_bits()
    number = 0
    for axis, bit in halved:
        number = number * 2 + (lax.axis_index(axis) // bit) % 2
    return number.astype(jnp.int32).reshape(1)


def halving(axis, bit):
    def step(value):
        half = value.shape[0] // 2
        got = partner_value(value[half:], axis, bit)
        return lambda: value[:half] + got

    return step


def doubling(axis, bit):
    def step(value):
        got = partner_value(value, axis, bit)
        return lambda: value + got

    return step


def joining(axis, bit):
    def step(value):
        got = partner_value(value, axis, bit)
        return lambda: jnp.concatenate([value, got], 0)

    return step


def run_beside(value, steps, state, stages):
    stages = list(stages)
    for index, step in enumerate(steps):
        value, state = tied(value, state)
        join = step(value)
        due = -(-len(stages) // (len(steps) - index))
        for _ in range(due):
            state = stages.pop(0)(state)
        value = join()
        if due:
            value, state = tied(value, state)
    return value, state


def local(vectors, hessian, block_cols, live_blocks, halo_lists, bounds):
    row_blocks, stored, size, _ = hessian.shape
    rows, modes = vectors.shape
    splits = lax.axis_size("split")
    region_blocks = row_blocks * splits
    halo_blocks = halo_lists.shape[2]
    whole = halo_blocks == region_blocks and region_blocks <= 256
    total_rows = rows * lax.axis_size(AXES)

    paired = whole and splits == 2
    core = lax.axis_index("split").astype(jnp.int32)
    swapped = lambda value: lax.ppermute(value, "split", [(0, 1), (1, 0)])
    near_first = [core * row_blocks, (1 - core) * row_blocks] if paired else [0]
    bases = jnp.stack(near_first).astype(jnp.int32) if paired else jnp.zeros((1,), jnp.int32)

    def sent(operand, region):
        if whole:
            return operand, operand
        width = modes // splits
        start = core * width
        blocks = region[:, :rows].reshape(region_blocks, size, modes)
        share = lambda listed: lax.dynamic_slice_in_dim(blocks[listed], start, width, 2).reshape(-1, width)
        return share(halo_lists[0, 1]), share(halo_lists[0, 0])

    def gathered(value):
        if paired:
            return [value[None], swapped(value)[None]]
        if whole:
            return [lax.all_gather(value, "split", axis=0)]
        return [lax.all_gather(value, "split", axis=1, tiled=True)[None]]

    listed = jnp.pad(halo_lists[0], ((0, LIST_ROWS - 2), (0, modes - halo_blocks)))
    first = vectors.astype(jnp.bfloat16)
    if whole:
        first = jnp.concatenate([first, listed.astype(jnp.bfloat16)], 0)

    def near_parts(operand):
        if paired:
            return [operand[None], swapped(operand)[None]]
        return [lax.all_gather(operand, "split", axis=0)]

    def exchange(operand):
        near = near_parts(operand)
        up, down = sent(operand, near[0])
        return near, shifted(up, "region", 1), shifted(down, "region", -1)

    first_near, first_lower, first_upper = exchange(first)
    if whole:
        orders = [first_lower[rows + 1, :halo_blocks], first_upper[rows, :halo_blocks]]
        lists = jnp.stack(orders).astype(jnp.int32)
    else:
        lists = jnp.broadcast_to(jnp.arange(halo_blocks, dtype=jnp.int32), (2, halo_blocks))

    wide = jax.ShapeDtypeStruct((rows, modes), jnp.float32)
    narrow = jax.ShapeDtypeStruct((rows, modes), jnp.bfloat16)
    square = jax.ShapeDtypeStruct((modes, modes), jnp.float32)
    tile_rows = len(lower_tiles(modes // TILE)) * TILE
    work = 2 * rows * size * modes
    square_work = 2 * rows * modes * modes
    traffic = hessian.size * 2 + 3 * rows * modes * 4
    number = device_number()
    halo_slots = (row_blocks, 2 * halo_blocks + 1)

    def step(body, outs, near, lower, upper, scalars, extra):
        call = kernel_call(
            functools.partial(near_body, region_blocks),
            wide,
            [SMEM] * 3 + [VMEM] * (1 + len(near)),
            work * region_blocks,
            traffic,
            (row_blocks, region_blocks + 1),
        )
        total = call(block_cols, live_blocks, bases, hessian, *near)
        lower, upper, total = lax.optimization_barrier((lower, upper, total))
        pairs = list(zip(gathered(lower), gathered(upper)))
        for which, pair in enumerate(pairs):
            last = which == len(pairs) - 1
            given = (block_cols, live_blocks, lists, bases, hessian, *pair, total) + ((*scalars, *extra) if last else ())
            specs = [SMEM] * 4 + [VMEM] * 4 + ([SMEM] * len(scalars) + [VMEM] * len(extra) if last else [])
            body_of = functools.partial(body if last else middle_body, region_blocks, which)
            cost = 2 * work * halo_blocks // len(pairs)
            total = kernel_call(body_of, outs if last else wide, specs, cost, traffic, halo_slots)(*given)
        return total

    one, one_cast = step(first_body, (wide, narrow), first_near, first_lower, first_upper, (bounds,), (vectors,))
    two, two_cast = step(second_body, (wide, narrow), *exchange(one_cast), (bounds,), (one, vectors))

    (cores, across), doubled = halving_bits()
    *between, near_chip = doubled
    packed = jax.ShapeDtypeStruct((tile_rows, TILE), jnp.float32)
    third = exchange(two_cast)
    gram = kernel_call(gram_body, packed, [SMEM, VMEM], square_work, traffic)(number, two)
    for step_of in [halving(*cores), halving(*across)] + [doubling(*bit) for bit in between]:
        gram = step_of(gram)()
    cross = step(third_body, square, *third, (number,), (two,))
    cross = halving(*cores)(cross)()

    fold = modes // TILE
    cut = gram.shape[0] // fold
    folded = jnp.concatenate([gram[at * cut : (at + 1) * cut] for at in range(fold)], 1)
    flat = lambda value: [value[:, at * TILE : (at + 1) * TILE] for at in range(fold)]
    both = doubling(*near_chip)(jnp.concatenate([folded, cross], 0))()
    half = cut + cross.shape[0] // 2
    got = partner_value(jnp.concatenate([both[:cut], both[half:]], 0), *across)
    gram = jnp.concatenate(flat(both[:cut]) + flat(got[:cut]), 0)
    cross = both[cut:half] + got[cut:]
    gram = joining(*cores)(gram)()
    stages = factor_stages(float(total_rows), modes // TILE, number, two)
    steps = [doubling(*bit) for bit in between] + [joining(*across), joining(*cores)]
    cross, (basis, inverse) = run_beside(cross, steps, gram, stages)
    body_of = functools.partial(projected_body, float(total_rows))
    call = kernel_call(body_of, square, [SMEM] + [VMEM] * 2, 2 * square_work, traffic)
    return basis, call(number, cross, inverse)


def solution(mesh):
    placed = (
        P(("region", "split"), None),
        P(("region", "split"), None, None, None),
        P(("region", "split"), None),
        P(("region", "split")),
        P("region", None, None),
        P(),
    )
    return jax.shard_map(
        local,
        mesh=mesh,
        in_specs=placed,
        out_specs=(P(("region", "split"), None), P()),
        check_vma=False,
    )
```

```python
import functools
import jax
import jax.numpy as jnp
from jax import lax
from jax.experimental import pallas as pl
from jax.experimental.pallas import tpu as pltpu
from jax.sharding import PartitionSpec as P

AXES = ("region", "split")
VMEM = pl.BlockSpec(memory_space=pltpu.VMEM)
SMEM = pl.BlockSpec(memory_space=pltpu.SMEM)
EXACT = lax.Precision.HIGHEST
NN = (((1,), (0,)), ((), ()))
NT = (((1,), (1,)), ((), ()))
TN = (((0,), (0,)), ((), ()))
GROUP = 8
TILE = 128
VMEM_LIMIT = 12 * 1024 * 1024
LIST_ROWS = 16
PIECES = 4


def shifted(value, axis, steps):
    count = lax.axis_size(axis)
    pairs = [(source, (source + steps) % count) for source in range(count)]
    return lax.ppermute(value, axis, pairs)


def exact_dot(left, right, dims=NN):
    return lax.dot_general(left, right, dims, precision=EXACT, preferred_element_type=jnp.float32)


def kernel_call(body, out_shape, in_specs, flops, bytes_accessed, slots=None):
    return pl.pallas_call(
        body,
        out_shape=out_shape,
        in_specs=in_specs,
        out_specs=jax.tree.map(lambda _: VMEM, out_shape),
        scratch_shapes=[] if slots is None else [pltpu.SMEM(slots, jnp.int32)],
        compiler_params=pltpu.CompilerParams(vmem_limit_bytes=VMEM_LIMIT),
        cost_estimate=pl.CostEstimate(flops=flops // 16, bytes_accessed=bytes_accessed // 16, transcendentals=0),
    )


def fill_slots(slots_ref, cols_ref, live_ref, first, place_of):
    rows, stored = cols_ref.shape
    count = slots_ref.shape[1] - 1
    for row in range(rows):
        for index in range(count):
            slots_ref[row, index] = -1
        for at in range(stored):
            name = cols_ref[row, at] - first
            inside = (name >= 0) & (name < count) & (at < live_ref[row])
            slots_ref[row, jnp.where(inside, place_of(jnp.clip(name, 0, count - 1)), count)] = at


def accumulate(slots_ref, hessian_ref, operand_ref, base, total):
    rows, _, size, _ = hessian_ref.shape
    shards, shard_rows, _ = operand_ref.shape
    each = shard_rows // size
    for index in range(shards * each):
        start = index % each * size
        block = operand_ref[index // each, start : start + size, :]
        parts = []
        for row in range(rows):
            slot = slots_ref[row, base + index]
            live = jnp.where(slot >= 0, 1.0, 0.0).astype(jnp.float32)
            stored = hessian_ref[row, jnp.maximum(slot, 0)]
            parts.append(stored * jnp.broadcast_to(live, (size, size)).astype(jnp.bfloat16))
        term = jnp.dot(jnp.concatenate(parts, 0), block, preferred_element_type=jnp.float32)
        total = term if total is None else total + term
    return total


def near_body(count, *refs):
    cols_ref, live_ref, bases_ref, hessian_ref = refs[:4]
    operands, (out_ref, slots_ref) = refs[4:-2], refs[-2:]
    fill_slots(slots_ref, cols_ref, live_ref, 0, lambda name: name)
    total = None
    for at, operand_ref in enumerate(operands):
        total = accumulate(slots_ref, hessian_ref, operand_ref, bases_ref[at], total)
    out_ref[...] = total


def halo_total(first, which, cols_ref, live_ref, lists_ref, bases_ref, hessian_ref, lower_ref, upper_ref, total_ref, slots_ref):
    halo = lists_ref.shape[1]
    fill_slots(slots_ref, cols_ref, live_ref, first, lambda name: list_place(lists_ref, name))
    total = accumulate(slots_ref, hessian_ref, lower_ref, bases_ref[which], total_ref[...])
    return accumulate(slots_ref, hessian_ref, upper_ref, halo + bases_ref[which], total)


def list_place(lists_ref, name):
    halo = lists_ref.shape[1]
    side = jnp.where(name >= halo, 1, 0).astype(jnp.int32)
    return side * halo + lists_ref[side, name - side * halo]


def middle_body(first, which, *refs):
    out_ref, slots_ref = refs[-2:]
    out_ref[...] = halo_total(first, which, *refs[:-2], slots_ref)


def interval(bounds_ref):
    return 0.5 * (bounds_ref[0] + bounds_ref[1]), 0.5 * (bounds_ref[1] - bounds_ref[0])


def first_body(first, which, *refs):
    *operands, bounds_ref, vectors_ref, one_ref, cast_ref, slots_ref = refs
    centre, half = interval(bounds_ref)
    total = halo_total(first, which, *operands, slots_ref)
    one = (total - centre * vectors_ref[...]) / half
    one_ref[...] = one
    cast_ref[...] = one.astype(jnp.bfloat16)


def second_body(first, which, *refs):
    *operands, bounds_ref, one_ref, vectors_ref, two_ref, cast_ref, slots_ref = refs
    centre, half = interval(bounds_ref)
    total = halo_total(first, which, *operands, slots_ref)
    two = 2.0 * (total - centre * one_ref[...]) / half - vectors_ref[...]
    two_ref[...] = two
    cast_ref[...] = two.astype(jnp.bfloat16)


def place_rows(number_ref, piece, rows):
    return pl.ds(pl.multiple_of((piece ^ number_ref[0]) * rows, GROUP), rows)


def scatter_pieces(number_ref, out_ref, value):
    rows = out_ref.shape[0] // PIECES
    for piece in range(PIECES):
        out_ref[place_rows(number_ref, piece, rows), :] = value[piece * rows : (piece + 1) * rows, :]


def ordered_pieces(number_ref, in_ref):
    rows = in_ref.shape[0] // PIECES
    return jnp.concatenate([in_ref[place_rows(number_ref, piece, rows), :] for piece in range(PIECES)], 0)


def lower_tiles(count):
    return [(row, col) for row in range(count) for col in range(row + 1)]


def gram_body(number_ref, two_ref, out_ref):
    two = two_ref[...]
    cols = [two[:, at * TILE : (at + 1) * TILE] for at in range(two.shape[1] // TILE)]
    tiles = [exact_dot(cols[row], cols[col], TN) for row, col in lower_tiles(len(cols))]
    scatter_pieces(number_ref, out_ref, jnp.concatenate(tiles, 0))


def third_body(first, which, *refs):
    *operands, number_ref, two_ref, out_ref, slots_ref = refs
    image = halo_total(first, which, *operands, slots_ref)
    scatter_pieces(number_ref, out_ref, exact_dot(two_ref[...], image, TN))


def over_lanes(value, lane):
    return jnp.broadcast_to(value[:, lane : lane + 1], value.shape)


def over_rows(value, row):
    return jnp.broadcast_to(value[row : row + 1, :], value.shape)


def eliminate(tile, first, last):
    count = tile.shape[0] // GROUP
    rows = [tile[index * GROUP : (index + 1) * GROUP, :] for index in range(count)]
    sub = lax.broadcasted_iota(jnp.int32, rows[0].shape, 0)
    lane = lax.broadcasted_iota(jnp.int32, rows[0].shape, 1)
    for step in range(first, last):
        start = step * GROUP
        pivot_cols = [over_lanes(rows[step], start + col) for col in range(GROUP)]
        factors = {
            below: [over_lanes(rows[below], start + col) for col in range(GROUP)]
            for below in range(step + 1, count)
        }
        inside = (lane >= start) & (lane < start + GROUP)
        forward = jnp.where(inside, jnp.where(lane - start == sub, 1.0, 0.0), rows[step])
        solved = forward
        for pivot in range(GROUP):
            here = sub == pivot
            value = over_rows(pivot_cols[pivot], pivot)
            inverse = 1.0 / value
            ratio = pivot_cols[pivot] * inverse
            row = over_rows(forward, pivot)
            forward = jnp.where(
                here, row * lax.rsqrt(value), jnp.where(sub > pivot, forward - ratio * row, forward)
            )
            solved = jnp.where(here, row * inverse, solved - ratio * row)
            for col in range(pivot + 1, GROUP):
                top = over_rows(pivot_cols[col], pivot)
                pivot_cols[col] = jnp.where(here, top * inverse, pivot_cols[col] - ratio * top)
        rows[step] = jnp.where(lane < start + GROUP, forward, 0.0)
        solved_rows = [over_rows(solved, pivot) for pivot in range(GROUP)]
        for below in range(step + 1, count):
            terms = [factors[below][col] * solved_rows[col] for col in range(GROUP)]
            while len(terms) > 1:
                terms = [terms[at] + terms[at + 1] for at in range(0, len(terms), 2)]
            rows[below] = jnp.where(inside, 0.0, rows[below]) - terms[0]
    return jnp.concatenate(rows, 0)


def unpack_body(total_rows, number_ref, gram_ref, *tile_refs):
    tiles = ordered_pieces(number_ref, gram_ref) / total_rows
    for at, tile_ref in enumerate(tile_refs):
        tile_ref[...] = tiles[at * TILE : (at + 1) * TILE, :]


def eliminate_body(first, last, tile_ref, out_ref):
    out_ref[...] = eliminate(tile_ref[...], first, last)


def update_body(at, count, *refs):
    inputs = refs[: len(refs) // 2]
    outputs = refs[len(refs) // 2 :]
    names = [name for name in lower_tiles(count) if name[1] >= at]
    tiles = {name: ref[...] for name, ref in zip(names, inputs)}
    column = {row: exact_dot(tiles[row, at], tiles[at, at], NT) for row in range(at + 1, count)}
    for (row, col), out_ref in zip(names, outputs):
        if row == at:
            out_ref[...] = tiles[row, col]
        elif col == at:
            out_ref[...] = column[row]
        else:
            out_ref[...] = tiles[row, col] - exact_dot(column[row], column[col], NT)


def basis_body(count, *refs):
    *tile_refs, two_ref, basis_ref, inverse_ref = refs
    tiles = {name: ref[...] for name, ref in zip(lower_tiles(count), tile_refs)}
    inverse = {}
    for row in range(count):
        inverse[row, row] = tiles[row, row]
        for col in range(row):
            mixed = exact_dot(tiles[row, col], inverse[col, col])
            for mid in range(col + 1, row):
                mixed = mixed + exact_dot(tiles[row, mid], inverse[mid, col])
            inverse[row, col] = -exact_dot(tiles[row, row], mixed)
    zero = jnp.zeros((TILE, TILE), jnp.float32)
    whole = jnp.concatenate(
        [
            jnp.concatenate([inverse[row, col] if col <= row else zero for col in range(count)], 1)
            for row in range(count)
        ],
        0,
    )
    inverse_ref[...] = whole
    basis_ref[...] = exact_dot(two_ref[...], whole, NT)


def projected_body(total_rows, number_ref, cross_ref, inverse_ref, projected_ref):
    cross = ordered_pieces(number_ref, cross_ref) / total_rows
    projected_ref[...] = exact_dot(exact_dot(inverse_ref[...], cross), inverse_ref[...], NT)


def factor_stages(total_rows, count, number, two):
    rows, modes = two.shape
    tile = jax.ShapeDtypeStruct((TILE, TILE), jnp.float32)
    names = lower_tiles(count)
    work = 4 * 10 ** 9

    def unpack(gram):
        body = functools.partial(unpack_body, total_rows)
        return kernel_call(body, (tile,) * len(names), [SMEM, VMEM], work // 8, gram.size)(number, gram)

    def elimination(at, first, last):
        def stage(tiles):
            place = names.index((at, at))
            call = kernel_call(functools.partial(eliminate_body, first, last), tile, [VMEM], work // 2, TILE * TILE)
            return tiles[:place] + (call(tiles[place]),) + tiles[place + 1 :]

        return stage

    def update(at):
        def stage(tiles):
            picked = [index for index, name in enumerate(names) if name[1] >= at]
            body = functools.partial(update_body, at, count)
            call = kernel_call(body, (tile,) * len(picked), [VMEM] * len(picked), work // 4, TILE * TILE)
            new = call(*[tiles[index] for index in picked])
            return tuple(new[picked.index(index)] if index in picked else old for index, old in enumerate(tiles))

        return stage

    def finish(tiles):
        outs = (jax.ShapeDtypeStruct((rows, modes), jnp.float32), jax.ShapeDtypeStruct((modes, modes), jnp.float32))
        body = functools.partial(basis_body, count)
        return kernel_call(body, outs, [VMEM] * (len(names) + 1), work // 2, rows * modes)(*tiles, two)

    groups = TILE // GROUP
    cuts = [0, groups // 4, groups // 2 + 1, groups]
    stages = [unpack]
    for at in range(count):
        stages += [elimination(at, first, last) for first, last in zip(cuts, cuts[1:])]
        if at + 1 < count:
            stages.append(update(at))
    return stages + [finish]


def tied(left, right):
    return lax.optimization_barrier((left, right))


def partner_value(value, axis, bit):
    return lax.ppermute(value, axis, [(at, at ^ bit) for at in range(lax.axis_size(axis))])


def axis_bits(axis):
    return [(axis, 1 << at) for at in range(lax.axis_size(axis).bit_length() - 1)]


def device_number(halved):
    number = 0
    for axis, bit in halved:
        number = number * 2 + (lax.axis_index(axis) // bit) % 2
    return number.astype(jnp.int32).reshape(1)


def halving(axis, bit):
    def step(value):
        half = value.shape[0] // 2
        got = partner_value(value[half:], axis, bit)
        return lambda: value[:half] + got

    return step


def doubling(axis, bit):
    def step(value):
        got = partner_value(value, axis, bit)
        return lambda: value + got

    return step


def joining(axis, bit):
    def step(value):
        got = partner_value(value, axis, bit)
        return lambda: jnp.concatenate([value, got], 0)

    return step


def run_beside(value, steps, state, stages):
    stages = list(stages)
    for index, step in enumerate(steps):
        value, state = tied(value, state)
        join = step(value)
        due = -(-len(stages) // (len(steps) - index))
        for _ in range(due):
            state = stages.pop(0)(state)
        value = join()
        if due:
            value, state = tied(value, state)
    return value, state


def local(vectors, hessian, block_cols, live_blocks, halo_lists, bounds):
    row_blocks, stored, size, _ = hessian.shape
    rows, modes = vectors.shape
    splits = lax.axis_size("split")
    region_blocks = row_blocks * splits
    halo_blocks = halo_lists.shape[2]
    whole = halo_blocks == region_blocks and region_blocks <= 256
    total_rows = rows * lax.axis_size(AXES)

    paired = whole and splits == 2
    core = lax.axis_index("split").astype(jnp.int32)
    swapped = lambda value: lax.ppermute(value, "split", [(0, 1), (1, 0)])
    near_first = [core * row_blocks, (1 - core) * row_blocks] if paired else [0]
    bases = jnp.stack(near_first).astype(jnp.int32) if paired else jnp.zeros((1,), jnp.int32)

    def sent(operand, region):
        if whole:
            return operand, operand
        width = modes // splits
        start = core * width
        blocks = region[:, :rows].reshape(region_blocks, size, modes)
        share = lambda listed: lax.dynamic_slice_in_dim(blocks[listed], start, width, 2).reshape(-1, width)
        return share(halo_lists[0, 1]), share(halo_lists[0, 0])

    def gathered(value):
        if paired:
            return [value[None], swapped(value)[None]]
        if whole:
            return [lax.all_gather(value, "split", axis=0)]
        return [lax.all_gather(value, "split", axis=1, tiled=True)[None]]

    listed = jnp.pad(halo_lists[0], ((0, LIST_ROWS - 2), (0, modes - halo_blocks)))
    first = vectors.astype(jnp.bfloat16)
    if whole:
        first = jnp.concatenate([first, listed.astype(jnp.bfloat16)], 0)

    def near_parts(operand):
        if paired:
            return [operand[None], swapped(operand)[None]]
        return [lax.all_gather(operand, "split", axis=0)]

    def exchange(operand):
        near = near_parts(operand)
        up, down = sent(operand, near[0])
        return near, shifted(up, "region", 1), shifted(down, "region", -1)

    first_near, first_lower, first_upper = exchange(first)
    if whole:
        orders = [first_lower[rows + 1, :halo_blocks], first_upper[rows, :halo_blocks]]
        lists = jnp.stack(orders).astype(jnp.int32)
    else:
        lists = jnp.broadcast_to(jnp.arange(halo_blocks, dtype=jnp.int32), (2, halo_blocks))

    wide = jax.ShapeDtypeStruct((rows, modes), jnp.float32)
    narrow = jax.ShapeDtypeStruct((rows, modes), jnp.bfloat16)
    square = jax.ShapeDtypeStruct((modes, modes), jnp.float32)
    tile_rows = len(lower_tiles(modes // TILE)) * TILE
    work = 2 * rows * size * modes
    square_work = 2 * rows * modes * modes
    traffic = hessian.size * 2 + 3 * rows * modes * 4
    cores, *other_cores = axis_bits("split")
    near, across, *far = axis_bits("region")
    between = other_cores + far
    gram_number, cross_number = device_number([cores, across]), device_number([cores, near])
    halo_slots = (row_blocks, 2 * halo_blocks + 1)

    def step(body, outs, own, lower, upper, scalars, extra, beside=()):
        call = kernel_call(
            functools.partial(near_body, region_blocks),
            wide,
            [SMEM] * 3 + [VMEM] * (1 + len(own)),
            work * region_blocks,
            traffic,
            (row_blocks, region_blocks + 1),
        )
        total = call(block_cols, live_blocks, bases, hessian, *own)
        lower, upper, total, beside = lax.optimization_barrier((lower, upper, total, beside))
        pairs = list(zip(gathered(lower), gathered(upper)))
        for which, pair in enumerate(pairs):
            last = which == len(pairs) - 1
            given = (block_cols, live_blocks, lists, bases, hessian, *pair, total) + ((*scalars, *extra) if last else ())
            specs = [SMEM] * 4 + [VMEM] * 4 + ([SMEM] * len(scalars) + [VMEM] * len(extra) if last else [])
            body_of = functools.partial(body if last else middle_body, region_blocks, which)
            cost = 2 * work * halo_blocks // len(pairs)
            total = kernel_call(body_of, outs if last else wide, specs, cost, traffic, halo_slots)(*given)
        return (total, beside) if beside else total

    one, one_cast = step(first_body, (wide, narrow), first_near, first_lower, first_upper, (bounds,), (vectors,))
    two, two_cast = step(second_body, (wide, narrow), *exchange(one_cast), (bounds,), (one, vectors))

    packed = jax.ShapeDtypeStruct((tile_rows, TILE), jnp.float32)
    third = exchange(two_cast)
    gram = kernel_call(gram_body, packed, [SMEM, VMEM], square_work, traffic)(gram_number, two)
    for step_of in [halving(*cores), halving(*across)] + [doubling(*bit) for bit in between]:
        gram = step_of(gram)()
    cross, (gram,) = step(third_body, square, *third, (cross_number,), (two,), (gram,))
    cross = halving(*cores)(cross)()

    fold = modes // TILE
    cut = gram.shape[0] // fold
    folded = jnp.concatenate([gram[at * cut : (at + 1) * cut] for at in range(fold)], 1)
    flat = lambda value: [value[:, at * TILE : (at + 1) * TILE] for at in range(fold)]
    half = cross.shape[0] // 2
    got = partner_value(jnp.concatenate([folded, cross[half:]], 0), *near)
    both = jnp.concatenate([folded, cross[:half]], 0) + got
    got = partner_value(both, *across)
    gram = joining(*cores)(jnp.concatenate(flat(both[:cut]) + flat(got[:cut]), 0))()
    cross = both[cut:] + got[cut:]
    stages = factor_stages(float(total_rows), modes // TILE, gram_number, two)
    steps = [doubling(*bit) for bit in between] + [joining(*near), joining(*cores)]
    cross, (basis, inverse) = run_beside(cross, steps, gram, stages)
    body_of = functools.partial(projected_body, float(total_rows))
    call = kernel_call(body_of, square, [SMEM] + [VMEM] * 2, 2 * square_work, traffic)
    return basis, call(cross_number, cross, inverse)


def solution(mesh):
    placed = (
        P(("region", "split"), None),
        P(("region", "split"), None, None, None),
        P(("region", "split"), None),
        P(("region", "split")),
        P("region", None, None),
        P(),
    )
    return jax.shard_map(
        local,
        mesh=mesh,
        in_specs=placed,
        out_specs=(P(("region", "split"), None), P()),
        check_vma=False,
    )
```

```python
import functools
import jax
import jax.numpy as jnp
from jax import lax
from jax.experimental import pallas as pl
from jax.experimental.pallas import tpu as pltpu
from jax.sharding import PartitionSpec as P

AXES = ("region", "split")
VMEM = pl.BlockSpec(memory_space=pltpu.VMEM)
SMEM = pl.BlockSpec(memory_space=pltpu.SMEM)
EXACT = lax.Precision.HIGHEST
NN = (((1,), (0,)), ((), ()))
NT = (((1,), (1,)), ((), ()))
TN = (((0,), (0,)), ((), ()))
GROUP = 8
TILE = 128
VMEM_LIMIT = 12 * 1024 * 1024
LIST_ROWS = 16
PIECES = 4
CHUNKS = 2


def shifted(value, axis, steps):
    count = lax.axis_size(axis)
    pairs = [(source, (source + steps) % count) for source in range(count)]
    return lax.ppermute(value, axis, pairs)


def exact_dot(left, right, dims=NN):
    return lax.dot_general(left, right, dims, precision=EXACT, preferred_element_type=jnp.float32)


def kernel_call(body, outs, in_specs, flops, bytes_accessed, slots=None):
    pinned = lambda out: out[1] if isinstance(out, tuple) else pltpu.VMEM(out.shape, out.dtype)
    call = pl.pallas_call(
        body,
        out_shape=[pinned(out) for out in outs],
        in_specs=in_specs,
        out_specs=[VMEM for _ in outs],
        scratch_shapes=[] if slots is None else [pltpu.SMEM(slots, jnp.int32)],
        compiler_params=pltpu.CompilerParams(vmem_limit_bytes=VMEM_LIMIT),
        cost_estimate=pl.CostEstimate(flops=flops // 16, bytes_accessed=bytes_accessed // 16, transcendentals=0),
    )

    def run(*operands):
        placed = [
            pltpu.with_memory_space_constraint(value, pltpu.VMEM) if spec is VMEM else value
            for spec, value in zip(in_specs, operands)
        ]
        return call(*placed)

    return run


def fill_slots(slots_ref, cols_ref, live_ref, sections):
    rows, stored = cols_ref.shape
    unused = slots_ref.shape[1] - 1
    for row in range(rows):
        for index in range(unused):
            slots_ref[row, index] = -1
        for at in range(stored):
            place = unused
            for first, count, column, column_of in sections:
                name = cols_ref[row, at] - first
                inside = (name >= 0) & (name < count) & (at < live_ref[row])
                place = jnp.where(inside, column + column_of(jnp.clip(name, 0, count - 1)), place)
            slots_ref[row, place] = at


def accumulate(slots_ref, hessian_ref, chunk_refs, base, total):
    rows, _, size, _ = hessian_ref.shape
    shards, shard_rows, _ = chunk_refs[0].shape
    each = shard_rows // size
    for index in range(shards * each):
        start = index % each * size
        block = jnp.concatenate([ref[index // each, start : start + size, :] for ref in chunk_refs], 1)
        parts = []
        for row in range(rows):
            slot = slots_ref[row, base + index]
            live = jnp.where(slot >= 0, 1.0, 0.0).astype(jnp.float32)
            stored = hessian_ref[row, jnp.maximum(slot, 0)]
            parts.append(stored * jnp.broadcast_to(live, (size, size)).astype(jnp.bfloat16))
        term = jnp.dot(jnp.concatenate(parts, 0), block, preferred_element_type=jnp.float32)
        total = term if total is None else total + term
    return total


def near_body(region, halo, chunks, *refs):
    cols_ref, live_ref, list_ref, places_ref, hessian_ref = refs[:5]
    operands, (out_ref, slots_ref) = refs[5:-2], refs[-2:]
    groups = [operands[at : at + chunks] for at in range(0, len(operands), chunks)]
    sections = [(0, region, 0, lambda name: name)]
    if len(groups) > 2:
        sections.append((places_ref[2], halo, region, lambda name: list_ref[name]))
    fill_slots(slots_ref, cols_ref, live_ref, sections)
    total = None
    for at, group in enumerate(groups):
        total = accumulate(slots_ref, hessian_ref, group, places_ref[at % 2] + at // 2 * region, total)
    out_ref[...] = total


def halo_total(halo, chunks, which, cols_ref, live_ref, list_ref, places_ref, hessian_ref, *rest):
    *group, total_ref, slots_ref = rest
    fill_slots(slots_ref, cols_ref, live_ref, [(places_ref[3], halo, 0, lambda name: list_ref[name])])
    return accumulate(slots_ref, hessian_ref, group, places_ref[which], total_ref[...])


def split_refs(refs, chunks, extra):
    cut = 5 + chunks + 1
    return refs[:cut], refs[cut : cut + extra], refs[cut + extra : -1], refs[-1]


def middle_body(halo, chunks, which, *refs):
    common, _, (out_ref,), slots_ref = split_refs(refs, chunks, 0)
    out_ref[...] = halo_total(halo, chunks, which, *common, slots_ref)


def interval(bounds_ref):
    return 0.5 * (bounds_ref[0] + bounds_ref[1]), 0.5 * (bounds_ref[1] - bounds_ref[0])


def store_cast(value, cast_refs):
    width = value.shape[1] // len(cast_refs)
    for at, cast_ref in enumerate(cast_refs):
        cast_ref[...] = value[:, at * width : (at + 1) * width].astype(jnp.bfloat16)


def first_body(halo, chunks, which, *refs):
    common, (bounds_ref, vectors_ref), (one_ref, *cast_refs), slots_ref = split_refs(refs, chunks, 2)
    centre, half = interval(bounds_ref)
    total = halo_total(halo, chunks, which, *common, slots_ref)
    one = (total - centre * vectors_ref[...]) / half
    one_ref[...] = one
    store_cast(one, cast_refs)


def second_body(halo, chunks, which, *refs):
    common, (bounds_ref, one_ref, vectors_ref), (two_ref, *cast_refs), slots_ref = split_refs(refs, chunks, 3)
    centre, half = interval(bounds_ref)
    total = halo_total(halo, chunks, which, *common, slots_ref)
    two = 2.0 * (total - centre * one_ref[...]) / half - vectors_ref[...]
    two_ref[...] = two
    store_cast(two, cast_refs)


def place_rows(number_ref, piece, rows):
    return pl.ds(pl.multiple_of((piece ^ number_ref[0]) * rows, GROUP), rows)


def scatter_pieces(number_ref, out_ref, value):
    rows = out_ref.shape[0] // PIECES
    for piece in range(PIECES):
        out_ref[place_rows(number_ref, piece, rows), :] = value[piece * rows : (piece + 1) * rows, :]


def ordered_pieces(number_ref, in_ref):
    rows = in_ref.shape[0] // PIECES
    return jnp.concatenate([in_ref[place_rows(number_ref, piece, rows), :] for piece in range(PIECES)], 0)


def lower_tiles(count):
    return [(row, col) for row in range(count) for col in range(row + 1)]


def gram_body(number_ref, two_ref, out_ref):
    two = two_ref[...]
    cols = [two[:, at * TILE : (at + 1) * TILE] for at in range(two.shape[1] // TILE)]
    tiles = [exact_dot(cols[row], cols[col], TN) for row, col in lower_tiles(len(cols))]
    scatter_pieces(number_ref, out_ref, jnp.concatenate(tiles, 0))


def third_body(halo, chunks, which, *refs):
    common, (number_ref, two_ref), (out_ref,), slots_ref = split_refs(refs, chunks, 2)
    image = halo_total(halo, chunks, which, *common, slots_ref)
    scatter_pieces(number_ref, out_ref, exact_dot(two_ref[...], image, TN))


def over_lanes(value, lane):
    return jnp.broadcast_to(value[:, lane : lane + 1], value.shape)


def over_rows(value, row):
    return jnp.broadcast_to(value[row : row + 1, :], value.shape)


def eliminate(tile, first, last):
    count = tile.shape[0] // GROUP
    rows = [tile[index * GROUP : (index + 1) * GROUP, :] for index in range(count)]
    sub = lax.broadcasted_iota(jnp.int32, rows[0].shape, 0)
    lane = lax.broadcasted_iota(jnp.int32, rows[0].shape, 1)
    for step in range(first, last):
        start = step * GROUP
        pivot_cols = [over_lanes(rows[step], start + col) for col in range(GROUP)]
        factors = {
            below: [over_lanes(rows[below], start + col) for col in range(GROUP)]
            for below in range(step + 1, count)
        }
        inside = (lane >= start) & (lane < start + GROUP)
        forward = jnp.where(inside, jnp.where(lane - start == sub, 1.0, 0.0), rows[step])
        solved = forward
        for pivot in range(GROUP):
            here = sub == pivot
            value = over_rows(pivot_cols[pivot], pivot)
            inverse = 1.0 / value
            ratio = pivot_cols[pivot] * inverse
            row = over_rows(forward, pivot)
            forward = jnp.where(
                here, row * lax.rsqrt(value), jnp.where(sub > pivot, forward - ratio * row, forward)
            )
            solved = jnp.where(here, row * inverse, solved - ratio * row)
            for col in range(pivot + 1, GROUP):
                top = over_rows(pivot_cols[col], pivot)
                pivot_cols[col] = jnp.where(here, top * inverse, pivot_cols[col] - ratio * top)
        rows[step] = jnp.where(lane < start + GROUP, forward, 0.0)
        solved_rows = [over_rows(solved, pivot) for pivot in range(GROUP)]
        for below in range(step + 1, count):
            terms = [factors[below][col] * solved_rows[col] for col in range(GROUP)]
            while len(terms) > 1:
                terms = [terms[at] + terms[at + 1] for at in range(0, len(terms), 2)]
            rows[below] = jnp.where(inside, 0.0, rows[below]) - terms[0]
    return jnp.concatenate(rows, 0)


def unpack_body(total_rows, number_ref, gram_ref, *tile_refs):
    tiles = ordered_pieces(number_ref, gram_ref) / total_rows
    for at, tile_ref in enumerate(tile_refs):
        tile_ref[...] = tiles[at * TILE : (at + 1) * TILE, :]


def eliminate_body(first, last, tile_ref, out_ref):
    out_ref[...] = eliminate(tile_ref[...], first, last)


def update_body(at, count, *refs):
    inputs = refs[: len(refs) // 2]
    outputs = refs[len(refs) // 2 :]
    names = [name for name in lower_tiles(count) if name[1] >= at]
    tiles = {name: ref[...] for name, ref in zip(names, inputs)}
    column = {row: exact_dot(tiles[row, at], tiles[at, at], NT) for row in range(at + 1, count)}
    for (row, col), out_ref in zip(names, outputs):
        if row == at:
            out_ref[...] = tiles[row, col]
        elif col == at:
            out_ref[...] = column[row]
        else:
            out_ref[...] = tiles[row, col] - exact_dot(column[row], column[col], NT)


def basis_body(count, *refs):
    *tile_refs, two_ref, basis_ref, inverse_ref = refs
    tiles = {name: ref[...] for name, ref in zip(lower_tiles(count), tile_refs)}
    inverse = {}
    for row in range(count):
        inverse[row, row] = tiles[row, row]
        for col in range(row):
            mixed = exact_dot(tiles[row, col], inverse[col, col])
            for mid in range(col + 1, row):
                mixed = mixed + exact_dot(tiles[row, mid], inverse[mid, col])
            inverse[row, col] = -exact_dot(tiles[row, row], mixed)
    zero = jnp.zeros((TILE, TILE), jnp.float32)
    whole = jnp.concatenate(
        [
            jnp.concatenate([inverse[row, col] if col <= row else zero for col in range(count)], 1)
            for row in range(count)
        ],
        0,
    )
    inverse_ref[...] = whole
    basis_ref[...] = exact_dot(two_ref[...], whole, NT)


def projected_body(total_rows, number_ref, cross_ref, inverse_ref, projected_ref):
    cross = ordered_pieces(number_ref, cross_ref) / total_rows
    projected_ref[...] = exact_dot(exact_dot(inverse_ref[...], cross), inverse_ref[...], NT)


def factor_stages(total_rows, count, number, two):
    rows, modes = two.shape
    tile = jax.ShapeDtypeStruct((TILE, TILE), jnp.float32)
    names = lower_tiles(count)
    work = 4 * 10 ** 9

    def unpack(gram):
        body = functools.partial(unpack_body, total_rows)
        return tuple(kernel_call(body, [tile] * len(names), [SMEM, VMEM], work // 8, gram.size)(number, gram))

    def elimination(at, first, last):
        def stage(tiles):
            place = names.index((at, at))
            call = kernel_call(functools.partial(eliminate_body, first, last), [tile], [VMEM], work // 2, TILE * TILE)
            return tiles[:place] + tuple(call(tiles[place])) + tiles[place + 1 :]

        return stage

    def update(at):
        def stage(tiles):
            picked = [index for index, name in enumerate(names) if name[1] >= at]
            body = functools.partial(update_body, at, count)
            call = kernel_call(body, [tile] * len(picked), [VMEM] * len(picked), work // 4, TILE * TILE)
            new = call(*[tiles[index] for index in picked])
            return tuple(new[picked.index(index)] if index in picked else old for index, old in enumerate(tiles))

        return stage

    def finish(tiles):
        outs = [(None, jax.ShapeDtypeStruct((rows, modes), jnp.float32)), jax.ShapeDtypeStruct((modes, modes), jnp.float32)]
        body = functools.partial(basis_body, count)
        return tuple(kernel_call(body, outs, [VMEM] * (len(names) + 1), work // 2, rows * modes)(*tiles, two))

    groups = TILE // GROUP
    cuts = [0, groups // 4, groups // 2 + 1, groups]
    stages = [unpack]
    for at in range(count):
        stages += [elimination(at, first, last) for first, last in zip(cuts, cuts[1:])]
        if at + 1 < count:
            stages.append(update(at))
    return stages + [finish]


def tied(left, right):
    return lax.optimization_barrier((left, right))


def partner_value(value, axis, bit):
    return lax.ppermute(value, axis, [(at, at ^ bit) for at in range(lax.axis_size(axis))])


def axis_bits(axis):
    return [(axis, 1 << at) for at in range(lax.axis_size(axis).bit_length() - 1)]


def device_number(halved):
    number = 0
    for axis, bit in halved:
        number = number * 2 + (lax.axis_index(axis) // bit) % 2
    return number.astype(jnp.int32).reshape(1)


def halving(axis, bit):
    def step(value):
        half = value.shape[0] // 2
        got = partner_value(value[half:], axis, bit)
        return lambda: value[:half] + got

    return step


def doubling(axis, bit):
    def step(value):
        got = partner_value(value, axis, bit)
        return lambda: value + got

    return step


def joining(axis, bit):
    def step(value):
        got = partner_value(value, axis, bit)
        return lambda: jnp.concatenate([value, got], 0)

    return step


def run_beside(value, steps, state, stages):
    stages = list(stages)
    for index, step in enumerate(steps):
        value, state = tied(value, state)
        join = step(value)
        due = -(-len(stages) // (len(steps) - index))
        for _ in range(due):
            state = stages.pop(0)(state)
        value = join()
        if due:
            value, state = tied(value, state)
    return value, state


def local(vectors, hessian, block_cols, live_blocks, halo_lists, bounds):
    row_blocks, stored, size, _ = hessian.shape
    rows, modes = vectors.shape
    splits, regions = lax.axis_size("split"), lax.axis_size("region")
    region_blocks = row_blocks * splits
    halo_blocks = halo_lists.shape[2]
    total_rows = float(rows * splits * regions)
    relayed = halo_blocks == region_blocks <= 256 and splits == 2 and regions % 2 == 0
    chunks = CHUNKS if relayed else 1
    width = modes // chunks
    core = lax.axis_index("split").astype(jnp.int32)
    odd = (lax.axis_index("region") % 2).astype(jnp.int32)

    cores, *other_cores = axis_bits("split")
    near, across, *far = axis_bits("region")
    between = other_cores + far
    gram_number, cross_number = device_number([cores, across]), device_number([cores, near])

    wide = jax.ShapeDtypeStruct((rows, modes), jnp.float32)
    casts = [jax.ShapeDtypeStruct((rows, width), jnp.bfloat16)] * chunks
    square = jax.ShapeDtypeStruct((modes, modes), jnp.float32)
    work = 2 * rows * size * modes
    square_work = 2 * rows * modes * modes
    traffic = hessian.size * 2 + 3 * rows * modes * 4

    def other_core(parts):
        return [partner_value(part, *cores) for part in parts]

    def passed_on(value):
        pairs = [(at, (at + (-2 if at % 2 else 2)) % regions) for at in range(regions)]
        return lax.ppermute(value, "region", pairs)

    def wrapped(parts):
        return [part[None] for part in parts]

    if relayed:
        near_places = [core * row_blocks, (1 - core) * row_blocks]
        partner_first = region_blocks + halo_blocks * (1 - odd)
        places = jnp.stack(near_places + [partner_first, region_blocks + halo_blocks * odd]).astype(jnp.int32)
        side_places = [places, places]
    else:
        side_places = [jnp.array([0, 0, 0, region_blocks + side * halo_blocks], jnp.int32) for side in range(2)]
        places = side_places[0]

    def exchange(parts):
        if relayed:
            partner = [partner_value(part, *near) for part in parts]
            distant = [passed_on(part) for part in partner]
            return [parts, other_core(parts), partner, other_core(partner)], [distant]
        (operand,) = parts
        region = lax.all_gather(operand, "split", axis=0)
        share = modes // splits
        blocks = region.reshape(region_blocks, size, modes)
        sent = lambda listed: lax.dynamic_slice_in_dim(blocks[listed], core * share, share, 2).reshape(-1, share)
        lower = shifted(sent(halo_lists[0, 1]), "region", 1)
        upper = shifted(sent(halo_lists[0, 0]), "region", -1)
        return [[region]], [[lower], [upper]]

    def step(body, outs, exchanged, lists, extra, extra_specs, beside=()):
        nearby, sides = exchanged
        nearby = [group if group[0].ndim == 3 else wrapped(group) for group in nearby]
        operands = [part for group in nearby for part in group]
        columns = region_blocks + (halo_blocks if relayed else 0) + 1
        call = kernel_call(
            functools.partial(near_body, region_blocks, halo_blocks, chunks),
            [wide],
            [SMEM] * 4 + [VMEM] * (1 + len(operands)),
            work * columns,
            traffic,
            (row_blocks, columns),
        )
        (total,) = call(block_cols, live_blocks, lists[0], places, hessian, *operands)
        sides, total, beside = lax.optimization_barrier((sides, total, beside))
        pieces = []
        for side, parts in enumerate(sides):
            if relayed:
                pieces += [(side, 0, wrapped(parts)), (side, 1, wrapped(other_core(parts)))]
            else:
                pieces.append((side, 0, [lax.all_gather(parts[0], "split", axis=1, tiled=True)[None]]))
        for at, (side, which, parts) in enumerate(pieces):
            last = at == len(pieces) - 1
            given = (block_cols, live_blocks, lists[-1 if relayed else side], side_places[side], hessian, *parts, total)
            specs = [SMEM] * 4 + [VMEM] * (2 + len(parts))
            body_of = functools.partial(body if last else middle_body, halo_blocks, chunks, which)
            cost, table = work * halo_blocks // len(pieces), (row_blocks, halo_blocks + 1)
            if last:
                result = kernel_call(body_of, outs, specs + extra_specs, cost, traffic, table)(*given, *extra)
            else:
                (total,) = kernel_call(body_of, [wide], specs, cost, traffic, table)(*given)
        return (result, beside) if beside else result

    first = vectors.astype(jnp.bfloat16)
    parts = [first[:, at * width : (at + 1) * width] for at in range(chunks)]
    if relayed:
        listed = jnp.pad(halo_lists[0], ((0, LIST_ROWS - 2), (0, width - halo_blocks)))
        parts[0] = jnp.concatenate([parts[0], listed.astype(jnp.bfloat16)], 0)
    exchanged = exchange(parts)
    if relayed:
        partner, ((distant, *_),) = exchanged[0][2][0], exchanged[1]
        numbers = lambda part: part[rows : rows + 2, :halo_blocks].astype(jnp.int32)
        chosen = lambda pair, side: jnp.where(side == 0, pair[0], pair[1])
        lists = [chosen(numbers(partner), odd), chosen(numbers(distant), 1 - odd)]
    else:
        lists = [jnp.arange(halo_blocks, dtype=jnp.int32)] * 2

    filtering = [SMEM, VMEM, VMEM]
    one, *parts = step(first_body, [wide] + casts, exchanged, lists, (bounds, vectors), filtering[:2])
    two, *parts = step(second_body, [wide] + casts, exchange(parts), lists, (bounds, one, vectors), filtering)

    tile_rows = len(lower_tiles(modes // TILE)) * TILE
    packed = jax.ShapeDtypeStruct((tile_rows, TILE), jnp.float32)
    third = exchange(parts)
    (gram,) = kernel_call(gram_body, [packed], [SMEM, VMEM], square_work, traffic)(gram_number, two)
    for step_of in [halving(*cores), halving(*across), doubling(*near)]:
        gram = step_of(gram)()
    (cross,), (gram,) = step(third_body, [square], third, lists, (cross_number, two), [SMEM, VMEM], (gram,))
    cross = halving(*near)(halving(*cores)(cross)())()

    fold = modes // TILE
    cut = gram.shape[0] // fold
    folded = jnp.concatenate([gram[at * cut : (at + 1) * cut] for at in range(fold)], 1)
    flat = lambda value: [value[:, at * TILE : (at + 1) * TILE] for at in range(fold)]
    both = jnp.concatenate([folded, cross], 0)
    for bit in between:
        both = doubling(*bit)(both)()
    got = partner_value(both, *across)
    gram = joining(*cores)(jnp.concatenate(flat(both[:cut]) + flat(got[:cut]), 0))()
    cross = both[cut:] + got[cut:]
    stages = factor_stages(total_rows, modes // TILE, gram_number, two)
    steps = [joining(*near), joining(*cores)]
    cross, (basis, inverse) = run_beside(cross, steps, gram, stages)
    body_of = functools.partial(projected_body, total_rows)
    call = kernel_call(body_of, [(None, square)], [SMEM] + [VMEM] * 2, 2 * square_work, traffic)
    return basis, call(cross_number, cross, inverse)[0]


def solution(mesh):
    placed = (
        P(("region", "split"), None),
        P(("region", "split"), None, None, None),
        P(("region", "split"), None),
        P(("region", "split")),
        P("region", None, None),
        P(),
    )
    return jax.shard_map(
        local,
        mesh=mesh,
        in_specs=placed,
        out_specs=(P(("region", "split"), None), P()),
        check_vma=False,
    )
```

```python
import functools
import jax
import jax.numpy as jnp
from jax import lax
from jax.experimental import pallas as pl
from jax.experimental.pallas import tpu as pltpu
from jax.sharding import PartitionSpec as P

AXES = ("region", "split")
VMEM = pl.BlockSpec(memory_space=pltpu.VMEM)
SMEM = pl.BlockSpec(memory_space=pltpu.SMEM)
EXACT = lax.Precision.HIGHEST
NN = (((1,), (0,)), ((), ()))
NT = (((1,), (1,)), ((), ()))
TN = (((0,), (0,)), ((), ()))
GROUP = 8
TILE = 128
VMEM_LIMIT = 12 * 1024 * 1024
LIST_ROWS = 16
PIECES = 4


def shifted(value, axis, steps):
    count = lax.axis_size(axis)
    pairs = [(source, (source + steps) % count) for source in range(count)]
    return lax.ppermute(value, axis, pairs)


def exact_dot(left, right, dims=NN):
    return lax.dot_general(left, right, dims, precision=EXACT, preferred_element_type=jnp.float32)


def kernel_call(body, out_shape, in_specs, flops, bytes_accessed, slots=None):
    return pl.pallas_call(
        body,
        out_shape=out_shape,
        in_specs=in_specs,
        out_specs=jax.tree.map(lambda _: VMEM, out_shape),
        scratch_shapes=[] if slots is None else [pltpu.SMEM(slots, jnp.int32)],
        compiler_params=pltpu.CompilerParams(vmem_limit_bytes=VMEM_LIMIT),
        cost_estimate=pl.CostEstimate(flops=flops, bytes_accessed=bytes_accessed // 16, transcendentals=0),
    )


def fill_slots(slots_ref, cols_ref, live_ref, first, place_of):
    rows, stored = cols_ref.shape
    count = slots_ref.shape[1] - 1
    for row in range(rows):
        for index in range(count):
            slots_ref[row, index] = -1
        for at in range(stored):
            name = cols_ref[row, at] - first
            inside = (name >= 0) & (name < count) & (at < live_ref[row])
            slots_ref[row, jnp.where(inside, place_of(jnp.clip(name, 0, count - 1)), count)] = at


def accumulate(slots_ref, hessian_ref, operand_ref, base, total):
    rows, _, size, _ = hessian_ref.shape
    shards, shard_rows, _ = operand_ref.shape
    each = shard_rows // size
    for index in range(shards * each):
        start = index % each * size
        block = operand_ref[index // each, start : start + size, :]
        parts = []
        for row in range(rows):
            slot = slots_ref[row, base + index]
            live = jnp.where(slot >= 0, 1.0, 0.0).astype(jnp.float32)
            stored = hessian_ref[row, jnp.maximum(slot, 0)]
            parts.append(stored * jnp.broadcast_to(live, (size, size)).astype(jnp.bfloat16))
        term = jnp.dot(jnp.concatenate(parts, 0), block, preferred_element_type=jnp.float32)
        total = term if total is None else total + term
    return total


def near_body(count, *refs):
    cols_ref, live_ref, bases_ref, hessian_ref = refs[:4]
    operands, (out_ref, token_ref, slots_ref) = refs[4:-3], refs[-3:]
    fill_slots(slots_ref, cols_ref, live_ref, 0, lambda name: name)
    total = None
    for at, operand_ref in enumerate(operands):
        total = accumulate(slots_ref, hessian_ref, operand_ref, bases_ref[at], total)
    out_ref[...] = total
    token_ref[...] = total[:GROUP, :TILE]


def halo_total(first, which, cols_ref, live_ref, lists_ref, bases_ref, hessian_ref, lower_ref, upper_ref, total_ref, slots_ref):
    halo = lists_ref.shape[1]
    fill_slots(slots_ref, cols_ref, live_ref, first, lambda name: list_place(lists_ref, name))
    total = accumulate(slots_ref, hessian_ref, lower_ref, bases_ref[which], total_ref[...])
    return accumulate(slots_ref, hessian_ref, upper_ref, halo + bases_ref[which], total)


def list_place(lists_ref, name):
    halo = lists_ref.shape[1]
    side = jnp.where(name >= halo, 1, 0).astype(jnp.int32)
    return side * halo + lists_ref[side, name - side * halo]


def middle_body(first, which, *refs):
    out_ref, token_ref, slots_ref = refs[-3:]
    total = halo_total(first, which, *refs[:-3], slots_ref)
    out_ref[...] = total
    token_ref[...] = total[:GROUP, :TILE]


def interval(bounds_ref):
    return 0.5 * (bounds_ref[0] + bounds_ref[1]), 0.5 * (bounds_ref[1] - bounds_ref[0])


def first_body(first, which, *refs):
    *operands, bounds_ref, vectors_ref, one_ref, cast_ref, slots_ref = refs
    centre, half = interval(bounds_ref)
    total = halo_total(first, which, *operands, slots_ref)
    one = (total - centre * vectors_ref[...]) / half
    one_ref[...] = one
    cast_ref[...] = one.astype(jnp.bfloat16)


def second_body(first, which, *refs):
    *operands, bounds_ref, one_ref, vectors_ref, two_ref, cast_ref, slots_ref = refs
    centre, half = interval(bounds_ref)
    total = halo_total(first, which, *operands, slots_ref)
    two = 2.0 * (total - centre * one_ref[...]) / half - vectors_ref[...]
    two_ref[...] = two
    cast_ref[...] = two.astype(jnp.bfloat16)


def place_rows(number_ref, piece, rows):
    return pl.ds(pl.multiple_of((piece ^ number_ref[0]) * rows, GROUP), rows)


def scatter_pieces(number_ref, out_ref, value):
    rows = out_ref.shape[0] // PIECES
    for piece in range(PIECES):
        out_ref[place_rows(number_ref, piece, rows), :] = value[piece * rows : (piece + 1) * rows, :]


def ordered_pieces(number_ref, in_ref):
    rows = in_ref.shape[0] // PIECES
    return jnp.concatenate([in_ref[place_rows(number_ref, piece, rows), :] for piece in range(PIECES)], 0)


def lower_tiles(count):
    return [(row, col) for row in range(count) for col in range(row + 1)]


def gram_body(number_ref, two_ref, _, out_ref):
    two = two_ref[...]
    cols = [two[:, at * TILE : (at + 1) * TILE] for at in range(two.shape[1] // TILE)]
    tiles = [exact_dot(cols[row], cols[col], TN) for row, col in lower_tiles(len(cols))]
    scatter_pieces(number_ref, out_ref, jnp.concatenate(tiles, 0))


def third_body(first, which, *refs):
    *operands, number_ref, two_ref, _, out_ref, slots_ref = refs
    image = halo_total(first, which, *operands, slots_ref)
    scatter_pieces(number_ref, out_ref, exact_dot(two_ref[...], image, TN))


def over_lanes(value, lane):
    return jnp.broadcast_to(value[:, lane : lane + 1], value.shape)


def over_rows(value, row):
    return jnp.broadcast_to(value[row : row + 1, :], value.shape)


def eliminate(tile, first, last):
    count = tile.shape[0] // GROUP
    rows = [tile[index * GROUP : (index + 1) * GROUP, :] for index in range(count)]
    sub = lax.broadcasted_iota(jnp.int32, rows[0].shape, 0)
    lane = lax.broadcasted_iota(jnp.int32, rows[0].shape, 1)
    for step in range(first, last):
        start = step * GROUP
        pivot_cols = [over_lanes(rows[step], start + col) for col in range(GROUP)]
        factors = {
            below: [over_lanes(rows[below], start + col) for col in range(GROUP)]
            for below in range(step + 1, count)
        }
        inside = (lane >= start) & (lane < start + GROUP)
        forward = jnp.where(inside, jnp.where(lane - start == sub, 1.0, 0.0), rows[step])
        solved = forward
        for pivot in range(GROUP):
            here = sub == pivot
            value = over_rows(pivot_cols[pivot], pivot)
            inverse = 1.0 / value
            ratio = pivot_cols[pivot] * inverse
            row = over_rows(forward, pivot)
            forward = jnp.where(
                here, row * lax.rsqrt(value), jnp.where(sub > pivot, forward - ratio * row, forward)
            )
            solved = jnp.where(here, row * inverse, solved - ratio * row)
            for col in range(pivot + 1, GROUP):
                top = over_rows(pivot_cols[col], pivot)
                pivot_cols[col] = jnp.where(here, top * inverse, pivot_cols[col] - ratio * top)
        rows[step] = jnp.where(lane < start + GROUP, forward, 0.0)
        solved_rows = [over_rows(solved, pivot) for pivot in range(GROUP)]
        for below in range(step + 1, count):
            terms = [factors[below][col] * solved_rows[col] for col in range(GROUP)]
            while len(terms) > 1:
                terms = [terms[at] + terms[at + 1] for at in range(0, len(terms), 2)]
            rows[below] = jnp.where(inside, 0.0, rows[below]) - terms[0]
    return jnp.concatenate(rows, 0)


def unpack_body(total_rows, number_ref, gram_ref, *tile_refs):
    tiles = ordered_pieces(number_ref, gram_ref) / total_rows
    for at, tile_ref in enumerate(tile_refs):
        tile_ref[...] = tiles[at * TILE : (at + 1) * TILE, :]


def eliminate_body(first, last, tile_ref, out_ref):
    out_ref[...] = eliminate(tile_ref[...], first, last)


def update_body(at, count, *refs):
    inputs = refs[: len(refs) // 2]
    outputs = refs[len(refs) // 2 :]
    names = [name for name in lower_tiles(count) if name[1] >= at]
    tiles = {name: ref[...] for name, ref in zip(names, inputs)}
    column = {row: exact_dot(tiles[row, at], tiles[at, at], NT) for row in range(at + 1, count)}
    for (row, col), out_ref in zip(names, outputs):
        if row == at:
            out_ref[...] = tiles[row, col]
        elif col == at:
            out_ref[...] = column[row]
        else:
            out_ref[...] = tiles[row, col] - exact_dot(column[row], column[col], NT)


def basis_body(count, *refs):
    *tile_refs, two_ref, basis_ref, inverse_ref = refs
    tiles = {name: ref[...] for name, ref in zip(lower_tiles(count), tile_refs)}
    inverse = {}
    for row in range(count):
        inverse[row, row] = tiles[row, row]
        for col in range(row):
            mixed = exact_dot(tiles[row, col], inverse[col, col])
            for mid in range(col + 1, row):
                mixed = mixed + exact_dot(tiles[row, mid], inverse[mid, col])
            inverse[row, col] = -exact_dot(tiles[row, row], mixed)
    zero = jnp.zeros((TILE, TILE), jnp.float32)
    whole = jnp.concatenate(
        [
            jnp.concatenate([inverse[row, col] if col <= row else zero for col in range(count)], 1)
            for row in range(count)
        ],
        0,
    )
    inverse_ref[...] = whole
    basis_ref[...] = exact_dot(two_ref[...], whole, NT)


def projected_body(total_rows, number_ref, cross_ref, inverse_ref, projected_ref):
    cross = ordered_pieces(number_ref, cross_ref) / total_rows
    projected_ref[...] = exact_dot(exact_dot(inverse_ref[...], cross), inverse_ref[...], NT)


def factor_stages(total_rows, count, number, two):
    rows, modes = two.shape
    tile = jax.ShapeDtypeStruct((TILE, TILE), jnp.float32)
    names = lower_tiles(count)
    work = 10 ** 8

    def unpack(gram):
        body = functools.partial(unpack_body, total_rows)
        return kernel_call(body, (tile,) * len(names), [SMEM, VMEM], work // 8, gram.size)(number, gram)

    def elimination(at, first, last):
        def stage(tiles):
            place = names.index((at, at))
            call = kernel_call(functools.partial(eliminate_body, first, last), tile, [VMEM], work // 2, TILE * TILE)
            return tiles[:place] + (call(tiles[place]),) + tiles[place + 1 :]

        return stage

    def update(at):
        def stage(tiles):
            picked = [index for index, name in enumerate(names) if name[1] >= at]
            body = functools.partial(update_body, at, count)
            call = kernel_call(body, (tile,) * len(picked), [VMEM] * len(picked), work // 4, TILE * TILE)
            new = call(*[tiles[index] for index in picked])
            return tuple(new[picked.index(index)] if index in picked else old for index, old in enumerate(tiles))

        return stage

    def finish(tiles):
        outs = (jax.ShapeDtypeStruct((rows, modes), jnp.float32), jax.ShapeDtypeStruct((modes, modes), jnp.float32))
        body = functools.partial(basis_body, count)
        return kernel_call(body, outs, [VMEM] * (len(names) + 1), work // 2, rows * modes)(*tiles, two)

    groups = TILE // GROUP
    cuts = [0, groups // 4, groups // 2 + 1, groups]
    stages = [unpack]
    for at in range(count):
        stages += [elimination(at, first, last) for first, last in zip(cuts, cuts[1:])]
        if at + 1 < count:
            stages.append(update(at))
    return stages + [finish]


def tied(left, right):
    return lax.optimization_barrier((left, right))


def partner_value(value, axis, bit):
    return lax.ppermute(value, axis, [(at, at ^ bit) for at in range(lax.axis_size(axis))])


def axis_bits(axis):
    return [(axis, 1 << at) for at in range(lax.axis_size(axis).bit_length() - 1)]


def device_number(halved):
    number = 0
    for axis, bit in halved:
        number = number * 2 + (lax.axis_index(axis) // bit) % 2
    return number.astype(jnp.int32).reshape(1)


def halving(axis, bit):
    def step(value):
        half = value.shape[0] // 2
        got = partner_value(value[half:], axis, bit)
        return lambda: value[:half] + got

    return step


def doubling(axis, bit):
    def step(value):
        got = partner_value(value, axis, bit)
        return lambda: value + got

    return step


def joining(axis, bit):
    def step(value):
        got = partner_value(value, axis, bit)
        return lambda: jnp.concatenate([value, got], 0)

    return step


def run_beside(value, steps, state, stages):
    stages = list(stages)
    for index, step in enumerate(steps):
        value, state = tied(value, state)
        join = step(value)
        due = -(-len(stages) // (len(steps) - index))
        for _ in range(due):
            state = stages.pop(0)(state)
        value = join()
        if due:
            value, state = tied(value, state)
    return value, state


def local(vectors, hessian, block_cols, live_blocks, halo_lists, bounds):
    row_blocks, stored, size, _ = hessian.shape
    rows, modes = vectors.shape
    splits = lax.axis_size("split")
    region_blocks = row_blocks * splits
    halo_blocks = halo_lists.shape[2]
    whole = halo_blocks == region_blocks and region_blocks <= 256
    total_rows = rows * lax.axis_size(AXES)

    paired = whole and splits == 2
    core = lax.axis_index("split").astype(jnp.int32)
    swapped = lambda value: lax.ppermute(value, "split", [(0, 1), (1, 0)])
    near_first = [core * row_blocks, (1 - core) * row_blocks] if paired else [0]
    bases = jnp.stack(near_first).astype(jnp.int32) if paired else jnp.zeros((1,), jnp.int32)

    def sent(operand, region):
        if whole:
            return operand, operand
        width = modes // splits
        start = core * width
        blocks = region[:, :rows].reshape(region_blocks, size, modes)
        share = lambda listed: lax.dynamic_slice_in_dim(blocks[listed], start, width, 2).reshape(-1, width)
        return share(halo_lists[0, 1]), share(halo_lists[0, 0])

    def gathered(value):
        if paired:
            return [value[None], swapped(value)[None]]
        if whole:
            return [lax.all_gather(value, "split", axis=0)]
        return [lax.all_gather(value, "split", axis=1, tiled=True)[None]]

    listed = jnp.pad(halo_lists[0], ((0, LIST_ROWS - 2), (0, modes - halo_blocks)))
    first = vectors.astype(jnp.bfloat16)
    if whole:
        first = jnp.concatenate([first, listed.astype(jnp.bfloat16)], 0)

    def near_parts(operand):
        if paired:
            return [operand[None], swapped(operand)[None]]
        return [lax.all_gather(operand, "split", axis=0)]

    def exchange(operand):
        near = near_parts(operand)
        up, down = sent(operand, near[0])
        return near, shifted(up, "region", 1), shifted(down, "region", -1)

    first_near, first_lower, first_upper = exchange(first)
    if whole:
        orders = [first_lower[rows + 1, :halo_blocks], first_upper[rows, :halo_blocks]]
        lists = jnp.stack(orders).astype(jnp.int32)
    else:
        lists = jnp.broadcast_to(jnp.arange(halo_blocks, dtype=jnp.int32), (2, halo_blocks))

    wide = jax.ShapeDtypeStruct((rows, modes), jnp.float32)
    narrow = jax.ShapeDtypeStruct((rows, modes), jnp.bfloat16)
    square = jax.ShapeDtypeStruct((modes, modes), jnp.float32)
    tile_rows = len(lower_tiles(modes // TILE)) * TILE
    work = 2 * rows * size * modes
    square_work = 2 * rows * modes * modes
    traffic = hessian.size * 2 + 3 * rows * modes * 4
    cores, *other_cores = axis_bits("split")
    near, across, *far = axis_bits("region")
    between = other_cores + far
    gram_number, cross_number = device_number([cores, across]), device_number([cores, near])
    halo_slots = (row_blocks, 2 * halo_blocks + 1)

    covering, free = 3 * 10 ** 10, 10 ** 7
    token = jax.ShapeDtypeStruct((GROUP, TILE), jnp.float32)

    def near_total(own):
        call = kernel_call(
            functools.partial(near_body, region_blocks),
            (wide, token),
            [SMEM] * 3 + [VMEM] * (1 + len(own)),
            free,
            traffic,
            (row_blocks, region_blocks + 1),
        )
        return call(block_cols, live_blocks, bases, hessian, *own)

    def halo_part(body, outs, which, pair, total, scalars=(), extra=()):
        specs = [SMEM] * 4 + [VMEM] * 4 + [SMEM] * len(scalars) + [VMEM] * len(extra)
        body_of = functools.partial(body, region_blocks, which)
        call = kernel_call(body_of, outs, specs, covering, traffic, halo_slots)
        return call(block_cols, live_blocks, lists, bases, hessian, *pair, total, *scalars, *extra)

    def step(body, outs, exchanged, scalars, extra):
        own, lower, upper = exchanged
        total, _ = near_total(own)
        *pairs, last = zip(gathered(lower), gathered(upper))
        for which, pair in enumerate(pairs):
            total, _ = halo_part(middle_body, (wide, token), which, pair, total)
        return halo_part(body, outs, len(pairs), last, total, scalars, extra)

    one, one_cast = step(first_body, (wide, narrow), (first_near, first_lower, first_upper), (bounds,), (vectors,))
    two, two_cast = step(second_body, (wide, narrow), exchange(one_cast), (bounds,), (one, vectors))

    own, lower, upper = exchange(two_cast)
    total, after = near_total(own)
    packed = jax.ShapeDtypeStruct((tile_rows, TILE), jnp.float32)
    gram = kernel_call(gram_body, packed, [SMEM, VMEM, VMEM], free, traffic)(gram_number, two, after)
    for step_of in [halving(*cores), halving(*across)]:
        gram = step_of(gram)()
    *pairs, last = zip(gathered(lower), gathered(upper))
    for which, pair in enumerate(pairs):
        total, after = halo_part(middle_body, (wide, token), which, pair, total)
    gram, after = tied(gram, after)
    cross = halo_part(third_body, square, len(pairs), last, total, (cross_number,), (two, after))
    gram = doubling(*near)(gram)()
    for bit in between[:-1]:
        end = doubling(*bit)(gram)
        cross, gram = tied(halving(*cores)(cross)() if bit is between[0] else cross, end())
    ends = [doubling(*between[-1])(gram), halving(*near)(cross)]
    gram, cross = [end() for end in ends]

    fold = modes // TILE
    cut = gram.shape[0] // fold
    folded = jnp.concatenate([gram[at * cut : (at + 1) * cut] for at in range(fold)], 1)
    flat = lambda value: [value[:, at * TILE : (at + 1) * TILE] for at in range(fold)]
    got = partner_value(jnp.concatenate([folded, cross], 0), *across)
    gram = joining(*cores)(jnp.concatenate(flat(folded) + flat(got[:cut]), 0))()
    cross = cross + got[cut:]
    stages = factor_stages(float(total_rows), modes // TILE, gram_number, two)
    steps = [doubling(*bit) for bit in between] + [joining(*near), joining(*cores)]
    cross, (basis, inverse) = run_beside(cross, steps, gram, stages)
    body_of = functools.partial(projected_body, float(total_rows))
    call = kernel_call(body_of, square, [SMEM] + [VMEM] * 2, 2 * square_work, traffic)
    return basis, call(cross_number, cross, inverse)


def solution(mesh):
    placed = (
        P(("region", "split"), None),
        P(("region", "split"), None, None, None),
        P(("region", "split"), None),
        P(("region", "split")),
        P("region", None, None),
        P(),
    )
    return jax.shard_map(
        local,
        mesh=mesh,
        in_specs=placed,
        out_specs=(P(("region", "split"), None), P()),
        check_vma=False,
    )
```

```python
import functools
import jax
import jax.numpy as jnp
from jax import lax
from jax.experimental import pallas as pl
from jax.experimental.pallas import tpu as pltpu
from jax.sharding import PartitionSpec as P

AXES = ("region", "split")
VMEM = pl.BlockSpec(memory_space=pltpu.VMEM)
SMEM = pl.BlockSpec(memory_space=pltpu.SMEM)
EXACT = lax.Precision.HIGHEST
NN = (((1,), (0,)), ((), ()))
NT = (((1,), (1,)), ((), ()))
TN = (((0,), (0,)), ((), ()))
GROUP = 8
TILE = 128
VMEM_LIMIT = 12 * 1024 * 1024
LIST_ROWS = 16
PIECES = 4


def shifted(value, axis, steps):
    count = lax.axis_size(axis)
    pairs = [(source, (source + steps) % count) for source in range(count)]
    return lax.ppermute(value, axis, pairs)


def exact_dot(left, right, dims=NN):
    return lax.dot_general(left, right, dims, precision=EXACT, preferred_element_type=jnp.float32)


def kernel_call(body, out_shape, in_specs, flops, bytes_accessed, slots=None):
    return pl.pallas_call(
        body,
        out_shape=out_shape,
        in_specs=in_specs,
        out_specs=jax.tree.map(lambda _: VMEM, out_shape),
        scratch_shapes=[] if slots is None else [pltpu.SMEM(slots, jnp.int32)],
        compiler_params=pltpu.CompilerParams(vmem_limit_bytes=VMEM_LIMIT),
        cost_estimate=pl.CostEstimate(flops=flops, bytes_accessed=bytes_accessed // 16, transcendentals=0),
    )


def fill_slots(slots_ref, cols_ref, live_ref, first, place_of):
    rows, stored = cols_ref.shape
    count = slots_ref.shape[1] - 1
    for row in range(rows):
        for index in range(count):
            slots_ref[row, index] = -1
        for at in range(stored):
            name = cols_ref[row, at] - first
            inside = (name >= 0) & (name < count) & (at < live_ref[row])
            slots_ref[row, jnp.where(inside, place_of(jnp.clip(name, 0, count - 1)), count)] = at


def accumulate(slots_ref, hessian_ref, operand_ref, base, total):
    rows, _, size, _ = hessian_ref.shape
    shards, shard_rows, _ = operand_ref.shape
    each = shard_rows // size
    for index in range(shards * each):
        start = index % each * size
        block = operand_ref[index // each, start : start + size, :]
        parts = []
        for row in range(rows):
            slot = slots_ref[row, base + index]
            live = jnp.where(slot >= 0, 1.0, 0.0).astype(jnp.float32)
            stored = hessian_ref[row, jnp.maximum(slot, 0)]
            parts.append(stored * jnp.broadcast_to(live, (size, size)).astype(jnp.bfloat16))
        term = jnp.dot(jnp.concatenate(parts, 0), block, preferred_element_type=jnp.float32)
        total = term if total is None else total + term
    return total


def hold_body(blocks_ref, out_ref):
    pltpu.sync_copy(blocks_ref, out_ref)


def near_body(count, *refs):
    cols_ref, live_ref, bases_ref, hessian_ref = refs[:4]
    operands, (out_ref, token_ref, slots_ref) = refs[4:-3], refs[-3:]
    fill_slots(slots_ref, cols_ref, live_ref, 0, lambda name: name)
    total = None
    for at, operand_ref in enumerate(operands):
        total = accumulate(slots_ref, hessian_ref, operand_ref, bases_ref[at], total)
    out_ref[...] = total
    token_ref[...] = total[:GROUP, :TILE]


def halo_total(first, which, cols_ref, live_ref, lists_ref, bases_ref, hessian_ref, lower_ref, upper_ref, total_ref, slots_ref):
    halo = lists_ref.shape[1]
    fill_slots(slots_ref, cols_ref, live_ref, first, lambda name: list_place(lists_ref, name))
    total = accumulate(slots_ref, hessian_ref, lower_ref, bases_ref[which], total_ref[...])
    return accumulate(slots_ref, hessian_ref, upper_ref, halo + bases_ref[which], total)


def list_place(lists_ref, name):
    halo = lists_ref.shape[1]
    side = jnp.where(name >= halo, 1, 0).astype(jnp.int32)
    return side * halo + lists_ref[side, name - side * halo]


def middle_body(first, which, *refs):
    out_ref, token_ref, slots_ref = refs[-3:]
    total = halo_total(first, which, *refs[:-3], slots_ref)
    out_ref[...] = total
    token_ref[...] = total[:GROUP, :TILE]


def interval(bounds_ref):
    return 0.5 * (bounds_ref[0] + bounds_ref[1]), 0.5 * (bounds_ref[1] - bounds_ref[0])


def first_body(first, which, *refs):
    *operands, bounds_ref, vectors_ref, one_ref, cast_ref, slots_ref = refs
    centre, half = interval(bounds_ref)
    total = halo_total(first, which, *operands, slots_ref)
    one = (total - centre * vectors_ref[...]) / half
    one_ref[...] = one
    cast_ref[...] = one.astype(jnp.bfloat16)


def second_body(first, which, *refs):
    *operands, bounds_ref, one_ref, vectors_ref, two_ref, cast_ref, slots_ref = refs
    centre, half = interval(bounds_ref)
    total = halo_total(first, which, *operands, slots_ref)
    two = 2.0 * (total - centre * one_ref[...]) / half - vectors_ref[...]
    two_ref[...] = two
    cast_ref[...] = two.astype(jnp.bfloat16)


def place_rows(number_ref, piece, rows):
    return pl.ds(pl.multiple_of((piece ^ number_ref[0]) * rows, GROUP), rows)


def scatter_pieces(number_ref, out_ref, value):
    rows = out_ref.shape[0] // PIECES
    for piece in range(PIECES):
        out_ref[place_rows(number_ref, piece, rows), :] = value[piece * rows : (piece + 1) * rows, :]


def ordered_pieces(number_ref, in_ref):
    rows = in_ref.shape[0] // PIECES
    return jnp.concatenate([in_ref[place_rows(number_ref, piece, rows), :] for piece in range(PIECES)], 0)


def lower_tiles(count):
    return [(row, col) for row in range(count) for col in range(row + 1)]


def gram_body(number_ref, two_ref, _, out_ref):
    two = two_ref[...]
    cols = [two[:, at * TILE : (at + 1) * TILE] for at in range(two.shape[1] // TILE)]
    tiles = [exact_dot(cols[row], cols[col], TN) for row, col in lower_tiles(len(cols))]
    scatter_pieces(number_ref, out_ref, jnp.concatenate(tiles, 0))


def third_body(first, which, *refs):
    *operands, number_ref, two_ref, _, out_ref, slots_ref = refs
    image = halo_total(first, which, *operands, slots_ref)
    scatter_pieces(number_ref, out_ref, exact_dot(two_ref[...], image, TN))


def over_lanes(value, lane):
    return jnp.broadcast_to(value[:, lane : lane + 1], value.shape)


def over_rows(value, row):
    return jnp.broadcast_to(value[row : row + 1, :], value.shape)


def eliminate(tile):
    count = tile.shape[0] // GROUP
    rows = [tile[index * GROUP : (index + 1) * GROUP, :] for index in range(count)]
    sub = lax.broadcasted_iota(jnp.int32, rows[0].shape, 0)
    lane = lax.broadcasted_iota(jnp.int32, rows[0].shape, 1)
    for step in range(count):
        start = step * GROUP
        pivot_cols = [over_lanes(rows[step], start + col) for col in range(GROUP)]
        factors = {
            below: [over_lanes(rows[below], start + col) for col in range(GROUP)]
            for below in range(step + 1, count)
        }
        inside = (lane >= start) & (lane < start + GROUP)
        forward = jnp.where(inside, jnp.where(lane - start == sub, 1.0, 0.0), rows[step])
        solved = forward
        for one in range(0, GROUP, 2):
            two = one + 1
            left, right = pivot_cols[one], pivot_cols[two]
            top, cross, low = over_rows(left, one), over_rows(left, two), over_rows(right, two)
            inverse = 1.0 / (top * low - cross * cross)
            top_inverse, cross_inverse, low_inverse = low * inverse, -(cross * inverse), top * inverse

            def solve(value):
                upper, lower = over_rows(value, one), over_rows(value, two)
                return top_inverse * upper + cross_inverse * lower, cross_inverse * upper + low_inverse * lower

            def without(value, upper, lower):
                return value - (left * upper + right * lower)

            def reduced(value):
                upper, lower = solve(value)
                return jnp.where(sub == one, upper, jnp.where(sub == two, lower, without(value, upper, lower)))

            for col in range(two + 1, GROUP):
                pivot_cols[col] = reduced(pivot_cols[col])
            upper, lower = solve(forward)
            over_top = 1.0 / top
            first, second = over_rows(forward, one), over_rows(forward, two)
            below_first = (second - cross * over_top * first) * lax.rsqrt(low - cross * cross * over_top)
            below = jnp.where(sub > two, without(forward, upper, lower), forward)
            solved = reduced(solved)
            forward = jnp.where(sub == one, first * lax.rsqrt(top), jnp.where(sub == two, below_first, below))
        rows[step] = jnp.where(lane < start + GROUP, forward, 0.0)
        solved_rows = [over_rows(solved, pivot) for pivot in range(GROUP)]
        for below in range(step + 1, count):
            terms = [factors[below][col] * solved_rows[col] for col in range(GROUP)]
            while len(terms) > 1:
                terms = [terms[at] + terms[at + 1] for at in range(0, len(terms), 2)]
            rows[below] = jnp.where(inside, 0.0, rows[below]) - terms[0]
    return jnp.concatenate(rows, 0)


def scaled_tiles(tiles, count):
    names = lower_tiles(count)
    index = lambda dim: lax.broadcasted_iota(jnp.int32, (TILE, TILE), dim)
    diagonal = {row: jnp.where(index(0) == index(1), tiles[names.index((row, row))], 0.0) for row in range(count)}
    down = {row: lax.rsqrt(jnp.sum(diagonal[row], 1, keepdims=True)) for row in range(count)}
    along = {row: lax.rsqrt(jnp.sum(diagonal[row], 0, keepdims=True)) for row in range(count)}
    return [tile * down[row] * along[col] for (row, col), tile in zip(names, tiles)], along


def first_tile_body(count, total_rows, number_ref, gram_ref, *refs):
    *tile_refs, scale_ref = refs
    packed = ordered_pieces(number_ref, gram_ref) / total_rows
    tiles = [packed[at * TILE : (at + 1) * TILE, :] for at in range(len(tile_refs))]
    tiles, along = scaled_tiles(tiles, count)
    for row in range(count):
        scale_ref[row * GROUP : (row + 1) * GROUP, :] = jnp.broadcast_to(along[row], (GROUP, TILE))
    finish_tile(0, count, dict(zip(lower_tiles(count), tiles)), tile_refs)


def next_tile_body(at, count, *refs):
    names = lower_tiles(count)
    tiles = {name: ref[...] for name, ref in zip(names, refs)}
    finish_tile(at, count, tiles, refs[len(names) :])


def finish_tile(at, count, tiles, out_refs):
    tiles = dict(tiles)
    tiles[at, at] = eliminate(tiles[at, at])
    for row in range(at + 1, count):
        tiles[row, at] = exact_dot(tiles[row, at], tiles[at, at], NT)
    for row in range(at + 1, count):
        for col in range(at + 1, row + 1):
            tiles[row, col] = tiles[row, col] - exact_dot(tiles[row, at], tiles[col, at], NT)
    for name, out_ref in zip(lower_tiles(count), out_refs):
        out_ref[...] = tiles[name]


def basis_body(count, *refs):
    *tile_refs, scale_ref, two_ref, basis_ref, inverse_ref = refs
    tiles = {name: ref[...] for name, ref in zip(lower_tiles(count), tile_refs)}
    inverse = {}
    for row in range(count):
        inverse[row, row] = tiles[row, row]
        for col in range(row):
            mixed = exact_dot(tiles[row, col], inverse[col, col])
            for mid in range(col + 1, row):
                mixed = mixed + exact_dot(tiles[row, mid], inverse[mid, col])
            inverse[row, col] = -exact_dot(tiles[row, row], mixed)
    zero = jnp.zeros((TILE, TILE), jnp.float32)
    whole = jnp.concatenate(
        [
            jnp.concatenate(
                [inverse[row, col] * scale_ref[col * GROUP, :][None] if col <= row else zero for col in range(count)], 1
            )
            for row in range(count)
        ],
        0,
    )
    inverse_ref[...] = whole
    basis_ref[...] = exact_dot(two_ref[...], whole, NT)


def projected_body(total_rows, number_ref, cross_ref, inverse_ref, projected_ref):
    cross = ordered_pieces(number_ref, cross_ref) / total_rows
    projected_ref[...] = exact_dot(exact_dot(inverse_ref[...], cross), inverse_ref[...], NT)


def factor_stages(total_rows, count, number, two):
    rows, modes = two.shape
    tile = jax.ShapeDtypeStruct((TILE, TILE), jnp.float32)
    scale = jax.ShapeDtypeStruct((count * GROUP, TILE), jnp.float32)
    names = lower_tiles(count)
    work = 10**8

    def first(gram):
        body = functools.partial(first_tile_body, count, total_rows)
        return tuple(kernel_call(body, (tile,) * len(names) + (scale,), [SMEM, VMEM], work, gram.size)(number, gram))

    def following(at):
        def stage(state):
            body = functools.partial(next_tile_body, at, count)
            call = kernel_call(body, (tile,) * len(names), [VMEM] * len(names), work, TILE * TILE)
            return tuple(call(*state[:-1])) + state[-1:]

        return stage

    def finish(state):
        outs = (jax.ShapeDtypeStruct((rows, modes), jnp.float32), jax.ShapeDtypeStruct((modes, modes), jnp.float32))
        body = functools.partial(basis_body, count)
        return tuple(kernel_call(body, outs, [VMEM] * (len(names) + 2), work, rows * modes)(*state, two))

    return [first] + [following(at) for at in range(1, count)] + [finish]


def tied(left, right):
    return lax.optimization_barrier((left, right))


def partner_value(value, axis, bit):
    return lax.ppermute(value, axis, [(at, at ^ bit) for at in range(lax.axis_size(axis))])


def axis_bits(axis):
    return [(axis, 1 << at) for at in range(lax.axis_size(axis).bit_length() - 1)]


def device_number(halved):
    number = 0
    for axis, bit in halved:
        number = number * 2 + (lax.axis_index(axis) // bit) % 2
    return number.astype(jnp.int32).reshape(1)


def halving(axis, bit):
    def step(value):
        half = value.shape[0] // 2
        got = partner_value(value[half:], axis, bit)
        return lambda: value[:half] + got

    return step


def doubling(axis, bit):
    def step(value):
        got = partner_value(value, axis, bit)
        return lambda: value + got

    return step


def joining(axis, bit):
    def step(value):
        got = partner_value(value, axis, bit)
        return lambda: jnp.concatenate([value, got], 0)

    return step


def run_beside(value, steps, state, stages):
    stages = list(stages)
    for index, step in enumerate(steps):
        value, state = tied(value, state)
        join = step(value)
        due = -(-len(stages) // (len(steps) - index))
        for _ in range(due):
            state = stages.pop(0)(state)
        value = join()
        if due:
            value, state = tied(value, state)
    return value, state


def local(vectors, hessian, block_cols, live_blocks, halo_lists, bounds):
    row_blocks, stored, size, _ = hessian.shape
    rows, modes = vectors.shape
    splits = lax.axis_size("split")
    region_blocks = row_blocks * splits
    halo_blocks = halo_lists.shape[2]
    whole = halo_blocks == region_blocks and region_blocks <= 256
    total_rows = rows * lax.axis_size(AXES)

    paired = whole and splits == 2
    core = lax.axis_index("split").astype(jnp.int32)
    swapped = lambda value: lax.ppermute(value, "split", [(0, 1), (1, 0)])
    near_first = [core * row_blocks, (1 - core) * row_blocks] if paired else [0]
    bases = jnp.stack(near_first).astype(jnp.int32) if paired else jnp.zeros((1,), jnp.int32)

    def sent(operand, region):
        if whole:
            return operand, operand
        width = modes // splits
        start = core * width
        blocks = region[:, :rows].reshape(region_blocks, size, modes)
        share = lambda listed: lax.dynamic_slice_in_dim(blocks[listed], start, width, 2).reshape(-1, width)
        return share(halo_lists[0, 1]), share(halo_lists[0, 0])

    def gathered(value):
        if paired:
            return [value[None], swapped(value)[None]]
        if whole:
            return [lax.all_gather(value, "split", axis=0)]
        return [lax.all_gather(value, "split", axis=1, tiled=True)[None]]

    listed = jnp.pad(halo_lists[0], ((0, LIST_ROWS - 2), (0, modes - halo_blocks)))
    first = vectors.astype(jnp.bfloat16)
    if whole:
        first = jnp.concatenate([first, listed.astype(jnp.bfloat16)], 0)

    def near_parts(operand):
        if paired:
            return [operand[None], swapped(operand)[None]]
        return [lax.all_gather(operand, "split", axis=0)]

    def exchange(operand):
        near = near_parts(operand)
        up, down = sent(operand, near[0])
        return near, shifted(up, "region", 1), shifted(down, "region", -1)

    first_near, first_lower, first_upper = exchange(first)
    if whole:
        orders = [first_lower[rows + 1, :halo_blocks], first_upper[rows, :halo_blocks]]
        lists = jnp.stack(orders).astype(jnp.int32)
    else:
        lists = jnp.broadcast_to(jnp.arange(halo_blocks, dtype=jnp.int32), (2, halo_blocks))

    wide = jax.ShapeDtypeStruct((rows, modes), jnp.float32)
    narrow = jax.ShapeDtypeStruct((rows, modes), jnp.bfloat16)
    square = jax.ShapeDtypeStruct((modes, modes), jnp.float32)
    tile_rows = len(lower_tiles(modes // TILE)) * TILE
    work = 2 * rows * size * modes
    square_work = 2 * rows * modes * modes
    traffic = hessian.size * 2 + 3 * rows * modes * 4
    cores, *other_cores = axis_bits("split")
    near, across, *far = axis_bits("region")
    between = other_cores + far
    gram_number, cross_number = device_number([cores, across]), device_number([cores, near])
    halo_slots = (row_blocks, 2 * halo_blocks + 1)

    covering, free = 3 * 10 ** 10, 10 ** 7
    token = jax.ShapeDtypeStruct((GROUP, TILE), jnp.float32)

    held = pl.pallas_call(
        hold_body,
        out_shape=pltpu.VMEM(hessian.shape, hessian.dtype),
        in_specs=[pl.BlockSpec(memory_space=pl.ANY)],
        out_specs=VMEM,
        compiler_params=pltpu.CompilerParams(vmem_limit_bytes=VMEM_LIMIT),
    )(hessian)

    def near_total(own):
        call = kernel_call(
            functools.partial(near_body, region_blocks),
            (wide, token),
            [SMEM] * 3 + [VMEM] * (1 + len(own)),
            free,
            traffic,
            (row_blocks, region_blocks + 1),
        )
        return call(block_cols, live_blocks, bases, held, *own)

    def halo_part(body, outs, which, pair, total, scalars=(), extra=()):
        specs = [SMEM] * 4 + [VMEM] * 4 + [SMEM] * len(scalars) + [VMEM] * len(extra)
        body_of = functools.partial(body, region_blocks, which)
        call = kernel_call(body_of, outs, specs, covering, traffic, halo_slots)
        return call(block_cols, live_blocks, lists, bases, held, *pair, total, *scalars, *extra)

    def step(body, outs, exchanged, scalars, extra):
        own, lower, upper = exchanged
        total, _ = near_total(own)
        *pairs, last = zip(gathered(lower), gathered(upper))
        for which, pair in enumerate(pairs):
            total, _ = halo_part(middle_body, (wide, token), which, pair, total)
        return halo_part(body, outs, len(pairs), last, total, scalars, extra)

    one, one_cast = step(first_body, (wide, narrow), (first_near, first_lower, first_upper), (bounds,), (vectors,))
    two, two_cast = step(second_body, (wide, narrow), exchange(one_cast), (bounds,), (one, vectors))

    own, lower, upper = exchange(two_cast)
    total, after = near_total(own)
    packed = jax.ShapeDtypeStruct((tile_rows, TILE), jnp.float32)
    gram = kernel_call(gram_body, packed, [SMEM, VMEM, VMEM], free, traffic)(gram_number, two, after)
    for step_of in [halving(*cores), halving(*across)]:
        gram = step_of(gram)()
    *pairs, last = zip(gathered(lower), gathered(upper))
    for which, pair in enumerate(pairs):
        total, after = halo_part(middle_body, (wide, token), which, pair, total)
    gram, after = tied(gram, after)
    cross = halo_part(third_body, square, len(pairs), last, total, (cross_number,), (two, after))
    cross = halving(*cores)(cross)()

    fold = modes // TILE
    cut = gram.shape[0] // fold
    folded = jnp.concatenate([gram[at * cut : (at + 1) * cut] for at in range(fold)], 1)
    flat = lambda value: [value[:, at * TILE : (at + 1) * TILE] for at in range(fold)]
    half = cross.shape[0] // 2
    got = partner_value(jnp.concatenate([folded, cross[half:]], 0), *near)
    both = jnp.concatenate([folded, cross[:half]], 0) + got
    for bit in between:
        both = doubling(*bit)(both)()
    got = partner_value(both, *across)
    gram = joining(*cores)(jnp.concatenate(flat(both[:cut]) + flat(got[:cut]), 0))()
    cross = both[cut:] + got[cut:]
    stages = factor_stages(float(total_rows), modes // TILE, gram_number, two)
    steps = [joining(*near), joining(*cores)]
    cross, (basis, inverse) = run_beside(cross, steps, gram, stages)
    body_of = functools.partial(projected_body, float(total_rows))
    call = kernel_call(body_of, square, [SMEM] + [VMEM] * 2, 2 * square_work, traffic)
    return basis, call(cross_number, cross, inverse)


def solution(mesh):
    placed = (
        P(("region", "split"), None),
        P(("region", "split"), None, None, None),
        P(("region", "split"), None),
        P(("region", "split")),
        P("region", None, None),
        P(),
    )
    return jax.shard_map(
        local,
        mesh=mesh,
        in_specs=placed,
        out_specs=(P(("region", "split"), None), P()),
        check_vma=False,
    )
```

```python
import functools
import jax
import jax.numpy as jnp
from jax import lax
from jax.experimental import pallas as pl
from jax.experimental.pallas import tpu as pltpu
from jax.sharding import PartitionSpec as P

AXES = ("region", "split")
VMEM = pl.BlockSpec(memory_space=pltpu.VMEM)
SMEM = pl.BlockSpec(memory_space=pltpu.SMEM)
EXACT = lax.Precision.HIGHEST
NN = (((1,), (0,)), ((), ()))
NT = (((1,), (1,)), ((), ()))
TN = (((0,), (0,)), ((), ()))
GROUP = 8
TILE = 128
VMEM_LIMIT = 12 * 1024 * 1024
LIST_ROWS = 16
PIECES = 4


def shifted(value, axis, steps):
    count = lax.axis_size(axis)
    pairs = [(source, (source + steps) % count) for source in range(count)]
    return lax.ppermute(value, axis, pairs)


def exact_dot(left, right, dims=NN):
    return lax.dot_general(left, right, dims, precision=EXACT, preferred_element_type=jnp.float32)


def kernel_call(body, out_shape, in_specs, flops, bytes_accessed, slots=None, scratch=()):
    return pl.pallas_call(
        body,
        out_shape=out_shape,
        in_specs=in_specs,
        out_specs=jax.tree.map(lambda _: VMEM, out_shape),
        scratch_shapes=([] if slots is None else [pltpu.SMEM(slots, jnp.int32)]) + list(scratch),
        compiler_params=pltpu.CompilerParams(vmem_limit_bytes=VMEM_LIMIT),
        cost_estimate=pl.CostEstimate(flops=flops, bytes_accessed=bytes_accessed // 16, transcendentals=0),
    )


def fill_slots(slots_ref, cols_ref, live_ref, first, place_of):
    rows, stored = cols_ref.shape
    count = slots_ref.shape[1] - 1

    @pl.loop(0, count)
    def _(index):
        for row in range(rows):
            slots_ref[row, index] = -1

    @pl.loop(0, stored)
    def _(at):
        for row in range(rows):
            name = cols_ref[row, at] - first
            inside = (name >= 0) & (name < count) & (at < live_ref[row])
            slots_ref[row, jnp.where(inside, place_of(jnp.clip(name, 0, count - 1)), count)] = at


def accumulate(slots_ref, hessian_ref, operand_ref, base, total_ref):
    rows, _, size, _ = hessian_ref.shape
    shards, shard_rows, _ = operand_ref.shape
    each = shard_rows // size
    for shard in range(shards):

        @pl.loop(0, each)
        def _(at):
            block = operand_ref[shard, pl.ds(pl.multiple_of(at * size, size), size), :]
            for row in range(rows):
                slot = slots_ref[row, base + shard * each + at]
                live = jnp.where(slot >= 0, 1.0, 0.0).astype(jnp.float32)
                stored = hessian_ref[row, jnp.maximum(slot, 0)]
                masked = stored * jnp.broadcast_to(live, (size, size)).astype(jnp.bfloat16)
                term = jnp.dot(masked, block, preferred_element_type=jnp.float32)
                place = slice(row * size, (row + 1) * size)
                total_ref[place, :] += term


def hold_body(blocks_ref, out_ref):
    pltpu.sync_copy(blocks_ref, out_ref)


def near_body(count, *refs):
    cols_ref, live_ref, bases_ref, hessian_ref = refs[:4]
    operands, (out_ref, token_ref, slots_ref) = refs[4:-3], refs[-3:]
    fill_slots(slots_ref, cols_ref, live_ref, 0, lambda name: name)
    out_ref[...] = jnp.zeros_like(out_ref)
    for at, operand_ref in enumerate(operands):
        accumulate(slots_ref, hessian_ref, operand_ref, bases_ref[at], out_ref)
    token_ref[...] = out_ref[:GROUP, :TILE]


def halo_total(first, which, out_ref, cols_ref, live_ref, lists_ref, bases_ref, hessian_ref, lower_ref, upper_ref, total_ref, slots_ref):
    out_ref[...] = total_ref[...]
    halo = lists_ref.shape[1]
    fill_slots(slots_ref, cols_ref, live_ref, first, lambda name: list_place(lists_ref, name))
    accumulate(slots_ref, hessian_ref, lower_ref, bases_ref[which], out_ref)
    accumulate(slots_ref, hessian_ref, upper_ref, halo + bases_ref[which], out_ref)


def list_place(lists_ref, name):
    halo = lists_ref.shape[1]
    side = jnp.where(name >= halo, 1, 0).astype(jnp.int32)
    return side * halo + lists_ref[side, name - side * halo]


def middle_body(first, which, *refs):
    out_ref, token_ref, slots_ref = refs[-3:]
    halo_total(first, which, out_ref, *refs[:-3], slots_ref)
    token_ref[...] = out_ref[:GROUP, :TILE]


def interval(bounds_ref):
    return 0.5 * (bounds_ref[0] + bounds_ref[1]), 0.5 * (bounds_ref[1] - bounds_ref[0])


def first_body(first, which, *refs):
    *operands, bounds_ref, vectors_ref, one_ref, cast_ref, slots_ref = refs
    centre, half = interval(bounds_ref)
    halo_total(first, which, one_ref, *operands, slots_ref)
    one = (one_ref[...] - centre * vectors_ref[...]) / half
    one_ref[...] = one
    cast_ref[...] = one.astype(jnp.bfloat16)


def second_body(first, which, *refs):
    *operands, bounds_ref, one_ref, vectors_ref, two_ref, cast_ref, slots_ref = refs
    centre, half = interval(bounds_ref)
    halo_total(first, which, two_ref, *operands, slots_ref)
    two = 2.0 * (two_ref[...] - centre * one_ref[...]) / half - vectors_ref[...]
    two_ref[...] = two
    cast_ref[...] = two.astype(jnp.bfloat16)


def place_rows(number_ref, piece, rows):
    return pl.ds(pl.multiple_of((piece ^ number_ref[0]) * rows, GROUP), rows)


def scatter_pieces(number_ref, out_ref, value):
    rows = out_ref.shape[0] // PIECES
    for piece in range(PIECES):
        out_ref[place_rows(number_ref, piece, rows), :] = value[piece * rows : (piece + 1) * rows, :]


def ordered_pieces(number_ref, in_ref):
    rows = in_ref.shape[0] // PIECES
    return jnp.concatenate([in_ref[place_rows(number_ref, piece, rows), :] for piece in range(PIECES)], 0)


def lower_tiles(count):
    return [(row, col) for row in range(count) for col in range(row + 1)]


def gram_body(number_ref, two_ref, _, out_ref):
    two = two_ref[...]
    cols = [two[:, at * TILE : (at + 1) * TILE] for at in range(two.shape[1] // TILE)]
    tiles = [exact_dot(cols[row], cols[col], TN) for row, col in lower_tiles(len(cols))]
    scatter_pieces(number_ref, out_ref, jnp.concatenate(tiles, 0))


def third_body(first, which, *refs):
    *operands, number_ref, two_ref, _, out_ref, slots_ref, image_ref = refs
    halo_total(first, which, image_ref, *operands, slots_ref)
    scatter_pieces(number_ref, out_ref, exact_dot(two_ref[...], image_ref[...], TN))


def over_lanes(value, lane):
    return jnp.take_along_axis(value, jnp.full(value.shape, lane, jnp.int32), axis=1)


def over_rows(value, row):
    return jnp.broadcast_to(value[row : row + 1, :], value.shape)


def pivot_rows(block, start):
    sub = lax.broadcasted_iota(jnp.int32, block.shape, 0)
    lane = lax.broadcasted_iota(jnp.int32, block.shape, 1)
    pivot_cols = [over_lanes(block, start + col) for col in range(GROUP)]
    inside = (lane >= start) & (lane < start + GROUP)
    forward = jnp.where(inside, jnp.where(lane - start == sub, 1.0, 0.0), block)
    solved = forward
    for one in range(0, GROUP, 2):
        two = one + 1
        left, right = pivot_cols[one], pivot_cols[two]
        top, cross, low = over_rows(left, one), over_rows(left, two), over_rows(right, two)
        inverse = 1.0 / (top * low - cross * cross)
        top_inverse, cross_inverse, low_inverse = low * inverse, -(cross * inverse), top * inverse

        def solve(value):
            upper, lower = over_rows(value, one), over_rows(value, two)
            return top_inverse * upper + cross_inverse * lower, cross_inverse * upper + low_inverse * lower

        def without(value, upper, lower):
            return value - (left * upper + right * lower)

        def reduced(value):
            upper, lower = solve(value)
            return jnp.where(sub == one, upper, jnp.where(sub == two, lower, without(value, upper, lower)))

        for col in range(two + 1, GROUP):
            pivot_cols[col] = reduced(pivot_cols[col])
        upper, lower = solve(forward)
        over_top = 1.0 / top
        first, second = over_rows(forward, one), over_rows(forward, two)
        below_first = (second - cross * over_top * first) * lax.rsqrt(low - cross * cross * over_top)
        below = jnp.where(sub > two, without(forward, upper, lower), forward)
        solved = reduced(solved)
        forward = jnp.where(sub == one, first * lax.rsqrt(top), jnp.where(sub == two, below_first, below))
    return jnp.where(lane < start + GROUP, forward, 0.0), solved


def eliminate(tile_ref):
    count = tile_ref.shape[0] // GROUP
    cuts = [0, count // 2, count]
    for begin, end in zip(cuts, cuts[1:]):

        @pl.loop(begin, end)
        def _(step):
            start = pl.multiple_of(step * GROUP, GROUP)
            lane = lax.broadcasted_iota(jnp.int32, (GROUP, tile_ref.shape[1]), 1)
            inside = (lane >= start) & (lane < start + GROUP)
            forward, solved = pivot_rows(tile_ref[pl.ds(start, GROUP), :], start)
            solved_rows = [over_rows(solved, pivot) for pivot in range(GROUP)]
            for below in range(begin, count):
                place = slice(below * GROUP, (below + 1) * GROUP)
                block = tile_ref[place, :]
                terms = [over_lanes(block, start + col) * solved_rows[col] for col in range(GROUP)]
                while len(terms) > 1:
                    terms = [terms[at] + terms[at + 1] for at in range(0, len(terms), 2)]
                kept = jnp.where(inside, 0.0, block) - terms[0]
                tile_ref[place, :] = jnp.where(below > step, kept, jnp.where(below == step, forward, block))


def scaled_tiles(tiles, count):
    names = lower_tiles(count)
    index = lambda dim: lax.broadcasted_iota(jnp.int32, (TILE, TILE), dim)
    diagonal = {row: jnp.where(index(0) == index(1), tiles[names.index((row, row))], 0.0) for row in range(count)}
    down = {row: lax.rsqrt(jnp.sum(diagonal[row], 1, keepdims=True)) for row in range(count)}
    along = {row: lax.rsqrt(jnp.sum(diagonal[row], 0, keepdims=True)) for row in range(count)}
    return [tile * down[row] * along[col] for (row, col), tile in zip(names, tiles)], along


def first_tile_body(count, total_rows, number_ref, gram_ref, *refs):
    *tile_refs, scale_ref = refs
    packed = ordered_pieces(number_ref, gram_ref) / total_rows
    tiles = [packed[at * TILE : (at + 1) * TILE, :] for at in range(len(tile_refs))]
    tiles, along = scaled_tiles(tiles, count)
    for row in range(count):
        scale_ref[row * GROUP : (row + 1) * GROUP, :] = jnp.broadcast_to(along[row], (GROUP, TILE))
    finish_tile(0, count, dict(zip(lower_tiles(count), tiles)), tile_refs)


def next_tile_body(at, count, *refs):
    names = lower_tiles(count)
    tiles = {name: ref[...] for name, ref in zip(names, refs)}
    finish_tile(at, count, tiles, refs[len(names) :])


def finish_tile(at, count, tiles, out_refs):
    tiles = dict(tiles)
    pivot_ref = out_refs[lower_tiles(count).index((at, at))]
    pivot_ref[...] = tiles[at, at]
    eliminate(pivot_ref)
    tiles[at, at] = pivot_ref[...]
    for row in range(at + 1, count):
        tiles[row, at] = exact_dot(tiles[row, at], tiles[at, at], NT)
    for row in range(at + 1, count):
        for col in range(at + 1, row + 1):
            tiles[row, col] = tiles[row, col] - exact_dot(tiles[row, at], tiles[col, at], NT)
    for name, out_ref in zip(lower_tiles(count), out_refs):
        out_ref[...] = tiles[name]


def basis_body(count, *refs):
    *tile_refs, scale_ref, two_ref, basis_ref, inverse_ref = refs
    tiles = {name: ref[...] for name, ref in zip(lower_tiles(count), tile_refs)}
    inverse = {}
    for row in range(count):
        inverse[row, row] = tiles[row, row]
        for col in range(row):
            mixed = exact_dot(tiles[row, col], inverse[col, col])
            for mid in range(col + 1, row):
                mixed = mixed + exact_dot(tiles[row, mid], inverse[mid, col])
            inverse[row, col] = -exact_dot(tiles[row, row], mixed)
    zero = jnp.zeros((TILE, TILE), jnp.float32)
    whole = jnp.concatenate(
        [
            jnp.concatenate(
                [inverse[row, col] * scale_ref[col * GROUP, :][None] if col <= row else zero for col in range(count)], 1
            )
            for row in range(count)
        ],
        0,
    )
    inverse_ref[...] = whole
    basis_ref[...] = exact_dot(two_ref[...], whole, NT)


def projected_body(total_rows, number_ref, cross_ref, inverse_ref, projected_ref):
    cross = ordered_pieces(number_ref, cross_ref) / total_rows
    projected_ref[...] = exact_dot(exact_dot(inverse_ref[...], cross), inverse_ref[...], NT)


def factor_stages(total_rows, count, number, two):
    rows, modes = two.shape
    tile = jax.ShapeDtypeStruct((TILE, TILE), jnp.float32)
    scale = jax.ShapeDtypeStruct((count * GROUP, TILE), jnp.float32)
    names = lower_tiles(count)
    work = 10**8

    def first(gram):
        body = functools.partial(first_tile_body, count, total_rows)
        return tuple(kernel_call(body, (tile,) * len(names) + (scale,), [SMEM, VMEM], work, gram.size)(number, gram))

    def following(at):
        def stage(state):
            body = functools.partial(next_tile_body, at, count)
            call = kernel_call(body, (tile,) * len(names), [VMEM] * len(names), work, TILE * TILE)
            return tuple(call(*state[:-1])) + state[-1:]

        return stage

    def finish(state):
        outs = (jax.ShapeDtypeStruct((rows, modes), jnp.float32), jax.ShapeDtypeStruct((modes, modes), jnp.float32))
        body = functools.partial(basis_body, count)
        return tuple(kernel_call(body, outs, [VMEM] * (len(names) + 2), work, rows * modes)(*state, two))

    return [first] + [following(at) for at in range(1, count)] + [finish]


def tied(left, right):
    return lax.optimization_barrier((left, right))


def partner_value(value, axis, bit):
    return lax.ppermute(value, axis, [(at, at ^ bit) for at in range(lax.axis_size(axis))])


def axis_bits(axis):
    return [(axis, 1 << at) for at in range(lax.axis_size(axis).bit_length() - 1)]


def device_number(halved):
    number = 0
    for axis, bit in halved:
        number = number * 2 + (lax.axis_index(axis) // bit) % 2
    return number.astype(jnp.int32).reshape(1)


def halving(axis, bit):
    def step(value):
        half = value.shape[0] // 2
        got = partner_value(value[half:], axis, bit)
        return lambda: value[:half] + got

    return step


def doubling(axis, bit):
    def step(value):
        got = partner_value(value, axis, bit)
        return lambda: value + got

    return step


def joining(axis, bit):
    def step(value):
        got = partner_value(value, axis, bit)
        return lambda: jnp.concatenate([value, got], 0)

    return step


def run_beside(value, steps, state, stages):
    stages = list(stages)
    for index, step in enumerate(steps):
        value, state = tied(value, state)
        join = step(value)
        due = -(-len(stages) // (len(steps) - index))
        for _ in range(due):
            state = stages.pop(0)(state)
        value = join()
        if due:
            value, state = tied(value, state)
    return value, state


def local(vectors, hessian, block_cols, live_blocks, halo_lists, bounds):
    row_blocks, stored, size, _ = hessian.shape
    rows, modes = vectors.shape
    splits = lax.axis_size("split")
    region_blocks = row_blocks * splits
    halo_blocks = halo_lists.shape[2]
    whole = halo_blocks == region_blocks and region_blocks <= 256
    total_rows = rows * lax.axis_size(AXES)

    paired = whole and splits == 2
    core = lax.axis_index("split").astype(jnp.int32)
    swapped = lambda value: lax.ppermute(value, "split", [(0, 1), (1, 0)])
    near_first = [core * row_blocks, (1 - core) * row_blocks] if paired else [0]
    bases = jnp.stack(near_first).astype(jnp.int32) if paired else jnp.zeros((1,), jnp.int32)

    def sent(operand, region):
        if whole:
            return operand, operand
        width = modes // splits
        start = core * width
        blocks = region[:, :rows].reshape(region_blocks, size, modes)
        share = lambda listed: lax.dynamic_slice_in_dim(blocks[listed], start, width, 2).reshape(-1, width)
        return share(halo_lists[0, 1]), share(halo_lists[0, 0])

    def gathered(value):
        if paired:
            return [value[None], swapped(value)[None]]
        if whole:
            return [lax.all_gather(value, "split", axis=0)]
        return [lax.all_gather(value, "split", axis=1, tiled=True)[None]]

    listed = jnp.pad(halo_lists[0], ((0, LIST_ROWS - 2), (0, modes - halo_blocks)))
    first = vectors.astype(jnp.bfloat16)
    if whole:
        first = jnp.concatenate([first, listed.astype(jnp.bfloat16)], 0)

    def near_parts(operand):
        if paired:
            return [operand[None], swapped(operand)[None]]
        return [lax.all_gather(operand, "split", axis=0)]

    def exchange(operand):
        near = near_parts(operand)
        up, down = sent(operand, near[0])
        return near, shifted(up, "region", 1), shifted(down, "region", -1)

    first_near, first_lower, first_upper = exchange(first)
    if whole:
        orders = [first_lower[rows + 1, :halo_blocks], first_upper[rows, :halo_blocks]]
        lists = jnp.stack(orders).astype(jnp.int32)
    else:
        lists = jnp.broadcast_to(jnp.arange(halo_blocks, dtype=jnp.int32), (2, halo_blocks))

    wide = jax.ShapeDtypeStruct((rows, modes), jnp.float32)
    narrow = jax.ShapeDtypeStruct((rows, modes), jnp.bfloat16)
    square = jax.ShapeDtypeStruct((modes, modes), jnp.float32)
    tile_rows = len(lower_tiles(modes // TILE)) * TILE
    work = 2 * rows * size * modes
    square_work = 2 * rows * modes * modes
    traffic = hessian.size * 2 + 3 * rows * modes * 4
    cores, *other_cores = axis_bits("split")
    near, across, *far = axis_bits("region")
    between = other_cores + far
    gram_number, cross_number = device_number([cores, across]), device_number([cores, near])
    halo_slots = (row_blocks, 2 * halo_blocks + 1)

    covering, free = 3 * 10 ** 10, 10 ** 7
    token = jax.ShapeDtypeStruct((GROUP, TILE), jnp.float32)

    held = pl.pallas_call(
        hold_body,
        out_shape=pltpu.VMEM(hessian.shape, hessian.dtype),
        in_specs=[pl.BlockSpec(memory_space=pl.ANY)],
        out_specs=VMEM,
        compiler_params=pltpu.CompilerParams(vmem_limit_bytes=VMEM_LIMIT),
    )(hessian)

    def near_total(own):
        call = kernel_call(
            functools.partial(near_body, region_blocks),
            (wide, token),
            [SMEM] * 3 + [VMEM] * (1 + len(own)),
            free,
            traffic,
            (row_blocks, region_blocks + 1),
        )
        return call(block_cols, live_blocks, bases, held, *own)

    def halo_part(body, outs, which, pair, total, scalars=(), extra=(), scratch=()):
        specs = [SMEM] * 4 + [VMEM] * 4 + [SMEM] * len(scalars) + [VMEM] * len(extra)
        body_of = functools.partial(body, region_blocks, which)
        call = kernel_call(body_of, outs, specs, covering, traffic, halo_slots, scratch)
        return call(block_cols, live_blocks, lists, bases, held, *pair, total, *scalars, *extra)

    def step(body, outs, exchanged, scalars, extra):
        own, lower, upper = exchanged
        total, _ = near_total(own)
        *pairs, last = zip(gathered(lower), gathered(upper))
        for which, pair in enumerate(pairs):
            total, _ = halo_part(middle_body, (wide, token), which, pair, total)
        return halo_part(body, outs, len(pairs), last, total, scalars, extra)

    one, one_cast = step(first_body, (wide, narrow), (first_near, first_lower, first_upper), (bounds,), (vectors,))
    two, two_cast = step(second_body, (wide, narrow), exchange(one_cast), (bounds,), (one, vectors))

    own, lower, upper = exchange(two_cast)
    total, after = near_total(own)
    packed = jax.ShapeDtypeStruct((tile_rows, TILE), jnp.float32)
    gram = kernel_call(gram_body, packed, [SMEM, VMEM, VMEM], free, traffic)(gram_number, two, after)
    for step_of in [halving(*cores), halving(*across)]:
        gram = step_of(gram)()
    *pairs, last = zip(gathered(lower), gathered(upper))
    for which, pair in enumerate(pairs):
        total, after = halo_part(middle_body, (wide, token), which, pair, total)
    gram, after = tied(gram, after)
    image = pltpu.VMEM((rows, modes), jnp.float32)
    cross = halo_part(third_body, square, len(pairs), last, total, (cross_number,), (two, after), (image,))
    cross = halving(*cores)(cross)()

    fold = modes // TILE
    cut = gram.shape[0] // fold
    folded = jnp.concatenate([gram[at * cut : (at + 1) * cut] for at in range(fold)], 1)
    flat = lambda value: [value[:, at * TILE : (at + 1) * TILE] for at in range(fold)]
    half = cross.shape[0] // 2
    got = partner_value(jnp.concatenate([folded, cross[half:]], 0), *near)
    both = jnp.concatenate([folded, cross[:half]], 0) + got
    for bit in between:
        both = doubling(*bit)(both)()
    got = partner_value(both, *across)
    gram = joining(*cores)(jnp.concatenate(flat(both[:cut]) + flat(got[:cut]), 0))()
    cross = both[cut:] + got[cut:]
    stages = factor_stages(float(total_rows), modes // TILE, gram_number, two)
    steps = [joining(*near), joining(*cores)]
    cross, (basis, inverse) = run_beside(cross, steps, gram, stages)
    body_of = functools.partial(projected_body, float(total_rows))
    call = kernel_call(body_of, square, [SMEM] + [VMEM] * 2, 2 * square_work, traffic)
    return basis, call(cross_number, cross, inverse)


def solution(mesh):
    placed = (
        P(("region", "split"), None),
        P(("region", "split"), None, None, None),
        P(("region", "split"), None),
        P(("region", "split")),
        P("region", None, None),
        P(),
    )
    return jax.shard_map(
        local,
        mesh=mesh,
        in_specs=placed,
        out_specs=(P(("region", "split"), None), P()),
        check_vma=False,
    )
```

```python
import functools
import jax
import jax.numpy as jnp
from jax import lax
from jax.experimental import pallas as pl
from jax.experimental.pallas import tpu as pltpu
from jax.sharding import PartitionSpec as P

AXES = ("region", "split")
VMEM = pl.BlockSpec(memory_space=pltpu.VMEM)
SMEM = pl.BlockSpec(memory_space=pltpu.SMEM)
EXACT = lax.Precision.HIGHEST
NN = (((1,), (0,)), ((), ()))
NT = (((1,), (1,)), ((), ()))
TN = (((0,), (0,)), ((), ()))
GROUP = 8
PIVOTS = 16
TILE = 128
VMEM_LIMIT = 12 * 1024 * 1024
LIST_ROWS = 16
PIECES = 4


def shifted(value, axis, steps):
    count = lax.axis_size(axis)
    pairs = [(source, (source + steps) % count) for source in range(count)]
    return lax.ppermute(value, axis, pairs)


def exact_dot(left, right, dims=NN):
    return lax.dot_general(left, right, dims, precision=EXACT, preferred_element_type=jnp.float32)


def kernel_call(body, out_shape, in_specs, flops, bytes_accessed, slots=None):
    return pl.pallas_call(
        body,
        out_shape=out_shape,
        in_specs=in_specs,
        out_specs=jax.tree.map(lambda out: SMEM if out.dtype == jnp.int32 else VMEM, out_shape),
        scratch_shapes=[] if slots is None else [pltpu.SMEM(slots, jnp.int32)],
        compiler_params=pltpu.CompilerParams(vmem_limit_bytes=VMEM_LIMIT),
        cost_estimate=pl.CostEstimate(flops=flops, bytes_accessed=bytes_accessed // 16, transcendentals=0),
    )


def fill_slots(slots_ref, cols_ref, live_ref, first, place_of):
    rows, stored = cols_ref.shape
    count = slots_ref.shape[1] - 1
    for row in range(rows):
        for index in range(count):
            slots_ref[row, index] = -1
        for at in range(stored):
            name = cols_ref[row, at] - first
            inside = (name >= 0) & (name < count) & (at < live_ref[row])
            slots_ref[row, jnp.where(inside, place_of(jnp.clip(name, 0, count - 1)), count)] = at


def accumulate(slots_ref, hessian_ref, operand_ref, base, total):
    rows, _, size, _ = hessian_ref.shape
    shards, shard_rows, _ = operand_ref.shape
    each = shard_rows // size
    for index in range(shards * each):
        start = index % each * size
        block = operand_ref[index // each, start : start + size, :]
        parts = []
        for row in range(rows):
            slot = slots_ref[row, base + index]
            live = jnp.where(slot >= 0, 1.0, 0.0).astype(jnp.float32)
            stored = hessian_ref[row, jnp.maximum(slot, 0)]
            parts.append(stored * jnp.broadcast_to(live, (size, size)).astype(jnp.bfloat16))
        term = jnp.dot(jnp.concatenate(parts, 0), block, preferred_element_type=jnp.float32)
        total = term if total is None else total + term
    return total


def hold_body(blocks_ref, out_ref):
    pltpu.sync_copy(blocks_ref, out_ref)


def near_body(count, tokens, *refs):
    cols_ref, live_ref, bases_ref, hessian_ref, region_ref, out_ref, *token_refs, slots_ref = refs
    fill_slots(slots_ref, cols_ref, live_ref, 0, lambda name: name)
    total = accumulate(slots_ref, hessian_ref, region_ref, 0, None)
    out_ref[...] = total
    for token_ref in token_refs:
        token_ref[...] = total[:GROUP, :TILE]


def list_place(lists_ref, name):
    halo = lists_ref.shape[1]
    side = jnp.where(name >= halo, 1, 0).astype(jnp.int32)
    return side * halo + lists_ref[side, name - side * halo]


def halo_total(which, slots_ref, bases_ref, hessian_ref, lower_ref, upper_ref, total_ref):
    halo = (slots_ref.shape[1] - 1) // 2
    total = accumulate(slots_ref, hessian_ref, lower_ref, bases_ref[which], total_ref[...])
    return accumulate(slots_ref, hessian_ref, upper_ref, halo + bases_ref[which], total)


def table_body(first, which, cols_ref, live_ref, lists_ref, *refs):
    *operands, out_ref, slots_ref = refs
    fill_slots(slots_ref, cols_ref, live_ref, first, lambda name: list_place(lists_ref, name))
    out_ref[...] = halo_total(which, slots_ref, *operands)


def middle_body(which, *refs):
    operands, (out_ref, *token_refs) = refs[:6], refs[6:]
    total = halo_total(which, *operands)
    out_ref[...] = total
    for token_ref in token_refs:
        token_ref[...] = total[:GROUP, :TILE]


def interval(bounds_ref):
    return 0.5 * (bounds_ref[0] + bounds_ref[1]), 0.5 * (bounds_ref[1] - bounds_ref[0])


def first_body(which, *refs):
    *operands, bounds_ref, vectors_ref, one_ref, cast_ref = refs
    centre, half = interval(bounds_ref)
    total = halo_total(which, *operands)
    one = (total - centre * vectors_ref[...]) / half
    one_ref[...] = one
    cast_ref[...] = one.astype(jnp.bfloat16)


def second_body(which, *refs):
    *operands, bounds_ref, one_ref, vectors_ref, two_ref, cast_ref = refs
    centre, half = interval(bounds_ref)
    total = halo_total(which, *operands)
    two = 2.0 * (total - centre * one_ref[...]) / half - vectors_ref[...]
    two_ref[...] = two
    cast_ref[...] = two.astype(jnp.bfloat16)


def place_rows(number_ref, piece, rows):
    return pl.ds(pl.multiple_of((piece ^ number_ref[0]) * rows, GROUP), rows)


def scatter_pieces(number_ref, out_ref, value):
    rows = out_ref.shape[0] // PIECES
    for piece in range(PIECES):
        out_ref[place_rows(number_ref, piece, rows), :] = value[piece * rows : (piece + 1) * rows, :]


def ordered_pieces(number_ref, in_ref):
    rows = in_ref.shape[0] // PIECES
    return jnp.concatenate([in_ref[place_rows(number_ref, piece, rows), :] for piece in range(PIECES)], 0)


def lower_tiles(count):
    return [(row, col) for row in range(count) for col in range(row + 1)]


def gram_body(number_ref, two_ref, _, out_ref):
    two = two_ref[...]
    cols = [two[:, at * TILE : (at + 1) * TILE] for at in range(two.shape[1] // TILE)]
    tiles = [exact_dot(cols[row], cols[col], TN) for row, col in lower_tiles(len(cols))]
    scatter_pieces(number_ref, out_ref, jnp.concatenate(tiles, 0))


def third_body(which, *refs):
    *operands, number_ref, two_ref, _, out_ref = refs
    image = halo_total(which, *operands)
    scatter_pieces(number_ref, out_ref, exact_dot(two_ref[...], image, TN))


def over_lanes(value, lane):
    return jnp.broadcast_to(value[:, lane : lane + 1], value.shape)


def over_rows(value, row):
    return jnp.broadcast_to(value[row : row + 1, :], value.shape)


def eliminate(tile):
    count = tile.shape[0] // PIVOTS
    rows = [tile[index * PIVOTS : (index + 1) * PIVOTS, :] for index in range(count)]
    sub = lax.broadcasted_iota(jnp.int32, rows[0].shape, 0)
    lane = lax.broadcasted_iota(jnp.int32, rows[0].shape, 1)
    for step in range(count):
        start = step * PIVOTS
        pivot_cols = [over_lanes(rows[step], start + col) for col in range(PIVOTS)]
        factors = {
            below: [over_lanes(rows[below], start + col) for col in range(PIVOTS)]
            for below in range(step + 1, count)
        }
        inside = (lane >= start) & (lane < start + PIVOTS)
        forward = jnp.where(inside, jnp.where(lane - start == sub, 1.0, 0.0), rows[step])
        solved = forward
        for one in range(0, PIVOTS, 2):
            two = one + 1
            left, right = pivot_cols[one], pivot_cols[two]
            top, cross, low = over_rows(left, one), over_rows(left, two), over_rows(right, two)
            inverse = 1.0 / (top * low - cross * cross)
            top_inverse, cross_inverse, low_inverse = low * inverse, -(cross * inverse), top * inverse

            def solve(value):
                upper, lower = over_rows(value, one), over_rows(value, two)
                return top_inverse * upper + cross_inverse * lower, cross_inverse * upper + low_inverse * lower

            def without(value, upper, lower):
                return value - (left * upper + right * lower)

            def reduced(value):
                upper, lower = solve(value)
                return jnp.where(sub == one, upper, jnp.where(sub == two, lower, without(value, upper, lower)))

            for col in range(two + 1, PIVOTS):
                pivot_cols[col] = reduced(pivot_cols[col])
            upper, lower = solve(forward)
            over_top = 1.0 / top
            first, second = over_rows(forward, one), over_rows(forward, two)
            below_first = (second - cross * over_top * first) * lax.rsqrt(low - cross * cross * over_top)
            below = jnp.where(sub > two, without(forward, upper, lower), forward)
            solved = reduced(solved)
            forward = jnp.where(sub == one, first * lax.rsqrt(top), jnp.where(sub == two, below_first, below))
        rows[step] = jnp.where(lane < start + PIVOTS, forward, 0.0)
        solved_rows = [over_rows(solved, pivot) for pivot in range(PIVOTS)]
        for below in range(step + 1, count):
            terms = [factors[below][col] * solved_rows[col] for col in range(PIVOTS)]
            while len(terms) > 1:
                terms = [terms[at] + terms[at + 1] for at in range(0, len(terms), 2)]
            rows[below] = jnp.where(inside, 0.0, rows[below]) - terms[0]
    return jnp.concatenate(rows, 0)


def scaled_tiles(tiles, count):
    names = lower_tiles(count)
    index = lambda dim: lax.broadcasted_iota(jnp.int32, (TILE, TILE), dim)
    diagonal = {row: jnp.where(index(0) == index(1), tiles[names.index((row, row))], 0.0) for row in range(count)}
    down = {row: lax.rsqrt(jnp.sum(diagonal[row], 1, keepdims=True)) for row in range(count)}
    along = {row: lax.rsqrt(jnp.sum(diagonal[row], 0, keepdims=True)) for row in range(count)}
    return [tile * down[row] * along[col] for (row, col), tile in zip(names, tiles)], along


def first_tile_body(count, total_rows, number_ref, gram_ref, *refs):
    *tile_refs, scale_ref = refs
    packed = ordered_pieces(number_ref, gram_ref) / total_rows
    tiles = [packed[at * TILE : (at + 1) * TILE, :] for at in range(len(tile_refs))]
    tiles, along = scaled_tiles(tiles, count)
    for row in range(count):
        scale_ref[row * GROUP : (row + 1) * GROUP, :] = jnp.broadcast_to(along[row], (GROUP, TILE))
    finish_tile(0, count, dict(zip(lower_tiles(count), tiles)), tile_refs)


def next_tile_body(at, count, *refs):
    names = lower_tiles(count)
    tiles = {name: ref[...] for name, ref in zip(names, refs)}
    finish_tile(at, count, tiles, refs[len(names) :])


def finish_tile(at, count, tiles, out_refs):
    tiles = dict(tiles)
    tiles[at, at] = eliminate(tiles[at, at])
    for row in range(at + 1, count):
        tiles[row, at] = exact_dot(tiles[row, at], tiles[at, at], NT)
    for row in range(at + 1, count):
        for col in range(at + 1, row + 1):
            tiles[row, col] = tiles[row, col] - exact_dot(tiles[row, at], tiles[col, at], NT)
    for name, out_ref in zip(lower_tiles(count), out_refs):
        out_ref[...] = tiles[name]


def basis_body(count, *refs):
    *tile_refs, scale_ref, two_ref, basis_ref, inverse_ref = refs
    tiles = {name: ref[...] for name, ref in zip(lower_tiles(count), tile_refs)}
    inverse = {}
    for row in range(count):
        inverse[row, row] = tiles[row, row]
        for col in range(row):
            mixed = exact_dot(tiles[row, col], inverse[col, col])
            for mid in range(col + 1, row):
                mixed = mixed + exact_dot(tiles[row, mid], inverse[mid, col])
            inverse[row, col] = -exact_dot(tiles[row, row], mixed)
    zero = jnp.zeros((TILE, TILE), jnp.float32)
    whole = jnp.concatenate(
        [
            jnp.concatenate(
                [inverse[row, col] * scale_ref[col * GROUP, :][None] if col <= row else zero for col in range(count)], 1
            )
            for row in range(count)
        ],
        0,
    )
    inverse_ref[...] = whole
    basis_ref[...] = exact_dot(two_ref[...], whole, NT)


def projected_body(total_rows, number_ref, cross_ref, inverse_ref, projected_ref):
    cross = ordered_pieces(number_ref, cross_ref) / total_rows
    projected_ref[...] = exact_dot(exact_dot(inverse_ref[...], cross), inverse_ref[...], NT)


def factor_stages(total_rows, count, number, two):
    rows, modes = two.shape
    tile = jax.ShapeDtypeStruct((TILE, TILE), jnp.float32)
    scale = jax.ShapeDtypeStruct((count * GROUP, TILE), jnp.float32)
    names = lower_tiles(count)
    work = 10**8

    def first(gram):
        body = functools.partial(first_tile_body, count, total_rows)
        return tuple(kernel_call(body, (tile,) * len(names) + (scale,), [SMEM, VMEM], work, gram.size)(number, gram))

    def following(at):
        def stage(state):
            body = functools.partial(next_tile_body, at, count)
            call = kernel_call(body, (tile,) * len(names), [VMEM] * len(names), work, TILE * TILE)
            return tuple(call(*state[:-1])) + state[-1:]

        return stage

    def finish(state):
        outs = (jax.ShapeDtypeStruct((rows, modes), jnp.float32), jax.ShapeDtypeStruct((modes, modes), jnp.float32))
        body = functools.partial(basis_body, count)
        return tuple(kernel_call(body, outs, [VMEM] * (len(names) + 2), work, rows * modes)(*state, two))

    return [first] + [following(at) for at in range(1, count)] + [finish]


def tied(left, right):
    return lax.optimization_barrier((left, right))


def partner_value(value, axis, bit):
    return lax.ppermute(value, axis, [(at, at ^ bit) for at in range(lax.axis_size(axis))])


def axis_bits(axis):
    return [(axis, 1 << at) for at in range(lax.axis_size(axis).bit_length() - 1)]


def device_number(halved):
    number = 0
    for axis, bit in halved:
        number = number * 2 + (lax.axis_index(axis) // bit) % 2
    return number.astype(jnp.int32).reshape(1)


def halving(axis, bit):
    def step(value):
        half = value.shape[0] // 2
        got = partner_value(value[half:], axis, bit)
        return lambda: value[:half] + got

    return step


def doubling(axis, bit):
    def step(value):
        got = partner_value(value, axis, bit)
        return lambda: value + got

    return step


def joining(axis, bit):
    def step(value):
        got = partner_value(value, axis, bit)
        return lambda: jnp.concatenate([value, got], 0)

    return step


def run_beside(value, steps, state, stages):
    stages = list(stages)
    for index, step in enumerate(steps):
        value, state = tied(value, state)
        join = step(value)
        due = -(-len(stages) // (len(steps) - index))
        for _ in range(due):
            state = stages.pop(0)(state)
        value = join()
        if due:
            value, state = tied(value, state)
    return value, state


def local(vectors, hessian, block_cols, live_blocks, halo_lists, bounds):
    row_blocks, stored, size, _ = hessian.shape
    rows, modes = vectors.shape
    splits = lax.axis_size("split")
    region_blocks = row_blocks * splits
    halo_blocks = halo_lists.shape[2]
    whole = halo_blocks == region_blocks and region_blocks <= 256
    total_rows = rows * lax.axis_size(AXES)

    paired = whole and splits == 2
    core = lax.axis_index("split").astype(jnp.int32)
    swapped = lambda value: lax.ppermute(value, "split", [(0, 1), (1, 0)])
    halo_first = [core * row_blocks, (1 - core) * row_blocks] if paired else [0]
    bases = jnp.stack(halo_first).astype(jnp.int32) if paired else jnp.zeros((1,), jnp.int32)

    def sent(operand, region):
        if whole:
            return operand, operand
        width = modes // splits
        start = core * width
        blocks = region[:, :rows].reshape(region_blocks, size, modes)
        share = lambda listed: lax.dynamic_slice_in_dim(blocks[listed], start, width, 2).reshape(-1, width)
        return share(halo_lists[0, 1]), share(halo_lists[0, 0])

    def gathered(value):
        if paired:
            return [value[None], swapped(value)[None]]
        if whole:
            return [lax.all_gather(value, "split", axis=0)]
        return [lax.all_gather(value, "split", axis=1, tiled=True)[None]]

    listed = jnp.pad(halo_lists[0], ((0, LIST_ROWS - 2), (0, modes - halo_blocks)))
    first = vectors.astype(jnp.bfloat16)
    if whole:
        first = jnp.concatenate([first, listed.astype(jnp.bfloat16)], 0)

    def exchange(operand):
        region = lax.all_gather(operand, "split", axis=0)
        up, down = sent(operand, region)
        return region, shifted(up, "region", 1), shifted(down, "region", -1)

    first_region, first_lower, first_upper = exchange(first)
    if whole:
        orders = [first_lower[rows + 1, :halo_blocks], first_upper[rows, :halo_blocks]]
        lists = jnp.stack(orders).astype(jnp.int32)
    else:
        lists = jnp.broadcast_to(jnp.arange(halo_blocks, dtype=jnp.int32), (2, halo_blocks))

    wide = jax.ShapeDtypeStruct((rows, modes), jnp.float32)
    narrow = jax.ShapeDtypeStruct((rows, modes), jnp.bfloat16)
    square = jax.ShapeDtypeStruct((modes, modes), jnp.float32)
    tile_rows = len(lower_tiles(modes // TILE)) * TILE
    work = 2 * rows * size * modes
    square_work = 2 * rows * modes * modes
    traffic = hessian.size * 2 + 3 * rows * modes * 4
    cores, *other_cores = axis_bits("split")
    near, across, *far = axis_bits("region")
    between = other_cores + far
    gram_number, cross_number = device_number([cores, across]), device_number([cores, near])
    halo_slots = (row_blocks, 2 * halo_blocks + 1)

    covering, free = 3 * 10 ** 10, 10 ** 7
    token = jax.ShapeDtypeStruct((GROUP, TILE), jnp.float32)

    held = pl.pallas_call(
        hold_body,
        out_shape=pltpu.VMEM(hessian.shape, hessian.dtype),
        in_specs=[pl.BlockSpec(memory_space=pl.ANY)],
        out_specs=VMEM,
        compiler_params=pltpu.CompilerParams(vmem_limit_bytes=VMEM_LIMIT),
    )(hessian)

    def near_total(region, tokens=()):
        call = kernel_call(
            functools.partial(near_body, region_blocks, len(tokens)),
            (wide,) + tokens,
            [SMEM] * 3 + [VMEM] * 2,
            free,
            traffic,
            (row_blocks, region_blocks + 1),
        )
        return call(block_cols, live_blocks, bases, held, region)

    def halo_part(body, outs, table, pair, total, scalars=(), extra=()):
        specs = [SMEM] * 2 + [VMEM] * 4 + [SMEM] * len(scalars) + [VMEM] * len(extra)
        call = kernel_call(body, outs, specs, covering, traffic)
        return call(table, bases, held, *pair, total, *scalars, *extra)

    def pairs_of(lower, upper):
        *pairs, last = zip(gathered(lower), gathered(upper))
        return pairs, last

    (total,) = near_total(first_region)
    pairs, last = pairs_of(first_lower, first_upper)
    pairs.append(last)
    body_of = functools.partial(table_body, region_blocks, 0)
    table_shape = jax.ShapeDtypeStruct(halo_slots, jnp.int32)
    specs = [SMEM] * 4 + [VMEM] * 4
    call = kernel_call(body_of, (wide, table_shape), specs, covering, traffic)
    if len(pairs) == 1:
        pairs.append(tuple(jnp.zeros_like(part) for part in last))
    total, table = call(block_cols, live_blocks, lists, bases, held, *pairs[0], total)
    which = len(pairs) - 1 if paired else 0
    body_of = functools.partial(first_body, which)
    one, one_cast = halo_part(body_of, (wide, narrow), table, pairs[-1], total, (bounds,), (vectors,))

    region, lower, upper = exchange(one_cast)
    (total,) = near_total(region)
    pairs, last = pairs_of(lower, upper)
    for which, pair in enumerate(pairs):
        (total,) = halo_part(functools.partial(middle_body, which), (wide,), table, pair, total)
    body_of = functools.partial(second_body, len(pairs))
    two, two_cast = halo_part(body_of, (wide, narrow), table, last, total, (bounds,), (one, vectors))

    region, lower, upper = exchange(two_cast)
    total, after = near_total(region, (token,))
    packed = jax.ShapeDtypeStruct((tile_rows, TILE), jnp.float32)
    gram = kernel_call(gram_body, packed, [SMEM, VMEM, VMEM], free, traffic)(gram_number, two, after)
    for step_of in [halving(*cores), halving(*across)]:
        gram = step_of(gram)()
    pairs, last = pairs_of(lower, upper)
    for which, pair in enumerate(pairs):
        total, after = halo_part(functools.partial(middle_body, which), (wide, token), table, pair, total)
    gram, after = tied(gram, after)
    body_of = functools.partial(third_body, len(pairs))
    cross = halo_part(body_of, square, table, last, total, (cross_number,), (two, after))
    cross = halving(*cores)(cross)()

    fold = modes // TILE
    cut = gram.shape[0] // fold
    folded = jnp.concatenate([gram[at * cut : (at + 1) * cut] for at in range(fold)], 1)
    half = cross.shape[0] // 2
    got = partner_value(jnp.concatenate([folded, cross[half:]], 0), *near)
    both = jnp.concatenate([folded, cross[:half]], 0) + got
    both = doubling(*between[0])(both)()
    gram = jnp.concatenate([both[:cut, at * TILE : (at + 1) * TILE] for at in range(fold)], 0)
    cross = both[cut:]
    for step_of in [doubling(*bit) for bit in between[1:]] + [joining(*across), joining(*cores)]:
        gram = step_of(gram)()
    stages = factor_stages(float(total_rows), modes // TILE, gram_number, two)
    steps = [doubling(*bit) for bit in between[1:]] + [doubling(*across), joining(*near), joining(*cores)]
    cross, (basis, inverse) = run_beside(cross, steps, gram, stages)
    body_of = functools.partial(projected_body, float(total_rows))
    call = kernel_call(body_of, square, [SMEM] + [VMEM] * 2, 2 * square_work, traffic)
    return basis, call(cross_number, cross, inverse)


def solution(mesh):
    placed = (
        P(("region", "split"), None),
        P(("region", "split"), None, None, None),
        P(("region", "split"), None),
        P(("region", "split")),
        P("region", None, None),
        P(),
    )
    return jax.shard_map(
        local,
        mesh=mesh,
        in_specs=placed,
        out_specs=(P(("region", "split"), None), P()),
        check_vma=False,
    )
```

```python
import functools
import jax
import jax.numpy as jnp
from jax import lax
from jax.experimental import pallas as pl
from jax.experimental.pallas import tpu as pltpu
from jax.sharding import PartitionSpec as P

AXES = ("region", "split")
VMEM = pl.BlockSpec(memory_space=pltpu.VMEM)
SMEM = pl.BlockSpec(memory_space=pltpu.SMEM)
EXACT = lax.Precision.HIGHEST
NN = (((1,), (0,)), ((), ()))
NT = (((1,), (1,)), ((), ()))
TN = (((0,), (0,)), ((), ()))
GROUP = 8
PIVOTS = 16
TILE = 128
VMEM_LIMIT = 12 * 1024 * 1024
LIST_ROWS = 16
PIECES = 4


def shifted(value, axis, steps):
    count = lax.axis_size(axis)
    pairs = [(source, (source + steps) % count) for source in range(count)]
    return lax.ppermute(value, axis, pairs)


def exact_dot(left, right, dims=NN):
    return lax.dot_general(left, right, dims, precision=EXACT, preferred_element_type=jnp.float32)


def kernel_call(body, out_shape, in_specs, flops, bytes_accessed, slots=None):
    return pl.pallas_call(
        body,
        out_shape=out_shape,
        in_specs=in_specs,
        out_specs=jax.tree.map(lambda out: SMEM if out.dtype == jnp.int32 else VMEM, out_shape),
        scratch_shapes=[] if slots is None else [pltpu.SMEM(slots, jnp.int32)],
        compiler_params=pltpu.CompilerParams(vmem_limit_bytes=VMEM_LIMIT),
        cost_estimate=pl.CostEstimate(flops=flops, bytes_accessed=bytes_accessed // 16, transcendentals=0),
    )


def fill_slots(slots_ref, cols_ref, live_ref, first, place_of):
    rows, stored = cols_ref.shape
    count = slots_ref.shape[1] - 1
    for row in range(rows):
        for index in range(count):
            slots_ref[row, index] = -1
        for at in range(stored):
            name = cols_ref[row, at] - first
            inside = (name >= 0) & (name < count) & (at < live_ref[row])
            slots_ref[row, jnp.where(inside, place_of(jnp.clip(name, 0, count - 1)), count)] = at


def accumulate(slots_ref, hessian_ref, operand_ref, base, total):
    rows, _, size, _ = hessian_ref.shape
    shards, shard_rows, _ = operand_ref.shape
    each = shard_rows // size
    for index in range(shards * each):
        start = index % each * size
        block = operand_ref[index // each, start : start + size, :]
        parts = []
        for row in range(rows):
            slot = slots_ref[row, base + index]
            live = jnp.where(slot >= 0, 1.0, 0.0).astype(jnp.float32)
            stored = hessian_ref[row, jnp.maximum(slot, 0)]
            parts.append(stored * jnp.broadcast_to(live, (size, size)).astype(jnp.bfloat16))
        term = jnp.dot(jnp.concatenate(parts, 0), block, preferred_element_type=jnp.float32)
        total = term if total is None else total + term
    return total


def hold_body(blocks_ref, out_ref):
    pltpu.sync_copy(blocks_ref, out_ref)


def near_body(groups, tokens, linear, *refs):
    cols_ref, live_ref, bases_ref, hessian_ref = refs[:4]
    operands, refs = refs[4 : 4 + groups], refs[4 + groups :]
    *terms, out_ref = refs[: len(refs) - 1 - tokens]
    *token_refs, slots_ref = refs[len(refs) - 1 - tokens :]
    fill_slots(slots_ref, cols_ref, live_ref, 0, lambda name: name)
    total = None
    for at, operand_ref in enumerate(operands):
        total = accumulate(slots_ref, hessian_ref, operand_ref, bases_ref[at], total)
    out_ref[...] = linear(total, *terms)
    for token_ref in token_refs:
        token_ref[...] = total[:GROUP, :TILE]


def no_terms(total):
    return total


def first_terms(total, bounds_ref, vectors_ref):
    centre, _ = interval(bounds_ref)
    return total - centre * vectors_ref[...]


def second_terms(total, bounds_ref, one_ref, vectors_ref):
    centre, half = interval(bounds_ref)
    return total - centre * one_ref[...] - (0.5 * half) * vectors_ref[...]


def list_place(lists_ref, name):
    halo = lists_ref.shape[1]
    side = jnp.where(name >= halo, 1, 0).astype(jnp.int32)
    return side * halo + lists_ref[side, name - side * halo]


def halo_total(which, slots_ref, bases_ref, hessian_ref, lower_ref, upper_ref, total_ref):
    halo = (slots_ref.shape[1] - 1) // 2
    total = accumulate(slots_ref, hessian_ref, lower_ref, bases_ref[which], total_ref[...])
    return accumulate(slots_ref, hessian_ref, upper_ref, halo + bases_ref[which], total)


def table_body(first, which, cols_ref, live_ref, lists_ref, *refs):
    *operands, out_ref, slots_ref = refs
    fill_slots(slots_ref, cols_ref, live_ref, first, lambda name: list_place(lists_ref, name))
    out_ref[...] = halo_total(which, slots_ref, *operands)


def middle_body(which, *refs):
    operands, (out_ref, *token_refs) = refs[:6], refs[6:]
    total = halo_total(which, *operands)
    out_ref[...] = total
    for token_ref in token_refs:
        token_ref[...] = total[:GROUP, :TILE]


def interval(bounds_ref):
    return 0.5 * (bounds_ref[0] + bounds_ref[1]), 0.5 * (bounds_ref[1] - bounds_ref[0])


def scaled_body(which, factor, *refs):
    *operands, bounds_ref, out_ref, cast_ref = refs
    _, half = interval(bounds_ref)
    value = factor * halo_total(which, *operands) / half
    out_ref[...] = value
    cast_ref[...] = value.astype(jnp.bfloat16)


def place_rows(number_ref, piece, rows):
    return pl.ds(pl.multiple_of((piece ^ number_ref[0]) * rows, GROUP), rows)


def scatter_pieces(number_ref, out_ref, value):
    rows = out_ref.shape[0] // PIECES
    for piece in range(PIECES):
        out_ref[place_rows(number_ref, piece, rows), :] = value[piece * rows : (piece + 1) * rows, :]


def ordered_pieces(number_ref, in_ref):
    rows = in_ref.shape[0] // PIECES
    return jnp.concatenate([in_ref[place_rows(number_ref, piece, rows), :] for piece in range(PIECES)], 0)


def lower_tiles(count):
    return [(row, col) for row in range(count) for col in range(row + 1)]


def gram_body(number_ref, two_ref, _, out_ref):
    two = two_ref[...]
    cols = [two[:, at * TILE : (at + 1) * TILE] for at in range(two.shape[1] // TILE)]
    tiles = [exact_dot(cols[row], cols[col], TN) for row, col in lower_tiles(len(cols))]
    scatter_pieces(number_ref, out_ref, jnp.concatenate(tiles, 0))


def third_body(which, *refs):
    *operands, number_ref, two_ref, _, out_ref = refs
    image = halo_total(which, *operands)
    scatter_pieces(number_ref, out_ref, exact_dot(two_ref[...], image, TN))


def over_lanes(value, lane):
    return jnp.broadcast_to(value[:, lane : lane + 1], value.shape)


def over_rows(value, row):
    return jnp.broadcast_to(value[row : row + 1, :], value.shape)


def eliminate(tile):
    count = tile.shape[0] // PIVOTS
    rows = [tile[index * PIVOTS : (index + 1) * PIVOTS, :] for index in range(count)]
    sub = lax.broadcasted_iota(jnp.int32, rows[0].shape, 0)
    lane = lax.broadcasted_iota(jnp.int32, rows[0].shape, 1)
    for step in range(count):
        start = step * PIVOTS
        pivot_cols = [over_lanes(rows[step], start + col) for col in range(PIVOTS)]
        factors = {
            below: [over_lanes(rows[below], start + col) for col in range(PIVOTS)]
            for below in range(step + 1, count)
        }
        inside = (lane >= start) & (lane < start + PIVOTS)
        forward = jnp.where(inside, jnp.where(lane - start == sub, 1.0, 0.0), rows[step])
        solved = forward
        for one in range(0, PIVOTS, 2):
            two = one + 1
            left, right = pivot_cols[one], pivot_cols[two]
            top, cross, low = over_rows(left, one), over_rows(left, two), over_rows(right, two)
            inverse = 1.0 / (top * low - cross * cross)
            top_inverse, cross_inverse, low_inverse = low * inverse, -(cross * inverse), top * inverse

            def solve(value):
                upper, lower = over_rows(value, one), over_rows(value, two)
                return top_inverse * upper + cross_inverse * lower, cross_inverse * upper + low_inverse * lower

            def without(value, upper, lower):
                return value - (left * upper + right * lower)

            def reduced(value):
                upper, lower = solve(value)
                return jnp.where(sub == one, upper, jnp.where(sub == two, lower, without(value, upper, lower)))

            for col in range(two + 1, PIVOTS):
                pivot_cols[col] = reduced(pivot_cols[col])
            upper, lower = solve(forward)
            over_top = 1.0 / top
            first, second = over_rows(forward, one), over_rows(forward, two)
            below_first = (second - cross * over_top * first) * lax.rsqrt(low - cross * cross * over_top)
            below = jnp.where(sub > two, without(forward, upper, lower), forward)
            solved = reduced(solved)
            forward = jnp.where(sub == one, first * lax.rsqrt(top), jnp.where(sub == two, below_first, below))
        rows[step] = jnp.where(lane < start + PIVOTS, forward, 0.0)
        solved_rows = [over_rows(solved, pivot) for pivot in range(PIVOTS)]
        for below in range(step + 1, count):
            terms = [factors[below][col] * solved_rows[col] for col in range(PIVOTS)]
            while len(terms) > 1:
                terms = [terms[at] + terms[at + 1] for at in range(0, len(terms), 2)]
            rows[below] = jnp.where(inside, 0.0, rows[below]) - terms[0]
    return jnp.concatenate(rows, 0)


def scaled_tiles(tiles, count):
    names = lower_tiles(count)
    index = lambda dim: lax.broadcasted_iota(jnp.int32, (TILE, TILE), dim)
    diagonal = {row: jnp.where(index(0) == index(1), tiles[names.index((row, row))], 0.0) for row in range(count)}
    down = {row: lax.rsqrt(jnp.sum(diagonal[row], 1, keepdims=True)) for row in range(count)}
    along = {row: lax.rsqrt(jnp.sum(diagonal[row], 0, keepdims=True)) for row in range(count)}
    return [tile * down[row] * along[col] for (row, col), tile in zip(names, tiles)], along


def first_tile_body(count, total_rows, number_ref, gram_ref, *refs):
    *tile_refs, scale_ref = refs
    packed = ordered_pieces(number_ref, gram_ref) / total_rows
    tiles = [packed[at * TILE : (at + 1) * TILE, :] for at in range(len(tile_refs))]
    tiles, along = scaled_tiles(tiles, count)
    for row in range(count):
        scale_ref[row * GROUP : (row + 1) * GROUP, :] = jnp.broadcast_to(along[row], (GROUP, TILE))
    finish_tile(0, count, dict(zip(lower_tiles(count), tiles)), tile_refs)


def next_tile_body(at, count, *refs):
    names = lower_tiles(count)
    tiles = {name: ref[...] for name, ref in zip(names, refs)}
    finish_tile(at, count, tiles, refs[len(names) :])


def finish_tile(at, count, tiles, out_refs):
    tiles = dict(tiles)
    tiles[at, at] = eliminate(tiles[at, at])
    for row in range(at + 1, count):
        tiles[row, at] = exact_dot(tiles[row, at], tiles[at, at], NT)
    for row in range(at + 1, count):
        for col in range(at + 1, row + 1):
            tiles[row, col] = tiles[row, col] - exact_dot(tiles[row, at], tiles[col, at], NT)
    for name, out_ref in zip(lower_tiles(count), out_refs):
        out_ref[...] = tiles[name]


def basis_body(count, *refs):
    *tile_refs, scale_ref, two_ref, basis_ref, inverse_ref = refs
    tiles = {name: ref[...] for name, ref in zip(lower_tiles(count), tile_refs)}
    inverse = {}
    for row in range(count):
        inverse[row, row] = tiles[row, row]
        for col in range(row):
            mixed = exact_dot(tiles[row, col], inverse[col, col])
            for mid in range(col + 1, row):
                mixed = mixed + exact_dot(tiles[row, mid], inverse[mid, col])
            inverse[row, col] = -exact_dot(tiles[row, row], mixed)
    zero = jnp.zeros((TILE, TILE), jnp.float32)
    whole = jnp.concatenate(
        [
            jnp.concatenate(
                [inverse[row, col] * scale_ref[col * GROUP, :][None] if col <= row else zero for col in range(count)], 1
            )
            for row in range(count)
        ],
        0,
    )
    inverse_ref[...] = whole
    basis_ref[...] = exact_dot(two_ref[...], whole, NT)


def projected_body(total_rows, number_ref, cross_ref, inverse_ref, projected_ref):
    cross = ordered_pieces(number_ref, cross_ref) / total_rows
    projected_ref[...] = exact_dot(exact_dot(inverse_ref[...], cross), inverse_ref[...], NT)


def factor_stages(total_rows, count, number, two):
    rows, modes = two.shape
    tile = jax.ShapeDtypeStruct((TILE, TILE), jnp.float32)
    scale = jax.ShapeDtypeStruct((count * GROUP, TILE), jnp.float32)
    names = lower_tiles(count)
    work = 10**8

    def first(gram):
        body = functools.partial(first_tile_body, count, total_rows)
        return tuple(kernel_call(body, (tile,) * len(names) + (scale,), [SMEM, VMEM], work, gram.size)(number, gram))

    def following(at):
        def stage(state):
            body = functools.partial(next_tile_body, at, count)
            call = kernel_call(body, (tile,) * len(names), [VMEM] * len(names), work, TILE * TILE)
            return tuple(call(*state[:-1])) + state[-1:]

        return stage

    def finish(state):
        outs = (jax.ShapeDtypeStruct((rows, modes), jnp.float32), jax.ShapeDtypeStruct((modes, modes), jnp.float32))
        body = functools.partial(basis_body, count)
        return tuple(kernel_call(body, outs, [VMEM] * (len(names) + 2), work, rows * modes)(*state, two))

    return [first] + [following(at) for at in range(1, count)] + [finish]


def tied(left, right):
    return lax.optimization_barrier((left, right))


def partner_value(value, axis, bit):
    return lax.ppermute(value, axis, [(at, at ^ bit) for at in range(lax.axis_size(axis))])


def axis_bits(axis):
    return [(axis, 1 << at) for at in range(lax.axis_size(axis).bit_length() - 1)]


def device_number(halved):
    number = 0
    for axis, bit in halved:
        number = number * 2 + (lax.axis_index(axis) // bit) % 2
    return number.astype(jnp.int32).reshape(1)


def halving(axis, bit):
    def step(value):
        half = value.shape[0] // 2
        got = partner_value(value[half:], axis, bit)
        return lambda: value[:half] + got

    return step


def doubling(axis, bit):
    def step(value):
        got = partner_value(value, axis, bit)
        return lambda: value + got

    return step


def joining(axis, bit):
    def step(value):
        got = partner_value(value, axis, bit)
        return lambda: jnp.concatenate([value, got], 0)

    return step


def run_beside(value, steps, state, stages):
    stages = list(stages)
    for index, step in enumerate(steps):
        value, state = tied(value, state)
        join = step(value)
        due = -(-len(stages) // (len(steps) - index))
        for _ in range(due):
            state = stages.pop(0)(state)
        value = join()
        if due:
            value, state = tied(value, state)
    return value, state


def local(vectors, hessian, block_cols, live_blocks, halo_lists, bounds):
    row_blocks, stored, size, _ = hessian.shape
    rows, modes = vectors.shape
    splits = lax.axis_size("split")
    region_blocks = row_blocks * splits
    halo_blocks = halo_lists.shape[2]
    whole = halo_blocks == region_blocks and region_blocks <= 256
    total_rows = rows * lax.axis_size(AXES)

    paired = whole and splits == 2
    core = lax.axis_index("split").astype(jnp.int32)
    swapped = lambda value: lax.ppermute(value, "split", [(0, 1), (1, 0)])
    halo_first = [core * row_blocks, (1 - core) * row_blocks] if paired else [0]
    bases = jnp.stack(halo_first).astype(jnp.int32) if paired else jnp.zeros((1,), jnp.int32)

    def sent(operand, region):
        if whole:
            return operand, operand
        width = modes // splits
        start = core * width
        blocks = region[:, :rows].reshape(region_blocks, size, modes)
        share = lambda listed: lax.dynamic_slice_in_dim(blocks[listed], start, width, 2).reshape(-1, width)
        return share(halo_lists[0, 1]), share(halo_lists[0, 0])

    def gathered(value):
        if paired:
            return [value[None], swapped(value)[None]]
        if whole:
            return [lax.all_gather(value, "split", axis=0)]
        return [lax.all_gather(value, "split", axis=1, tiled=True)[None]]

    listed = jnp.pad(halo_lists[0], ((0, LIST_ROWS - 2), (0, modes - halo_blocks)))
    first = vectors.astype(jnp.bfloat16)
    if whole:
        first = jnp.concatenate([first, listed.astype(jnp.bfloat16)], 0)

    def exchange(operand, gather=True):
        if gather or not paired:
            groups = [lax.all_gather(operand, "split", axis=0)]
        else:
            groups = [operand[None], swapped(operand)[None]]
        up, down = sent(operand, groups[0])
        return groups, shifted(up, "region", 1), shifted(down, "region", -1)

    first_near, first_lower, first_upper = exchange(first)
    if whole:
        orders = [first_lower[rows + 1, :halo_blocks], first_upper[rows, :halo_blocks]]
        lists = jnp.stack(orders).astype(jnp.int32)
    else:
        lists = jnp.broadcast_to(jnp.arange(halo_blocks, dtype=jnp.int32), (2, halo_blocks))

    wide = jax.ShapeDtypeStruct((rows, modes), jnp.float32)
    narrow = jax.ShapeDtypeStruct((rows, modes), jnp.bfloat16)
    square = jax.ShapeDtypeStruct((modes, modes), jnp.float32)
    tile_rows = len(lower_tiles(modes // TILE)) * TILE
    work = 2 * rows * size * modes
    square_work = 2 * rows * modes * modes
    traffic = hessian.size * 2 + 3 * rows * modes * 4
    cores, *other_cores = axis_bits("split")
    near, across, *far = axis_bits("region")
    between = other_cores + far
    gram_number, cross_number = device_number([cores, across]), device_number([cores, near])
    halo_slots = (row_blocks, 2 * halo_blocks + 1)

    covering, free = 3 * 10 ** 10, 10 ** 7
    token = jax.ShapeDtypeStruct((GROUP, TILE), jnp.float32)

    held = pl.pallas_call(
        hold_body,
        out_shape=pltpu.VMEM(hessian.shape, hessian.dtype),
        in_specs=[pl.BlockSpec(memory_space=pl.ANY)],
        out_specs=VMEM,
        compiler_params=pltpu.CompilerParams(vmem_limit_bytes=VMEM_LIMIT),
    )(hessian)

    def near_total(groups, linear, scalars=(), terms=(), tokens=()):
        call = kernel_call(
            functools.partial(near_body, len(groups), len(tokens), linear),
            (wide,) + tokens,
            [SMEM] * 3 + [VMEM] * (1 + len(groups)) + [SMEM] * len(scalars) + [VMEM] * len(terms),
            free,
            traffic,
            (row_blocks, region_blocks + 1),
        )
        near_bases = bases if len(groups) > 1 else jnp.zeros_like(bases)
        return call(block_cols, live_blocks, near_bases, held, *groups, *scalars, *terms)

    def halo_part(body, outs, table, pair, total, scalars=(), extra=()):
        specs = [SMEM] * 2 + [VMEM] * 4 + [SMEM] * len(scalars) + [VMEM] * len(extra)
        call = kernel_call(body, outs, specs, covering, traffic)
        return call(table, bases, held, *pair, total, *scalars, *extra)

    def pairs_of(lower, upper):
        *pairs, last = zip(gathered(lower), gathered(upper))
        return pairs, last

    (total,) = near_total(first_near, first_terms, (bounds,), (vectors,))
    pairs, last = pairs_of(first_lower, first_upper)
    pairs.append(last)
    body_of = functools.partial(table_body, region_blocks, 0)
    table_shape = jax.ShapeDtypeStruct(halo_slots, jnp.int32)
    specs = [SMEM] * 4 + [VMEM] * 4
    call = kernel_call(body_of, (wide, table_shape), specs, covering, traffic)
    if len(pairs) == 1:
        pairs.append(tuple(jnp.zeros_like(part) for part in last))
    total, table = call(block_cols, live_blocks, lists, bases, held, *pairs[0], total)
    which = len(pairs) - 1 if paired else 0
    body_of = functools.partial(scaled_body, which, 1.0)
    one, one_cast = halo_part(body_of, (wide, narrow), table, pairs[-1], total, (bounds,))

    own, lower, upper = exchange(one_cast)
    (total,) = near_total(own, second_terms, (bounds,), (one, vectors))
    pairs, last = pairs_of(lower, upper)
    for which, pair in enumerate(pairs):
        (total,) = halo_part(functools.partial(middle_body, which), (wide,), table, pair, total)
    body_of = functools.partial(scaled_body, len(pairs), 2.0)
    two, two_cast = halo_part(body_of, (wide, narrow), table, last, total, (bounds,))

    own, lower, upper = exchange(two_cast, gather=False)
    total, after = near_total(own, no_terms, tokens=(token,))
    packed = jax.ShapeDtypeStruct((tile_rows, TILE), jnp.float32)
    gram = kernel_call(gram_body, packed, [SMEM, VMEM, VMEM], free, traffic)(gram_number, two, after)
    for step_of in [halving(*cores), halving(*across)]:
        gram = step_of(gram)()
    pairs, last = pairs_of(lower, upper)
    for which, pair in enumerate(pairs):
        total, after = halo_part(functools.partial(middle_body, which), (wide, token), table, pair, total)
    gram, after = tied(gram, after)
    body_of = functools.partial(third_body, len(pairs))
    cross = halo_part(body_of, square, table, last, total, (cross_number,), (two, after))
    cross = halving(*cores)(cross)()

    fold = modes // TILE
    cut = gram.shape[0] // fold
    folded = jnp.concatenate([gram[at * cut : (at + 1) * cut] for at in range(fold)], 1)
    flat = lambda value: [value[:, at * TILE : (at + 1) * TILE] for at in range(fold)]
    half = cross.shape[0] // 2
    got = partner_value(jnp.concatenate([folded, cross[half:]], 0), *near)
    both = jnp.concatenate([folded, cross[:half]], 0) + got
    for bit in between:
        both = doubling(*bit)(both)()
    got = partner_value(both, *across)
    gram = joining(*cores)(jnp.concatenate(flat(both[:cut]) + flat(got[:cut]), 0))()
    cross = both[cut:] + got[cut:]
    stages = factor_stages(float(total_rows), modes // TILE, gram_number, two)
    steps = [joining(*near), joining(*cores)]
    cross, (basis, inverse) = run_beside(cross, steps, gram, stages)
    body_of = functools.partial(projected_body, float(total_rows))
    call = kernel_call(body_of, square, [SMEM] + [VMEM] * 2, 2 * square_work, traffic)
    return basis, call(cross_number, cross, inverse)


def solution(mesh):
    placed = (
        P(("region", "split"), None),
        P(("region", "split"), None, None, None),
        P(("region", "split"), None),
        P(("region", "split")),
        P("region", None, None),
        P(),
    )
    return jax.shard_map(
        local,
        mesh=mesh,
        in_specs=placed,
        out_specs=(P(("region", "split"), None), P()),
        check_vma=False,
    )
```

```python
import functools
import jax
import jax.numpy as jnp
from jax import lax
from jax.experimental import pallas as pl
from jax.experimental.pallas import tpu as pltpu
from jax.sharding import PartitionSpec as P

AXES = ("region", "split")
VMEM = pl.BlockSpec(memory_space=pltpu.VMEM)
SMEM = pl.BlockSpec(memory_space=pltpu.SMEM)
EXACT = lax.Precision.HIGHEST
NN = (((1,), (0,)), ((), ()))
NT = (((1,), (1,)), ((), ()))
TN = (((0,), (0,)), ((), ()))
GROUP = 8
PIVOTS = 16
TILE = 128
VMEM_LIMIT = 6 * 1024 * 1024
LIST_ROWS = 16
PIECES = 4


def shifted(value, axis, steps):
    count = lax.axis_size(axis)
    pairs = [(source, (source + steps) % count) for source in range(count)]
    return lax.ppermute(value, axis, pairs)


def exact_dot(left, right, dims=NN):
    return lax.dot_general(left, right, dims, precision=EXACT, preferred_element_type=jnp.float32)


def kernel_call(body, out_shape, in_specs, flops, bytes_accessed, slots=None):
    return pl.pallas_call(
        body,
        out_shape=out_shape,
        in_specs=in_specs,
        out_specs=jax.tree.map(lambda out: SMEM if out.dtype == jnp.int32 else VMEM, out_shape),
        scratch_shapes=[] if slots is None else [pltpu.SMEM(slots, jnp.int32)],
        compiler_params=pltpu.CompilerParams(vmem_limit_bytes=VMEM_LIMIT),
        cost_estimate=pl.CostEstimate(flops=flops, bytes_accessed=bytes_accessed // 16, transcendentals=0),
    )


def fill_slots(slots_ref, cols_ref, live_ref, first, place_of):
    rows, stored = cols_ref.shape
    count = slots_ref.shape[1] - 1
    for row in range(rows):
        for index in range(count):
            slots_ref[row, index] = -1
        for at in range(stored):
            name = cols_ref[row, at] - first
            inside = (name >= 0) & (name < count) & (at < live_ref[row])
            slots_ref[row, jnp.where(inside, place_of(jnp.clip(name, 0, count - 1)), count)] = at


def accumulate(slots_ref, hessian_ref, operand_ref, base, total):
    rows, _, size, _ = hessian_ref.shape
    shards, shard_rows, _ = operand_ref.shape
    each = shard_rows // size
    for index in range(shards * each):
        start = index % each * size
        block = operand_ref[index // each, start : start + size, :]
        parts = []
        for row in range(rows):
            slot = slots_ref[row, base + index]
            live = jnp.where(slot >= 0, 1.0, 0.0).astype(jnp.float32)
            stored = hessian_ref[row, jnp.maximum(slot, 0)]
            parts.append(stored * jnp.broadcast_to(live, (size, size)).astype(jnp.bfloat16))
        term = jnp.dot(jnp.concatenate(parts, 0), block, preferred_element_type=jnp.float32)
        total = term if total is None else total + term
    return total


def hold_body(blocks_ref, out_ref):
    pltpu.sync_copy(blocks_ref, out_ref)


def near_body(groups, tokens, linear, *refs):
    cols_ref, live_ref, bases_ref, hessian_ref = refs[:4]
    operands, refs = refs[4 : 4 + groups], refs[4 + groups :]
    *terms, out_ref = refs[: len(refs) - 1 - tokens]
    *token_refs, slots_ref = refs[len(refs) - 1 - tokens :]
    fill_slots(slots_ref, cols_ref, live_ref, 0, lambda name: name)
    total = None
    for at, operand_ref in enumerate(operands):
        total = accumulate(slots_ref, hessian_ref, operand_ref, bases_ref[at], total)
    out_ref[...] = linear(total, *terms)
    for token_ref in token_refs:
        token_ref[...] = total[:GROUP, :TILE]


def no_terms(total):
    return total


def first_terms(total, bounds_ref, vectors_ref):
    centre, _ = interval(bounds_ref)
    return total - centre * vectors_ref[...]


def second_terms(total, bounds_ref, one_ref, vectors_ref):
    centre, half = interval(bounds_ref)
    return total - centre * one_ref[...] - (0.5 * half) * vectors_ref[...]


def list_place(lists_ref, name):
    halo = lists_ref.shape[1]
    side = jnp.where(name >= halo, 1, 0).astype(jnp.int32)
    return side * halo + lists_ref[side, name - side * halo]


def halo_total(which, slots_ref, bases_ref, hessian_ref, lower_ref, upper_ref, total_ref):
    halo = (slots_ref.shape[1] - 1) // 2
    total = accumulate(slots_ref, hessian_ref, lower_ref, bases_ref[which], total_ref[...])
    return accumulate(slots_ref, hessian_ref, upper_ref, halo + bases_ref[which], total)


def table_body(first, which, cols_ref, live_ref, lists_ref, *refs):
    *operands, out_ref, slots_ref = refs
    fill_slots(slots_ref, cols_ref, live_ref, first, lambda name: list_place(lists_ref, name))
    out_ref[...] = halo_total(which, slots_ref, *operands)


def middle_body(which, *refs):
    operands, (out_ref, *token_refs) = refs[:6], refs[6:]
    total = halo_total(which, *operands)
    out_ref[...] = total
    for token_ref in token_refs:
        token_ref[...] = total[:GROUP, :TILE]


def interval(bounds_ref):
    return 0.5 * (bounds_ref[0] + bounds_ref[1]), 0.5 * (bounds_ref[1] - bounds_ref[0])


def scaled_body(which, factor, *refs):
    *operands, bounds_ref, out_ref, cast_ref = refs
    _, half = interval(bounds_ref)
    value = factor * halo_total(which, *operands) / half
    out_ref[...] = value
    cast_ref[...] = value.astype(jnp.bfloat16)


def place_rows(number_ref, piece, rows):
    return pl.ds(pl.multiple_of((piece ^ number_ref[0]) * rows, GROUP), rows)


def scatter_pieces(number_ref, out_ref, value):
    rows = out_ref.shape[0] // PIECES
    for piece in range(PIECES):
        out_ref[place_rows(number_ref, piece, rows), :] = value[piece * rows : (piece + 1) * rows, :]


def ordered_pieces(number_ref, in_ref):
    rows = in_ref.shape[0] // PIECES
    return jnp.concatenate([in_ref[place_rows(number_ref, piece, rows), :] for piece in range(PIECES)], 0)


def lower_tiles(count):
    return [(row, col) for row in range(count) for col in range(row + 1)]


def gram_body(number_ref, two_ref, _, out_ref):
    two = two_ref[...]
    cols = [two[:, at * TILE : (at + 1) * TILE] for at in range(two.shape[1] // TILE)]
    tiles = [exact_dot(cols[row], cols[col], TN) for row, col in lower_tiles(len(cols))]
    scatter_pieces(number_ref, out_ref, jnp.concatenate(tiles, 0))


def third_body(which, *refs):
    *operands, number_ref, two_ref, _, out_ref = refs
    image = halo_total(which, *operands)
    scatter_pieces(number_ref, out_ref, exact_dot(two_ref[...], image, TN))


def over_lanes(value, lane):
    return jnp.broadcast_to(value[:, lane : lane + 1], value.shape)


def over_rows(value, row):
    return jnp.broadcast_to(value[row : row + 1, :], value.shape)


def eliminate(tile):
    count = tile.shape[0] // PIVOTS
    rows = [tile[index * PIVOTS : (index + 1) * PIVOTS, :] for index in range(count)]
    sub = lax.broadcasted_iota(jnp.int32, rows[0].shape, 0)
    lane = lax.broadcasted_iota(jnp.int32, rows[0].shape, 1)
    for step in range(count):
        start = step * PIVOTS
        pivot_cols = [over_lanes(rows[step], start + col) for col in range(PIVOTS)]
        factors = {
            below: [over_lanes(rows[below], start + col) for col in range(PIVOTS)]
            for below in range(step + 1, count)
        }
        inside = (lane >= start) & (lane < start + PIVOTS)
        forward = jnp.where(inside, jnp.where(lane - start == sub, 1.0, 0.0), rows[step])
        solved = forward
        for one in range(0, PIVOTS, 2):
            two = one + 1
            left, right = pivot_cols[one], pivot_cols[two]
            top, cross, low = over_rows(left, one), over_rows(left, two), over_rows(right, two)
            inverse = 1.0 / (top * low - cross * cross)
            top_inverse, cross_inverse, low_inverse = low * inverse, -(cross * inverse), top * inverse

            def solve(value):
                upper, lower = over_rows(value, one), over_rows(value, two)
                return top_inverse * upper + cross_inverse * lower, cross_inverse * upper + low_inverse * lower

            def without(value, upper, lower):
                return value - (left * upper + right * lower)

            def reduced(value):
                upper, lower = solve(value)
                return jnp.where(sub == one, upper, jnp.where(sub == two, lower, without(value, upper, lower)))

            for col in range(two + 1, PIVOTS):
                pivot_cols[col] = reduced(pivot_cols[col])
            upper, lower = solve(forward)
            over_top = 1.0 / top
            first, second = over_rows(forward, one), over_rows(forward, two)
            below_first = (second - cross * over_top * first) * lax.rsqrt(low - cross * cross * over_top)
            below = jnp.where(sub > two, without(forward, upper, lower), forward)
            solved = reduced(solved)
            forward = jnp.where(sub == one, first * lax.rsqrt(top), jnp.where(sub == two, below_first, below))
        rows[step] = jnp.where(lane < start + PIVOTS, forward, 0.0)
        solved_rows = [over_rows(solved, pivot) for pivot in range(PIVOTS)]
        for below in range(step + 1, count):
            terms = [factors[below][col] * solved_rows[col] for col in range(PIVOTS)]
            while len(terms) > 1:
                terms = [terms[at] + terms[at + 1] for at in range(0, len(terms), 2)]
            rows[below] = jnp.where(inside, 0.0, rows[below]) - terms[0]
    return jnp.concatenate(rows, 0)


def scaled_tiles(tiles, count):
    names = lower_tiles(count)
    index = lambda dim: lax.broadcasted_iota(jnp.int32, (TILE, TILE), dim)
    diagonal = {row: jnp.where(index(0) == index(1), tiles[names.index((row, row))], 0.0) for row in range(count)}
    down = {row: lax.rsqrt(jnp.sum(diagonal[row], 1, keepdims=True)) for row in range(count)}
    along = {row: lax.rsqrt(jnp.sum(diagonal[row], 0, keepdims=True)) for row in range(count)}
    return [tile * down[row] * along[col] for (row, col), tile in zip(names, tiles)], along


def first_tile_body(count, total_rows, number_ref, gram_ref, *refs):
    *tile_refs, scale_ref = refs
    packed = ordered_pieces(number_ref, gram_ref) / total_rows
    tiles = [packed[at * TILE : (at + 1) * TILE, :] for at in range(len(tile_refs))]
    tiles, along = scaled_tiles(tiles, count)
    for row in range(count):
        scale_ref[row * GROUP : (row + 1) * GROUP, :] = jnp.broadcast_to(along[row], (GROUP, TILE))
    finish_tile(0, count, dict(zip(lower_tiles(count), tiles)), tile_refs)


def next_tile_body(at, count, *refs):
    names = lower_tiles(count)
    tiles = {name: ref[...] for name, ref in zip(names, refs)}
    finish_tile(at, count, tiles, refs[len(names) :])


def finish_tile(at, count, tiles, out_refs):
    tiles = dict(tiles)
    tiles[at, at] = eliminate(tiles[at, at])
    for row in range(at + 1, count):
        tiles[row, at] = exact_dot(tiles[row, at], tiles[at, at], NT)
    for row in range(at + 1, count):
        for col in range(at + 1, row + 1):
            tiles[row, col] = tiles[row, col] - exact_dot(tiles[row, at], tiles[col, at], NT)
    for name, out_ref in zip(lower_tiles(count), out_refs):
        out_ref[...] = tiles[name]


def basis_body(count, *refs):
    *tile_refs, scale_ref, two_ref, basis_ref, inverse_ref = refs
    tiles = {name: ref[...] for name, ref in zip(lower_tiles(count), tile_refs)}
    inverse = {}
    for row in range(count):
        inverse[row, row] = tiles[row, row]
        for col in range(row):
            mixed = exact_dot(tiles[row, col], inverse[col, col])
            for mid in range(col + 1, row):
                mixed = mixed + exact_dot(tiles[row, mid], inverse[mid, col])
            inverse[row, col] = -exact_dot(tiles[row, row], mixed)
    zero = jnp.zeros((TILE, TILE), jnp.float32)
    whole = jnp.concatenate(
        [
            jnp.concatenate(
                [inverse[row, col] * scale_ref[col * GROUP, :][None] if col <= row else zero for col in range(count)], 1
            )
            for row in range(count)
        ],
        0,
    )
    inverse_ref[...] = whole
    basis_ref[...] = exact_dot(two_ref[...], whole, NT)


def projected_body(total_rows, number_ref, cross_ref, inverse_ref, projected_ref):
    cross = ordered_pieces(number_ref, cross_ref) / total_rows
    projected_ref[...] = exact_dot(exact_dot(inverse_ref[...], cross), inverse_ref[...], NT)


def factor_stages(total_rows, count, number, two):
    rows, modes = two.shape
    tile = jax.ShapeDtypeStruct((TILE, TILE), jnp.float32)
    scale = jax.ShapeDtypeStruct((count * GROUP, TILE), jnp.float32)
    names = lower_tiles(count)
    work = 10**8

    def first(gram):
        body = functools.partial(first_tile_body, count, total_rows)
        return tuple(kernel_call(body, (tile,) * len(names) + (scale,), [SMEM, VMEM], work, gram.size)(number, gram))

    def following(at):
        def stage(state):
            body = functools.partial(next_tile_body, at, count)
            call = kernel_call(body, (tile,) * len(names), [VMEM] * len(names), work, TILE * TILE)
            return tuple(call(*state[:-1])) + state[-1:]

        return stage

    def finish(state):
        outs = (jax.ShapeDtypeStruct((rows, modes), jnp.float32), jax.ShapeDtypeStruct((modes, modes), jnp.float32))
        body = functools.partial(basis_body, count)
        return tuple(kernel_call(body, outs, [VMEM] * (len(names) + 2), work, rows * modes)(*state, two))

    return [first] + [following(at) for at in range(1, count)] + [finish]


def tied(left, right):
    return lax.optimization_barrier((left, right))


def partner_value(value, axis, bit):
    return lax.ppermute(value, axis, [(at, at ^ bit) for at in range(lax.axis_size(axis))])


def axis_bits(axis):
    return [(axis, 1 << at) for at in range(lax.axis_size(axis).bit_length() - 1)]


def device_number(halved):
    number = 0
    for axis, bit in halved:
        number = number * 2 + (lax.axis_index(axis) // bit) % 2
    return number.astype(jnp.int32).reshape(1)


def halving(axis, bit):
    def step(value):
        half = value.shape[0] // 2
        got = partner_value(value[half:], axis, bit)
        return lambda: value[:half] + got

    return step


def doubling(axis, bit):
    def step(value):
        got = partner_value(value, axis, bit)
        return lambda: value + got

    return step


def joining(axis, bit):
    def step(value):
        got = partner_value(value, axis, bit)
        return lambda: jnp.concatenate([value, got], 0)

    return step


def run_beside(value, steps, state, stages):
    stages = list(stages)
    for index, step in enumerate(steps):
        value, state = tied(value, state)
        join = step(value)
        due = -(-len(stages) // (len(steps) - index))
        for _ in range(due):
            state = stages.pop(0)(state)
        value = join()
        if due:
            value, state = tied(value, state)
    return value, state


def local(vectors, hessian, block_cols, live_blocks, halo_lists, bounds):
    row_blocks, stored, size, _ = hessian.shape
    rows, modes = vectors.shape
    splits = lax.axis_size("split")
    region_blocks = row_blocks * splits
    halo_blocks = halo_lists.shape[2]
    whole = halo_blocks == region_blocks and region_blocks <= 256
    total_rows = rows * lax.axis_size(AXES)

    paired = whole and splits == 2
    core = lax.axis_index("split").astype(jnp.int32)
    swapped = lambda value: lax.ppermute(value, "split", [(0, 1), (1, 0)])
    halo_first = [core * row_blocks, (1 - core) * row_blocks] if paired else [0]
    bases = jnp.stack(halo_first).astype(jnp.int32) if paired else jnp.zeros((1,), jnp.int32)

    def sent(operand, region):
        if whole:
            return operand, operand
        width = modes // splits
        start = core * width
        blocks = region[:, :rows].reshape(region_blocks, size, modes)
        share = lambda listed: lax.dynamic_slice_in_dim(blocks[listed], start, width, 2).reshape(-1, width)
        return share(halo_lists[0, 1]), share(halo_lists[0, 0])

    def gathered(value):
        if paired:
            return [value[None], swapped(value)[None]]
        if whole:
            return [lax.all_gather(value, "split", axis=0)]
        return [lax.all_gather(value, "split", axis=1, tiled=True)[None]]

    listed = jnp.pad(halo_lists[0], ((0, LIST_ROWS - 2), (0, modes - halo_blocks)))
    first = vectors.astype(jnp.bfloat16)
    if whole:
        first = jnp.concatenate([first, listed.astype(jnp.bfloat16)], 0)

    def exchange(operand, gather=True):
        if gather or not paired:
            groups = [lax.all_gather(operand, "split", axis=0)]
        else:
            groups = [operand[None], swapped(operand)[None]]
        up, down = sent(operand, groups[0])
        return groups, shifted(up, "region", 1), shifted(down, "region", -1)

    first_near, first_lower, first_upper = exchange(first)
    if whole:
        orders = [first_lower[rows + 1, :halo_blocks], first_upper[rows, :halo_blocks]]
        lists = jnp.stack(orders).astype(jnp.int32)
    else:
        lists = jnp.broadcast_to(jnp.arange(halo_blocks, dtype=jnp.int32), (2, halo_blocks))

    wide = jax.ShapeDtypeStruct((rows, modes), jnp.float32)
    narrow = jax.ShapeDtypeStruct((rows, modes), jnp.bfloat16)
    square = jax.ShapeDtypeStruct((modes, modes), jnp.float32)
    tile_rows = len(lower_tiles(modes // TILE)) * TILE
    work = 2 * rows * size * modes
    square_work = 2 * rows * modes * modes
    traffic = hessian.size * 2 + 3 * rows * modes * 4
    cores, *other_cores = axis_bits("split")
    near, across, *far = axis_bits("region")
    between = other_cores + far
    gram_number, cross_number = device_number([cores, across]), device_number([cores, near])
    halo_slots = (row_blocks, 2 * halo_blocks + 1)

    covering, free = 3 * 10 ** 10, 10 ** 7
    token = jax.ShapeDtypeStruct((GROUP, TILE), jnp.float32)

    held = pl.pallas_call(
        hold_body,
        out_shape=pltpu.VMEM(hessian.shape, hessian.dtype),
        in_specs=[pl.BlockSpec(memory_space=pl.ANY)],
        out_specs=VMEM,
        compiler_params=pltpu.CompilerParams(vmem_limit_bytes=VMEM_LIMIT),
    )(hessian)

    def near_total(groups, linear, scalars=(), terms=(), tokens=()):
        call = kernel_call(
            functools.partial(near_body, len(groups), len(tokens), linear),
            (wide,) + tokens,
            [SMEM] * 3 + [VMEM] * (1 + len(groups)) + [SMEM] * len(scalars) + [VMEM] * len(terms),
            free,
            traffic,
            (row_blocks, region_blocks + 1),
        )
        near_bases = bases if len(groups) > 1 else jnp.zeros_like(bases)
        return call(block_cols, live_blocks, near_bases, held, *groups, *scalars, *terms)

    def halo_part(body, outs, table, pair, total, scalars=(), extra=()):
        specs = [SMEM] * 2 + [VMEM] * 4 + [SMEM] * len(scalars) + [VMEM] * len(extra)
        call = kernel_call(body, outs, specs, covering, traffic)
        return call(table, bases, held, *pair, total, *scalars, *extra)

    def pairs_of(lower, upper):
        *pairs, last = zip(gathered(lower), gathered(upper))
        return pairs, last

    (total,) = near_total(first_near, first_terms, (bounds,), (vectors,))
    pairs, last = pairs_of(first_lower, first_upper)
    pairs.append(last)
    body_of = functools.partial(table_body, region_blocks, 0)
    table_shape = jax.ShapeDtypeStruct(halo_slots, jnp.int32)
    specs = [SMEM] * 4 + [VMEM] * 4
    call = kernel_call(body_of, (wide, table_shape), specs, covering, traffic)
    if len(pairs) == 1:
        pairs.append(tuple(jnp.zeros_like(part) for part in last))
    total, table = call(block_cols, live_blocks, lists, bases, held, *pairs[0], total)
    which = len(pairs) - 1 if paired else 0
    body_of = functools.partial(scaled_body, which, 1.0)
    one, one_cast = halo_part(body_of, (wide, narrow), table, pairs[-1], total, (bounds,))

    own, lower, upper = exchange(one_cast)
    (total,) = near_total(own, second_terms, (bounds,), (one, vectors))
    pairs, last = pairs_of(lower, upper)
    for which, pair in enumerate(pairs):
        (total,) = halo_part(functools.partial(middle_body, which), (wide,), table, pair, total)
    body_of = functools.partial(scaled_body, len(pairs), 2.0)
    two, two_cast = halo_part(body_of, (wide, narrow), table, last, total, (bounds,))

    own, lower, upper = exchange(two_cast, gather=False)
    total, after = near_total(own, no_terms, tokens=(token,))
    packed = jax.ShapeDtypeStruct((tile_rows, TILE), jnp.float32)
    gram = kernel_call(gram_body, packed, [SMEM, VMEM, VMEM], free, traffic)(gram_number, two, after)
    for step_of in [halving(*cores), halving(*across)]:
        gram = step_of(gram)()
    pairs, last = pairs_of(lower, upper)
    for which, pair in enumerate(pairs):
        total, after = halo_part(functools.partial(middle_body, which), (wide, token), table, pair, total)
    gram, after = tied(gram, after)
    body_of = functools.partial(third_body, len(pairs))
    cross = halo_part(body_of, square, table, last, total, (cross_number,), (two, after))
    cross = halving(*cores)(cross)()

    fold = modes // TILE
    cut = gram.shape[0] // fold
    folded = jnp.concatenate([gram[at * cut : (at + 1) * cut] for at in range(fold)], 1)
    flat = lambda value: [value[:, at * TILE : (at + 1) * TILE] for at in range(fold)]
    half = cross.shape[0] // 2
    got = partner_value(jnp.concatenate([folded, cross[half:]], 0), *near)
    both = jnp.concatenate([folded, cross[:half]], 0) + got
    for bit in between:
        both = doubling(*bit)(both)()
    got = partner_value(both, *across)
    gram = joining(*cores)(jnp.concatenate(flat(both[:cut]) + flat(got[:cut]), 0))()
    cross = both[cut:] + got[cut:]
    stages = factor_stages(float(total_rows), modes // TILE, gram_number, two)
    steps = [joining(*near), joining(*cores)]
    cross, (basis, inverse) = run_beside(cross, steps, gram, stages)
    body_of = functools.partial(projected_body, float(total_rows))
    call = kernel_call(body_of, square, [SMEM] + [VMEM] * 2, 2 * square_work, traffic)
    return basis, call(cross_number, cross, inverse)


def solution(mesh):
    placed = (
        P(("region", "split"), None),
        P(("region", "split"), None, None, None),
        P(("region", "split"), None),
        P(("region", "split")),
        P("region", None, None),
        P(),
    )
    return jax.shard_map(
        local,
        mesh=mesh,
        in_specs=placed,
        out_specs=(P(("region", "split"), None), P()),
        check_vma=False,
    )
```

```python
import functools
import jax
import jax.numpy as jnp
from jax import lax
from jax.experimental import pallas as pl
from jax.experimental.pallas import tpu as pltpu
from jax.sharding import PartitionSpec as P

AXES = ("region", "split")
VMEM = pl.BlockSpec(memory_space=pltpu.VMEM)
SMEM = pl.BlockSpec(memory_space=pltpu.SMEM)
EXACT = lax.Precision.HIGHEST
NN = (((1,), (0,)), ((), ()))
NT = (((1,), (1,)), ((), ()))
TN = (((0,), (0,)), ((), ()))
GROUP = 8
PANEL = 32
TILE = 128
VMEM_LIMIT = 6 * 1024 * 1024
LIST_ROWS = 16
PIECES = 4


def shifted(value, axis, steps):
    count = lax.axis_size(axis)
    pairs = [(source, (source + steps) % count) for source in range(count)]
    return lax.ppermute(value, axis, pairs)


def exact_dot(left, right, dims=NN):
    return lax.dot_general(left, right, dims, precision=EXACT, preferred_element_type=jnp.float32)


def kernel_call(body, out_shape, in_specs, flops, bytes_accessed, slots=None):
    return pl.pallas_call(
        body,
        out_shape=out_shape,
        in_specs=in_specs,
        out_specs=jax.tree.map(lambda out: SMEM if out.dtype == jnp.int32 else VMEM, out_shape),
        scratch_shapes=[] if slots is None else [pltpu.SMEM(slots, jnp.int32)],
        compiler_params=pltpu.CompilerParams(vmem_limit_bytes=VMEM_LIMIT),
        cost_estimate=pl.CostEstimate(flops=flops, bytes_accessed=bytes_accessed // 16, transcendentals=0),
    )


def fill_slots(slots_ref, cols_ref, live_ref, first, place_of):
    rows, stored = cols_ref.shape
    count = slots_ref.shape[1] - 1
    for row in range(rows):
        for index in range(count):
            slots_ref[row, index] = -1
        for at in range(stored):
            name = cols_ref[row, at] - first
            inside = (name >= 0) & (name < count) & (at < live_ref[row])
            slots_ref[row, jnp.where(inside, place_of(jnp.clip(name, 0, count - 1)), count)] = at


def accumulate(slots_ref, hessian_ref, operand_ref, base, total):
    rows, _, size, _ = hessian_ref.shape
    shards, shard_rows, _ = operand_ref.shape
    each = shard_rows // size
    for index in range(shards * each):
        start = index % each * size
        block = operand_ref[index // each, start : start + size, :]
        parts = []
        for row in range(rows):
            slot = slots_ref[row, base + index]
            live = jnp.where(slot >= 0, 1.0, 0.0).astype(jnp.float32)
            stored = hessian_ref[row, jnp.maximum(slot, 0)]
            parts.append(stored * jnp.broadcast_to(live, (size, size)).astype(jnp.bfloat16))
        term = jnp.dot(jnp.concatenate(parts, 0), block, preferred_element_type=jnp.float32)
        total = term if total is None else total + term
    return total


def hold_body(blocks_ref, out_ref):
    pltpu.sync_copy(blocks_ref, out_ref)


def near_body(groups, linear, *refs):
    cols_ref, live_ref, bases_ref, hessian_ref = refs[:4]
    operands, (*terms, out_ref, slots_ref) = refs[4 : 4 + groups], refs[4 + groups :]
    fill_slots(slots_ref, cols_ref, live_ref, 0, lambda name: name)
    total = None
    for at, operand_ref in enumerate(operands):
        total = accumulate(slots_ref, hessian_ref, operand_ref, bases_ref[at], total)
    out_ref[...] = linear(total, *terms)


def near_gram_body(groups, *refs):
    *operands, number_ref, two_ref, out_ref, gram_ref, slots_ref = refs
    near_body(groups, lambda total: total, *operands, out_ref, slots_ref)
    gram_part(number_ref, two_ref, gram_ref)


def first_terms(total, bounds_ref, vectors_ref):
    centre, _ = interval(bounds_ref)
    return total - centre * vectors_ref[...]


def second_terms(total, bounds_ref, one_ref, vectors_ref):
    centre, half = interval(bounds_ref)
    return total - centre * one_ref[...] - (0.5 * half) * vectors_ref[...]


def list_place(lists_ref, name):
    halo = lists_ref.shape[1]
    side = jnp.where(name >= halo, 1, 0).astype(jnp.int32)
    return side * halo + lists_ref[side, name - side * halo]


def halo_total(which, slots_ref, bases_ref, hessian_ref, lower_ref, upper_ref, total_ref):
    halo = (slots_ref.shape[1] - 1) // 2
    total = accumulate(slots_ref, hessian_ref, lower_ref, bases_ref[which], total_ref[...])
    return accumulate(slots_ref, hessian_ref, upper_ref, halo + bases_ref[which], total)


def table_body(first, which, cols_ref, live_ref, lists_ref, *refs):
    *operands, out_ref, slots_ref = refs
    fill_slots(slots_ref, cols_ref, live_ref, first, lambda name: list_place(lists_ref, name))
    out_ref[...] = halo_total(which, slots_ref, *operands)


def middle_body(which, *refs):
    operands, (out_ref, *token_refs) = refs[:6], refs[6:]
    total = halo_total(which, *operands)
    out_ref[...] = total
    for token_ref in token_refs:
        token_ref[...] = total[:GROUP, :TILE]


def interval(bounds_ref):
    return 0.5 * (bounds_ref[0] + bounds_ref[1]), 0.5 * (bounds_ref[1] - bounds_ref[0])


def scaled_body(which, factor, *refs):
    *operands, bounds_ref, out_ref, cast_ref = refs
    _, half = interval(bounds_ref)
    value = factor * halo_total(which, *operands) / half
    out_ref[...] = value
    cast_ref[...] = value.astype(jnp.bfloat16)


def place_rows(number_ref, piece, rows):
    return pl.ds(pl.multiple_of((piece ^ number_ref[0]) * rows, GROUP), rows)


def scatter_pieces(number_ref, out_ref, value):
    rows = out_ref.shape[0] // PIECES
    for piece in range(PIECES):
        out_ref[place_rows(number_ref, piece, rows), :] = value[piece * rows : (piece + 1) * rows, :]


def ordered_pieces(number_ref, in_ref):
    rows = in_ref.shape[0] // PIECES
    return jnp.concatenate([in_ref[place_rows(number_ref, piece, rows), :] for piece in range(PIECES)], 0)


def lower_tiles(count):
    return [(row, col) for row in range(count) for col in range(row + 1)]


def gram_part(number_ref, two_ref, out_ref):
    two = two_ref[...]
    cols = [two[:, at * TILE : (at + 1) * TILE] for at in range(two.shape[1] // TILE)]
    tiles = [exact_dot(cols[row], cols[col], TN) for row, col in lower_tiles(len(cols))]
    scatter_pieces(number_ref, out_ref, jnp.concatenate(tiles, 0))


def third_body(which, *refs):
    *operands, number_ref, two_ref, _, out_ref = refs
    image = halo_total(which, *operands)
    scatter_pieces(number_ref, out_ref, exact_dot(two_ref[...], image, TN))


def over_lanes(value, lane):
    return jnp.broadcast_to(value[:, lane : lane + 1], value.shape)


def over_rows(value, row):
    return jnp.broadcast_to(value[row : row + 1, :], value.shape)


def eliminate(tile):
    count, panel = tile.shape[0] // GROUP, PANEL // GROUP
    rows = [tile[index * GROUP : (index + 1) * GROUP, :] for index in range(count)]
    sub = lax.broadcasted_iota(jnp.int32, rows[0].shape, 0)
    lane = lax.broadcasted_iota(jnp.int32, rows[0].shape, 1)
    for begin in range(0, count, panel):
        end = begin + panel
        reduced = []
        for step in range(begin, end):
            start = step * GROUP
            pivot_cols = [over_lanes(rows[step], start + col) for col in range(GROUP)]
            factors = {
                below: [over_lanes(rows[below], start + col) for col in range(GROUP)] for below in range(step + 1, end)
            }
            inside = (lane >= start) & (lane < start + GROUP)
            forward = jnp.where(inside, jnp.where(lane - start == sub, 1.0, 0.0), rows[step])
            solved = forward
            for pivot in range(GROUP):
                here = sub == pivot
                value = over_rows(pivot_cols[pivot], pivot)
                inverse = 1.0 / value
                ratio = pivot_cols[pivot] * inverse
                row = over_rows(forward, pivot)
                below_row = jnp.where(sub > pivot, forward - ratio * row, forward)
                forward = jnp.where(here, row * lax.rsqrt(value), below_row)
                solved = jnp.where(here, row * inverse, solved - ratio * row)
                for col in range(pivot + 1, GROUP):
                    top = over_rows(pivot_cols[col], pivot)
                    pivot_cols[col] = jnp.where(here, top * inverse, pivot_cols[col] - ratio * top)
            own_part = (lane < start + GROUP) | (lane >= end * GROUP)
            reduced.append((forward, jnp.where(own_part, forward, 0.0)))
            rows[step] = jnp.where(lane < start + GROUP, forward, 0.0)
            solved_rows = [over_rows(solved, pivot) for pivot in range(GROUP)]
            for below in range(step + 1, end):
                terms = [factors[below][col] * solved_rows[col] for col in range(GROUP)]
                while len(terms) > 1:
                    terms = [terms[at] + terms[at + 1] for at in range(0, len(terms), 2)]
                rows[below] = jnp.where(inside, 0.0, rows[below]) - terms[0]
        if end < count:
            factor_rows, solved_rows = [jnp.concatenate(parts, 0) for parts in zip(*reduced)]
            share = exact_dot(factor_rows, solved_rows, TN)
            inside = (lane >= begin * GROUP) & (lane < end * GROUP)
            for below in range(end, count):
                rows[below] = jnp.where(inside, 0.0, rows[below]) - share[below * GROUP : (below + 1) * GROUP, :]
    return jnp.concatenate(rows, 0)


def first_tile_body(count, total_rows, number_ref, gram_ref, *tile_refs):
    packed = ordered_pieces(number_ref, gram_ref) / total_rows
    tiles = [packed[at * TILE : (at + 1) * TILE, :] for at in range(len(tile_refs))]
    finish_tile(0, count, dict(zip(lower_tiles(count), tiles)), tile_refs)


def next_tile_body(at, count, *refs):
    names = lower_tiles(count)
    tiles = {name: ref[...] for name, ref in zip(names, refs)}
    finish_tile(at, count, tiles, refs[len(names) :])


def finish_tile(at, count, tiles, out_refs):
    tiles = dict(tiles)
    tiles[at, at] = eliminate(tiles[at, at])
    for row in range(at + 1, count):
        tiles[row, at] = exact_dot(tiles[row, at], tiles[at, at], NT)
    for row in range(at + 1, count):
        for col in range(at + 1, row + 1):
            tiles[row, col] = tiles[row, col] - exact_dot(tiles[row, at], tiles[col, at], NT)
    for name, out_ref in zip(lower_tiles(count), out_refs):
        out_ref[...] = tiles[name]


def basis_body(count, *refs):
    *tile_refs, two_ref, basis_ref, inverse_ref = refs
    tiles = {name: ref[...] for name, ref in zip(lower_tiles(count), tile_refs)}
    inverse = {}
    for row in range(count):
        inverse[row, row] = tiles[row, row]
        for col in range(row):
            mixed = exact_dot(tiles[row, col], inverse[col, col])
            for mid in range(col + 1, row):
                mixed = mixed + exact_dot(tiles[row, mid], inverse[mid, col])
            inverse[row, col] = -exact_dot(tiles[row, row], mixed)
    zero = jnp.zeros((TILE, TILE), jnp.float32)
    whole = jnp.concatenate(
        [
            jnp.concatenate([inverse[row, col] if col <= row else zero for col in range(count)], 1)
            for row in range(count)
        ],
        0,
    )
    inverse_ref[...] = whole
    basis_ref[...] = exact_dot(two_ref[...], whole, NT)


def projected_body(total_rows, number_ref, cross_ref, inverse_ref, projected_ref):
    cross = ordered_pieces(number_ref, cross_ref) / total_rows
    projected_ref[...] = exact_dot(exact_dot(inverse_ref[...], cross), inverse_ref[...], NT)


def factor_stages(total_rows, count, number, two):
    rows, modes = two.shape
    tile = jax.ShapeDtypeStruct((TILE, TILE), jnp.float32)
    names = lower_tiles(count)
    work = 10**8

    def first(gram):
        body = functools.partial(first_tile_body, count, total_rows)
        return tuple(kernel_call(body, (tile,) * len(names), [SMEM, VMEM], work, gram.size)(number, gram))

    def following(at):
        def stage(state):
            body = functools.partial(next_tile_body, at, count)
            call = kernel_call(body, (tile,) * len(names), [VMEM] * len(names), work, TILE * TILE)
            return tuple(call(*state))

        return stage

    def finish(state):
        outs = (jax.ShapeDtypeStruct((rows, modes), jnp.float32), jax.ShapeDtypeStruct((modes, modes), jnp.float32))
        body = functools.partial(basis_body, count)
        return tuple(kernel_call(body, outs, [VMEM] * (len(names) + 1), work, rows * modes)(*state, two))

    return [first] + [following(at) for at in range(1, count)] + [finish]


def tied(left, right):
    return lax.optimization_barrier((left, right))


def partner_value(value, axis, bit):
    return lax.ppermute(value, axis, [(at, at ^ bit) for at in range(lax.axis_size(axis))])


def axis_bits(axis):
    return [(axis, 1 << at) for at in range(lax.axis_size(axis).bit_length() - 1)]


def device_number(halved):
    number = 0
    for axis, bit in halved:
        number = number * 2 + (lax.axis_index(axis) // bit) % 2
    return number.astype(jnp.int32).reshape(1)


def halving(axis, bit):
    def step(value):
        half = value.shape[0] // 2
        got = partner_value(value[half:], axis, bit)
        return lambda: value[:half] + got

    return step


def doubling(axis, bit):
    def step(value):
        got = partner_value(value, axis, bit)
        return lambda: value + got

    return step


def joining(axis, bit):
    def step(value):
        got = partner_value(value, axis, bit)
        return lambda: jnp.concatenate([value, got], 0)

    return step


def run_beside(value, steps, state, stages):
    stages = list(stages)
    for index, step in enumerate(steps):
        value, state = tied(value, state)
        join = step(value)
        due = -(-len(stages) // (len(steps) - index))
        for _ in range(due):
            state = stages.pop(0)(state)
        value = join()
        if due:
            value, state = tied(value, state)
    return value, state


def local(vectors, hessian, block_cols, live_blocks, halo_lists, bounds):
    row_blocks, stored, size, _ = hessian.shape
    rows, modes = vectors.shape
    splits = lax.axis_size("split")
    region_blocks = row_blocks * splits
    halo_blocks = halo_lists.shape[2]
    whole = halo_blocks == region_blocks and region_blocks <= 256
    total_rows = rows * lax.axis_size(AXES)

    paired = whole and splits == 2
    core = lax.axis_index("split").astype(jnp.int32)
    swapped = lambda value: lax.ppermute(value, "split", [(0, 1), (1, 0)])
    halo_first = [core * row_blocks, (1 - core) * row_blocks] if paired else [0]
    bases = jnp.stack(halo_first).astype(jnp.int32) if paired else jnp.zeros((1,), jnp.int32)

    def sent(operand, region):
        if whole:
            return operand, operand
        width = modes // splits
        start = core * width
        blocks = region[:, :rows].reshape(region_blocks, size, modes)
        share = lambda listed: lax.dynamic_slice_in_dim(blocks[listed], start, width, 2).reshape(-1, width)
        return share(halo_lists[0, 1]), share(halo_lists[0, 0])

    def gathered(value):
        if paired:
            return [value[None], swapped(value)[None]]
        if whole:
            return [lax.all_gather(value, "split", axis=0)]
        return [lax.all_gather(value, "split", axis=1, tiled=True)[None]]

    listed = jnp.pad(halo_lists[0], ((0, LIST_ROWS - 2), (0, modes - halo_blocks)))
    first = vectors.astype(jnp.bfloat16)
    if whole:
        first = jnp.concatenate([first, listed.astype(jnp.bfloat16)], 0)

    def exchange(operand, gather=True):
        if gather or not paired:
            groups = [lax.all_gather(operand, "split", axis=0)]
        else:
            groups = [operand[None], swapped(operand)[None]]
        up, down = sent(operand, groups[0])
        return groups, shifted(up, "region", 1), shifted(down, "region", -1)

    first_near, first_lower, first_upper = exchange(first)
    if whole:
        orders = [first_lower[rows + 1, :halo_blocks], first_upper[rows, :halo_blocks]]
        lists = jnp.stack(orders).astype(jnp.int32)
    else:
        lists = jnp.broadcast_to(jnp.arange(halo_blocks, dtype=jnp.int32), (2, halo_blocks))

    wide = jax.ShapeDtypeStruct((rows, modes), jnp.float32)
    narrow = jax.ShapeDtypeStruct((rows, modes), jnp.bfloat16)
    square = jax.ShapeDtypeStruct((modes, modes), jnp.float32)
    tile_rows = len(lower_tiles(modes // TILE)) * TILE
    work = 2 * rows * size * modes
    square_work = 2 * rows * modes * modes
    traffic = hessian.size * 2 + 3 * rows * modes * 4
    cores, *other_cores = axis_bits("split")
    near, across, *far = axis_bits("region")
    between = other_cores + far
    gram_number, cross_number = device_number([cores, across]), device_number([cores, near])
    halo_slots = (row_blocks, 2 * halo_blocks + 1)

    covering, free = 3 * 10 ** 10, 10 ** 7
    token = jax.ShapeDtypeStruct((GROUP, TILE), jnp.float32)

    held = pl.pallas_call(
        hold_body,
        out_shape=pltpu.VMEM(hessian.shape, hessian.dtype),
        in_specs=[pl.BlockSpec(memory_space=pl.ANY)],
        out_specs=VMEM,
        compiler_params=pltpu.CompilerParams(vmem_limit_bytes=VMEM_LIMIT),
    )(hessian)

    def near_total(body, outs, groups, scalars, terms):
        specs = [SMEM] * 3 + [VMEM] * (1 + len(groups)) + [SMEM] * len(scalars) + [VMEM] * len(terms)
        call = kernel_call(body, outs, specs, free, traffic, (row_blocks, region_blocks + 1))
        near_bases = bases if len(groups) > 1 else jnp.zeros_like(bases)
        return call(block_cols, live_blocks, near_bases, held, *groups, *scalars, *terms)

    def halo_part(body, outs, table, pair, total, scalars=(), extra=()):
        specs = [SMEM] * 2 + [VMEM] * 4 + [SMEM] * len(scalars) + [VMEM] * len(extra)
        call = kernel_call(body, outs, specs, covering, traffic)
        return call(table, bases, held, *pair, total, *scalars, *extra)

    def pairs_of(lower, upper):
        *pairs, last = zip(gathered(lower), gathered(upper))
        return pairs, last

    body_of = functools.partial(near_body, len(first_near), first_terms)
    (total,) = near_total(body_of, (wide,), first_near, (bounds,), (vectors,))
    pairs, last = pairs_of(first_lower, first_upper)
    pairs.append(last)
    body_of = functools.partial(table_body, region_blocks, 0)
    table_shape = jax.ShapeDtypeStruct(halo_slots, jnp.int32)
    specs = [SMEM] * 4 + [VMEM] * 4
    call = kernel_call(body_of, (wide, table_shape), specs, covering, traffic)
    if len(pairs) == 1:
        pairs.append(tuple(jnp.zeros_like(part) for part in last))
    total, table = call(block_cols, live_blocks, lists, bases, held, *pairs[0], total)
    which = len(pairs) - 1 if paired else 0
    body_of = functools.partial(scaled_body, which, 1.0)
    one, one_cast = halo_part(body_of, (wide, narrow), table, pairs[-1], total, (bounds,))

    own, lower, upper = exchange(one_cast)
    body_of = functools.partial(near_body, len(own), second_terms)
    (total,) = near_total(body_of, (wide,), own, (bounds,), (one, vectors))
    pairs, last = pairs_of(lower, upper)
    for which, pair in enumerate(pairs):
        (total,) = halo_part(functools.partial(middle_body, which), (wide,), table, pair, total)
    body_of = functools.partial(scaled_body, len(pairs), 2.0)
    two, two_cast = halo_part(body_of, (wide, narrow), table, last, total, (bounds,))

    own, lower, upper = exchange(two_cast, gather=False)
    packed = jax.ShapeDtypeStruct((tile_rows, TILE), jnp.float32)
    body_of = functools.partial(near_gram_body, len(own))
    total, gram = near_total(body_of, (wide, packed), own, (gram_number,), (two,))
    for step_of in [halving(*cores), halving(*across)]:
        gram = step_of(gram)()
    pairs, last = pairs_of(lower, upper)
    after = jnp.zeros(token.shape, token.dtype)
    for which, pair in enumerate(pairs):
        total, after = halo_part(functools.partial(middle_body, which), (wide, token), table, pair, total)
    gram, after = tied(gram, after)
    body_of = functools.partial(third_body, len(pairs))
    cross = halo_part(body_of, square, table, last, total, (cross_number,), (two, after))
    cross = halving(*cores)(cross)()

    fold = modes // TILE
    cut = gram.shape[0] // fold
    folded = jnp.concatenate([gram[at * cut : (at + 1) * cut] for at in range(fold)], 1)
    flat = lambda value: [value[:, at * TILE : (at + 1) * TILE] for at in range(fold)]
    half = cross.shape[0] // 2
    got = partner_value(jnp.concatenate([folded, cross[half:]], 0), *near)
    both = jnp.concatenate([folded, cross[:half]], 0) + got
    for bit in between:
        both = doubling(*bit)(both)()
    got = partner_value(both, *across)
    gram = joining(*cores)(jnp.concatenate(flat(both[:cut]) + flat(got[:cut]), 0))()
    cross = both[cut:] + got[cut:]
    stages = factor_stages(float(total_rows), modes // TILE, gram_number, two)
    steps = [joining(*near), joining(*cores)]
    cross, (basis, inverse) = run_beside(cross, steps, gram, stages)
    body_of = functools.partial(projected_body, float(total_rows))
    call = kernel_call(body_of, square, [SMEM] + [VMEM] * 2, 2 * square_work, traffic)
    return basis, call(cross_number, cross, inverse)


def solution(mesh):
    placed = (
        P(("region", "split"), None),
        P(("region", "split"), None, None, None),
        P(("region", "split"), None),
        P(("region", "split")),
        P("region", None, None),
        P(),
    )
    return jax.shard_map(
        local,
        mesh=mesh,
        in_specs=placed,
        out_specs=(P(("region", "split"), None), P()),
        check_vma=False,
    )
```

```python
import functools
import jax
import jax.numpy as jnp
from jax import lax
from jax.experimental import pallas as pl
from jax.experimental.pallas import tpu as pltpu
from jax.sharding import PartitionSpec as P

AXES = ("region", "split")
VMEM = pl.BlockSpec(memory_space=pltpu.VMEM)
SMEM = pl.BlockSpec(memory_space=pltpu.SMEM)
EXACT = lax.Precision.HIGHEST
NN = (((1,), (0,)), ((), ()))
NT = (((1,), (1,)), ((), ()))
TN = (((0,), (0,)), ((), ()))
GROUP = 8
PANEL = 32
TILE = 128
VMEM_LIMIT = 6 * 1024 * 1024
LIST_ROWS = 16
PIECES = 4


def shifted(value, axis, steps):
    count = lax.axis_size(axis)
    pairs = [(source, (source + steps) % count) for source in range(count)]
    return lax.ppermute(value, axis, pairs)


def exact_dot(left, right, dims=NN):
    return lax.dot_general(left, right, dims, precision=EXACT, preferred_element_type=jnp.float32)


def kernel_call(body, out_shape, in_specs, flops, bytes_accessed, slots=None):
    return pl.pallas_call(
        body,
        out_shape=out_shape,
        in_specs=in_specs,
        out_specs=jax.tree.map(lambda out: SMEM if out.dtype == jnp.int32 else VMEM, out_shape),
        scratch_shapes=[] if slots is None else [pltpu.SMEM(slots, jnp.int32)],
        compiler_params=pltpu.CompilerParams(vmem_limit_bytes=VMEM_LIMIT),
        cost_estimate=pl.CostEstimate(flops=flops, bytes_accessed=bytes_accessed // 16, transcendentals=0),
    )


def fill_slots(slots_ref, cols_ref, live_ref, first, place_of):
    rows, stored = cols_ref.shape
    count = slots_ref.shape[1] - 1
    for row in range(rows):
        for index in range(count):
            slots_ref[row, index] = -1
        for at in range(stored):
            name = cols_ref[row, at] - first
            inside = (name >= 0) & (name < count) & (at < live_ref[row])
            slots_ref[row, jnp.where(inside, place_of(jnp.clip(name, 0, count - 1)), count)] = at


def accumulate(slots_ref, hessian_ref, operand_ref, base, total):
    rows, _, size, _ = hessian_ref.shape
    shards, shard_rows, _ = operand_ref.shape
    each = shard_rows // size
    for index in range(shards * each):
        start = index % each * size
        block = operand_ref[index // each, start : start + size, :]
        parts = []
        for row in range(rows):
            slot = slots_ref[row, base + index]
            live = jnp.where(slot >= 0, 1.0, 0.0).astype(jnp.float32)
            stored = hessian_ref[row, jnp.maximum(slot, 0)]
            parts.append(stored * jnp.broadcast_to(live, (size, size)).astype(jnp.bfloat16))
        term = jnp.dot(jnp.concatenate(parts, 0), block, preferred_element_type=jnp.float32)
        total = term if total is None else total + term
    return total


def hold_body(blocks_ref, out_ref):
    pltpu.sync_copy(blocks_ref, out_ref)


def near_body(groups, linear, *refs):
    cols_ref, live_ref, bases_ref, hessian_ref = refs[:4]
    operands, (*terms, out_ref, slots_ref) = refs[4 : 4 + groups], refs[4 + groups :]
    fill_slots(slots_ref, cols_ref, live_ref, 0, lambda name: name)
    total = None
    for at, operand_ref in enumerate(operands):
        total = accumulate(slots_ref, hessian_ref, operand_ref, bases_ref[at], total)
    out_ref[...] = linear(total, *terms)


def near_gram_body(groups, *refs):
    *operands, number_ref, two_ref, out_ref, gram_ref, slots_ref = refs
    near_body(groups, lambda total: total, *operands, out_ref, slots_ref)
    gram_part(number_ref, two_ref, gram_ref)


def first_terms(total, bounds_ref, vectors_ref):
    centre, _ = interval(bounds_ref)
    return total - centre * vectors_ref[...]


def second_terms(total, bounds_ref, one_ref, vectors_ref):
    centre, half = interval(bounds_ref)
    return total - centre * one_ref[...] - (0.5 * half) * vectors_ref[...]


def list_place(lists_ref, name):
    halo = lists_ref.shape[1]
    side = jnp.where(name >= halo, 1, 0).astype(jnp.int32)
    return side * halo + lists_ref[side, name - side * halo]


def halo_total(which, slots_ref, bases_ref, hessian_ref, lower_ref, upper_ref, total_ref):
    halo = (slots_ref.shape[1] - 1) // 2
    total = accumulate(slots_ref, hessian_ref, lower_ref, bases_ref[which], total_ref[...])
    return accumulate(slots_ref, hessian_ref, upper_ref, halo + bases_ref[which], total)


def table_body(first, which, cols_ref, live_ref, lists_ref, *refs):
    *operands, out_ref, slots_ref = refs
    fill_slots(slots_ref, cols_ref, live_ref, first, lambda name: list_place(lists_ref, name))
    out_ref[...] = halo_total(which, slots_ref, *operands)


def middle_body(which, *refs):
    operands, (out_ref, *token_refs) = refs[:6], refs[6:]
    total = halo_total(which, *operands)
    out_ref[...] = total
    for token_ref in token_refs:
        token_ref[...] = total[:GROUP, :TILE]


def interval(bounds_ref):
    return 0.5 * (bounds_ref[0] + bounds_ref[1]), 0.5 * (bounds_ref[1] - bounds_ref[0])


def scaled_body(which, factor, *refs):
    *operands, bounds_ref, out_ref, cast_ref = refs
    _, half = interval(bounds_ref)
    value = factor * halo_total(which, *operands) / half
    out_ref[...] = value
    cast_ref[...] = value.astype(jnp.bfloat16)


def place_rows(number_ref, piece, rows):
    return pl.ds(pl.multiple_of((piece ^ number_ref[0]) * rows, GROUP), rows)


def scatter_pieces(number_ref, out_ref, value):
    rows = out_ref.shape[0] // PIECES
    for piece in range(PIECES):
        out_ref[place_rows(number_ref, piece, rows), :] = value[piece * rows : (piece + 1) * rows, :]


def ordered_pieces(number_ref, in_ref):
    rows = in_ref.shape[0] // PIECES
    return jnp.concatenate([in_ref[place_rows(number_ref, piece, rows), :] for piece in range(PIECES)], 0)


def lower_tiles(count):
    return [(row, col) for row in range(count) for col in range(row + 1)]


def gram_part(number_ref, two_ref, out_ref):
    two = two_ref[...]
    cols = [two[:, at * TILE : (at + 1) * TILE] for at in range(two.shape[1] // TILE)]
    tiles = [exact_dot(cols[row], cols[col], TN) for row, col in lower_tiles(len(cols))]
    scatter_pieces(number_ref, out_ref, jnp.concatenate(tiles, 0))


def third_body(which, *refs):
    *operands, number_ref, two_ref, _, out_ref = refs
    image = halo_total(which, *operands)
    scatter_pieces(number_ref, out_ref, exact_dot(two_ref[...], image, TN))


def over_lanes(value, lane):
    return jnp.broadcast_to(value[:, lane : lane + 1], value.shape)


def over_rows(value, row):
    return jnp.broadcast_to(value[row : row + 1, :], value.shape)


def eliminate(tile):
    count, panel = tile.shape[0] // GROUP, PANEL // GROUP
    rows = [tile[index * GROUP : (index + 1) * GROUP, :] for index in range(count)]
    sub = lax.broadcasted_iota(jnp.int32, rows[0].shape, 0)
    lane = lax.broadcasted_iota(jnp.int32, rows[0].shape, 1)
    for begin in range(0, count, panel):
        end = begin + panel
        reduced = []
        for step in range(begin, end):
            start = step * GROUP
            pivot_cols = [over_lanes(rows[step], start + col) for col in range(GROUP)]
            factors = {
                below: [over_lanes(rows[below], start + col) for col in range(GROUP)] for below in range(step + 1, end)
            }
            inside = (lane >= start) & (lane < start + GROUP)
            forward = jnp.where(inside, jnp.where(lane - start == sub, 1.0, 0.0), rows[step])
            solved = forward
            scalars = {
                (row, col): over_rows(pivot_cols[col], row) for row in range(GROUP) for col in range(row + 1)
            }
            for pivot in range(GROUP):
                inverse = 1.0 / scalars[pivot, pivot]
                for row in range(pivot + 1, GROUP):
                    multiple = scalars[row, pivot] * inverse
                    for col in range(pivot + 1, row + 1):
                        scalars[row, col] = scalars[row, col] - multiple * scalars[col, pivot]
                here = sub == pivot
                ratio = pivot_cols[pivot] * inverse
                row = over_rows(forward, pivot)
                below_row = jnp.where(sub > pivot, forward - ratio * row, forward)
                forward = jnp.where(here, row * lax.rsqrt(scalars[pivot, pivot]), below_row)
                solved = jnp.where(here, row * inverse, solved - ratio * row)
                for col in range(pivot + 1, GROUP):
                    top = scalars[col, pivot]
                    pivot_cols[col] = jnp.where(here, top * inverse, pivot_cols[col] - ratio * top)
            own_part = (lane < start + GROUP) | (lane >= end * GROUP)
            reduced.append((forward, jnp.where(own_part, forward, 0.0)))
            rows[step] = jnp.where(lane < start + GROUP, forward, 0.0)
            solved_rows = [over_rows(solved, pivot) for pivot in range(GROUP)]
            for below in range(step + 1, end):
                terms = [factors[below][col] * solved_rows[col] for col in range(GROUP)]
                while len(terms) > 1:
                    terms = [terms[at] + terms[at + 1] for at in range(0, len(terms), 2)]
                rows[below] = jnp.where(inside, 0.0, rows[below]) - terms[0]
        if end < count:
            factor_rows, solved_rows = [jnp.concatenate(parts, 0) for parts in zip(*reduced)]
            share = exact_dot(factor_rows, solved_rows, TN)
            inside = (lane >= begin * GROUP) & (lane < end * GROUP)
            for below in range(end, count):
                rows[below] = jnp.where(inside, 0.0, rows[below]) - share[below * GROUP : (below + 1) * GROUP, :]
    return jnp.concatenate(rows, 0)


def first_tile_body(count, total_rows, number_ref, gram_ref, *tile_refs):
    packed = ordered_pieces(number_ref, gram_ref) / total_rows
    tiles = [packed[at * TILE : (at + 1) * TILE, :] for at in range(len(tile_refs))]
    finish_tile(0, count, dict(zip(lower_tiles(count), tiles)), tile_refs)


def next_tile_body(at, count, *refs):
    names = lower_tiles(count)
    tiles = {name: ref[...] for name, ref in zip(names, refs)}
    finish_tile(at, count, tiles, refs[len(names) :])


def finish_tile(at, count, tiles, out_refs):
    tiles = dict(tiles)
    tiles[at, at] = eliminate(tiles[at, at])
    for row in range(at + 1, count):
        tiles[row, at] = exact_dot(tiles[row, at], tiles[at, at], NT)
    for row in range(at + 1, count):
        for col in range(at + 1, row + 1):
            tiles[row, col] = tiles[row, col] - exact_dot(tiles[row, at], tiles[col, at], NT)
    for name, out_ref in zip(lower_tiles(count), out_refs):
        out_ref[...] = tiles[name]


def basis_body(count, *refs):
    *tile_refs, two_ref, basis_ref, inverse_ref = refs
    tiles = {name: ref[...] for name, ref in zip(lower_tiles(count), tile_refs)}
    inverse = {}
    for row in range(count):
        inverse[row, row] = tiles[row, row]
        for col in range(row):
            mixed = exact_dot(tiles[row, col], inverse[col, col])
            for mid in range(col + 1, row):
                mixed = mixed + exact_dot(tiles[row, mid], inverse[mid, col])
            inverse[row, col] = -exact_dot(tiles[row, row], mixed)
    zero = jnp.zeros((TILE, TILE), jnp.float32)
    whole = jnp.concatenate(
        [
            jnp.concatenate([inverse[row, col] if col <= row else zero for col in range(count)], 1)
            for row in range(count)
        ],
        0,
    )
    inverse_ref[...] = whole
    basis_ref[...] = exact_dot(two_ref[...], whole, NT)


def projected_body(total_rows, number_ref, cross_ref, inverse_ref, projected_ref):
    cross = ordered_pieces(number_ref, cross_ref) / total_rows
    projected_ref[...] = exact_dot(exact_dot(inverse_ref[...], cross), inverse_ref[...], NT)


def factor_stages(total_rows, count, number, two):
    rows, modes = two.shape
    tile = jax.ShapeDtypeStruct((TILE, TILE), jnp.float32)
    names = lower_tiles(count)
    work = 10**8

    def first(gram):
        body = functools.partial(first_tile_body, count, total_rows)
        return tuple(kernel_call(body, (tile,) * len(names), [SMEM, VMEM], work, gram.size)(number, gram))

    def following(at):
        def stage(state):
            body = functools.partial(next_tile_body, at, count)
            call = kernel_call(body, (tile,) * len(names), [VMEM] * len(names), work, TILE * TILE)
            return tuple(call(*state))

        return stage

    def finish(state):
        outs = (jax.ShapeDtypeStruct((rows, modes), jnp.float32), jax.ShapeDtypeStruct((modes, modes), jnp.float32))
        body = functools.partial(basis_body, count)
        return tuple(kernel_call(body, outs, [VMEM] * (len(names) + 1), work, rows * modes)(*state, two))

    return [first] + [following(at) for at in range(1, count)] + [finish]


def tied(left, right):
    return lax.optimization_barrier((left, right))


def partner_value(value, axis, bit):
    return lax.ppermute(value, axis, [(at, at ^ bit) for at in range(lax.axis_size(axis))])


def axis_bits(axis):
    return [(axis, 1 << at) for at in range(lax.axis_size(axis).bit_length() - 1)]


def device_number(halved):
    number = 0
    for axis, bit in halved:
        number = number * 2 + (lax.axis_index(axis) // bit) % 2
    return number.astype(jnp.int32).reshape(1)


def halving(axis, bit):
    def step(value):
        half = value.shape[0] // 2
        got = partner_value(value[half:], axis, bit)
        return lambda: value[:half] + got

    return step


def doubling(axis, bit):
    def step(value):
        got = partner_value(value, axis, bit)
        return lambda: value + got

    return step


def joining(axis, bit):
    def step(value):
        got = partner_value(value, axis, bit)
        return lambda: jnp.concatenate([value, got], 0)

    return step


def run_beside(value, steps, state, stages):
    stages = list(stages)
    for index, step in enumerate(steps):
        value, state = tied(value, state)
        join = step(value)
        due = -(-len(stages) // (len(steps) - index))
        for _ in range(due):
            state = stages.pop(0)(state)
        value = join()
        if due:
            value, state = tied(value, state)
    return value, state


def local(vectors, hessian, block_cols, live_blocks, halo_lists, bounds):
    row_blocks, stored, size, _ = hessian.shape
    rows, modes = vectors.shape
    splits = lax.axis_size("split")
    region_blocks = row_blocks * splits
    halo_blocks = halo_lists.shape[2]
    whole = halo_blocks == region_blocks and region_blocks <= 256
    total_rows = rows * lax.axis_size(AXES)

    paired = whole and splits == 2
    core = lax.axis_index("split").astype(jnp.int32)
    swapped = lambda value: lax.ppermute(value, "split", [(0, 1), (1, 0)])
    halo_first = [core * row_blocks, (1 - core) * row_blocks] if paired else [0]
    bases = jnp.stack(halo_first).astype(jnp.int32) if paired else jnp.zeros((1,), jnp.int32)

    def sent(operand, region):
        if whole:
            return operand, operand
        width = modes // splits
        start = core * width
        blocks = region[:, :rows].reshape(region_blocks, size, modes)
        share = lambda listed: lax.dynamic_slice_in_dim(blocks[listed], start, width, 2).reshape(-1, width)
        return share(halo_lists[0, 1]), share(halo_lists[0, 0])

    def gathered(value):
        if paired:
            return [value[None], swapped(value)[None]]
        if whole:
            return [lax.all_gather(value, "split", axis=0)]
        return [lax.all_gather(value, "split", axis=1, tiled=True)[None]]

    listed = jnp.pad(halo_lists[0], ((0, LIST_ROWS - 2), (0, modes - halo_blocks)))
    first = vectors.astype(jnp.bfloat16)
    if whole:
        first = jnp.concatenate([first, listed.astype(jnp.bfloat16)], 0)

    def exchange(operand, gather=True):
        if gather or not paired:
            groups = [lax.all_gather(operand, "split", axis=0)]
        else:
            groups = [operand[None], swapped(operand)[None]]
        up, down = sent(operand, groups[0])
        return groups, shifted(up, "region", 1), shifted(down, "region", -1)

    first_near, first_lower, first_upper = exchange(first)
    if whole:
        orders = [first_lower[rows + 1, :halo_blocks], first_upper[rows, :halo_blocks]]
        lists = jnp.stack(orders).astype(jnp.int32)
    else:
        lists = jnp.broadcast_to(jnp.arange(halo_blocks, dtype=jnp.int32), (2, halo_blocks))

    wide = jax.ShapeDtypeStruct((rows, modes), jnp.float32)
    narrow = jax.ShapeDtypeStruct((rows, modes), jnp.bfloat16)
    square = jax.ShapeDtypeStruct((modes, modes), jnp.float32)
    tile_rows = len(lower_tiles(modes // TILE)) * TILE
    work = 2 * rows * size * modes
    square_work = 2 * rows * modes * modes
    traffic = hessian.size * 2 + 3 * rows * modes * 4
    cores, *other_cores = axis_bits("split")
    near, across, *far = axis_bits("region")
    between = other_cores + far
    gram_number, cross_number = device_number([cores, across]), device_number([cores, near])
    halo_slots = (row_blocks, 2 * halo_blocks + 1)

    covering, free = 3 * 10 ** 10, 10 ** 7
    token = jax.ShapeDtypeStruct((GROUP, TILE), jnp.float32)

    held = pl.pallas_call(
        hold_body,
        out_shape=pltpu.VMEM(hessian.shape, hessian.dtype),
        in_specs=[pl.BlockSpec(memory_space=pl.ANY)],
        out_specs=VMEM,
        compiler_params=pltpu.CompilerParams(vmem_limit_bytes=VMEM_LIMIT),
    )(hessian)

    def near_total(body, outs, groups, scalars, terms):
        specs = [SMEM] * 3 + [VMEM] * (1 + len(groups)) + [SMEM] * len(scalars) + [VMEM] * len(terms)
        call = kernel_call(body, outs, specs, free, traffic, (row_blocks, region_blocks + 1))
        near_bases = bases if len(groups) > 1 else jnp.zeros_like(bases)
        return call(block_cols, live_blocks, near_bases, held, *groups, *scalars, *terms)

    def halo_part(body, outs, table, pair, total, scalars=(), extra=()):
        specs = [SMEM] * 2 + [VMEM] * 4 + [SMEM] * len(scalars) + [VMEM] * len(extra)
        call = kernel_call(body, outs, specs, covering, traffic)
        return call(table, bases, held, *pair, total, *scalars, *extra)

    def pairs_of(lower, upper):
        *pairs, last = zip(gathered(lower), gathered(upper))
        return pairs, last

    body_of = functools.partial(near_body, len(first_near), first_terms)
    (total,) = near_total(body_of, (wide,), first_near, (bounds,), (vectors,))
    pairs, last = pairs_of(first_lower, first_upper)
    pairs.append(last)
    body_of = functools.partial(table_body, region_blocks, 0)
    table_shape = jax.ShapeDtypeStruct(halo_slots, jnp.int32)
    specs = [SMEM] * 4 + [VMEM] * 4
    call = kernel_call(body_of, (wide, table_shape), specs, covering, traffic)
    if len(pairs) == 1:
        pairs.append(tuple(jnp.zeros_like(part) for part in last))
    total, table = call(block_cols, live_blocks, lists, bases, held, *pairs[0], total)
    which = len(pairs) - 1 if paired else 0
    body_of = functools.partial(scaled_body, which, 1.0)
    one, one_cast = halo_part(body_of, (wide, narrow), table, pairs[-1], total, (bounds,))

    own, lower, upper = exchange(one_cast)
    body_of = functools.partial(near_body, len(own), second_terms)
    (total,) = near_total(body_of, (wide,), own, (bounds,), (one, vectors))
    pairs, last = pairs_of(lower, upper)
    for which, pair in enumerate(pairs):
        (total,) = halo_part(functools.partial(middle_body, which), (wide,), table, pair, total)
    body_of = functools.partial(scaled_body, len(pairs), 2.0)
    two, two_cast = halo_part(body_of, (wide, narrow), table, last, total, (bounds,))

    own, lower, upper = exchange(two_cast, gather=False)
    packed = jax.ShapeDtypeStruct((tile_rows, TILE), jnp.float32)
    body_of = functools.partial(near_gram_body, len(own))
    total, gram = near_total(body_of, (wide, packed), own, (gram_number,), (two,))
    for step_of in [halving(*cores), halving(*across)]:
        gram = step_of(gram)()
    pairs, last = pairs_of(lower, upper)
    after = jnp.zeros(token.shape, token.dtype)
    for which, pair in enumerate(pairs):
        total, after = halo_part(functools.partial(middle_body, which), (wide, token), table, pair, total)
    gram, after = tied(gram, after)
    body_of = functools.partial(third_body, len(pairs))
    cross = halo_part(body_of, square, table, last, total, (cross_number,), (two, after))
    cross = halving(*cores)(cross)()

    fold = modes // TILE
    cut = gram.shape[0] // fold
    folded = jnp.concatenate([gram[at * cut : (at + 1) * cut] for at in range(fold)], 1)
    flat = lambda value: [value[:, at * TILE : (at + 1) * TILE] for at in range(fold)]
    half = cross.shape[0] // 2
    got = partner_value(jnp.concatenate([folded, cross[half:]], 0), *near)
    both = jnp.concatenate([folded, cross[:half]], 0) + got
    for bit in between:
        both = doubling(*bit)(both)()
    got = partner_value(both, *across)
    gram = joining(*cores)(jnp.concatenate(flat(both[:cut]) + flat(got[:cut]), 0))()
    cross = both[cut:] + got[cut:]
    stages = factor_stages(float(total_rows), modes // TILE, gram_number, two)
    steps = [joining(*near), joining(*cores)]
    cross, (basis, inverse) = run_beside(cross, steps, gram, stages)
    body_of = functools.partial(projected_body, float(total_rows))
    call = kernel_call(body_of, square, [SMEM] + [VMEM] * 2, 2 * square_work, traffic)
    return basis, call(cross_number, cross, inverse)


def solution(mesh):
    placed = (
        P(("region", "split"), None),
        P(("region", "split"), None, None, None),
        P(("region", "split"), None),
        P(("region", "split")),
        P("region", None, None),
        P(),
    )
    return jax.shard_map(
        local,
        mesh=mesh,
        in_specs=placed,
        out_specs=(P(("region", "split"), None), P()),
        check_vma=False,
    )
```

```python
import functools
import jax
import jax.numpy as jnp
from jax import lax
from jax.experimental import pallas as pl
from jax.experimental.pallas import tpu as pltpu
from jax.sharding import PartitionSpec as P

AXES = ("region", "split")
VMEM = pl.BlockSpec(memory_space=pltpu.VMEM)
SMEM = pl.BlockSpec(memory_space=pltpu.SMEM)
EXACT = lax.Precision.HIGHEST
NN = (((1,), (0,)), ((), ()))
NT = (((1,), (1,)), ((), ()))
TN = (((0,), (0,)), ((), ()))
GROUP = 8
PANEL = 32
TILE = 128
VMEM_LIMIT = 6 * 1024 * 1024
LIST_ROWS = 16
PIECES = 4


def shifted(value, axis, steps):
    count = lax.axis_size(axis)
    pairs = [(source, (source + steps) % count) for source in range(count)]
    return lax.ppermute(value, axis, pairs)


def exact_dot(left, right, dims=NN):
    return lax.dot_general(left, right, dims, precision=EXACT, preferred_element_type=jnp.float32)


def kernel_call(body, out_shape, in_specs, flops, bytes_accessed, slots=None):
    return pl.pallas_call(
        body,
        out_shape=out_shape,
        in_specs=in_specs,
        out_specs=jax.tree.map(lambda out: SMEM if out.dtype == jnp.int32 else VMEM, out_shape),
        scratch_shapes=[] if slots is None else [pltpu.SMEM(slots, jnp.int32)],
        compiler_params=pltpu.CompilerParams(vmem_limit_bytes=VMEM_LIMIT),
        cost_estimate=pl.CostEstimate(flops=flops, bytes_accessed=bytes_accessed // 16, transcendentals=0),
    )


def fill_slots(slots_ref, cols_ref, live_ref, first, place_of):
    rows, stored = cols_ref.shape
    count = slots_ref.shape[1] - 1
    for row in range(rows):
        for index in range(count):
            slots_ref[row, index] = -1
        for at in range(stored):
            name = cols_ref[row, at] - first
            inside = (name >= 0) & (name < count) & (at < live_ref[row])
            slots_ref[row, jnp.where(inside, place_of(jnp.clip(name, 0, count - 1)), count)] = at


def accumulate(slots_ref, hessian_ref, operand_ref, base, total):
    rows, _, size, _ = hessian_ref.shape
    shards, shard_rows, _ = operand_ref.shape
    each = shard_rows // size
    for index in range(shards * each):
        start = index % each * size
        block = operand_ref[index // each, start : start + size, :]
        parts = []
        for row in range(rows):
            slot = slots_ref[row, base + index]
            live = jnp.where(slot >= 0, 1.0, 0.0).astype(jnp.float32)
            stored = hessian_ref[row, jnp.maximum(slot, 0)]
            parts.append(stored * jnp.broadcast_to(live, (size, size)).astype(jnp.bfloat16))
        term = jnp.dot(jnp.concatenate(parts, 0), block, preferred_element_type=jnp.float32)
        total = term if total is None else total + term
    return total


def hold_body(blocks_ref, out_ref):
    pltpu.sync_copy(blocks_ref, out_ref)


def near_body(groups, linear, *refs):
    cols_ref, live_ref, bases_ref, hessian_ref = refs[:4]
    operands, (*terms, out_ref, slots_ref) = refs[4 : 4 + groups], refs[4 + groups :]
    fill_slots(slots_ref, cols_ref, live_ref, 0, lambda name: name)
    total = None
    for at, operand_ref in enumerate(operands):
        total = accumulate(slots_ref, hessian_ref, operand_ref, bases_ref[at], total)
    out_ref[...] = linear(total, *terms)


def near_gram_body(groups, *refs):
    *operands, number_ref, two_ref, out_ref, gram_ref, slots_ref = refs
    near_body(groups, lambda total: total, *operands, out_ref, slots_ref)
    gram_part(number_ref, two_ref, gram_ref)


def first_terms(total, bounds_ref, vectors_ref):
    centre, _ = interval(bounds_ref)
    return total - centre * vectors_ref[...]


def second_terms(total, bounds_ref, one_ref, vectors_ref):
    centre, half = interval(bounds_ref)
    return total - centre * one_ref[...] - (0.5 * half) * vectors_ref[...]


def list_place(lists_ref, name):
    halo = lists_ref.shape[1]
    side = jnp.where(name >= halo, 1, 0).astype(jnp.int32)
    return side * halo + lists_ref[side, name - side * halo]


def halo_total(which, slots_ref, bases_ref, hessian_ref, lower_ref, upper_ref, total_ref):
    halo = (slots_ref.shape[1] - 1) // 2
    total = accumulate(slots_ref, hessian_ref, lower_ref, bases_ref[which], total_ref[...])
    return accumulate(slots_ref, hessian_ref, upper_ref, halo + bases_ref[which], total)


def table_body(first, which, cols_ref, live_ref, lists_ref, *refs):
    *operands, out_ref, slots_ref = refs
    fill_slots(slots_ref, cols_ref, live_ref, first, lambda name: list_place(lists_ref, name))
    out_ref[...] = halo_total(which, slots_ref, *operands)


def middle_body(which, *refs):
    operands, (out_ref, *token_refs) = refs[:6], refs[6:]
    total = halo_total(which, *operands)
    out_ref[...] = total
    for token_ref in token_refs:
        token_ref[...] = total[:GROUP, :TILE]


def interval(bounds_ref):
    return 0.5 * (bounds_ref[0] + bounds_ref[1]), 0.5 * (bounds_ref[1] - bounds_ref[0])


def scaled_body(which, factor, *refs):
    *operands, bounds_ref, out_ref, cast_ref = refs
    _, half = interval(bounds_ref)
    value = factor * halo_total(which, *operands) / half
    out_ref[...] = value
    cast_ref[...] = value.astype(jnp.bfloat16)


def place_rows(number_ref, piece, rows):
    return pl.ds(pl.multiple_of((piece ^ number_ref[0]) * rows, GROUP), rows)


def scatter_pieces(number_ref, out_ref, value):
    rows = out_ref.shape[0] // PIECES
    for piece in range(PIECES):
        out_ref[place_rows(number_ref, piece, rows), :] = value[piece * rows : (piece + 1) * rows, :]


def ordered_pieces(number_ref, in_ref):
    rows = in_ref.shape[0] // PIECES
    return jnp.concatenate([in_ref[place_rows(number_ref, piece, rows), :] for piece in range(PIECES)], 0)


def lower_tiles(count):
    return [(row, col) for row in range(count) for col in range(row + 1)]


def gram_part(number_ref, two_ref, out_ref):
    two = two_ref[...]
    cols = [two[:, at * TILE : (at + 1) * TILE] for at in range(two.shape[1] // TILE)]
    tiles = [exact_dot(cols[row], cols[col], TN) for row, col in lower_tiles(len(cols))]
    scatter_pieces(number_ref, out_ref, jnp.concatenate(tiles, 0))


def third_body(which, *refs):
    *operands, number_ref, two_ref, _, out_ref = refs
    image = halo_total(which, *operands)
    scatter_pieces(number_ref, out_ref, exact_dot(two_ref[...], image, TN))


def over_lanes(value, lane):
    return jnp.broadcast_to(value[:, lane : lane + 1], value.shape)


def over_rows(value, row):
    return jnp.broadcast_to(value[row : row + 1, :], value.shape)


def refined_reciprocal(value):
    guess = pl.reciprocal(value, approx=True)
    guess = guess * (2.0 - value * guess)
    return guess * (2.0 - value * guess)


def eliminate(tile):
    count, panel = tile.shape[0] // GROUP, PANEL // GROUP
    rows = [tile[index * GROUP : (index + 1) * GROUP, :] for index in range(count)]
    sub = lax.broadcasted_iota(jnp.int32, rows[0].shape, 0)
    lane = lax.broadcasted_iota(jnp.int32, rows[0].shape, 1)
    for begin in range(0, count, panel):
        end = begin + panel
        reduced = []
        for step in range(begin, end):
            start = step * GROUP
            pivot_cols = [over_lanes(rows[step], start + col) for col in range(GROUP)]
            factors = {
                below: [over_lanes(rows[below], start + col) for col in range(GROUP)] for below in range(step + 1, end)
            }
            inside = (lane >= start) & (lane < start + GROUP)
            forward = jnp.where(inside, jnp.where(lane - start == sub, 1.0, 0.0), rows[step])
            solved = forward
            scalars = {
                (row, col): over_rows(pivot_cols[col], row) for row in range(GROUP) for col in range(row + 1)
            }
            for pivot in range(GROUP):
                inverse = refined_reciprocal(scalars[pivot, pivot])
                for row in range(pivot + 1, GROUP):
                    multiple = scalars[row, pivot] * inverse
                    for col in range(pivot + 1, row + 1):
                        scalars[row, col] = scalars[row, col] - multiple * scalars[col, pivot]
                here = sub == pivot
                ratio = pivot_cols[pivot] * inverse
                row = over_rows(forward, pivot)
                below_row = jnp.where(sub > pivot, forward - ratio * row, forward)
                forward = jnp.where(here, row * lax.rsqrt(scalars[pivot, pivot]), below_row)
                solved = jnp.where(here, row * inverse, solved - ratio * row)
                for col in range(pivot + 1, GROUP):
                    top = scalars[col, pivot]
                    pivot_cols[col] = jnp.where(here, top * inverse, pivot_cols[col] - ratio * top)
            own_part = (lane < start + GROUP) | (lane >= end * GROUP)
            reduced.append((forward, jnp.where(own_part, forward, 0.0)))
            rows[step] = jnp.where(lane < start + GROUP, forward, 0.0)
            solved_rows = [over_rows(solved, pivot) for pivot in range(GROUP)]
            for below in range(step + 1, end):
                terms = [factors[below][col] * solved_rows[col] for col in range(GROUP)]
                while len(terms) > 1:
                    terms = [terms[at] + terms[at + 1] for at in range(0, len(terms), 2)]
                rows[below] = jnp.where(inside, 0.0, rows[below]) - terms[0]
        if end < count:
            factor_rows, solved_rows = [jnp.concatenate(parts, 0) for parts in zip(*reduced)]
            share = exact_dot(factor_rows, solved_rows, TN)
            inside = (lane >= begin * GROUP) & (lane < end * GROUP)
            for below in range(end, count):
                rows[below] = jnp.where(inside, 0.0, rows[below]) - share[below * GROUP : (below + 1) * GROUP, :]
    return jnp.concatenate(rows, 0)


def first_tile_body(count, total_rows, number_ref, gram_ref, *tile_refs):
    packed = ordered_pieces(number_ref, gram_ref) / total_rows
    tiles = [packed[at * TILE : (at + 1) * TILE, :] for at in range(len(tile_refs))]
    finish_tile(0, count, dict(zip(lower_tiles(count), tiles)), tile_refs)


def next_tile_body(at, count, *refs):
    names = lower_tiles(count)
    tiles = {name: ref[...] for name, ref in zip(names, refs)}
    finish_tile(at, count, tiles, refs[len(names) :])


def finish_tile(at, count, tiles, out_refs):
    tiles = dict(tiles)
    tiles[at, at] = eliminate(tiles[at, at])
    for row in range(at + 1, count):
        tiles[row, at] = exact_dot(tiles[row, at], tiles[at, at], NT)
    for row in range(at + 1, count):
        for col in range(at + 1, row + 1):
            tiles[row, col] = tiles[row, col] - exact_dot(tiles[row, at], tiles[col, at], NT)
    for name, out_ref in zip(lower_tiles(count), out_refs):
        out_ref[...] = tiles[name]


def basis_body(count, *refs):
    *tile_refs, two_ref, basis_ref, inverse_ref = refs
    tiles = {name: ref[...] for name, ref in zip(lower_tiles(count), tile_refs)}
    inverse = {}
    for row in range(count):
        inverse[row, row] = tiles[row, row]
        for col in range(row):
            mixed = exact_dot(tiles[row, col], inverse[col, col])
            for mid in range(col + 1, row):
                mixed = mixed + exact_dot(tiles[row, mid], inverse[mid, col])
            inverse[row, col] = -exact_dot(tiles[row, row], mixed)
    zero = jnp.zeros((TILE, TILE), jnp.float32)
    whole = jnp.concatenate(
        [
            jnp.concatenate([inverse[row, col] if col <= row else zero for col in range(count)], 1)
            for row in range(count)
        ],
        0,
    )
    inverse_ref[...] = whole
    basis_ref[...] = exact_dot(two_ref[...], whole, NT)


def projected_body(total_rows, number_ref, cross_ref, inverse_ref, projected_ref):
    cross = ordered_pieces(number_ref, cross_ref) / total_rows
    projected_ref[...] = exact_dot(exact_dot(inverse_ref[...], cross), inverse_ref[...], NT)


def factor_stages(total_rows, count, number, two):
    rows, modes = two.shape
    tile = jax.ShapeDtypeStruct((TILE, TILE), jnp.float32)
    names = lower_tiles(count)
    work = 10**8

    def first(gram):
        body = functools.partial(first_tile_body, count, total_rows)
        return tuple(kernel_call(body, (tile,) * len(names), [SMEM, VMEM], work, gram.size)(number, gram))

    def following(at):
        def stage(state):
            body = functools.partial(next_tile_body, at, count)
            call = kernel_call(body, (tile,) * len(names), [VMEM] * len(names), work, TILE * TILE)
            return tuple(call(*state))

        return stage

    def finish(state):
        outs = (jax.ShapeDtypeStruct((rows, modes), jnp.float32), jax.ShapeDtypeStruct((modes, modes), jnp.float32))
        body = functools.partial(basis_body, count)
        return tuple(kernel_call(body, outs, [VMEM] * (len(names) + 1), work, rows * modes)(*state, two))

    return [first] + [following(at) for at in range(1, count)] + [finish]


def tied(left, right):
    return lax.optimization_barrier((left, right))


def partner_value(value, axis, bit):
    return lax.ppermute(value, axis, [(at, at ^ bit) for at in range(lax.axis_size(axis))])


def axis_bits(axis):
    return [(axis, 1 << at) for at in range(lax.axis_size(axis).bit_length() - 1)]


def device_number(halved):
    number = 0
    for axis, bit in halved:
        number = number * 2 + (lax.axis_index(axis) // bit) % 2
    return number.astype(jnp.int32).reshape(1)


def halving(axis, bit):
    def step(value):
        half = value.shape[0] // 2
        got = partner_value(value[half:], axis, bit)
        return lambda: value[:half] + got

    return step


def doubling(axis, bit):
    def step(value):
        got = partner_value(value, axis, bit)
        return lambda: value + got

    return step


def joining(axis, bit):
    def step(value):
        got = partner_value(value, axis, bit)
        return lambda: jnp.concatenate([value, got], 0)

    return step


def run_beside(value, steps, state, stages):
    stages = list(stages)
    for index, step in enumerate(steps):
        value, state = tied(value, state)
        join = step(value)
        due = -(-len(stages) // (len(steps) - index))
        for _ in range(due):
            state = stages.pop(0)(state)
        value = join()
        if due:
            value, state = tied(value, state)
    return value, state


def local(vectors, hessian, block_cols, live_blocks, halo_lists, bounds):
    row_blocks, stored, size, _ = hessian.shape
    rows, modes = vectors.shape
    splits = lax.axis_size("split")
    region_blocks = row_blocks * splits
    halo_blocks = halo_lists.shape[2]
    whole = halo_blocks == region_blocks and region_blocks <= 256
    total_rows = rows * lax.axis_size(AXES)

    paired = whole and splits == 2
    core = lax.axis_index("split").astype(jnp.int32)
    swapped = lambda value: lax.ppermute(value, "split", [(0, 1), (1, 0)])
    halo_first = [core * row_blocks, (1 - core) * row_blocks] if paired else [0]
    bases = jnp.stack(halo_first).astype(jnp.int32) if paired else jnp.zeros((1,), jnp.int32)

    def sent(operand, region):
        if whole:
            return operand, operand
        width = modes // splits
        start = core * width
        blocks = region[:, :rows].reshape(region_blocks, size, modes)
        share = lambda listed: lax.dynamic_slice_in_dim(blocks[listed], start, width, 2).reshape(-1, width)
        return share(halo_lists[0, 1]), share(halo_lists[0, 0])

    def gathered(value):
        if paired:
            return [value[None], swapped(value)[None]]
        if whole:
            return [lax.all_gather(value, "split", axis=0)]
        return [lax.all_gather(value, "split", axis=1, tiled=True)[None]]

    listed = jnp.pad(halo_lists[0], ((0, LIST_ROWS - 2), (0, modes - halo_blocks)))
    first = vectors.astype(jnp.bfloat16)
    if whole:
        first = jnp.concatenate([first, listed.astype(jnp.bfloat16)], 0)

    def exchange(operand, gather=True):
        if gather or not paired:
            groups = [lax.all_gather(operand, "split", axis=0)]
        else:
            groups = [operand[None], swapped(operand)[None]]
        up, down = sent(operand, groups[0])
        return groups, shifted(up, "region", 1), shifted(down, "region", -1)

    first_near, first_lower, first_upper = exchange(first)
    if whole:
        orders = [first_lower[rows + 1, :halo_blocks], first_upper[rows, :halo_blocks]]
        lists = jnp.stack(orders).astype(jnp.int32)
    else:
        lists = jnp.broadcast_to(jnp.arange(halo_blocks, dtype=jnp.int32), (2, halo_blocks))

    wide = jax.ShapeDtypeStruct((rows, modes), jnp.float32)
    narrow = jax.ShapeDtypeStruct((rows, modes), jnp.bfloat16)
    square = jax.ShapeDtypeStruct((modes, modes), jnp.float32)
    tile_rows = len(lower_tiles(modes // TILE)) * TILE
    work = 2 * rows * size * modes
    square_work = 2 * rows * modes * modes
    traffic = hessian.size * 2 + 3 * rows * modes * 4
    cores, *other_cores = axis_bits("split")
    near, across, *far = axis_bits("region")
    between = other_cores + far
    gram_number, cross_number = device_number([cores, across]), device_number([cores, near])
    halo_slots = (row_blocks, 2 * halo_blocks + 1)

    covering, free = 3 * 10 ** 10, 10 ** 7
    token = jax.ShapeDtypeStruct((GROUP, TILE), jnp.float32)

    held = pl.pallas_call(
        hold_body,
        out_shape=pltpu.VMEM(hessian.shape, hessian.dtype),
        in_specs=[pl.BlockSpec(memory_space=pl.ANY)],
        out_specs=VMEM,
        compiler_params=pltpu.CompilerParams(vmem_limit_bytes=VMEM_LIMIT),
    )(hessian)

    def near_total(body, outs, groups, scalars, terms):
        specs = [SMEM] * 3 + [VMEM] * (1 + len(groups)) + [SMEM] * len(scalars) + [VMEM] * len(terms)
        call = kernel_call(body, outs, specs, free, traffic, (row_blocks, region_blocks + 1))
        near_bases = bases if len(groups) > 1 else jnp.zeros_like(bases)
        return call(block_cols, live_blocks, near_bases, held, *groups, *scalars, *terms)

    def halo_part(body, outs, table, pair, total, scalars=(), extra=()):
        specs = [SMEM] * 2 + [VMEM] * 4 + [SMEM] * len(scalars) + [VMEM] * len(extra)
        call = kernel_call(body, outs, specs, covering, traffic)
        return call(table, bases, held, *pair, total, *scalars, *extra)

    def pairs_of(lower, upper):
        *pairs, last = zip(gathered(lower), gathered(upper))
        return pairs, last

    body_of = functools.partial(near_body, len(first_near), first_terms)
    (total,) = near_total(body_of, (wide,), first_near, (bounds,), (vectors,))
    pairs, last = pairs_of(first_lower, first_upper)
    pairs.append(last)
    body_of = functools.partial(table_body, region_blocks, 0)
    table_shape = jax.ShapeDtypeStruct(halo_slots, jnp.int32)
    specs = [SMEM] * 4 + [VMEM] * 4
    call = kernel_call(body_of, (wide, table_shape), specs, covering, traffic)
    if len(pairs) == 1:
        pairs.append(tuple(jnp.zeros_like(part) for part in last))
    total, table = call(block_cols, live_blocks, lists, bases, held, *pairs[0], total)
    which = len(pairs) - 1 if paired else 0
    body_of = functools.partial(scaled_body, which, 1.0)
    one, one_cast = halo_part(body_of, (wide, narrow), table, pairs[-1], total, (bounds,))

    own, lower, upper = exchange(one_cast)
    body_of = functools.partial(near_body, len(own), second_terms)
    (total,) = near_total(body_of, (wide,), own, (bounds,), (one, vectors))
    pairs, last = pairs_of(lower, upper)
    for which, pair in enumerate(pairs):
        (total,) = halo_part(functools.partial(middle_body, which), (wide,), table, pair, total)
    body_of = functools.partial(scaled_body, len(pairs), 2.0)
    two, two_cast = halo_part(body_of, (wide, narrow), table, last, total, (bounds,))

    own, lower, upper = exchange(two_cast, gather=False)
    packed = jax.ShapeDtypeStruct((tile_rows, TILE), jnp.float32)
    body_of = functools.partial(near_gram_body, len(own))
    total, gram = near_total(body_of, (wide, packed), own, (gram_number,), (two,))
    for step_of in [halving(*cores), halving(*across)]:
        gram = step_of(gram)()
    pairs, last = pairs_of(lower, upper)
    after = jnp.zeros(token.shape, token.dtype)
    for which, pair in enumerate(pairs):
        total, after = halo_part(functools.partial(middle_body, which), (wide, token), table, pair, total)
    gram, after = tied(gram, after)
    body_of = functools.partial(third_body, len(pairs))
    cross = halo_part(body_of, square, table, last, total, (cross_number,), (two, after))
    cross = halving(*cores)(cross)()

    fold = modes // TILE
    cut = gram.shape[0] // fold
    folded = jnp.concatenate([gram[at * cut : (at + 1) * cut] for at in range(fold)], 1)
    flat = lambda value: [value[:, at * TILE : (at + 1) * TILE] for at in range(fold)]
    half = cross.shape[0] // 2
    got = partner_value(jnp.concatenate([folded, cross[half:]], 0), *near)
    both = jnp.concatenate([folded, cross[:half]], 0) + got
    for bit in between:
        both = doubling(*bit)(both)()
    got = partner_value(both, *across)
    gram = joining(*cores)(jnp.concatenate(flat(both[:cut]) + flat(got[:cut]), 0))()
    cross = both[cut:] + got[cut:]
    stages = factor_stages(float(total_rows), modes // TILE, gram_number, two)
    steps = [joining(*near), joining(*cores)]
    cross, (basis, inverse) = run_beside(cross, steps, gram, stages)
    body_of = functools.partial(projected_body, float(total_rows))
    call = kernel_call(body_of, square, [SMEM] + [VMEM] * 2, 2 * square_work, traffic)
    return basis, call(cross_number, cross, inverse)


def solution(mesh):
    placed = (
        P(("region", "split"), None),
        P(("region", "split"), None, None, None),
        P(("region", "split"), None),
        P(("region", "split")),
        P("region", None, None),
        P(),
    )
    return jax.shard_map(
        local,
        mesh=mesh,
        in_specs=placed,
        out_specs=(P(("region", "split"), None), P()),
        check_vma=False,
    )
```

```python
import functools
import jax
import jax.numpy as jnp
from jax import lax
from jax.experimental import pallas as pl
from jax.experimental.pallas import tpu as pltpu
from jax.sharding import PartitionSpec as P

AXES = ("region", "split")
VMEM = pl.BlockSpec(memory_space=pltpu.VMEM)
SMEM = pl.BlockSpec(memory_space=pltpu.SMEM)
EXACT = lax.Precision.HIGHEST
NN = (((1,), (0,)), ((), ()))
NT = (((1,), (1,)), ((), ()))
TN = (((0,), (0,)), ((), ()))
GROUP = 8
PANEL = 32
TILE = 128
VMEM_LIMIT = 6 * 1024 * 1024
LIST_ROWS = 16
PIECES = 4


def shifted(value, axis, steps):
    count = lax.axis_size(axis)
    pairs = [(source, (source + steps) % count) for source in range(count)]
    return lax.ppermute(value, axis, pairs)


def exact_dot(left, right, dims=NN):
    return lax.dot_general(left, right, dims, precision=EXACT, preferred_element_type=jnp.float32)


def kernel_call(body, out_shape, in_specs, flops, bytes_accessed, scratch=()):
    return pl.pallas_call(
        body,
        out_shape=out_shape,
        in_specs=in_specs,
        out_specs=jax.tree.map(lambda out: SMEM if out.dtype == jnp.int32 else VMEM, out_shape),
        scratch_shapes=list(scratch),
        compiler_params=pltpu.CompilerParams(vmem_limit_bytes=VMEM_LIMIT),
        cost_estimate=pl.CostEstimate(flops=flops, bytes_accessed=bytes_accessed // 16, transcendentals=0),
    )


def fill_slots(slots_ref, cols_ref, live_ref):
    rows, stored = cols_ref.shape
    count = slots_ref.shape[1] - 1
    for row in range(rows):
        for index in range(count):
            slots_ref[row, index] = -1
        for at in range(stored):
            slots_ref[row, jnp.where(at < live_ref[row], cols_ref[row, at], count)] = at


def accumulate(slots_ref, hessian_ref, operand_ref, column_of, total):
    rows, _, size, _ = hessian_ref.shape
    shards, shard_rows, _ = operand_ref.shape
    each = shard_rows // size
    for index in range(shards * each):
        start = index % each * size
        block = operand_ref[index // each, start : start + size, :]
        column = column_of(index)
        parts = []
        for row in range(rows):
            slot = slots_ref[row, column]
            live = jnp.where(slot >= 0, 1.0, 0.0).astype(jnp.float32)
            stored = hessian_ref[row, jnp.maximum(slot, 0)]
            parts.append(stored * jnp.broadcast_to(live, (size, size)).astype(jnp.bfloat16))
        term = jnp.dot(jnp.concatenate(parts, 0), block, preferred_element_type=jnp.float32)
        total = term if total is None else total + term
    return total


def hold_body(blocks_ref, out_ref):
    pltpu.sync_copy(blocks_ref, out_ref)


def near_sum(slots_ref, bases_ref, hessian_ref, operands):
    total = None
    for at, operand_ref in enumerate(operands):
        total = accumulate(slots_ref, hessian_ref, operand_ref, lambda index: bases_ref[at] + index, total)
    return total


def table_body(cols_ref, live_ref, bases_ref, hessian_ref, operand_ref, bounds_ref, vectors_ref, out_ref, slots_ref):
    fill_slots(slots_ref, cols_ref, live_ref)
    out_ref[...] = first_terms(near_sum(slots_ref, bases_ref, hessian_ref, [operand_ref]), bounds_ref, vectors_ref)


def near_body(groups, linear, slots_ref, bases_ref, hessian_ref, *refs):
    operands, (*terms, out_ref) = refs[:groups], refs[groups:]
    out_ref[...] = linear(near_sum(slots_ref, bases_ref, hessian_ref, operands), *terms)


def near_gram_body(groups, *refs):
    *operands, number_ref, two_ref, out_ref, gram_ref = refs
    near_body(groups, lambda total: total, *operands, out_ref)
    gram_part(number_ref, two_ref, gram_ref)


def first_terms(total, bounds_ref, vectors_ref):
    centre, _ = interval(bounds_ref)
    return total - centre * vectors_ref[...]


def second_terms(total, bounds_ref, one_ref, vectors_ref):
    centre, half = interval(bounds_ref)
    return total - centre * one_ref[...] - (0.5 * half) * vectors_ref[...]


def halo_sum(which, slots_ref, lists_ref, bases_ref, hessian_ref, lower_ref, upper_ref, names_ref):
    halo = lists_ref.shape[1]
    near = slots_ref.shape[1] - 1 - 2 * halo
    for side in range(2):
        for at in range(halo):
            names_ref[side * halo + lists_ref[side, at]] = near + side * halo + at
    total = None
    for side, operand_ref in enumerate((lower_ref, upper_ref)):
        first = side * halo + bases_ref[which]
        total = accumulate(slots_ref, hessian_ref, operand_ref, lambda index: names_ref[first + index], total)
    return total


def middle_body(which, *refs):
    operands, (total_ref, out_ref, token_ref, names_ref, held_ref, done_ref) = refs[:6], refs[6:]
    copy = pltpu.make_async_copy(total_ref, held_ref, done_ref)
    copy.start()
    added = halo_sum(which, *operands, names_ref)
    copy.wait()
    total = held_ref[...] + added
    out_ref[...] = total
    token_ref[...] = total[:GROUP, :TILE]


def interval(bounds_ref):
    return 0.5 * (bounds_ref[0] + bounds_ref[1]), 0.5 * (bounds_ref[1] - bounds_ref[0])


def scaled_body(factor, which, *refs):
    operands, (total_ref, bounds_ref, out_ref, cast_ref, names_ref) = refs[:6], refs[6:]
    _, half = interval(bounds_ref)
    value = factor * (total_ref[...] + halo_sum(which, *operands, names_ref)) / half
    out_ref[...] = value
    cast_ref[...] = value.astype(jnp.bfloat16)


def place_rows(number_ref, piece, rows):
    return pl.ds(pl.multiple_of((piece ^ number_ref[0]) * rows, GROUP), rows)


def scatter_pieces(number_ref, out_ref, value):
    rows = out_ref.shape[0] // PIECES
    for piece in range(PIECES):
        out_ref[place_rows(number_ref, piece, rows), :] = value[piece * rows : (piece + 1) * rows, :]


def ordered_pieces(number_ref, in_ref):
    rows = in_ref.shape[0] // PIECES
    return jnp.concatenate([in_ref[place_rows(number_ref, piece, rows), :] for piece in range(PIECES)], 0)


def lower_tiles(count):
    return [(row, col) for row in range(count) for col in range(row + 1)]


def gram_part(number_ref, two_ref, out_ref):
    two = two_ref[...]
    cols = [two[:, at * TILE : (at + 1) * TILE] for at in range(two.shape[1] // TILE)]
    tiles = [exact_dot(cols[row], cols[col], TN) for row, col in lower_tiles(len(cols))]
    scatter_pieces(number_ref, out_ref, jnp.concatenate(tiles, 0))


def third_body(which, *refs):
    operands, (total_ref, number_ref, two_ref, _, out_ref, names_ref) = refs[:6], refs[6:]
    image = total_ref[...] + halo_sum(which, *operands, names_ref)
    scatter_pieces(number_ref, out_ref, exact_dot(two_ref[...], image, TN))


def over_lanes(value, lane):
    return jnp.broadcast_to(value[:, lane : lane + 1], value.shape)


def over_rows(value, row):
    return jnp.broadcast_to(value[row : row + 1, :], value.shape)


def eliminate(tile):
    count, panel = tile.shape[0] // GROUP, PANEL // GROUP
    rows = [tile[index * GROUP : (index + 1) * GROUP, :] for index in range(count)]
    sub = lax.broadcasted_iota(jnp.int32, rows[0].shape, 0)
    lane = lax.broadcasted_iota(jnp.int32, rows[0].shape, 1)
    for begin in range(0, count, panel):
        end = begin + panel
        reduced = []
        for step in range(begin, end):
            start = step * GROUP
            pivot_cols = [over_lanes(rows[step], start + col) for col in range(GROUP)]
            factors = {
                below: [over_lanes(rows[below], start + col) for col in range(GROUP)] for below in range(step + 1, end)
            }
            inside = (lane >= start) & (lane < start + GROUP)
            forward = jnp.where(inside, jnp.where(lane - start == sub, 1.0, 0.0), rows[step])
            solved = forward
            for pivot in range(GROUP):
                here = sub == pivot
                value = over_rows(pivot_cols[pivot], pivot)
                inverse = 1.0 / value
                ratio = pivot_cols[pivot] * inverse
                row = over_rows(forward, pivot)
                below_row = jnp.where(sub > pivot, forward - ratio * row, forward)
                forward = jnp.where(here, row * lax.rsqrt(value), below_row)
                solved = jnp.where(here, row * inverse, solved - ratio * row)
                for col in range(pivot + 1, GROUP):
                    top = over_rows(pivot_cols[col], pivot)
                    pivot_cols[col] = jnp.where(here, top * inverse, pivot_cols[col] - ratio * top)
            own_part = (lane < start + GROUP) | (lane >= end * GROUP)
            reduced.append((forward, jnp.where(own_part, forward, 0.0)))
            rows[step] = jnp.where(lane < start + GROUP, forward, 0.0)
            solved_rows = [over_rows(solved, pivot) for pivot in range(GROUP)]
            for below in range(step + 1, end):
                terms = [factors[below][col] * solved_rows[col] for col in range(GROUP)]
                while len(terms) > 1:
                    terms = [terms[at] + terms[at + 1] for at in range(0, len(terms), 2)]
                rows[below] = jnp.where(inside, 0.0, rows[below]) - terms[0]
        if end < count:
            factor_rows, solved_rows = [jnp.concatenate(parts, 0) for parts in zip(*reduced)]
            share = exact_dot(factor_rows, solved_rows, TN)
            inside = (lane >= begin * GROUP) & (lane < end * GROUP)
            for below in range(end, count):
                rows[below] = jnp.where(inside, 0.0, rows[below]) - share[below * GROUP : (below + 1) * GROUP, :]
    return jnp.concatenate(rows, 0)


def first_tile_body(count, total_rows, number_ref, gram_ref, *tile_refs):
    packed = ordered_pieces(number_ref, gram_ref) / total_rows
    tiles = [packed[at * TILE : (at + 1) * TILE, :] for at in range(len(tile_refs))]
    finish_tile(0, count, dict(zip(lower_tiles(count), tiles)), tile_refs)


def next_tile_body(at, count, *refs):
    names = lower_tiles(count)
    tiles = {name: ref[...] for name, ref in zip(names, refs)}
    finish_tile(at, count, tiles, refs[len(names) :])


def finish_tile(at, count, tiles, out_refs):
    tiles = dict(tiles)
    tiles[at, at] = eliminate(tiles[at, at])
    for row in range(at + 1, count):
        tiles[row, at] = exact_dot(tiles[row, at], tiles[at, at], NT)
    for row in range(at + 1, count):
        for col in range(at + 1, row + 1):
            tiles[row, col] = tiles[row, col] - exact_dot(tiles[row, at], tiles[col, at], NT)
    for name, out_ref in zip(lower_tiles(count), out_refs):
        out_ref[...] = tiles[name]


def basis_body(count, *refs):
    *tile_refs, two_ref, basis_ref, inverse_ref = refs
    tiles = {name: ref[...] for name, ref in zip(lower_tiles(count), tile_refs)}
    inverse = {}
    for row in range(count):
        inverse[row, row] = tiles[row, row]
        for col in range(row):
            mixed = exact_dot(tiles[row, col], inverse[col, col])
            for mid in range(col + 1, row):
                mixed = mixed + exact_dot(tiles[row, mid], inverse[mid, col])
            inverse[row, col] = -exact_dot(tiles[row, row], mixed)
    zero = jnp.zeros((TILE, TILE), jnp.float32)
    whole = jnp.concatenate(
        [
            jnp.concatenate([inverse[row, col] if col <= row else zero for col in range(count)], 1)
            for row in range(count)
        ],
        0,
    )
    inverse_ref[...] = whole
    basis_ref[...] = exact_dot(two_ref[...], whole, NT)


def projected_body(total_rows, number_ref, cross_ref, inverse_ref, projected_ref):
    cross = ordered_pieces(number_ref, cross_ref) / total_rows
    projected_ref[...] = exact_dot(exact_dot(inverse_ref[...], cross), inverse_ref[...], NT)


def factor_stages(total_rows, count, number, two):
    rows, modes = two.shape
    tile = jax.ShapeDtypeStruct((TILE, TILE), jnp.float32)
    names = lower_tiles(count)
    work = 10**8

    def first(gram):
        body = functools.partial(first_tile_body, count, total_rows)
        return tuple(kernel_call(body, (tile,) * len(names), [SMEM, VMEM], work, gram.size)(number, gram))

    def following(at):
        def stage(state):
            body = functools.partial(next_tile_body, at, count)
            call = kernel_call(body, (tile,) * len(names), [VMEM] * len(names), work, TILE * TILE)
            return tuple(call(*state))

        return stage

    def finish(state):
        outs = (jax.ShapeDtypeStruct((rows, modes), jnp.float32), jax.ShapeDtypeStruct((modes, modes), jnp.float32))
        body = functools.partial(basis_body, count)
        return tuple(kernel_call(body, outs, [VMEM] * (len(names) + 1), work, rows * modes)(*state, two))

    return [first] + [following(at) for at in range(1, count)] + [finish]


def tied(left, right):
    return lax.optimization_barrier((left, right))


def partner_value(value, axis, bit):
    return lax.ppermute(value, axis, [(at, at ^ bit) for at in range(lax.axis_size(axis))])


def axis_bits(axis):
    return [(axis, 1 << at) for at in range(lax.axis_size(axis).bit_length() - 1)]


def device_number(halved):
    number = 0
    for axis, bit in halved:
        number = number * 2 + (lax.axis_index(axis) // bit) % 2
    return number.astype(jnp.int32).reshape(1)


def halving(axis, bit):
    def step(value):
        half = value.shape[0] // 2
        got = partner_value(value[half:], axis, bit)
        return lambda: value[:half] + got

    return step


def doubling(axis, bit):
    def step(value):
        got = partner_value(value, axis, bit)
        return lambda: value + got

    return step


def joining(axis, bit):
    def step(value):
        got = partner_value(value, axis, bit)
        return lambda: jnp.concatenate([value, got], 0)

    return step


def run_beside(value, steps, state, stages):
    stages = list(stages)
    for index, step in enumerate(steps):
        value, state = tied(value, state)
        join = step(value)
        due = -(-len(stages) // (len(steps) - index))
        for _ in range(due):
            state = stages.pop(0)(state)
        value = join()
        if due:
            value, state = tied(value, state)
    return value, state


def local(vectors, hessian, block_cols, live_blocks, halo_lists, bounds):
    row_blocks, stored, size, _ = hessian.shape
    rows, modes = vectors.shape
    splits = lax.axis_size("split")
    region_blocks = row_blocks * splits
    halo_blocks = halo_lists.shape[2]
    whole = halo_blocks == region_blocks and region_blocks <= 256
    total_rows = rows * lax.axis_size(AXES)

    paired = whole and splits == 2
    core = lax.axis_index("split").astype(jnp.int32)
    swapped = lambda value: lax.ppermute(value, "split", [(0, 1), (1, 0)])
    halo_first = [core * row_blocks, (1 - core) * row_blocks] if paired else [0]
    bases = jnp.stack(halo_first).astype(jnp.int32) if paired else jnp.zeros((1,), jnp.int32)

    def sent(operand, region):
        if whole:
            return operand, operand
        width = modes // splits
        start = core * width
        blocks = region[:, :rows].reshape(region_blocks, size, modes)
        share = lambda listed: lax.dynamic_slice_in_dim(blocks[listed], start, width, 2).reshape(-1, width)
        return share(halo_lists[0, 1]), share(halo_lists[0, 0])

    def gathered(value):
        if paired:
            return [value[None], swapped(value)[None]]
        if whole:
            return [lax.all_gather(value, "split", axis=0)]
        return [lax.all_gather(value, "split", axis=1, tiled=True)[None]]

    listed = jnp.pad(halo_lists[0], ((0, LIST_ROWS - 2), (0, modes - halo_blocks)))
    first = vectors.astype(jnp.bfloat16)
    if whole:
        first = jnp.concatenate([first, listed.astype(jnp.bfloat16)], 0)

    def exchange(operand, gather=True):
        if gather or not paired:
            groups = [lax.all_gather(operand, "split", axis=0)]
        else:
            groups = [operand[None], swapped(operand)[None]]
        up, down = sent(operand, groups[0])
        return groups, shifted(up, "region", 1), shifted(down, "region", -1)

    first_near, first_lower, first_upper = exchange(first)
    if whole:
        orders = [first_lower[rows + 1, :halo_blocks], first_upper[rows, :halo_blocks]]
        lists = jnp.stack(orders).astype(jnp.int32)
    else:
        lists = jnp.broadcast_to(jnp.arange(halo_blocks, dtype=jnp.int32), (2, halo_blocks))

    wide = jax.ShapeDtypeStruct((rows, modes), jnp.float32)
    narrow = jax.ShapeDtypeStruct((rows, modes), jnp.bfloat16)
    square = jax.ShapeDtypeStruct((modes, modes), jnp.float32)
    tile_rows = len(lower_tiles(modes // TILE)) * TILE
    work = 2 * rows * size * modes
    square_work = 2 * rows * modes * modes
    traffic = hessian.size * 2 + 3 * rows * modes * 4
    cores, *other_cores = axis_bits("split")
    near, across, *far = axis_bits("region")
    between = other_cores + far
    gram_number, cross_number = device_number([cores, across]), device_number([cores, near])
    names = [pltpu.SMEM((2 * halo_blocks,), jnp.int32)]
    table_shape = jax.ShapeDtypeStruct((row_blocks, region_blocks + 2 * halo_blocks + 1), jnp.int32)

    covering, free = 3 * 10 ** 10, 10 ** 7
    token = jax.ShapeDtypeStruct((GROUP, TILE), jnp.float32)

    held = pl.pallas_call(
        hold_body,
        out_shape=pltpu.VMEM(hessian.shape, hessian.dtype),
        in_specs=[pl.BlockSpec(memory_space=pl.ANY)],
        out_specs=VMEM,
        compiler_params=pltpu.CompilerParams(vmem_limit_bytes=VMEM_LIMIT),
    )(hessian)

    def near_total(body, outs, groups, scalars, terms):
        specs = [SMEM] * 2 + [VMEM] * (1 + len(groups)) + [SMEM] * len(scalars) + [VMEM] * len(terms)
        near_bases = bases if len(groups) > 1 else jnp.zeros_like(bases)
        return kernel_call(body, outs, specs, free, traffic)(table, near_bases, held, *groups, *scalars, *terms)

    def last_part(body, outs, which, pair, total, scalars, extra=()):
        specs = [SMEM] * 3 + [VMEM] * 4 + [SMEM] * len(scalars) + [VMEM] * len(extra)
        call = kernel_call(functools.partial(body, which), outs, specs, covering, traffic, names)
        return call(table, lists, bases, held, *pair, total, *scalars, *extra)

    def before_last(lower, upper, total):
        *pairs, last = zip(gathered(lower), gathered(upper))
        after = jnp.zeros(token.shape, token.dtype)
        for which, pair in enumerate(pairs):
            specs = [SMEM] * 3 + [VMEM] * 3 + [pl.BlockSpec(memory_space=pl.ANY)]
            scratch = names + [pltpu.VMEM((rows, modes), jnp.float32), pltpu.SemaphoreType.DMA(())]
            body_of = functools.partial(middle_body, which)
            call = kernel_call(body_of, (wide, token), specs, covering, traffic, scratch)
            total, after = call(table, lists, bases, held, *pair, total)
        return total, after, len(pairs), last

    specs = [SMEM] * 3 + [VMEM] * 2 + [SMEM, VMEM]
    call = kernel_call(table_body, (wide, table_shape), specs, free, traffic)
    total, table = call(block_cols, live_blocks, jnp.zeros_like(bases), held, *first_near, bounds, vectors)
    total, _, which, last = before_last(first_lower, first_upper, total)
    one, one_cast = last_part(functools.partial(scaled_body, 1.0), (wide, narrow), which, last, total, (bounds,))

    own, lower, upper = exchange(one_cast)
    body_of = functools.partial(near_body, len(own), second_terms)
    (total,) = near_total(body_of, (wide,), own, (bounds,), (one, vectors))
    total, _, which, last = before_last(lower, upper, total)
    two, two_cast = last_part(functools.partial(scaled_body, 2.0), (wide, narrow), which, last, total, (bounds,))

    own, lower, upper = exchange(two_cast, gather=False)
    packed = jax.ShapeDtypeStruct((tile_rows, TILE), jnp.float32)
    body_of = functools.partial(near_gram_body, len(own))
    total, gram = near_total(body_of, (wide, packed), own, (gram_number,), (two,))
    for step_of in [halving(*cores), halving(*across)]:
        gram = step_of(gram)()
    total, after, which, last = before_last(lower, upper, total)
    gram, after = tied(gram, after)
    cross = last_part(third_body, square, which, last, total, (cross_number,), (two, after))
    cross = halving(*cores)(cross)()

    fold = modes // TILE
    cut = gram.shape[0] // fold
    folded = jnp.concatenate([gram[at * cut : (at + 1) * cut] for at in range(fold)], 1)
    flat = lambda value: [value[:, at * TILE : (at + 1) * TILE] for at in range(fold)]
    half = cross.shape[0] // 2
    got = partner_value(jnp.concatenate([folded, cross[half:]], 0), *near)
    both = jnp.concatenate([folded, cross[:half]], 0) + got
    for bit in between:
        both = doubling(*bit)(both)()
    got = partner_value(both, *across)
    gram = joining(*cores)(jnp.concatenate(flat(both[:cut]) + flat(got[:cut]), 0))()
    cross = both[cut:] + got[cut:]
    stages = factor_stages(float(total_rows), modes // TILE, gram_number, two)
    steps = [joining(*near), joining(*cores)]
    cross, (basis, inverse) = run_beside(cross, steps, gram, stages)
    body_of = functools.partial(projected_body, float(total_rows))
    call = kernel_call(body_of, square, [SMEM] + [VMEM] * 2, 2 * square_work, traffic)
    return basis, call(cross_number, cross, inverse)


def solution(mesh):
    placed = (
        P(("region", "split"), None),
        P(("region", "split"), None, None, None),
        P(("region", "split"), None),
        P(("region", "split")),
        P("region", None, None),
        P(),
    )
    return jax.shard_map(
        local,
        mesh=mesh,
        in_specs=placed,
        out_specs=(P(("region", "split"), None), P()),
        check_vma=False,
    )
```

```python
import functools
import jax
import jax.numpy as jnp
from jax import lax
from jax.experimental import pallas as pl
from jax.experimental.pallas import tpu as pltpu
from jax.sharding import PartitionSpec as P

AXES = ("region", "split")
VMEM = pl.BlockSpec(memory_space=pltpu.VMEM)
SMEM = pl.BlockSpec(memory_space=pltpu.SMEM)
EXACT = lax.Precision.HIGHEST
NN = (((1,), (0,)), ((), ()))
NT = (((1,), (1,)), ((), ()))
TN = (((0,), (0,)), ((), ()))
GROUP = 8
PANEL = 32
TILE = 128
VMEM_LIMIT = 6 * 1024 * 1024
LIST_ROWS = 16
PIECES = 4


def shifted(value, axis, steps):
    count = lax.axis_size(axis)
    pairs = [(source, (source + steps) % count) for source in range(count)]
    return lax.ppermute(value, axis, pairs)


def exact_dot(left, right, dims=NN):
    return lax.dot_general(left, right, dims, precision=EXACT, preferred_element_type=jnp.float32)


def kernel_call(body, out_shape, in_specs, flops, bytes_accessed, scratch=()):
    return pl.pallas_call(
        body,
        out_shape=out_shape,
        in_specs=in_specs,
        out_specs=jax.tree.map(lambda out: SMEM if out.dtype == jnp.int32 else VMEM, out_shape),
        scratch_shapes=list(scratch),
        compiler_params=pltpu.CompilerParams(vmem_limit_bytes=VMEM_LIMIT),
        cost_estimate=pl.CostEstimate(flops=flops, bytes_accessed=bytes_accessed // 16, transcendentals=0),
    )


def fill_slots(slots_ref, cols_ref, live_ref):
    rows, stored = cols_ref.shape
    count = slots_ref.shape[1] - 1
    for row in range(rows):
        for index in range(count):
            slots_ref[row, index] = -1
        for at in range(stored):
            slots_ref[row, jnp.where(at < live_ref[row], cols_ref[row, at], count)] = at


def accumulate(slots_ref, hessian_ref, operand_ref, column_of, total):
    rows, _, size, _ = hessian_ref.shape
    shards, shard_rows, _ = operand_ref.shape
    each = shard_rows // size
    for index in range(shards * each):
        start = index % each * size
        block = operand_ref[index // each, start : start + size, :]
        column = column_of(index)
        parts = []
        for row in range(rows):
            slot = slots_ref[row, column]
            live = jnp.where(slot >= 0, 1.0, 0.0).astype(jnp.float32)
            stored = hessian_ref[row, jnp.maximum(slot, 0)]
            parts.append(stored * jnp.broadcast_to(live, (size, size)).astype(jnp.bfloat16))
        term = jnp.dot(jnp.concatenate(parts, 0), block, preferred_element_type=jnp.float32)
        total = term if total is None else total + term
    return total


def hold_body(blocks_ref, out_ref):
    pltpu.sync_copy(blocks_ref, out_ref)


def near_sum(slots_ref, bases_ref, hessian_ref, operands):
    total = None
    for at, operand_ref in enumerate(operands):
        total = accumulate(slots_ref, hessian_ref, operand_ref, lambda index: bases_ref[at] + index, total)
    return total


def table_body(cols_ref, live_ref, bases_ref, hessian_ref, operand_ref, bounds_ref, vectors_ref, out_ref, slots_ref):
    fill_slots(slots_ref, cols_ref, live_ref)
    out_ref[...] = first_terms(near_sum(slots_ref, bases_ref, hessian_ref, [operand_ref]), bounds_ref, vectors_ref)


def near_body(groups, linear, slots_ref, bases_ref, hessian_ref, *refs):
    operands, (*terms, out_ref) = refs[:groups], refs[groups:]
    out_ref[...] = linear(near_sum(slots_ref, bases_ref, hessian_ref, operands), *terms)


def near_gram_body(groups, *refs):
    *operands, number_ref, two_ref, out_ref, gram_ref = refs
    near_body(groups, lambda total: total, *operands, out_ref)
    gram_part(number_ref, two_ref, gram_ref)


def first_terms(total, bounds_ref, vectors_ref):
    centre, _ = interval(bounds_ref)
    return total - centre * vectors_ref[...]


def second_terms(total, bounds_ref, one_ref, vectors_ref):
    centre, half = interval(bounds_ref)
    return total - centre * one_ref[...] - (0.5 * half) * vectors_ref[...]


def halo_sum(which, slots_ref, lists_ref, bases_ref, hessian_ref, lower_ref, upper_ref, names_ref):
    halo = lists_ref.shape[1]
    near = slots_ref.shape[1] - 1 - 2 * halo
    for side in range(2):
        for at in range(halo):
            names_ref[side * halo + lists_ref[side, at]] = near + side * halo + at
    total = None
    for side, operand_ref in enumerate((lower_ref, upper_ref)):
        first = side * halo + bases_ref[which]
        total = accumulate(slots_ref, hessian_ref, operand_ref, lambda index: names_ref[first + index], total)
    return total


def middle_body(which, *refs):
    operands, (total_ref, out_ref, token_ref, names_ref) = refs[:6], refs[6:]
    total = total_ref[...] + halo_sum(which, *operands, names_ref)
    out_ref[...] = total
    token_ref[...] = total[:GROUP, :TILE]


def interval(bounds_ref):
    return 0.5 * (bounds_ref[0] + bounds_ref[1]), 0.5 * (bounds_ref[1] - bounds_ref[0])


def scaled_body(factor, which, *refs):
    operands, (total_ref, bounds_ref, out_ref, cast_ref, names_ref) = refs[:6], refs[6:]
    _, half = interval(bounds_ref)
    value = factor * (total_ref[...] + halo_sum(which, *operands, names_ref)) / half
    out_ref[...] = value
    cast_ref[...] = value.astype(jnp.bfloat16)


def place_rows(number_ref, piece, rows):
    return pl.ds(pl.multiple_of((piece ^ number_ref[0]) * rows, GROUP), rows)


def scatter_pieces(number_ref, out_ref, value):
    rows = out_ref.shape[0] // PIECES
    for piece in range(PIECES):
        out_ref[place_rows(number_ref, piece, rows), :] = value[piece * rows : (piece + 1) * rows, :]


def ordered_pieces(number_ref, in_ref):
    rows = in_ref.shape[0] // PIECES
    return jnp.concatenate([in_ref[place_rows(number_ref, piece, rows), :] for piece in range(PIECES)], 0)


def lower_tiles(count):
    return [(row, col) for row in range(count) for col in range(row + 1)]


def gram_part(number_ref, two_ref, out_ref):
    two = two_ref[...]
    cols = [two[:, at * TILE : (at + 1) * TILE] for at in range(two.shape[1] // TILE)]
    tiles = [exact_dot(cols[row], cols[col], TN) for row, col in lower_tiles(len(cols))]
    scatter_pieces(number_ref, out_ref, jnp.concatenate(tiles, 0))


def third_body(which, *refs):
    operands, (total_ref, number_ref, two_ref, _, out_ref, names_ref) = refs[:6], refs[6:]
    image = total_ref[...] + halo_sum(which, *operands, names_ref)
    scatter_pieces(number_ref, out_ref, exact_dot(two_ref[...], image, TN))


def over_lanes(value, lane):
    return jnp.broadcast_to(value[:, lane : lane + 1], value.shape)


def over_rows(value, row):
    return jnp.broadcast_to(value[row : row + 1, :], value.shape)


def eliminate(tile):
    count, panel = tile.shape[0] // GROUP, PANEL // GROUP
    rows = [tile[index * GROUP : (index + 1) * GROUP, :] for index in range(count)]
    sub = lax.broadcasted_iota(jnp.int32, rows[0].shape, 0)
    lane = lax.broadcasted_iota(jnp.int32, rows[0].shape, 1)
    for begin in range(0, count, panel):
        end = begin + panel
        reduced = []
        for step in range(begin, end):
            start = step * GROUP
            pivot_cols = [over_lanes(rows[step], start + col) for col in range(GROUP)]
            factors = {
                below: [over_lanes(rows[below], start + col) for col in range(GROUP)] for below in range(step + 1, end)
            }
            inside = (lane >= start) & (lane < start + GROUP)
            forward = jnp.where(inside, jnp.where(lane - start == sub, 1.0, 0.0), rows[step])
            solved = forward
            for pivot in range(GROUP):
                here = sub == pivot
                value = over_rows(pivot_cols[pivot], pivot)
                inverse = 1.0 / value
                ratio = pivot_cols[pivot] * inverse
                row = over_rows(forward, pivot)
                below_row = jnp.where(sub > pivot, forward - ratio * row, forward)
                forward = jnp.where(here, row * lax.rsqrt(value), below_row)
                solved = jnp.where(here, row * inverse, solved - ratio * row)
                for col in range(pivot + 1, GROUP):
                    top = over_rows(pivot_cols[col], pivot)
                    pivot_cols[col] = jnp.where(here, top * inverse, pivot_cols[col] - ratio * top)
            own_part = (lane < start + GROUP) | (lane >= end * GROUP)
            reduced.append((forward, jnp.where(own_part, forward, 0.0)))
            rows[step] = jnp.where(lane < start + GROUP, forward, 0.0)
            solved_rows = [over_rows(solved, pivot) for pivot in range(GROUP)]
            for below in range(step + 1, end):
                terms = [factors[below][col] * solved_rows[col] for col in range(GROUP)]
                while len(terms) > 1:
                    terms = [terms[at] + terms[at + 1] for at in range(0, len(terms), 2)]
                rows[below] = jnp.where(inside, 0.0, rows[below]) - terms[0]
        if end < count:
            factor_rows, solved_rows = [jnp.concatenate(parts, 0) for parts in zip(*reduced)]
            share = exact_dot(factor_rows, solved_rows, TN)
            inside = (lane >= begin * GROUP) & (lane < end * GROUP)
            for below in range(end, count):
                rows[below] = jnp.where(inside, 0.0, rows[below]) - share[below * GROUP : (below + 1) * GROUP, :]
    return jnp.concatenate(rows, 0)


def first_tile_body(count, total_rows, number_ref, gram_ref, *tile_refs):
    packed = ordered_pieces(number_ref, gram_ref) / total_rows
    tiles = [packed[at * TILE : (at + 1) * TILE, :] for at in range(len(tile_refs))]
    finish_tile(0, count, dict(zip(lower_tiles(count), tiles)), tile_refs)


def next_tile_body(at, count, *refs):
    names = lower_tiles(count)
    tiles = {name: ref[...] for name, ref in zip(names, refs)}
    finish_tile(at, count, tiles, refs[len(names) :])


def finish_tile(at, count, tiles, out_refs):
    tiles = dict(tiles)
    tiles[at, at] = eliminate(tiles[at, at])
    for row in range(at + 1, count):
        tiles[row, at] = exact_dot(tiles[row, at], tiles[at, at], NT)
    for row in range(at + 1, count):
        for col in range(at + 1, row + 1):
            tiles[row, col] = tiles[row, col] - exact_dot(tiles[row, at], tiles[col, at], NT)
    for name, out_ref in zip(lower_tiles(count), out_refs):
        out_ref[...] = tiles[name]


def basis_body(count, *refs):
    *tile_refs, two_ref, basis_ref, inverse_ref = refs
    tiles = {name: ref[...] for name, ref in zip(lower_tiles(count), tile_refs)}
    inverse = {}
    for row in range(count):
        inverse[row, row] = tiles[row, row]
        for col in range(row):
            mixed = exact_dot(tiles[row, col], inverse[col, col])
            for mid in range(col + 1, row):
                mixed = mixed + exact_dot(tiles[row, mid], inverse[mid, col])
            inverse[row, col] = -exact_dot(tiles[row, row], mixed)
    zero = jnp.zeros((TILE, TILE), jnp.float32)
    whole = jnp.concatenate(
        [
            jnp.concatenate([inverse[row, col] if col <= row else zero for col in range(count)], 1)
            for row in range(count)
        ],
        0,
    )
    inverse_ref[...] = whole
    basis_ref[...] = exact_dot(two_ref[...], whole, NT)


def projected_body(total_rows, number_ref, cross_ref, inverse_ref, projected_ref):
    cross = ordered_pieces(number_ref, cross_ref) / total_rows
    projected_ref[...] = exact_dot(exact_dot(inverse_ref[...], cross), inverse_ref[...], NT)


def factor_stages(total_rows, count, number, two):
    rows, modes = two.shape
    tile = jax.ShapeDtypeStruct((TILE, TILE), jnp.float32)
    names = lower_tiles(count)
    work = 10**8

    def first(gram):
        body = functools.partial(first_tile_body, count, total_rows)
        return tuple(kernel_call(body, (tile,) * len(names), [SMEM, VMEM], work, gram.size)(number, gram))

    def following(at):
        def stage(state):
            body = functools.partial(next_tile_body, at, count)
            call = kernel_call(body, (tile,) * len(names), [VMEM] * len(names), work, TILE * TILE)
            return tuple(call(*state))

        return stage

    def finish(state):
        outs = (jax.ShapeDtypeStruct((rows, modes), jnp.float32), jax.ShapeDtypeStruct((modes, modes), jnp.float32))
        body = functools.partial(basis_body, count)
        return tuple(kernel_call(body, outs, [VMEM] * (len(names) + 1), work, rows * modes)(*state, two))

    return [first] + [following(at) for at in range(1, count)] + [finish]


def tied(left, right):
    return lax.optimization_barrier((left, right))


def partner_value(value, axis, bit):
    return lax.ppermute(value, axis, [(at, at ^ bit) for at in range(lax.axis_size(axis))])


def axis_bits(axis):
    return [(axis, 1 << at) for at in range(lax.axis_size(axis).bit_length() - 1)]


def device_number(halved):
    number = 0
    for axis, bit in halved:
        number = number * 2 + (lax.axis_index(axis) // bit) % 2
    return number.astype(jnp.int32).reshape(1)


def halving(axis, bit):
    def step(value):
        half = value.shape[0] // 2
        got = partner_value(value[half:], axis, bit)
        return lambda: value[:half] + got

    return step


def doubling(axis, bit):
    def step(value):
        got = partner_value(value, axis, bit)
        return lambda: value + got

    return step


def joining(axis, bit):
    def step(value):
        got = partner_value(value, axis, bit)
        return lambda: jnp.concatenate([value, got], 0)

    return step


def run_beside(value, steps, state, stages):
    stages = list(stages)
    for index, step in enumerate(steps):
        value, state = tied(value, state)
        join = step(value)
        due = -(-len(stages) // (len(steps) - index))
        for _ in range(due):
            state = stages.pop(0)(state)
        value = join()
        if due:
            value, state = tied(value, state)
    return value, state


def local(vectors, hessian, block_cols, live_blocks, halo_lists, bounds):
    row_blocks, stored, size, _ = hessian.shape
    rows, modes = vectors.shape
    splits = lax.axis_size("split")
    region_blocks = row_blocks * splits
    halo_blocks = halo_lists.shape[2]
    whole = halo_blocks == region_blocks and region_blocks <= 256
    total_rows = rows * lax.axis_size(AXES)

    paired = whole and splits == 2
    core = lax.axis_index("split").astype(jnp.int32)
    swapped = lambda value: lax.ppermute(value, "split", [(0, 1), (1, 0)])
    halo_first = [core * row_blocks, (1 - core) * row_blocks] if paired else [0]
    bases = jnp.stack(halo_first).astype(jnp.int32) if paired else jnp.zeros((1,), jnp.int32)

    def sent(operand, region):
        if whole:
            return operand, operand
        width = modes // splits
        start = core * width
        blocks = region[:, :rows].reshape(region_blocks, size, modes)
        share = lambda listed: lax.dynamic_slice_in_dim(blocks[listed], start, width, 2).reshape(-1, width)
        return share(halo_lists[0, 1]), share(halo_lists[0, 0])

    def gathered(value):
        if paired:
            return [value[None], swapped(value)[None]]
        if whole:
            return [lax.all_gather(value, "split", axis=0)]
        return [lax.all_gather(value, "split", axis=1, tiled=True)[None]]

    listed = jnp.pad(halo_lists[0], ((0, LIST_ROWS - 2), (0, modes - halo_blocks)))
    first = vectors.astype(jnp.bfloat16)
    if whole:
        first = jnp.concatenate([first, listed.astype(jnp.bfloat16)], 0)

    def exchange(operand, gather=True):
        if gather or not paired:
            groups = [lax.all_gather(operand, "split", axis=0)]
        else:
            groups = [operand[None], swapped(operand)[None]]
        up, down = sent(operand, groups[0])
        return groups, shifted(up, "region", 1), shifted(down, "region", -1)

    first_near, first_lower, first_upper = exchange(first)
    if whole:
        orders = [first_lower[rows + 1, :halo_blocks], first_upper[rows, :halo_blocks]]
        lists = jnp.stack(orders).astype(jnp.int32)
    else:
        lists = jnp.broadcast_to(jnp.arange(halo_blocks, dtype=jnp.int32), (2, halo_blocks))

    wide = jax.ShapeDtypeStruct((rows, modes), jnp.float32)
    narrow = jax.ShapeDtypeStruct((rows, modes), jnp.bfloat16)
    square = jax.ShapeDtypeStruct((modes, modes), jnp.float32)
    tile_rows = len(lower_tiles(modes // TILE)) * TILE
    work = 2 * rows * size * modes
    square_work = 2 * rows * modes * modes
    traffic = hessian.size * 2 + 3 * rows * modes * 4
    cores, *other_cores = axis_bits("split")
    near, across, *far = axis_bits("region")
    between = other_cores + far
    gram_number, cross_number = device_number([cores, across]), device_number([cores, near])
    names = [pltpu.SMEM((2 * halo_blocks,), jnp.int32)]
    table_shape = jax.ShapeDtypeStruct((row_blocks, region_blocks + 2 * halo_blocks + 1), jnp.int32)

    covering, free = 3 * 10 ** 10, 10 ** 7
    token = jax.ShapeDtypeStruct((GROUP, TILE), jnp.float32)

    held = pl.pallas_call(
        hold_body,
        out_shape=pltpu.VMEM(hessian.shape, hessian.dtype),
        in_specs=[pl.BlockSpec(memory_space=pl.ANY)],
        out_specs=VMEM,
        compiler_params=pltpu.CompilerParams(vmem_limit_bytes=VMEM_LIMIT),
    )(hessian)

    def near_total(body, outs, groups, scalars, terms):
        specs = [SMEM] * 2 + [VMEM] * (1 + len(groups)) + [SMEM] * len(scalars) + [VMEM] * len(terms)
        near_bases = bases if len(groups) > 1 else jnp.zeros_like(bases)
        return kernel_call(body, outs, specs, free, traffic)(table, near_bases, held, *groups, *scalars, *terms)

    def last_part(body, outs, which, pair, total, scalars, extra=()):
        specs = [SMEM] * 3 + [VMEM] * 4 + [SMEM] * len(scalars) + [VMEM] * len(extra)
        call = kernel_call(functools.partial(body, which), outs, specs, covering, traffic, names)
        return call(table, lists, bases, held, *pair, total, *scalars, *extra)

    def before_last(lower, upper, total):
        *pairs, last = zip(gathered(lower), gathered(upper))
        after = jnp.zeros(token.shape, token.dtype)
        for which, pair in enumerate(pairs):
            specs = [SMEM] * 3 + [VMEM] * 4
            body_of = functools.partial(middle_body, which)
            call = kernel_call(body_of, (wide, token), specs, covering, traffic, names)
            total, after = call(table, lists, bases, held, *pair, total)
        return total, after, len(pairs), last

    specs = [SMEM] * 3 + [VMEM] * 2 + [SMEM, VMEM]
    call = kernel_call(table_body, (wide, table_shape), specs, free, traffic)
    total, table = call(block_cols, live_blocks, jnp.zeros_like(bases), held, *first_near, bounds, vectors)
    total, _, which, last = before_last(first_lower, first_upper, total)
    one, one_cast = last_part(functools.partial(scaled_body, 1.0), (wide, narrow), which, last, total, (bounds,))

    own, lower, upper = exchange(one_cast)
    body_of = functools.partial(near_body, len(own), second_terms)
    (total,) = near_total(body_of, (wide,), own, (bounds,), (one, vectors))
    total, _, which, last = before_last(lower, upper, total)
    two, two_cast = last_part(functools.partial(scaled_body, 2.0), (wide, narrow), which, last, total, (bounds,))

    own, lower, upper = exchange(two_cast, gather=False)
    packed = jax.ShapeDtypeStruct((tile_rows, TILE), jnp.float32)
    body_of = functools.partial(near_gram_body, len(own))
    total, gram = near_total(body_of, (wide, packed), own, (gram_number,), (two,))
    for step_of in [halving(*cores), halving(*across)]:
        gram = step_of(gram)()
    total, after, which, last = before_last(lower, upper, total)
    gram, after = tied(gram, after)
    cross = last_part(third_body, square, which, last, total, (cross_number,), (two, after))
    cross = halving(*cores)(cross)()

    fold = modes // TILE
    cut = gram.shape[0] // fold
    folded = jnp.concatenate([gram[at * cut : (at + 1) * cut] for at in range(fold)], 1)
    flat = lambda value: [value[:, at * TILE : (at + 1) * TILE] for at in range(fold)]
    half = cross.shape[0] // 2
    got = partner_value(jnp.concatenate([folded, cross[half:]], 0), *near)
    both = jnp.concatenate([folded, cross[:half]], 0) + got
    for bit in between:
        both = doubling(*bit)(both)()
    got = partner_value(both, *across)
    gram = joining(*cores)(jnp.concatenate(flat(both[:cut]) + flat(got[:cut]), 0))()
    cross = both[cut:] + got[cut:]
    stages = factor_stages(float(total_rows), modes // TILE, gram_number, two)
    steps = [joining(*near), joining(*cores)]
    cross, (basis, inverse) = run_beside(cross, steps, gram, stages)
    body_of = functools.partial(projected_body, float(total_rows))
    call = kernel_call(body_of, square, [SMEM] + [VMEM] * 2, 2 * square_work, traffic)
    return basis, call(cross_number, cross, inverse)


def solution(mesh):
    placed = (
        P(("region", "split"), None),
        P(("region", "split"), None, None, None),
        P(("region", "split"), None),
        P(("region", "split")),
        P("region", None, None),
        P(),
    )
    return jax.shard_map(
        local,
        mesh=mesh,
        in_specs=placed,
        out_specs=(P(("region", "split"), None), P()),
        check_vma=False,
    )
```

```python
import functools
import jax
import jax.numpy as jnp
from jax import lax
from jax.experimental import pallas as pl
from jax.experimental.pallas import tpu as pltpu
from jax.sharding import PartitionSpec as P

AXES = ("region", "split")
VMEM = pl.BlockSpec(memory_space=pltpu.VMEM)
SMEM = pl.BlockSpec(memory_space=pltpu.SMEM)
EXACT = lax.Precision.HIGHEST
NN = (((1,), (0,)), ((), ()))
NT = (((1,), (1,)), ((), ()))
TN = (((0,), (0,)), ((), ()))
GROUP = 8
PANEL = 32
TILE = 128
VMEM_LIMIT = 6 * 1024 * 1024
LIST_ROWS = 16
PIECES = 4


def shifted(value, axis, steps):
    count = lax.axis_size(axis)
    pairs = [(source, (source + steps) % count) for source in range(count)]
    return lax.ppermute(value, axis, pairs)


def exact_dot(left, right, dims=NN):
    return lax.dot_general(left, right, dims, precision=EXACT, preferred_element_type=jnp.float32)


def kernel_call(body, out_shape, in_specs, flops, bytes_accessed, scratch=()):
    return pl.pallas_call(
        body,
        out_shape=out_shape,
        in_specs=in_specs,
        out_specs=jax.tree.map(lambda out: SMEM if out.dtype == jnp.int32 else VMEM, out_shape),
        scratch_shapes=list(scratch),
        compiler_params=pltpu.CompilerParams(vmem_limit_bytes=VMEM_LIMIT),
        cost_estimate=pl.CostEstimate(flops=flops, bytes_accessed=bytes_accessed // 16, transcendentals=0),
    )


def fill_slots(slots_ref, cols_ref, live_ref):
    rows, stored = cols_ref.shape
    count = slots_ref.shape[1] - 1
    for row in range(rows):
        for index in range(count):
            slots_ref[row, index] = -1
        for at in range(stored):
            slots_ref[row, jnp.where(at < live_ref[row], cols_ref[row, at], count)] = at


def accumulate(slots_ref, hessian_ref, operand_ref, column_of, total):
    rows, _, size, _ = hessian_ref.shape
    shards, shard_rows, _ = operand_ref.shape
    each = shard_rows // size
    for index in range(shards * each):
        start = index % each * size
        block = operand_ref[index // each, start : start + size, :]
        column = column_of(index)
        parts = []
        for row in range(rows):
            slot = slots_ref[row, column]
            live = jnp.where(slot >= 0, 1.0, 0.0).astype(jnp.float32)
            stored = hessian_ref[row, jnp.maximum(slot, 0)]
            parts.append(stored * jnp.broadcast_to(live, (size, size)).astype(jnp.bfloat16))
        term = jnp.dot(jnp.concatenate(parts, 0), block, preferred_element_type=jnp.float32)
        total = term if total is None else total + term
    return total


def hold_body(blocks_ref, out_ref):
    pltpu.sync_copy(blocks_ref, out_ref)


def near_sum(slots_ref, bases_ref, hessian_ref, operands):
    total = None
    for at, operand_ref in enumerate(operands):
        total = accumulate(slots_ref, hessian_ref, operand_ref, lambda index: bases_ref[at] + index, total)
    return total


def table_body(cols_ref, live_ref, bases_ref, hessian_ref, operand_ref, bounds_ref, vectors_ref, out_ref, slots_ref):
    fill_slots(slots_ref, cols_ref, live_ref)
    out_ref[...] = first_terms(near_sum(slots_ref, bases_ref, hessian_ref, [operand_ref]), bounds_ref, vectors_ref)


def near_body(groups, linear, slots_ref, bases_ref, hessian_ref, *refs):
    operands, (*terms, out_ref) = refs[:groups], refs[groups:]
    out_ref[...] = linear(near_sum(slots_ref, bases_ref, hessian_ref, operands), *terms)


def near_gram_body(groups, *refs):
    *operands, number_ref, two_ref, out_ref, gram_ref = refs
    near_body(groups, lambda total: total, *operands, out_ref)
    gram_part(number_ref, two_ref, gram_ref)


def first_terms(total, bounds_ref, vectors_ref):
    centre, _ = interval(bounds_ref)
    return total - centre * vectors_ref[...]


def second_terms(total, bounds_ref, one_ref, vectors_ref):
    centre, half = interval(bounds_ref)
    return total - centre * one_ref[...] - (0.5 * half) * vectors_ref[...]


def halo_sum(which, slots_ref, lists_ref, bases_ref, hessian_ref, lower_ref, upper_ref, names_ref):
    halo = lists_ref.shape[1]
    near = slots_ref.shape[1] - 1 - 2 * halo
    for side in range(2):
        for at in range(halo):
            names_ref[side * halo + lists_ref[side, at]] = near + side * halo + at
    total = None
    for side, operand_ref in enumerate((lower_ref, upper_ref)):
        first = side * halo + bases_ref[which]
        total = accumulate(slots_ref, hessian_ref, operand_ref, lambda index: names_ref[first + index], total)
    return total


def middle_body(which, *refs):
    operands, (total_ref, out_ref, token_ref, names_ref) = refs[:6], refs[6:]
    total = total_ref[...] + halo_sum(which, *operands, names_ref)
    out_ref[...] = total
    token_ref[...] = total[:GROUP, :TILE]


def interval(bounds_ref):
    return 0.5 * (bounds_ref[0] + bounds_ref[1]), 0.5 * (bounds_ref[1] - bounds_ref[0])


def scaled_body(factor, which, *refs):
    operands, (total_ref, bounds_ref, out_ref, cast_ref, names_ref) = refs[:6], refs[6:]
    _, half = interval(bounds_ref)
    value = factor * (total_ref[...] + halo_sum(which, *operands, names_ref)) / half
    out_ref[...] = value
    cast_ref[...] = value.astype(jnp.bfloat16)


def place_rows(number_ref, piece, rows):
    return pl.ds(pl.multiple_of((piece ^ number_ref[0]) * rows, GROUP), rows)


def scatter_pieces(number_ref, out_ref, value):
    rows = out_ref.shape[0] // PIECES
    for piece in range(PIECES):
        out_ref[place_rows(number_ref, piece, rows), :] = value[piece * rows : (piece + 1) * rows, :]


def ordered_pieces(number_ref, in_ref):
    rows = in_ref.shape[0] // PIECES
    return jnp.concatenate([in_ref[place_rows(number_ref, piece, rows), :] for piece in range(PIECES)], 0)


def lower_tiles(count):
    return [(row, col) for row in range(count) for col in range(row + 1)]


def gram_part(number_ref, two_ref, out_ref):
    two = two_ref[...]
    cols = [two[:, at * TILE : (at + 1) * TILE] for at in range(two.shape[1] // TILE)]
    tiles = [exact_dot(cols[row], cols[col], TN) for row, col in lower_tiles(len(cols))]
    scatter_pieces(number_ref, out_ref, jnp.concatenate(tiles, 0))


def third_body(which, *refs):
    operands, (total_ref, number_ref, two_ref, _, out_ref, names_ref) = refs[:6], refs[6:]
    image = total_ref[...] + halo_sum(which, *operands, names_ref)
    scatter_pieces(number_ref, out_ref, exact_dot(two_ref[...], image, TN))


def over_lanes(value, lane):
    return jnp.broadcast_to(value[:, lane : lane + 1], value.shape)


def over_rows(value, row):
    return jnp.broadcast_to(value[row : row + 1, :], value.shape)


def eliminate(tile):
    count, panel = tile.shape[0] // GROUP, PANEL // GROUP
    rows = [tile[index * GROUP : (index + 1) * GROUP, :] for index in range(count)]
    sub = lax.broadcasted_iota(jnp.int32, rows[0].shape, 0)
    lane = lax.broadcasted_iota(jnp.int32, rows[0].shape, 1)
    for begin in range(0, count, panel):
        end = begin + panel
        reduced = []
        for step in range(begin, end):
            start = step * GROUP
            pivot_cols = [over_lanes(rows[step], start + col) for col in range(GROUP)]
            factors = {
                below: [over_lanes(rows[below], start + col) for col in range(GROUP)] for below in range(step + 1, end)
            }
            inside = (lane >= start) & (lane < start + GROUP)
            forward = jnp.where(inside, jnp.where(lane - start == sub, 1.0, 0.0), rows[step])
            solved = forward
            for pivot in range(GROUP):
                here = sub == pivot
                value = over_rows(pivot_cols[pivot], pivot)
                inverse = 1.0 / value
                ratio = pivot_cols[pivot] * inverse
                row = over_rows(forward, pivot)
                below_row = jnp.where(sub > pivot, forward - ratio * row, forward)
                forward = jnp.where(here, row * lax.rsqrt(value), below_row)
                solved = jnp.where(here, row * inverse, solved - ratio * row)
                for col in range(pivot + 1, GROUP):
                    top = over_rows(pivot_cols[col], pivot)
                    pivot_cols[col] = jnp.where(here, top * inverse, pivot_cols[col] - ratio * top)
            own_part = (lane < start + GROUP) | (lane >= end * GROUP)
            reduced.append((forward, jnp.where(own_part, forward, 0.0)))
            rows[step] = jnp.where(lane < start + GROUP, forward, 0.0)
            solved_rows = [over_rows(solved, pivot) for pivot in range(GROUP)]
            for below in range(step + 1, end):
                terms = [factors[below][col] * solved_rows[col] for col in range(GROUP)]
                while len(terms) > 1:
                    terms = [terms[at] + terms[at + 1] for at in range(0, len(terms), 2)]
                rows[below] = jnp.where(inside, 0.0, rows[below]) - terms[0]
        if end < count:
            factor_rows, solved_rows = [jnp.concatenate(parts, 0) for parts in zip(*reduced)]
            share = exact_dot(factor_rows, solved_rows, TN)
            inside = (lane >= begin * GROUP) & (lane < end * GROUP)
            for below in range(end, count):
                rows[below] = jnp.where(inside, 0.0, rows[below]) - share[below * GROUP : (below + 1) * GROUP, :]
    return jnp.concatenate(rows, 0)


def first_tile_body(count, total_rows, number_ref, gram_ref, *tile_refs):
    packed = ordered_pieces(number_ref, gram_ref) / total_rows
    tiles = [packed[at * TILE : (at + 1) * TILE, :] for at in range(len(tile_refs))]
    finish_tile(0, count, dict(zip(lower_tiles(count), tiles)), tile_refs)


def next_tile_body(at, count, *refs):
    names = lower_tiles(count)
    tiles = {name: ref[...] for name, ref in zip(names, refs)}
    finish_tile(at, count, tiles, refs[len(names) :])


def finish_tile(at, count, tiles, out_refs):
    tiles = dict(tiles)
    tiles[at, at] = eliminate(tiles[at, at])
    for row in range(at + 1, count):
        tiles[row, at] = exact_dot(tiles[row, at], tiles[at, at], NT)
    for row in range(at + 1, count):
        for col in range(at + 1, row + 1):
            tiles[row, col] = tiles[row, col] - exact_dot(tiles[row, at], tiles[col, at], NT)
    for name, out_ref in zip(lower_tiles(count), out_refs):
        out_ref[...] = tiles[name]


def basis_body(count, total_rows, number_ref, cross_ref, *refs):
    *tile_refs, two_ref, basis_ref, projected_ref = refs
    tiles = {name: ref[...] for name, ref in zip(lower_tiles(count), tile_refs)}
    inverse = {}
    for row in range(count):
        inverse[row, row] = tiles[row, row]
        for col in range(row):
            mixed = exact_dot(tiles[row, col], inverse[col, col])
            for mid in range(col + 1, row):
                mixed = mixed + exact_dot(tiles[row, mid], inverse[mid, col])
            inverse[row, col] = -exact_dot(tiles[row, row], mixed)
    zero = jnp.zeros((TILE, TILE), jnp.float32)
    whole = jnp.concatenate(
        [
            jnp.concatenate([inverse[row, col] if col <= row else zero for col in range(count)], 1)
            for row in range(count)
        ],
        0,
    )
    cross = ordered_pieces(number_ref, cross_ref) / total_rows
    left = exact_dot(whole, cross)
    basis_ref[...] = exact_dot(two_ref[...], whole, NT)
    projected_ref[...] = exact_dot(left, whole, NT)


def factor_stages(total_rows, count, number, two, cross_number):
    rows, modes = two.shape
    tile = jax.ShapeDtypeStruct((TILE, TILE), jnp.float32)
    names = lower_tiles(count)
    work = 10**8

    def first(gram):
        body = functools.partial(first_tile_body, count, total_rows)
        return tuple(kernel_call(body, (tile,) * len(names), [SMEM, VMEM], work, gram.size)(number, gram))

    def following(at):
        def stage(state):
            body = functools.partial(next_tile_body, at, count)
            call = kernel_call(body, (tile,) * len(names), [VMEM] * len(names), work, TILE * TILE)
            return tuple(call(*state))

        return stage

    def finish(state, cross):
        outs = (jax.ShapeDtypeStruct((rows, modes), jnp.float32), jax.ShapeDtypeStruct((modes, modes), jnp.float32))
        body = functools.partial(basis_body, count, total_rows)
        call = kernel_call(body, outs, [SMEM] + [VMEM] * (len(names) + 2), work, rows * modes)
        return tuple(call(cross_number, cross, *state, two))

    return [first] + [following(at) for at in range(1, count)], finish


def tied(left, right):
    return lax.optimization_barrier((left, right))


def partner_value(value, axis, bit):
    return lax.ppermute(value, axis, [(at, at ^ bit) for at in range(lax.axis_size(axis))])


def axis_bits(axis):
    return [(axis, 1 << at) for at in range(lax.axis_size(axis).bit_length() - 1)]


def device_number(halved):
    number = 0
    for axis, bit in halved:
        number = number * 2 + (lax.axis_index(axis) // bit) % 2
    return number.astype(jnp.int32).reshape(1)


def halving(axis, bit):
    def step(value):
        half = value.shape[0] // 2
        got = partner_value(value[half:], axis, bit)
        return lambda: value[:half] + got

    return step


def doubling(axis, bit):
    def step(value):
        got = partner_value(value, axis, bit)
        return lambda: value + got

    return step


def joining(axis, bit):
    def step(value):
        got = partner_value(value, axis, bit)
        return lambda: jnp.concatenate([value, got], 0)

    return step


def run_beside(value, steps, state, stages):
    stages = list(stages)
    for index, step in enumerate(steps):
        value, state = tied(value, state)
        join = step(value)
        due = -(-len(stages) // (len(steps) - index))
        for _ in range(due):
            state = stages.pop(0)(state)
        value = join()
        if due:
            value, state = tied(value, state)
    return value, state


def local(vectors, hessian, block_cols, live_blocks, halo_lists, bounds):
    row_blocks, stored, size, _ = hessian.shape
    rows, modes = vectors.shape
    splits = lax.axis_size("split")
    region_blocks = row_blocks * splits
    halo_blocks = halo_lists.shape[2]
    whole = halo_blocks == region_blocks and region_blocks <= 256
    total_rows = rows * lax.axis_size(AXES)

    paired = whole and splits == 2
    core = lax.axis_index("split").astype(jnp.int32)
    swapped = lambda value: lax.ppermute(value, "split", [(0, 1), (1, 0)])
    halo_first = [core * row_blocks, (1 - core) * row_blocks] if paired else [0]
    bases = jnp.stack(halo_first).astype(jnp.int32) if paired else jnp.zeros((1,), jnp.int32)

    def sent(operand, region):
        if whole:
            return operand, operand
        width = modes // splits
        start = core * width
        blocks = region[:, :rows].reshape(region_blocks, size, modes)
        share = lambda listed: lax.dynamic_slice_in_dim(blocks[listed], start, width, 2).reshape(-1, width)
        return share(halo_lists[0, 1]), share(halo_lists[0, 0])

    def gathered(value):
        if paired:
            return [value[None], swapped(value)[None]]
        if whole:
            return [lax.all_gather(value, "split", axis=0)]
        return [lax.all_gather(value, "split", axis=1, tiled=True)[None]]

    listed = jnp.pad(halo_lists[0], ((0, LIST_ROWS - 2), (0, modes - halo_blocks)))
    first = vectors.astype(jnp.bfloat16)
    if whole:
        first = jnp.concatenate([first, listed.astype(jnp.bfloat16)], 0)

    def exchange(operand, gather=True):
        if gather or not paired:
            groups = [lax.all_gather(operand, "split", axis=0)]
        else:
            groups = [operand[None], swapped(operand)[None]]
        up, down = sent(operand, groups[0])
        return groups, shifted(up, "region", 1), shifted(down, "region", -1)

    first_near, first_lower, first_upper = exchange(first)
    if whole:
        orders = [first_lower[rows + 1, :halo_blocks], first_upper[rows, :halo_blocks]]
        lists = jnp.stack(orders).astype(jnp.int32)
    else:
        lists = jnp.broadcast_to(jnp.arange(halo_blocks, dtype=jnp.int32), (2, halo_blocks))

    wide = jax.ShapeDtypeStruct((rows, modes), jnp.float32)
    narrow = jax.ShapeDtypeStruct((rows, modes), jnp.bfloat16)
    square = jax.ShapeDtypeStruct((modes, modes), jnp.float32)
    tile_rows = len(lower_tiles(modes // TILE)) * TILE
    work = 2 * rows * size * modes
    square_work = 2 * rows * modes * modes
    traffic = hessian.size * 2 + 3 * rows * modes * 4
    cores, *other_cores = axis_bits("split")
    near, across, *far = axis_bits("region")
    between = other_cores + far
    gram_number, cross_number = device_number([cores, across]), device_number([cores, near])
    names = [pltpu.SMEM((2 * halo_blocks,), jnp.int32)]
    table_shape = jax.ShapeDtypeStruct((row_blocks, region_blocks + 2 * halo_blocks + 1), jnp.int32)

    covering, free = 3 * 10 ** 10, 10 ** 7
    token = jax.ShapeDtypeStruct((GROUP, TILE), jnp.float32)

    held = pl.pallas_call(
        hold_body,
        out_shape=pltpu.VMEM(hessian.shape, hessian.dtype),
        in_specs=[pl.BlockSpec(memory_space=pl.ANY)],
        out_specs=VMEM,
        compiler_params=pltpu.CompilerParams(vmem_limit_bytes=VMEM_LIMIT),
    )(hessian)

    def near_total(body, outs, groups, scalars, terms):
        specs = [SMEM] * 2 + [VMEM] * (1 + len(groups)) + [SMEM] * len(scalars) + [VMEM] * len(terms)
        near_bases = bases if len(groups) > 1 else jnp.zeros_like(bases)
        return kernel_call(body, outs, specs, free, traffic)(table, near_bases, held, *groups, *scalars, *terms)

    def last_part(body, outs, which, pair, total, scalars, extra=()):
        specs = [SMEM] * 3 + [VMEM] * 4 + [SMEM] * len(scalars) + [VMEM] * len(extra)
        call = kernel_call(functools.partial(body, which), outs, specs, covering, traffic, names)
        return call(table, lists, bases, held, *pair, total, *scalars, *extra)

    def before_last(lower, upper, total):
        *pairs, last = zip(gathered(lower), gathered(upper))
        after = jnp.zeros(token.shape, token.dtype)
        for which, pair in enumerate(pairs):
            specs = [SMEM] * 3 + [VMEM] * 4
            body_of = functools.partial(middle_body, which)
            call = kernel_call(body_of, (wide, token), specs, covering, traffic, names)
            total, after = call(table, lists, bases, held, *pair, total)
        return total, after, len(pairs), last

    specs = [SMEM] * 3 + [VMEM] * 2 + [SMEM, VMEM]
    call = kernel_call(table_body, (wide, table_shape), specs, free, traffic)
    total, table = call(block_cols, live_blocks, jnp.zeros_like(bases), held, *first_near, bounds, vectors)
    total, _, which, last = before_last(first_lower, first_upper, total)
    one, one_cast = last_part(functools.partial(scaled_body, 1.0), (wide, narrow), which, last, total, (bounds,))

    own, lower, upper = exchange(one_cast)
    body_of = functools.partial(near_body, len(own), second_terms)
    (total,) = near_total(body_of, (wide,), own, (bounds,), (one, vectors))
    total, _, which, last = before_last(lower, upper, total)
    two, two_cast = last_part(functools.partial(scaled_body, 2.0), (wide, narrow), which, last, total, (bounds,))

    own, lower, upper = exchange(two_cast, gather=False)
    packed = jax.ShapeDtypeStruct((tile_rows, TILE), jnp.float32)
    body_of = functools.partial(near_gram_body, len(own))
    total, gram = near_total(body_of, (wide, packed), own, (gram_number,), (two,))
    for step_of in [halving(*cores), halving(*across)]:
        gram = step_of(gram)()
    total, after, which, last = before_last(lower, upper, total)
    gram, after = tied(gram, after)
    cross = last_part(third_body, square, which, last, total, (cross_number,), (two, after))
    cross = halving(*cores)(cross)()

    fold = modes // TILE
    cut = gram.shape[0] // fold
    folded = jnp.concatenate([gram[at * cut : (at + 1) * cut] for at in range(fold)], 1)
    flat = lambda value: [value[:, at * TILE : (at + 1) * TILE] for at in range(fold)]
    half = cross.shape[0] // 2
    got = partner_value(jnp.concatenate([folded, cross[half:]], 0), *near)
    both = jnp.concatenate([folded, cross[:half]], 0) + got
    for bit in between:
        both = doubling(*bit)(both)()
    got = partner_value(both, *across)
    gram = joining(*cores)(jnp.concatenate(flat(both[:cut]) + flat(got[:cut]), 0))()
    cross = both[cut:] + got[cut:]
    stages, finish = factor_stages(float(total_rows), modes // TILE, gram_number, two, cross_number)
    steps = [joining(*near), joining(*cores)]
    cross, tiles = run_beside(cross, steps, gram, stages)
    return finish(tiles, cross)


def solution(mesh):
    placed = (
        P(("region", "split"), None),
        P(("region", "split"), None, None, None),
        P(("region", "split"), None),
        P(("region", "split")),
        P("region", None, None),
        P(),
    )
    return jax.shard_map(
        local,
        mesh=mesh,
        in_specs=placed,
        out_specs=(P(("region", "split"), None), P()),
        check_vma=False,
    )
```

```python
import functools
import jax
import jax.numpy as jnp
from jax import lax
from jax.experimental import pallas as pl
from jax.experimental.pallas import tpu as pltpu
from jax.sharding import PartitionSpec as P

AXES = ("region", "split")
VMEM = pl.BlockSpec(memory_space=pltpu.VMEM)
SMEM = pl.BlockSpec(memory_space=pltpu.SMEM)
EXACT = lax.Precision.HIGHEST
NN = (((1,), (0,)), ((), ()))
NT = (((1,), (1,)), ((), ()))
TN = (((0,), (0,)), ((), ()))
GROUP = 8
PANEL = 64
TILE = 128
VMEM_LIMIT = 6 * 1024 * 1024
LIST_ROWS = 16
PIECES = 4


def shifted(value, axis, steps):
    count = lax.axis_size(axis)
    pairs = [(source, (source + steps) % count) for source in range(count)]
    return lax.ppermute(value, axis, pairs)


def exact_dot(left, right, dims=NN):
    return lax.dot_general(left, right, dims, precision=EXACT, preferred_element_type=jnp.float32)


def kernel_call(body, out_shape, in_specs, flops, bytes_accessed, scratch=()):
    return pl.pallas_call(
        body,
        out_shape=out_shape,
        in_specs=in_specs,
        out_specs=jax.tree.map(lambda out: SMEM if out.dtype == jnp.int32 else VMEM, out_shape),
        scratch_shapes=list(scratch),
        compiler_params=pltpu.CompilerParams(vmem_limit_bytes=VMEM_LIMIT),
        cost_estimate=pl.CostEstimate(flops=flops, bytes_accessed=bytes_accessed // 16, transcendentals=0),
    )


def fill_slots(slots_ref, cols_ref, live_ref):
    rows, stored = cols_ref.shape
    count = slots_ref.shape[1] - 1
    for row in range(rows):
        for index in range(count):
            slots_ref[row, index] = -1
        for at in range(stored):
            slots_ref[row, jnp.where(at < live_ref[row], cols_ref[row, at], count)] = at


def accumulate(slots_ref, hessian_ref, operand_ref, column_of, total):
    rows, _, size, _ = hessian_ref.shape
    shards, shard_rows, _ = operand_ref.shape
    each = shard_rows // size
    for index in range(shards * each):
        start = index % each * size
        block = operand_ref[index // each, start : start + size, :]
        column = column_of(index)
        parts = []
        for row in range(rows):
            slot = slots_ref[row, column]
            live = jnp.where(slot >= 0, 1.0, 0.0).astype(jnp.float32)
            stored = hessian_ref[row, jnp.maximum(slot, 0)]
            parts.append(stored * jnp.broadcast_to(live, (size, size)).astype(jnp.bfloat16))
        term = jnp.dot(jnp.concatenate(parts, 0), block, preferred_element_type=jnp.float32)
        total = term if total is None else total + term
    return total


def hold_body(blocks_ref, out_ref):
    pltpu.sync_copy(blocks_ref, out_ref)


def near_sum(slots_ref, bases_ref, hessian_ref, operands):
    total = None
    for at, operand_ref in enumerate(operands):
        total = accumulate(slots_ref, hessian_ref, operand_ref, lambda index: bases_ref[at] + index, total)
    return total


def table_body(cols_ref, live_ref, bases_ref, hessian_ref, operand_ref, bounds_ref, vectors_ref, out_ref, slots_ref):
    fill_slots(slots_ref, cols_ref, live_ref)
    out_ref[...] = first_terms(near_sum(slots_ref, bases_ref, hessian_ref, [operand_ref]), bounds_ref, vectors_ref)


def near_body(groups, linear, slots_ref, bases_ref, hessian_ref, *refs):
    operands, (*terms, out_ref) = refs[:groups], refs[groups:]
    out_ref[...] = linear(near_sum(slots_ref, bases_ref, hessian_ref, operands), *terms)


def near_gram_body(groups, *refs):
    *operands, number_ref, two_ref, out_ref, gram_ref = refs
    near_body(groups, lambda total: total, *operands, out_ref)
    gram_part(number_ref, two_ref, gram_ref)


def first_terms(total, bounds_ref, vectors_ref):
    centre, _ = interval(bounds_ref)
    return total - centre * vectors_ref[...]


def second_terms(total, bounds_ref, one_ref, vectors_ref):
    centre, half = interval(bounds_ref)
    return total - centre * one_ref[...] - (0.5 * half) * vectors_ref[...]


def halo_sum(which, slots_ref, lists_ref, bases_ref, hessian_ref, lower_ref, upper_ref, names_ref):
    halo = lists_ref.shape[1]
    near = slots_ref.shape[1] - 1 - 2 * halo
    for side in range(2):
        for at in range(halo):
            names_ref[side * halo + lists_ref[side, at]] = near + side * halo + at
    total = None
    for side, operand_ref in enumerate((lower_ref, upper_ref)):
        first = side * halo + bases_ref[which]
        total = accumulate(slots_ref, hessian_ref, operand_ref, lambda index: names_ref[first + index], total)
    return total


def middle_body(which, *refs):
    operands, (total_ref, out_ref, token_ref, names_ref) = refs[:6], refs[6:]
    total = total_ref[...] + halo_sum(which, *operands, names_ref)
    out_ref[...] = total
    token_ref[...] = total[:GROUP, :TILE]


def interval(bounds_ref):
    return 0.5 * (bounds_ref[0] + bounds_ref[1]), 0.5 * (bounds_ref[1] - bounds_ref[0])


def scaled_body(factor, which, *refs):
    operands, (total_ref, bounds_ref, out_ref, cast_ref, names_ref) = refs[:6], refs[6:]
    _, half = interval(bounds_ref)
    value = factor * (total_ref[...] + halo_sum(which, *operands, names_ref)) / half
    out_ref[...] = value
    cast_ref[...] = value.astype(jnp.bfloat16)


def place_rows(number_ref, piece, rows):
    return pl.ds(pl.multiple_of((piece ^ number_ref[0]) * rows, GROUP), rows)


def scatter_pieces(number_ref, out_ref, value):
    rows = out_ref.shape[0] // PIECES
    for piece in range(PIECES):
        out_ref[place_rows(number_ref, piece, rows), :] = value[piece * rows : (piece + 1) * rows, :]


def ordered_pieces(number_ref, in_ref):
    rows = in_ref.shape[0] // PIECES
    return jnp.concatenate([in_ref[place_rows(number_ref, piece, rows), :] for piece in range(PIECES)], 0)


def lower_tiles(count):
    return [(row, col) for row in range(count) for col in range(row + 1)]


def gram_part(number_ref, two_ref, out_ref):
    two = two_ref[...]
    cols = [two[:, at * TILE : (at + 1) * TILE] for at in range(two.shape[1] // TILE)]
    tiles = [exact_dot(cols[row], cols[col], TN) for row, col in lower_tiles(len(cols))]
    scatter_pieces(number_ref, out_ref, jnp.concatenate(tiles, 0))


def third_body(which, *refs):
    operands, (total_ref, number_ref, two_ref, _, out_ref, names_ref) = refs[:6], refs[6:]
    image = total_ref[...] + halo_sum(which, *operands, names_ref)
    scatter_pieces(number_ref, out_ref, exact_dot(two_ref[...], image, TN))


def over_lanes(value, lane):
    return jnp.broadcast_to(value[:, lane : lane + 1], value.shape)


def over_rows(value, row):
    return jnp.broadcast_to(value[row : row + 1, :], value.shape)


def eliminate(tile):
    count, panel = tile.shape[0] // GROUP, PANEL // GROUP
    rows = [tile[index * GROUP : (index + 1) * GROUP, :] for index in range(count)]
    sub = lax.broadcasted_iota(jnp.int32, rows[0].shape, 0)
    lane = lax.broadcasted_iota(jnp.int32, rows[0].shape, 1)
    for begin in range(0, count, panel):
        end = begin + panel
        reduced = []
        for step in range(begin, end):
            start = step * GROUP
            pivot_cols = [over_lanes(rows[step], start + col) for col in range(GROUP)]
            factors = {
                below: [over_lanes(rows[below], start + col) for col in range(GROUP)] for below in range(step + 1, end)
            }
            inside = (lane >= start) & (lane < start + GROUP)
            forward = jnp.where(inside, jnp.where(lane - start == sub, 1.0, 0.0), rows[step])
            solved = forward
            for pivot in range(GROUP):
                here = sub == pivot
                value = over_rows(pivot_cols[pivot], pivot)
                inverse = 1.0 / value
                ratio = pivot_cols[pivot] * inverse
                row = over_rows(forward, pivot)
                below_row = jnp.where(sub > pivot, forward - ratio * row, forward)
                forward = jnp.where(here, row * lax.rsqrt(value), below_row)
                solved = jnp.where(here, row * inverse, solved - ratio * row)
                for col in range(pivot + 1, GROUP):
                    top = over_rows(pivot_cols[col], pivot)
                    pivot_cols[col] = jnp.where(here, top * inverse, pivot_cols[col] - ratio * top)
            own_part = (lane < start + GROUP) | (lane >= end * GROUP)
            reduced.append((forward, jnp.where(own_part, forward, 0.0)))
            rows[step] = jnp.where(lane < start + GROUP, forward, 0.0)
            solved_rows = [over_rows(solved, pivot) for pivot in range(GROUP)]
            for below in range(step + 1, end):
                terms = [factors[below][col] * solved_rows[col] for col in range(GROUP)]
                while len(terms) > 1:
                    terms = [terms[at] + terms[at + 1] for at in range(0, len(terms), 2)]
                rows[below] = jnp.where(inside, 0.0, rows[below]) - terms[0]
        if end < count:
            factor_rows, solved_rows = [jnp.concatenate(parts, 0) for parts in zip(*reduced)]
            share = exact_dot(factor_rows, solved_rows, TN)
            inside = (lane >= begin * GROUP) & (lane < end * GROUP)
            for below in range(end, count):
                rows[below] = jnp.where(inside, 0.0, rows[below]) - share[below * GROUP : (below + 1) * GROUP, :]
    return jnp.concatenate(rows, 0)


def first_tile_body(count, total_rows, number_ref, gram_ref, *tile_refs):
    packed = ordered_pieces(number_ref, gram_ref) / total_rows
    tiles = [packed[at * TILE : (at + 1) * TILE, :] for at in range(len(tile_refs))]
    finish_tile(0, count, dict(zip(lower_tiles(count), tiles)), tile_refs)


def next_tile_body(at, count, *refs):
    names = lower_tiles(count)
    tiles = {name: ref[...] for name, ref in zip(names, refs)}
    finish_tile(at, count, tiles, refs[len(names) :])


def finish_tile(at, count, tiles, out_refs):
    tiles = dict(tiles)
    tiles[at, at] = eliminate(tiles[at, at])
    for row in range(at + 1, count):
        tiles[row, at] = exact_dot(tiles[row, at], tiles[at, at], NT)
    for row in range(at + 1, count):
        for col in range(at + 1, row + 1):
            tiles[row, col] = tiles[row, col] - exact_dot(tiles[row, at], tiles[col, at], NT)
    for name, out_ref in zip(lower_tiles(count), out_refs):
        out_ref[...] = tiles[name]


def basis_body(count, total_rows, number_ref, cross_ref, *refs):
    *tile_refs, two_ref, basis_ref, projected_ref = refs
    tiles = {name: ref[...] for name, ref in zip(lower_tiles(count), tile_refs)}
    inverse = {}
    for row in range(count):
        inverse[row, row] = tiles[row, row]
        for col in range(row):
            mixed = exact_dot(tiles[row, col], inverse[col, col])
            for mid in range(col + 1, row):
                mixed = mixed + exact_dot(tiles[row, mid], inverse[mid, col])
            inverse[row, col] = -exact_dot(tiles[row, row], mixed)
    zero = jnp.zeros((TILE, TILE), jnp.float32)
    whole = jnp.concatenate(
        [
            jnp.concatenate([inverse[row, col] if col <= row else zero for col in range(count)], 1)
            for row in range(count)
        ],
        0,
    )
    cross = ordered_pieces(number_ref, cross_ref) / total_rows
    left = exact_dot(whole, cross)
    basis_ref[...] = exact_dot(two_ref[...], whole, NT)
    projected_ref[...] = exact_dot(left, whole, NT)


def factor_stages(total_rows, count, number, two, cross_number):
    rows, modes = two.shape
    tile = jax.ShapeDtypeStruct((TILE, TILE), jnp.float32)
    names = lower_tiles(count)
    work = 10**8

    def first(gram):
        body = functools.partial(first_tile_body, count, total_rows)
        return tuple(kernel_call(body, (tile,) * len(names), [SMEM, VMEM], work, gram.size)(number, gram))

    def following(at):
        def stage(state):
            body = functools.partial(next_tile_body, at, count)
            call = kernel_call(body, (tile,) * len(names), [VMEM] * len(names), work, TILE * TILE)
            return tuple(call(*state))

        return stage

    def finish(state, cross):
        outs = (jax.ShapeDtypeStruct((rows, modes), jnp.float32), jax.ShapeDtypeStruct((modes, modes), jnp.float32))
        body = functools.partial(basis_body, count, total_rows)
        call = kernel_call(body, outs, [SMEM] + [VMEM] * (len(names) + 2), work, rows * modes)
        return tuple(call(cross_number, cross, *state, two))

    return [first] + [following(at) for at in range(1, count)], finish


def tied(left, right):
    return lax.optimization_barrier((left, right))


def partner_value(value, axis, bit):
    return lax.ppermute(value, axis, [(at, at ^ bit) for at in range(lax.axis_size(axis))])


def axis_bits(axis):
    return [(axis, 1 << at) for at in range(lax.axis_size(axis).bit_length() - 1)]


def device_number(halved):
    number = 0
    for axis, bit in halved:
        number = number * 2 + (lax.axis_index(axis) // bit) % 2
    return number.astype(jnp.int32).reshape(1)


def halving(axis, bit):
    def step(value):
        half = value.shape[0] // 2
        got = partner_value(value[half:], axis, bit)
        return lambda: value[:half] + got

    return step


def doubling(axis, bit):
    def step(value):
        got = partner_value(value, axis, bit)
        return lambda: value + got

    return step


def joining(axis, bit):
    def step(value):
        got = partner_value(value, axis, bit)
        return lambda: jnp.concatenate([value, got], 0)

    return step


def run_beside(value, steps, state, stages):
    stages = list(stages)
    for index, step in enumerate(steps):
        value, state = tied(value, state)
        join = step(value)
        due = -(-len(stages) // (len(steps) - index))
        for _ in range(due):
            state = stages.pop(0)(state)
        value = join()
        if due:
            value, state = tied(value, state)
    return value, state


def local(vectors, hessian, block_cols, live_blocks, halo_lists, bounds):
    row_blocks, stored, size, _ = hessian.shape
    rows, modes = vectors.shape
    splits = lax.axis_size("split")
    region_blocks = row_blocks * splits
    halo_blocks = halo_lists.shape[2]
    whole = halo_blocks == region_blocks and region_blocks <= 256
    total_rows = rows * lax.axis_size(AXES)

    paired = whole and splits == 2
    core = lax.axis_index("split").astype(jnp.int32)
    swapped = lambda value: lax.ppermute(value, "split", [(0, 1), (1, 0)])
    halo_first = [core * row_blocks, (1 - core) * row_blocks] if paired else [0]
    bases = jnp.stack(halo_first).astype(jnp.int32) if paired else jnp.zeros((1,), jnp.int32)

    def sent(operand, region):
        if whole:
            return operand, operand
        width = modes // splits
        start = core * width
        blocks = region[:, :rows].reshape(region_blocks, size, modes)
        share = lambda listed: lax.dynamic_slice_in_dim(blocks[listed], start, width, 2).reshape(-1, width)
        return share(halo_lists[0, 1]), share(halo_lists[0, 0])

    def gathered(value):
        if paired:
            return [value[None], swapped(value)[None]]
        if whole:
            return [lax.all_gather(value, "split", axis=0)]
        return [lax.all_gather(value, "split", axis=1, tiled=True)[None]]

    listed = jnp.pad(halo_lists[0], ((0, LIST_ROWS - 2), (0, modes - halo_blocks)))
    first = vectors.astype(jnp.bfloat16)
    if whole:
        first = jnp.concatenate([first, listed.astype(jnp.bfloat16)], 0)

    def exchange(operand, gather=True):
        if gather or not paired:
            groups = [lax.all_gather(operand, "split", axis=0)]
        else:
            groups = [operand[None], swapped(operand)[None]]
        up, down = sent(operand, groups[0])
        return groups, shifted(up, "region", 1), shifted(down, "region", -1)

    first_near, first_lower, first_upper = exchange(first)
    if whole:
        orders = [first_lower[rows + 1, :halo_blocks], first_upper[rows, :halo_blocks]]
        lists = jnp.stack(orders).astype(jnp.int32)
    else:
        lists = jnp.broadcast_to(jnp.arange(halo_blocks, dtype=jnp.int32), (2, halo_blocks))

    wide = jax.ShapeDtypeStruct((rows, modes), jnp.float32)
    narrow = jax.ShapeDtypeStruct((rows, modes), jnp.bfloat16)
    square = jax.ShapeDtypeStruct((modes, modes), jnp.float32)
    tile_rows = len(lower_tiles(modes // TILE)) * TILE
    work = 2 * rows * size * modes
    square_work = 2 * rows * modes * modes
    traffic = hessian.size * 2 + 3 * rows * modes * 4
    cores, *other_cores = axis_bits("split")
    near, across, *far = axis_bits("region")
    between = other_cores + far
    gram_number, cross_number = device_number([cores, across]), device_number([cores, near])
    names = [pltpu.SMEM((2 * halo_blocks,), jnp.int32)]
    table_shape = jax.ShapeDtypeStruct((row_blocks, region_blocks + 2 * halo_blocks + 1), jnp.int32)

    covering, free = 3 * 10 ** 10, 10 ** 7
    token = jax.ShapeDtypeStruct((GROUP, TILE), jnp.float32)

    held = pl.pallas_call(
        hold_body,
        out_shape=pltpu.VMEM(hessian.shape, hessian.dtype),
        in_specs=[pl.BlockSpec(memory_space=pl.ANY)],
        out_specs=VMEM,
        compiler_params=pltpu.CompilerParams(vmem_limit_bytes=VMEM_LIMIT),
    )(hessian)

    def near_total(body, outs, groups, scalars, terms):
        specs = [SMEM] * 2 + [VMEM] * (1 + len(groups)) + [SMEM] * len(scalars) + [VMEM] * len(terms)
        near_bases = bases if len(groups) > 1 else jnp.zeros_like(bases)
        return kernel_call(body, outs, specs, free, traffic)(table, near_bases, held, *groups, *scalars, *terms)

    def last_part(body, outs, which, pair, total, scalars, extra=()):
        specs = [SMEM] * 3 + [VMEM] * 4 + [SMEM] * len(scalars) + [VMEM] * len(extra)
        call = kernel_call(functools.partial(body, which), outs, specs, covering, traffic, names)
        return call(table, lists, bases, held, *pair, total, *scalars, *extra)

    def before_last(lower, upper, total):
        *pairs, last = zip(gathered(lower), gathered(upper))
        after = jnp.zeros(token.shape, token.dtype)
        for which, pair in enumerate(pairs):
            specs = [SMEM] * 3 + [VMEM] * 4
            body_of = functools.partial(middle_body, which)
            call = kernel_call(body_of, (wide, token), specs, covering, traffic, names)
            total, after = call(table, lists, bases, held, *pair, total)
        return total, after, len(pairs), last

    specs = [SMEM] * 3 + [VMEM] * 2 + [SMEM, VMEM]
    call = kernel_call(table_body, (wide, table_shape), specs, free, traffic)
    total, table = call(block_cols, live_blocks, jnp.zeros_like(bases), held, *first_near, bounds, vectors)
    total, _, which, last = before_last(first_lower, first_upper, total)
    one, one_cast = last_part(functools.partial(scaled_body, 1.0), (wide, narrow), which, last, total, (bounds,))

    own, lower, upper = exchange(one_cast)
    body_of = functools.partial(near_body, len(own), second_terms)
    (total,) = near_total(body_of, (wide,), own, (bounds,), (one, vectors))
    total, _, which, last = before_last(lower, upper, total)
    two, two_cast = last_part(functools.partial(scaled_body, 2.0), (wide, narrow), which, last, total, (bounds,))

    own, lower, upper = exchange(two_cast, gather=False)
    packed = jax.ShapeDtypeStruct((tile_rows, TILE), jnp.float32)
    body_of = functools.partial(near_gram_body, len(own))
    total, gram = near_total(body_of, (wide, packed), own, (gram_number,), (two,))
    for step_of in [halving(*cores), halving(*across)]:
        gram = step_of(gram)()
    total, after, which, last = before_last(lower, upper, total)
    gram, after = tied(gram, after)
    cross = last_part(third_body, square, which, last, total, (cross_number,), (two, after))
    cross = halving(*cores)(cross)()

    fold = modes // TILE
    cut = gram.shape[0] // fold
    folded = jnp.concatenate([gram[at * cut : (at + 1) * cut] for at in range(fold)], 1)
    flat = lambda value: [value[:, at * TILE : (at + 1) * TILE] for at in range(fold)]
    half = cross.shape[0] // 2
    got = partner_value(jnp.concatenate([folded, cross[half:]], 0), *near)
    both = jnp.concatenate([folded, cross[:half]], 0) + got
    for bit in between:
        both = doubling(*bit)(both)()
    got = partner_value(both, *across)
    gram = joining(*cores)(jnp.concatenate(flat(both[:cut]) + flat(got[:cut]), 0))()
    cross = both[cut:] + got[cut:]
    stages, finish = factor_stages(float(total_rows), modes // TILE, gram_number, two, cross_number)
    steps = [joining(*near), joining(*cores)]
    cross, tiles = run_beside(cross, steps, gram, stages)
    return finish(tiles, cross)


def solution(mesh):
    placed = (
        P(("region", "split"), None),
        P(("region", "split"), None, None, None),
        P(("region", "split"), None),
        P(("region", "split")),
        P("region", None, None),
        P(),
    )
    return jax.shard_map(
        local,
        mesh=mesh,
        in_specs=placed,
        out_specs=(P(("region", "split"), None), P()),
        check_vma=False,
    )
```
